32 devices in a mesh: slide: 2 (over y), seq: 16 (over z, x, core), head: 1.
Axes of the slice: x: 2, y: 2, z: 4, core: 2. Of those that a mesh axis runs over, the one named last changes fastest.
Arguments:
- queries: bfloat16 [16384, 768], P(('slide', 'seq'), 'head'), parts along dimension 0, may hold values from -14 to 14
- key_states: bfloat16 [16384, 768], P(('slide', 'seq'), 'head'), parts along dimension 0, may hold values from -4 to 4
- value_states: bfloat16 [16384, 768], P(('slide', 'seq'), 'head'), parts along dimension 0, may hold values from -6 to 6
- offsets_mid: int32 [16], replicated, may hold values from 0 to 3
- offsets_top: int32 [16], replicated, may hold values from 0 to 3
- out_weight: bfloat16 [768, 768], P('head'), may hold values from -0.21875 to 0.21875
Outputs:
- projected: bfloat16 [16384, 768], P(('slide', 'seq', 'head')), parts along dimension 0
The draws below stay inside these ranges and needn't reach their ends.
There are 2 independent parts, one for each index of `slide`. The reference program is written for one: setup_inputs(seed, part) draws one part's arguments, and reference() takes and returns one part's arrays. A program takes and returns all parts, laid end to end along the dimension named above; an argument that names none is the same for every part. Nothing has to cross between parts.
All inputs are finite; a program needn't handle non-finite values.
Results may differ from the reference program's by a relative error of at most 0.0052.
Values may be sent and summed in bfloat16 or wider, within the bound.
No kernel may reach another device: no remote copies, remote signals or barrier semaphores. Data moves between devices by JAX's collectives and lax.ppermute only.
A program may use at most 64 MiB of HBM per device.

```python
import jax
import jax.numpy as jnp
from jax import lax

D = 768
HEADS = 16
SEG = 2048
SEQ = 8192
R_MID = 4
R_TOP = 4


def draw_key_states(key, part):
    own_key = jax.random.fold_in(key, 3)
    states = jnp.clip(jax.random.normal(own_key, (SEQ, D), jnp.float32), -4.0, 4.0)
    return states.astype(jnp.bfloat16)


def draw_queries(key, part):
    own_key = jax.random.fold_in(key, 5)
    states = jnp.clip(2.5 * jax.random.normal(own_key, (SEQ, D), jnp.float32), -10.0, 10.0)
    return states.astype(jnp.bfloat16)


def plant(result, key, low, high):
    index_at = [jax.random.randint(jax.random.fold_in(key, axis), (), 0, length) for axis, length in enumerate(result.shape)]
    main_axis = result.shape.index(max(result.shape))
    beside = index_at[:main_axis] + [(index_at[main_axis] + 1) % result.shape[main_axis]] + index_at[main_axis + 1:]
    return result.at[tuple(index_at)].set(low).at[tuple(beside)].set(high)


def level_of(stream_key, dims, shards, low, top_value):
    def one(dim, parts):
        draws = jax.random.uniform(jax.random.fold_in(jax.random.fold_in(stream_key, 6), dim), (parts,), jnp.float32, low / len(shards), top_value / len(shards))
        return jnp.repeat(jnp.exp(draws), dims[dim] // parts).reshape((-1,) + (1,) * (len(dims) - dim - 1))

    loudness = one(*shards[0])
    for cut in shards[1:]:
        loudness = loudness * one(*cut)
    return loudness


def centred(key, shape, scale, limit, cuts=(), dtype=jnp.bfloat16):
    array = scale * jax.random.normal(key, shape, jnp.float32)
    if cuts:
        array = array * level_of(key, shape, cuts, -0.22, 0.18)
    return jnp.clip(array, -limit, limit).astype(dtype)


def setup_inputs(seed: int = 0, part: int = 0) -> dict:
    arg_keys = jax.random.split(jax.random.key(seed), 7)
    own_keys = jax.random.split(jax.random.fold_in(arg_keys[6], part), 7)
    return {
        "queries": draw_queries(jax.random.fold_in(jax.random.fold_in(arg_keys[6], part), 71), part),
        "key_states": draw_key_states(jax.random.fold_in(jax.random.fold_in(arg_keys[6], part), 71), part),
        "value_states": centred(own_keys[2], (SEQ, D), 1.0, 6.0, ((0, 16),)),
        "offsets_mid": plant(jax.random.randint(arg_keys[3], (HEADS,), 0, R_MID), jax.random.fold_in(arg_keys[3], 1), 0, R_MID - 1).astype(jnp.int32),
        "offsets_top": plant(jax.random.randint(arg_keys[4], (HEADS,), 0, R_TOP), jax.random.fold_in(arg_keys[4], 1), 0, R_TOP - 1).astype(jnp.int32),
        "out_weight": centred(arg_keys[5], (D, D), D ** -0.5, 0.21875),
    }


def attend_head(triple_in):
    query_rows, key_rows, value_rows = triple_in
    score_scale = query_rows.shape[-1] ** -0.5
    scores = jnp.dot(query_rows, key_rows.T, preferred_element_type=jnp.float32) * score_scale
    row_max = jnp.max(scores, axis=1)
    shifted = jnp.exp(scores - row_max[:, None])
    row_total = jnp.sum(shifted, axis=1)
    weights = shifted.astype(jnp.bfloat16)
    numerator = jnp.dot(weights, value_rows, preferred_element_type=jnp.float32)
    return numerator, row_total, row_max


def pick_rows(states, offsets, rate):
    row_count, head_count, head_width = states.shape
    picker = (jnp.arange(rate)[:, None] == offsets[None, :]).astype(jnp.float32)
    folded = states.reshape(row_count // rate, rate, head_count, head_width).astype(jnp.float32)
    return jnp.einsum("arhd,rh->ahd", folded, picker).astype(jnp.bfloat16)


def level_terms(query_heads, key_heads, value_heads, offsets, rate):
    picked_q = pick_rows(query_heads, offsets, rate)
    picked_k = pick_rows(key_heads, offsets, rate)
    picked_v = pick_rows(value_heads, offsets, rate)
    picked_count, head_count, head_width = picked_q.shape
    group_count = picked_count // SEG

    def arrange(states):
        return states.reshape(group_count, SEG, head_count, head_width).transpose(2, 0, 1, 3)

    def per_head(triple_in):
        return lax.map(attend_head, triple_in)

    numerator, row_total, row_max = lax.map(per_head, (arrange(picked_q), arrange(picked_k), arrange(picked_v)))
    numerator = numerator.transpose(1, 2, 0, 3).reshape(picked_count, head_count, head_width)
    row_total = row_total.transpose(1, 2, 0).reshape(picked_count, head_count)
    row_max = row_max.transpose(1, 2, 0).reshape(picked_count, head_count)
    chosen = jnp.arange(rate)[:, None] == offsets[None, :]
    full_num = jnp.where(chosen[None, :, :, None], numerator[:, None], 0.0).reshape(picked_count * rate, head_count, head_width)
    full_total = jnp.where(chosen[None], row_total[:, None], 0.0).reshape(picked_count * rate, head_count)
    full_max = jnp.where(chosen[None], row_max[:, None], -1e30).reshape(picked_count * rate, head_count)
    return full_num, full_total, full_max


def reference(queries, key_states, value_states, offsets_mid, offsets_top, out_weight):
    head_width = D // HEADS
    query_heads = queries.reshape(SEQ, HEADS, head_width)
    key_heads = key_states.reshape(SEQ, HEADS, head_width)
    value_heads = value_states.reshape(SEQ, HEADS, head_width)
    zero_offsets = jnp.zeros((HEADS,), jnp.int32)
    levels = [
        level_terms(query_heads, key_heads, value_heads, zero_offsets, 1),
        level_terms(query_heads, key_heads, value_heads, offsets_mid.astype(jnp.int32), R_MID),
        level_terms(query_heads, key_heads, value_heads, offsets_top.astype(jnp.int32), R_TOP),
    ]
    overall = jnp.maximum(jnp.maximum(levels[0][2], levels[1][2]), levels[2][2])
    numerator = jnp.zeros((SEQ, HEADS, head_width), jnp.float32)
    row_total = jnp.zeros((SEQ, HEADS), jnp.float32)
    for level_num, level_total, level_max in levels:
        factor = jnp.exp(level_max - overall)
        numerator = numerator + factor[..., None] * level_num
        row_total = row_total + factor * level_total
    attention = (numerator / row_total[..., None]).astype(jnp.bfloat16).reshape(SEQ, D)
    return jnp.dot(attention, out_weight, preferred_element_type=jnp.float32).astype(jnp.bfloat16)
```

```python
import functools

import jax
import jax.numpy as jnp
from jax import lax
from jax.experimental import pallas as pl
from jax.experimental.pallas import tpu as pltpu
from jax.sharding import PartitionSpec as P

SEG = 2048
LOG2E = 1.4426950408889634
VMEM_LIMIT = 40 * 1024 * 1024
BF16 = jnp.bfloat16
F32 = jnp.float32


def partner_2(block, axis, apart):
    count = lax.axis_size(axis)
    route = []
    for low in range(count):
        high = low | 1 << apart
        if high != low and high < count:
            route += [(low, high), (high, low)]
    return lax.ppermute(block, axis, route)


def attend_head(triple_in):
    query_rows, key_rows, value_rows = triple_in
    score_scale = query_rows.shape[-1] ** (-0.5)
    scores = jnp.dot(query_rows, key_rows.T, preferred_element_type=jnp.float32) * score_scale
    row_max = jnp.max(scores, axis=1)
    shifted = jnp.exp(scores - row_max[:, None])
    row_total = jnp.sum(shifted, axis=1)
    weights = shifted.astype(jnp.bfloat16)
    numerator = jnp.dot(weights, value_rows, preferred_element_type=jnp.float32)
    return (numerator, row_total, row_max)


def attend_local(query_rows, pair_rows):
    return lax.map(
        attend_head,
        (
            query_rows.transpose(1, 0, 2),
            pair_rows[:, 0].transpose(1, 0, 2),
            pair_rows[:, 1].transpose(1, 0, 2),
        ),
    )


def pick_rows(states, offsets, rate):
    row_count, inner_count, heads_here, head_width = states.shape
    picker = (jnp.arange(rate)[:, None] == offsets[None, :]).astype(jnp.bfloat16)
    folded = states.reshape(row_count // rate, rate, inner_count, heads_here, head_width)
    return jnp.einsum("archd,rh->achd", folded, picker, preferred_element_type=jnp.float32).astype(
        jnp.bfloat16
    )


def spread_back(numerator, row_total, row_max, offsets, rate):
    heads_here, picked_count, head_width = numerator.shape
    chosen = jnp.arange(rate)[:, None] == offsets[None, :]
    full_num = jnp.where(chosen[None, :, :, None], numerator.transpose(1, 0, 2)[:, None], 0.0)
    full_total = jnp.where(chosen[None], row_total.T[:, None], 0.0)
    full_max = jnp.where(chosen[None], row_max.T[:, None], -1e30)
    return (
        full_num.reshape(picked_count * rate, heads_here, head_width),
        full_total.reshape(picked_count * rate, heads_here),
        full_max.reshape(picked_count * rate, heads_here),
    )


def doubling(buffer, steps_count):
    position = lax.axis_index("seq")
    for bit_index in range(steps_count):
        partner = partner_2(buffer, "seq", bit_index)
        is_lower = position >> bit_index & 1 == 0
        buffer = jnp.where(
            is_lower, jnp.concatenate([buffer, partner], 0), jnp.concatenate([partner, buffer], 0)
        )
    return buffer


def shards_general(queries, key_states, value_states, offsets_mid, offsets_top, out_weight):
    tok_rows = queries.shape[0]
    heads_local = offsets_mid.shape[0] // lax.axis_size("head")
    head_size = queries.shape[1] // heads_local
    seq_devices = lax.axis_size("seq")
    seq_total = tok_rows * seq_devices
    width_mid = min(16 * SEG, seq_total)
    rate_mid = width_mid // SEG
    rate_top = seq_total // SEG
    start_head = lax.axis_index("head") * heads_local
    mid_local = lax.dynamic_slice(offsets_mid, (start_head,), (heads_local,))
    top_local = lax.dynamic_slice(offsets_top, (start_head,), (heads_local,))
    query_heads = queries.reshape(tok_rows, 1, heads_local, head_size)
    paired = jnp.stack([key_states, value_states], axis=1).reshape(
        tok_rows, 2, heads_local, head_size
    )
    near_bits = (SEG // tok_rows).bit_length() - 1
    near_rows = doubling(paired.reshape(tok_rows, -1), near_bits).reshape(
        SEG, 2, heads_local, head_size
    )
    near_num, near_total, near_max = attend_local(query_heads[:, 0], near_rows)
    level_near = spread_back(
        near_num, near_total, near_max, jnp.zeros((heads_local,), jnp.int32), 1
    )
    mid_q = pick_rows(query_heads, mid_local, rate_mid)[:, 0]
    mid_kv = pick_rows(paired, mid_local, rate_mid)
    mid_group = width_mid // tok_rows
    mid_bits = mid_group.bit_length() - 1
    mid_rows = doubling(mid_kv.reshape(mid_kv.shape[0], -1), mid_bits).reshape(
        SEG, 2, heads_local, head_size
    )
    mid_num, mid_total, mid_max = attend_local(mid_q, mid_rows)
    level_mid = spread_back(mid_num, mid_total, mid_max, mid_local, rate_mid)
    top_q = pick_rows(query_heads, top_local, rate_top)[:, 0]
    top_kv = pick_rows(paired, top_local, rate_top)
    top_rows = lax.all_gather(
        top_kv.reshape(top_kv.shape[0], -1), "seq", axis=0, tiled=True
    ).reshape(SEG, 2, heads_local, head_size)
    top_num, top_total, top_max = attend_local(top_q, top_rows)
    level_top = spread_back(top_num, top_total, top_max, top_local, rate_top)
    levels = [level_near, level_mid, level_top]
    overall = jnp.maximum(jnp.maximum(level_near[2], level_mid[2]), level_top[2])
    numerator = jnp.zeros((tok_rows, heads_local, head_size), jnp.float32)
    row_total = jnp.zeros((tok_rows, heads_local), jnp.float32)
    for level_num, level_total, level_max in levels:
        factor = jnp.exp(level_max - overall)
        numerator = numerator + factor[..., None] * level_num
        row_total = row_total + factor * level_total
    attention = (
        (numerator / row_total[..., None])
        .astype(jnp.bfloat16)
        .reshape(tok_rows, heads_local * head_size)
    )
    result = lax.psum_scatter(
        jnp.dot(attention, out_weight, preferred_element_type=jnp.float32),
        "head",
        scatter_dimension=0,
        tiled=True,
    )
    return result.astype(jnp.bfloat16)


RATE = 4
GROUP = 4
HG = 4
DH = 48
BLK = 128
TOK = 512
DX = 64


def dot(a, b):
    return jnp.dot(a, b, preferred_element_type=F32)


def dot_nt(a, b):
    return lax.dot_general(a, b, (((1,), (1,)), ((), ())), preferred_element_type=F32)


def dot_tn(a, b):
    return lax.dot_general(a, b, (((0,), (0,)), ((), ())), preferred_element_type=F32)


def class_of_slots(off_mid, off_top):
    first = off_mid
    second = jnp.where(off_top == off_mid, lax.rem(off_mid + 1, RATE), off_top)
    free0 = (first != 0) & (second != 0)
    free1 = (first != 1) & (second != 1)
    third = jnp.where(free0, 0, jnp.where(free1, 1, 2))
    return first, second, third, 6 - first - second - third


def to_class_major(block):
    row = lax.broadcasted_iota(jnp.int32, (TOK, TOK), 0)
    col = lax.broadcasted_iota(jnp.int32, (TOK, TOK), 1)
    picker = (col == RATE * (row % BLK) + row // BLK).astype(BF16)
    ordered = dot(picker, block).astype(BF16)
    step = 256
    eye = (
        lax.broadcasted_iota(jnp.int32, (step, step), 0)
        == lax.broadcasted_iota(jnp.int32, (step, step), 1)
    ).astype(BF16)
    return [
        dot_nt(eye, ordered[:, c : c + step]).astype(BF16)
        for c in range(0, block.shape[1], step)
    ]


def fill_class_major(block, scratch):
    for i, part in enumerate(to_class_major(block)):
        scratch[i * 256 : (i + 1) * 256, :] = part


def lane_block(index):
    return pl.ds(pl.multiple_of(index * BLK, BLK), BLK)


def pack_kv_kernel(pos, mid, top, k_ref, v_ref, *rest):
    sel, far = rest[:GROUP], rest[GROUP : 2 * GROUP]
    k_t, v_t = rest[2 * GROUP :]
    fill_class_major(k_ref[...], k_t)
    fill_class_major(v_ref[...], v_t)
    for j in range(GROUP):
        group = pos[0] ^ j
        for h in range(HG):
            head = group * HG + h
            rows = pl.ds(pl.multiple_of(head * DH, 16), DH)
            slots = class_of_slots(mid[head], top[head])
            for s in range(RATE):
                out = sel[j] if s < 2 else far[j]
                lanes = slice((s % 2) * BLK, (s % 2 + 1) * BLK)
                out[h, 0:DH, lanes] = k_t[rows, lane_block(slots[s])]
                out[h, DH : 2 * DH, lanes] = v_t[rows, lane_block(slots[s])]


def pack_q_kernel(pos, q_ref, *rest):
    outs, q_t = rest[:GROUP], rest[GROUP]
    fill_class_major(q_ref[...], q_t)
    for j in range(GROUP):
        group = pos[0] ^ j
        for h in range(HG):
            rows = pl.ds(pl.multiple_of((group * HG + h) * DH, 16), DH)
            outs[j][h] = q_t[rows, :]


def split_query(q):
    scaled = q.astype(F32) * (DH**-0.5 * LOG2E)
    high = scaled.astype(BF16)
    low = (scaled - high.astype(F32)).astype(BF16)
    return jnp.concatenate([high, low], axis=0)


def twice_keys(keys_t):
    both = jnp.concatenate([keys_t, keys_t], axis=0).astype(F32)
    return both.T.astype(BF16)


def near_kernel(first, pos, mid, top, *refs):
    kv = refs[:GROUP]
    q = refs[GROUP : 2 * GROUP]
    refs = refs[2 * GROUP :]
    if first:
        acc_ref, max_ref, q_s, k_s, v_s = refs
    else:
        acc_in, max_in, acc_ref, max_ref, q_s, k_s, v_s = refs
    head = pos[0] * HG + pl.program_id(0)
    off_mid, off_top = mid[head], top[head]
    for j in range(GROUP):
        q_s[j] = split_query(q[j][0])
        for s in range(2):
            lanes = slice(s * BLK, (s + 1) * BLK)
            k_s[s, j * BLK : (j + 1) * BLK, :] = twice_keys(kv[j][0, 0:DH, lanes])
            v_s[s, 0:DH, j * BLK : (j + 1) * BLK] = kv[j][0, DH : 2 * DH, lanes]
    v_s[:, DH:DX, :] = jnp.ones((2, DX - DH, TOK), BF16)

    if first:
        cls = lax.broadcasted_iota(jnp.int32, (1, TOK), 1) // BLK
        is_mid = (cls == off_mid).astype(F32)
        is_top = (cls == off_top).astype(F32)
        same = (off_mid == off_top).astype(F32)
        times = (1.0 + is_mid + is_top * same, 1.0 + is_top * (1.0 - same))
        extra = [
            jnp.where(t > 2.5, 1.584962500721156, jnp.where(t > 1.5, 1.0, 0.0)) for t in times
        ]

    def step(i, carry):
        query = q_s[i]
        scores = [dot(k_s[s], query) for s in range(2)]
        top_score = jnp.maximum(
            jnp.max(scores[0], axis=0, keepdims=True), jnp.max(scores[1], axis=0, keepdims=True)
        )
        if first:
            shift = [top_score - extra[0], top_score - extra[1]]
        else:
            old_max = max_in[0, i, 0:1, :]
            top_score = jnp.maximum(top_score, old_max)
            shift = [top_score, top_score]
        acc = None
        for s in range(2):
            weights = jnp.exp2(scores[s] - shift[s]).astype(BF16)
            part = dot(v_s[s], weights)
            acc = part if acc is None else acc + part
        if not first:
            acc = acc + acc_in[0, i] * jnp.exp2(old_max - top_score)
        acc_ref[0, i] = acc
        max_ref[0, i] = jnp.broadcast_to(top_score, (8, TOK))
        return carry

    lax.fori_loop(0, GROUP, step, 0, unroll=2)


def far_kernel(last, pos, mid, top, *refs):
    kv = refs[:2]
    q = refs[2 : 2 + GROUP]
    acc_in, max_in = refs[2 + GROUP : 4 + GROUP]
    refs = refs[4 + GROUP :]
    if last:
        outs, (acc_ref, max_ref, q_s, k_s, v_s) = refs[:GROUP], refs[GROUP:]
    else:
        acc_ref, max_ref, q_s, k_s, v_s = refs
    head = pos[0] * HG + pl.program_id(0)
    off_mid, off_top = mid[head], top[head]
    slot_top = jnp.where(off_mid == off_top, 0, 1)
    acc_ref[...] = acc_in[...]
    max_ref[...] = max_in[...]
    for level, (cls, slot) in enumerate(((off_mid, 0), (off_top, slot_top))):
        for j in range(GROUP):
            here = slice(j * BLK, (j + 1) * BLK)
            source = kv[j // 2].at[j % 2, 0]
            lanes = lane_block(slot)
            k_s[level, here, :] = twice_keys(source[0:DH, lanes])
            v_s[level, 0:DH, here] = source[DH : 2 * DH, lanes]
            q_s[level, :, here] = split_query(q[j][0, :, lane_block(cls)])
    v_s[:, DH:DX, :] = jnp.ones((2, DX - DH, TOK), BF16)
    scores = [dot(k_s[level], q_s[level]) for level in range(2)]
    for level, cls in enumerate((off_mid, off_top)):
        lanes = lane_block(cls)
        old_max = jnp.concatenate(
            [max_ref[0, j, 0:1, lanes] for j in range(GROUP)], axis=1
        )
        top_score = jnp.maximum(old_max, jnp.max(scores[level], axis=0, keepdims=True))
        weights = jnp.exp2(scores[level] - top_score).astype(BF16)
        part = dot(v_s[level], weights)
        factor = jnp.exp2(old_max - top_score)
        for j in range(GROUP):
            here = slice(j * BLK, (j + 1) * BLK)
            acc_ref[0, j, :, lanes] = (
                acc_ref[0, j, :, lanes] * factor[:, here] + part[:, here]
            )
            max_ref[0, j, :, lanes] = jnp.broadcast_to(top_score[:, here], (8, BLK))
    if last:
        for j in range(GROUP):
            total = acc_ref[0, j, DH : DH + 1, :]
            outs[j][0] = (acc_ref[0, j, 0:DH, :] / total).astype(BF16)


def project_kernel(pos, *refs):
    parts = refs[:GROUP]
    w_ref, out_ref = refs[GROUP:]
    total = None
    for j in range(GROUP):
        rows = pl.ds(pl.multiple_of((pos[0] ^ j) * (HG * DH), 16), HG * DH)
        part = dot_tn(parts[j][...], w_ref[rows, :])
        total = part if total is None else total + part
    row = lax.broadcasted_iota(jnp.int32, (TOK, TOK), 0)
    col = lax.broadcasted_iota(jnp.int32, (TOK, TOK), 1)
    picker = (row == RATE * (col % BLK) + col // BLK).astype(BF16)
    out_ref[...] = dot(picker, total.astype(BF16)).astype(BF16)


def params():
    return pltpu.CompilerParams(vmem_limit_bytes=VMEM_LIMIT)


def cost(scores):
    return pl.CostEstimate(
        flops=scores * 1024, bytes_accessed=1 << 20, transcendentals=scores
    )


def whole(shape):
    return pl.BlockSpec(shape, lambda *_: (0,) * len(shape))


def per_head(shape, axis=0):
    return pl.BlockSpec(shape, lambda h, *_: (0,) * axis + (h,) + (0,) * (len(shape) - axis - 1))


def call(kernel, scalars, args, grid, in_specs, out_specs, out_shape, scratch, estimate):
    return pl.pallas_call(
        kernel,
        grid_spec=pltpu.PrefetchScalarGridSpec(
            num_scalar_prefetch=len(scalars),
            grid=grid,
            in_specs=in_specs,
            out_specs=out_specs,
            scratch_shapes=scratch,
        ),
        out_shape=out_shape,
        compiler_params=params(),
        cost_estimate=estimate,
    )(*scalars, *args)


def within(array, apart):
    count = lax.axis_size("seq")
    return lax.ppermute(array, "seq", [(i, i ^ apart) for i in range(count)])


def around(array):
    count = lax.axis_size("seq")
    return lax.ppermute(array, "seq", [(i, (i + GROUP) % count) for i in range(count)])


def shards_four(queries, key_states, value_states, offsets_mid, offsets_top, out_weight):
    width = queries.shape[1]
    heads_shape = jax.ShapeDtypeStruct((HG, 2 * DH, 2 * BLK), BF16)
    query_shape = jax.ShapeDtypeStruct((HG, DH, TOK), BF16)
    pos = (lax.axis_index("seq") % GROUP).astype(jnp.int32).reshape(1)
    offs = (pos, offsets_mid, offsets_top)

    packed = call(
        pack_kv_kernel, offs, (key_states, value_states), (1,),
        [whole((TOK, width))] * 2,
        [whole(heads_shape.shape)] * (2 * GROUP),
        [heads_shape] * (2 * GROUP),
        [pltpu.VMEM((width, TOK), BF16)] * 2,
        cost(1 << 19),
    )
    sel, far = list(packed[:GROUP]), list(packed[GROUP:])
    for j in range(1, GROUP):
        sel[j] = within(sel[j], j)
    query = call(
        pack_q_kernel, (pos,), (queries,), (1,),
        [whole((TOK, width))],
        [whole(query_shape.shape)] * GROUP,
        [query_shape] * GROUP,
        [pltpu.VMEM((width, TOK), BF16)],
        cost(1 << 18),
    )
    query = list(query)
    for j in range(1, GROUP):
        query[j] = within(query[j], j)
    for j in range(1, GROUP):
        far[j] = within(far[j], j)

    kv_spec = per_head((1, 2 * DH, 2 * BLK))
    q_spec = per_head((1, DH, TOK))
    acc_shape = jax.ShapeDtypeStruct((HG, GROUP, DX, TOK), F32)
    max_shape = jax.ShapeDtypeStruct((HG, GROUP, 8, TOK), F32)
    acc_spec = per_head((1, GROUP, DX, TOK))
    max_spec = per_head((1, GROUP, 8, TOK))
    near_scratch = [
        pltpu.VMEM((GROUP, 2 * DH, TOK), BF16),
        pltpu.VMEM((2, TOK, 2 * DH), BF16),
        pltpu.VMEM((2, DX, TOK), BF16),
    ]
    far_scratch = [
        pltpu.VMEM((2, 2 * DH, TOK), BF16),
        pltpu.VMEM((2, TOK, 2 * DH), BF16),
        pltpu.VMEM((2, DX, TOK), BF16),
    ]

    def near(first, keys, state):
        return call(
            functools.partial(near_kernel, first), offs, (*keys, *query, *state), (HG,),
            [kv_spec] * GROUP + [q_spec] * GROUP + ([] if first else [acc_spec, max_spec]),
            [acc_spec, max_spec],
            [acc_shape, max_shape],
            near_scratch,
            cost(HG * 2 * TOK * GROUP * TOK),
        )

    pair_spec = per_head((2, 1, 2 * DH, 2 * BLK), 1)

    def beyond(last, pairs, state):
        return call(
            functools.partial(far_kernel, last), offs, (*pairs, *query, *state), (HG,),
            [pair_spec] * 2 + [q_spec] * GROUP + [acc_spec, max_spec],
            [q_spec] * GROUP if last else [acc_spec, max_spec],
            [query_shape] * GROUP if last else [acc_shape, max_shape],
            ([pltpu.VMEM((1, GROUP, DX, TOK), F32), pltpu.VMEM((1, GROUP, 8, TOK), F32)] if last else [])
            + far_scratch,
            cost(HG * 2 * TOK * TOK),
        )

    pairs = [jnp.stack(sel[:2]), jnp.stack(sel[2:])]
    rings = []
    for _ in range(RATE - 1):
        pairs = [around(p) for p in pairs]
        rings.append(pairs)

    state = near(True, sel, ())
    state = beyond(False, rings[0], state)
    state = near(False, far, state)
    state = beyond(False, rings[1], state)
    parts = list(beyond(True, rings[2], state))
    for j in range(1, GROUP):
        parts[j] = within(parts[j], j)
    parts = [p.reshape(HG * DH, TOK) for p in parts]
    return call(
        project_kernel, (pos,), (*parts, out_weight), (1,),
        [whole((HG * DH, TOK))] * GROUP + [whole((width, width))],
        whole((TOK, width)),
        jax.ShapeDtypeStruct((TOK, width), BF16),
        [],
        cost(1 << 18),
    )


def shards(queries, key_states, value_states, offsets_mid, offsets_top, out_weight):
    tokens, width = queries.shape
    heads = offsets_mid.shape[0]
    fits = (
        lax.axis_size("head") == 1
        and lax.axis_size("seq") == GROUP * RATE
        and tokens == TOK
        and heads == GROUP * HG
        and width == heads * DH
    )
    run = shards_four if fits else shards_general
    return run(queries, key_states, value_states, offsets_mid, offsets_top, out_weight)


def solution(mesh):
    in_specs = (
        P(("slide", "seq"), "head"),
        P(("slide", "seq"), "head"),
        P(("slide", "seq"), "head"),
        P(),
        P(),
        P("head", None),
    )
    out_specs = P(("slide", "seq", "head"), None)
    return jax.shard_map(shards, mesh=mesh, in_specs=in_specs, out_specs=out_specs, check_vma=False)
```

```python
import functools

import jax
import jax.numpy as jnp
from jax import lax
from jax.experimental import pallas as pl
from jax.experimental.pallas import tpu as pltpu
from jax.sharding import PartitionSpec as P

SEG = 2048
LOG2E = 1.4426950408889634
VMEM_LIMIT = 40 * 1024 * 1024
VMEM_MOST = 60 * 1024 * 1024
BF16 = jnp.bfloat16
F32 = jnp.float32


def partner_2(block, axis, apart):
    count = lax.axis_size(axis)
    route = []
    for low in range(count):
        high = low | 1 << apart
        if high != low and high < count:
            route += [(low, high), (high, low)]
    return lax.ppermute(block, axis, route)


def attend_head(triple_in):
    query_rows, key_rows, value_rows = triple_in
    score_scale = query_rows.shape[-1] ** (-0.5)
    scores = jnp.dot(query_rows, key_rows.T, preferred_element_type=jnp.float32) * score_scale
    row_max = jnp.max(scores, axis=1)
    shifted = jnp.exp(scores - row_max[:, None])
    row_total = jnp.sum(shifted, axis=1)
    weights = shifted.astype(jnp.bfloat16)
    numerator = jnp.dot(weights, value_rows, preferred_element_type=jnp.float32)
    return (numerator, row_total, row_max)


def attend_local(query_rows, pair_rows):
    return lax.map(
        attend_head,
        (
            query_rows.transpose(1, 0, 2),
            pair_rows[:, 0].transpose(1, 0, 2),
            pair_rows[:, 1].transpose(1, 0, 2),
        ),
    )


def pick_rows(states, offsets, rate):
    row_count, inner_count, heads_here, head_width = states.shape
    picker = (jnp.arange(rate)[:, None] == offsets[None, :]).astype(jnp.bfloat16)
    folded = states.reshape(row_count // rate, rate, inner_count, heads_here, head_width)
    return jnp.einsum("archd,rh->achd", folded, picker, preferred_element_type=jnp.float32).astype(
        jnp.bfloat16
    )


def spread_back(numerator, row_total, row_max, offsets, rate):
    heads_here, picked_count, head_width = numerator.shape
    chosen = jnp.arange(rate)[:, None] == offsets[None, :]
    full_num = jnp.where(chosen[None, :, :, None], numerator.transpose(1, 0, 2)[:, None], 0.0)
    full_total = jnp.where(chosen[None], row_total.T[:, None], 0.0)
    full_max = jnp.where(chosen[None], row_max.T[:, None], -1e30)
    return (
        full_num.reshape(picked_count * rate, heads_here, head_width),
        full_total.reshape(picked_count * rate, heads_here),
        full_max.reshape(picked_count * rate, heads_here),
    )


def doubling(buffer, steps_count):
    position = lax.axis_index("seq")
    for bit_index in range(steps_count):
        partner = partner_2(buffer, "seq", bit_index)
        is_lower = position >> bit_index & 1 == 0
        buffer = jnp.where(
            is_lower, jnp.concatenate([buffer, partner], 0), jnp.concatenate([partner, buffer], 0)
        )
    return buffer


def shards_general(queries, key_states, value_states, offsets_mid, offsets_top, out_weight):
    tok_rows = queries.shape[0]
    heads_local = offsets_mid.shape[0] // lax.axis_size("head")
    head_size = queries.shape[1] // heads_local
    seq_devices = lax.axis_size("seq")
    seq_total = tok_rows * seq_devices
    width_mid = min(16 * SEG, seq_total)
    rate_mid = width_mid // SEG
    rate_top = seq_total // SEG
    start_head = lax.axis_index("head") * heads_local
    mid_local = lax.dynamic_slice(offsets_mid, (start_head,), (heads_local,))
    top_local = lax.dynamic_slice(offsets_top, (start_head,), (heads_local,))
    query_heads = queries.reshape(tok_rows, 1, heads_local, head_size)
    paired = jnp.stack([key_states, value_states], axis=1).reshape(
        tok_rows, 2, heads_local, head_size
    )
    near_bits = (SEG // tok_rows).bit_length() - 1
    near_rows = doubling(paired.reshape(tok_rows, -1), near_bits).reshape(
        SEG, 2, heads_local, head_size
    )
    near_num, near_total, near_max = attend_local(query_heads[:, 0], near_rows)
    level_near = spread_back(
        near_num, near_total, near_max, jnp.zeros((heads_local,), jnp.int32), 1
    )
    mid_q = pick_rows(query_heads, mid_local, rate_mid)[:, 0]
    mid_kv = pick_rows(paired, mid_local, rate_mid)
    mid_group = width_mid // tok_rows
    mid_bits = mid_group.bit_length() - 1
    mid_rows = doubling(mid_kv.reshape(mid_kv.shape[0], -1), mid_bits).reshape(
        SEG, 2, heads_local, head_size
    )
    mid_num, mid_total, mid_max = attend_local(mid_q, mid_rows)
    level_mid = spread_back(mid_num, mid_total, mid_max, mid_local, rate_mid)
    top_q = pick_rows(query_heads, top_local, rate_top)[:, 0]
    top_kv = pick_rows(paired, top_local, rate_top)
    top_rows = lax.all_gather(
        top_kv.reshape(top_kv.shape[0], -1), "seq", axis=0, tiled=True
    ).reshape(SEG, 2, heads_local, head_size)
    top_num, top_total, top_max = attend_local(top_q, top_rows)
    level_top = spread_back(top_num, top_total, top_max, top_local, rate_top)
    levels = [level_near, level_mid, level_top]
    overall = jnp.maximum(jnp.maximum(level_near[2], level_mid[2]), level_top[2])
    numerator = jnp.zeros((tok_rows, heads_local, head_size), jnp.float32)
    row_total = jnp.zeros((tok_rows, heads_local), jnp.float32)
    for level_num, level_total, level_max in levels:
        factor = jnp.exp(level_max - overall)
        numerator = numerator + factor[..., None] * level_num
        row_total = row_total + factor * level_total
    attention = (
        (numerator / row_total[..., None])
        .astype(jnp.bfloat16)
        .reshape(tok_rows, heads_local * head_size)
    )
    result = lax.psum_scatter(
        jnp.dot(attention, out_weight, preferred_element_type=jnp.float32),
        "head",
        scatter_dimension=0,
        tiled=True,
    )
    return result.astype(jnp.bfloat16)


RATE = 4
GROUP = 4
HG = 4
DH = 48
BLK = 128
TOK = 512
DX = 64


def dot(a, b):
    return jnp.dot(a, b, preferred_element_type=F32)


def dot_nt(a, b):
    return lax.dot_general(a, b, (((1,), (1,)), ((), ())), preferred_element_type=F32)


def dot_tn(a, b):
    return lax.dot_general(a, b, (((0,), (0,)), ((), ())), preferred_element_type=F32)


def class_of_slots(off_mid, off_top):
    first = off_mid
    second = jnp.where(off_top == off_mid, lax.rem(off_mid + 1, RATE), off_top)
    free0 = (first != 0) & (second != 0)
    free1 = (first != 1) & (second != 1)
    third = jnp.where(free0, 0, jnp.where(free1, 1, 2))
    return first, second, third, 6 - first - second - third


def to_class_major(block):
    row = lax.broadcasted_iota(jnp.int32, (TOK, TOK), 0)
    col = lax.broadcasted_iota(jnp.int32, (TOK, TOK), 1)
    picker = (col == RATE * (row % BLK) + row // BLK).astype(BF16)
    ordered = dot(picker, block).astype(BF16)
    step = 256
    eye = (
        lax.broadcasted_iota(jnp.int32, (step, step), 0)
        == lax.broadcasted_iota(jnp.int32, (step, step), 1)
    ).astype(BF16)
    return [
        dot_nt(eye, ordered[:, c : c + step]).astype(BF16)
        for c in range(0, block.shape[1], step)
    ]


def fill_class_major(block, scratch):
    for i, part in enumerate(to_class_major(block)):
        scratch[i * 256 : (i + 1) * 256, :] = part


def lane_block(index):
    return pl.ds(pl.multiple_of(index * BLK, BLK), BLK)


def pack_kv_kernel(pos, mid, top, k_ref, v_ref, *rest):
    sel, far = rest[:GROUP], rest[GROUP : 2 * GROUP]
    k_t, v_t = rest[2 * GROUP :]
    fill_class_major(k_ref[...], k_t)
    fill_class_major(v_ref[...], v_t)
    for j in range(GROUP):
        group = pos[0] ^ j
        for h in range(HG):
            head = group * HG + h
            rows = pl.ds(pl.multiple_of(head * DH, 16), DH)
            slots = class_of_slots(mid[head], top[head])
            for s in range(RATE):
                out = sel[j] if s < 2 else far[j]
                lanes = slice((s % 2) * BLK, (s % 2 + 1) * BLK)
                out[h, 0:DH, lanes] = k_t[rows, lane_block(slots[s])]
                out[h, DH : 2 * DH, lanes] = v_t[rows, lane_block(slots[s])]


def pack_q_kernel(pos, q_ref, *rest):
    outs, q_t = rest[:GROUP], rest[GROUP]
    fill_class_major(q_ref[...], q_t)
    for j in range(GROUP):
        group = pos[0] ^ j
        for h in range(HG):
            rows = pl.ds(pl.multiple_of((group * HG + h) * DH, 16), DH)
            outs[j][h] = q_t[rows, :]


def split_query(q):
    scaled = q.astype(F32) * (DH**-0.5 * LOG2E)
    high = scaled.astype(BF16)
    low = (scaled - high.astype(F32)).astype(BF16)
    return jnp.concatenate([high, low], axis=0)


def twice_keys(keys_t):
    both = jnp.concatenate([keys_t, keys_t], axis=0).astype(F32)
    return both.T.astype(BF16)


def near_kernel(first, pos, mid, top, *refs):
    kv = refs[:GROUP]
    q = refs[GROUP : 2 * GROUP]
    refs = refs[2 * GROUP :]
    if first:
        acc_ref, max_ref, q_s, k_s, v_s = refs
    else:
        acc_in, max_in, acc_ref, max_ref, q_s, k_s, v_s = refs
    head = pos[0] * HG + pl.program_id(0)
    off_mid, off_top = mid[head], top[head]
    for j in range(GROUP):
        q_s[j] = split_query(q[j][0])
        for s in range(2):
            lanes = slice(s * BLK, (s + 1) * BLK)
            k_s[s, j * BLK : (j + 1) * BLK, :] = twice_keys(kv[j][0, 0:DH, lanes])
            v_s[s, 0:DH, j * BLK : (j + 1) * BLK] = kv[j][0, DH : 2 * DH, lanes]
    v_s[:, DH:DX, :] = jnp.ones((2, DX - DH, TOK), BF16)

    if first:
        cls = lax.broadcasted_iota(jnp.int32, (1, TOK), 1) // BLK
        is_mid = (cls == off_mid).astype(F32)
        is_top = (cls == off_top).astype(F32)
        same = (off_mid == off_top).astype(F32)
        times = (1.0 + is_mid + is_top * same, 1.0 + is_top * (1.0 - same))
        extra = [
            jnp.where(t > 2.5, 1.584962500721156, jnp.where(t > 1.5, 1.0, 0.0)) for t in times
        ]

    def block(i):
        return i // 2, slice(i % 2 * 2 * BLK, (i % 2 + 1) * 2 * BLK)

    def score(i):
        j, lanes = block(i)
        query = q_s[j, :, lanes]
        return [dot(k_s[s], query) for s in range(2)]

    count = 2 * GROUP
    scores = score(0)
    for i in range(count):
        j, lanes = block(i)
        following = score(i + 1) if i + 1 < count else None
        top_score = jnp.maximum(
            jnp.max(scores[0], axis=0, keepdims=True), jnp.max(scores[1], axis=0, keepdims=True)
        )
        if first:
            shift = [top_score - extra[0][:, lanes], top_score - extra[1][:, lanes]]
        else:
            old_max = max_in[0, j, 0:1, lanes]
            top_score = jnp.maximum(top_score, old_max)
            shift = [top_score, top_score]
        acc = None
        for s in range(2):
            weights = jnp.exp2(scores[s] - shift[s]).astype(BF16)
            part = dot(v_s[s], weights)
            acc = part if acc is None else acc + part
        if not first:
            acc = acc + acc_in[0, j, :, lanes] * jnp.exp2(old_max - top_score)
        acc_ref[0, j, :, lanes] = acc
        max_ref[0, j, :, lanes] = jnp.broadcast_to(top_score, (8, 2 * BLK))
        scores = following


def far_kernel(last, pos, mid, top, *refs):
    kv = refs[:2]
    q = refs[2 : 2 + GROUP]
    acc_in, max_in = refs[2 + GROUP : 4 + GROUP]
    refs = refs[4 + GROUP :]
    if last:
        outs, (acc_ref, max_ref, q_s, k_s, v_s) = refs[:GROUP], refs[GROUP:]
    else:
        acc_ref, max_ref, q_s, k_s, v_s = refs
    head = pos[0] * HG + pl.program_id(0)
    off_mid, off_top = mid[head], top[head]
    slot_top = jnp.where(off_mid == off_top, 0, 1)
    acc_ref[...] = acc_in[...]
    max_ref[...] = max_in[...]
    for level, (cls, slot) in enumerate(((off_mid, 0), (off_top, slot_top))):
        for j in range(GROUP):
            here = slice(j * BLK, (j + 1) * BLK)
            source = kv[j // 2].at[j % 2, 0]
            lanes = lane_block(slot)
            k_s[level, here, :] = twice_keys(source[0:DH, lanes])
            v_s[level, 0:DH, here] = source[DH : 2 * DH, lanes]
            q_s[level, :, here] = split_query(q[j][0, :, lane_block(cls)])
    v_s[:, DH:DX, :] = jnp.ones((2, DX - DH, TOK), BF16)
    scores = [dot(k_s[level], q_s[level]) for level in range(2)]
    for level, cls in enumerate((off_mid, off_top)):
        lanes = lane_block(cls)
        old_max = jnp.concatenate(
            [max_ref[0, j, 0:1, lanes] for j in range(GROUP)], axis=1
        )
        top_score = jnp.maximum(old_max, jnp.max(scores[level], axis=0, keepdims=True))
        weights = jnp.exp2(scores[level] - top_score).astype(BF16)
        part = dot(v_s[level], weights)
        factor = jnp.exp2(old_max - top_score)
        for j in range(GROUP):
            here = slice(j * BLK, (j + 1) * BLK)
            acc_ref[0, j, :, lanes] = (
                acc_ref[0, j, :, lanes] * factor[:, here] + part[:, here]
            )
            max_ref[0, j, :, lanes] = jnp.broadcast_to(top_score[:, here], (8, BLK))
    if last:
        for j in range(GROUP):
            total = acc_ref[0, j, DH : DH + 1, :]
            outs[j][0] = (acc_ref[0, j, 0:DH, :] / total).astype(BF16)


def project_kernel(pos, *refs):
    parts = refs[:GROUP]
    w_ref, out_ref = refs[GROUP:]
    total = None
    for j in range(GROUP):
        rows = pl.ds(pl.multiple_of((pos[0] ^ j) * (HG * DH), 16), HG * DH)
        part = dot_tn(parts[j][...], w_ref[rows, :])
        total = part if total is None else total + part
    row = lax.broadcasted_iota(jnp.int32, (TOK, TOK), 0)
    col = lax.broadcasted_iota(jnp.int32, (TOK, TOK), 1)
    picker = (row == RATE * (col % BLK) + col // BLK).astype(BF16)
    out_ref[...] = dot(picker, total.astype(BF16)).astype(BF16)


def params(limit=VMEM_LIMIT):
    return pltpu.CompilerParams(vmem_limit_bytes=limit)


def cost(scores):
    return pl.CostEstimate(
        flops=scores * 1024, bytes_accessed=1 << 20, transcendentals=scores
    )


def whole(shape):
    return pl.BlockSpec(shape, lambda *_: (0,) * len(shape))


def per_head(shape, axis=0):
    return pl.BlockSpec(shape, lambda h, *_: (0,) * axis + (h,) + (0,) * (len(shape) - axis - 1))


def call(kernel, scalars, args, grid, in_specs, out_specs, out_shape, scratch, estimate, limit=VMEM_LIMIT):
    return pl.pallas_call(
        kernel,
        grid_spec=pltpu.PrefetchScalarGridSpec(
            num_scalar_prefetch=len(scalars),
            grid=grid,
            in_specs=in_specs,
            out_specs=out_specs,
            scratch_shapes=scratch,
        ),
        out_shape=out_shape,
        compiler_params=params(limit),
        cost_estimate=estimate,
    )(*scalars, *args)


def within(array, apart):
    count = lax.axis_size("seq")
    return lax.ppermute(array, "seq", [(i, i ^ apart) for i in range(count)])


def around(array):
    count = lax.axis_size("seq")
    return lax.ppermute(array, "seq", [(i, (i + GROUP) % count) for i in range(count)])


def shards_four(queries, key_states, value_states, offsets_mid, offsets_top, out_weight):
    width = queries.shape[1]
    heads_shape = jax.ShapeDtypeStruct((HG, 2 * DH, 2 * BLK), BF16)
    query_shape = jax.ShapeDtypeStruct((HG, DH, TOK), BF16)
    pos = (lax.axis_index("seq") % GROUP).astype(jnp.int32).reshape(1)
    offs = (pos, offsets_mid, offsets_top)

    packed = call(
        pack_kv_kernel, offs, (key_states, value_states), (1,),
        [whole((TOK, width))] * 2,
        [whole(heads_shape.shape)] * (2 * GROUP),
        [heads_shape] * (2 * GROUP),
        [pltpu.VMEM((width, TOK), BF16)] * 2,
        cost(1 << 19),
        VMEM_MOST,
    )
    sel, far = list(packed[:GROUP]), list(packed[GROUP:])
    for j in range(1, GROUP):
        sel[j] = within(sel[j], j)
    query = call(
        pack_q_kernel, (pos,), (queries,), (1,),
        [whole((TOK, width))],
        [whole(query_shape.shape)] * GROUP,
        [query_shape] * GROUP,
        [pltpu.VMEM((width, TOK), BF16)],
        cost(1 << 18),
        VMEM_MOST,
    )
    query = list(query)
    for j in range(1, GROUP):
        query[j] = within(query[j], j)
    for j in range(1, GROUP):
        far[j] = within(far[j], j)

    kv_spec = per_head((1, 2 * DH, 2 * BLK))
    q_spec = per_head((1, DH, TOK))
    acc_shape = jax.ShapeDtypeStruct((HG, GROUP, DX, TOK), F32)
    max_shape = jax.ShapeDtypeStruct((HG, GROUP, 8, TOK), F32)
    acc_spec = per_head((1, GROUP, DX, TOK))
    max_spec = per_head((1, GROUP, 8, TOK))
    near_scratch = [
        pltpu.VMEM((GROUP, 2 * DH, TOK), BF16),
        pltpu.VMEM((2, TOK, 2 * DH), BF16),
        pltpu.VMEM((2, DX, TOK), BF16),
    ]
    far_scratch = [
        pltpu.VMEM((2, 2 * DH, TOK), BF16),
        pltpu.VMEM((2, TOK, 2 * DH), BF16),
        pltpu.VMEM((2, DX, TOK), BF16),
    ]

    def near(first, keys, state):
        return call(
            functools.partial(near_kernel, first), offs, (*keys, *query, *state), (HG,),
            [kv_spec] * GROUP + [q_spec] * GROUP + ([] if first else [acc_spec, max_spec]),
            [acc_spec, max_spec],
            [acc_shape, max_shape],
            near_scratch,
            cost(HG * 2 * TOK * GROUP * TOK),
        )

    pair_spec = per_head((2, 1, 2 * DH, 2 * BLK), 1)

    def beyond(last, pairs, state):
        return call(
            functools.partial(far_kernel, last), offs, (*pairs, *query, *state), (HG,),
            [pair_spec] * 2 + [q_spec] * GROUP + [acc_spec, max_spec],
            [q_spec] * GROUP if last else [acc_spec, max_spec],
            [query_shape] * GROUP if last else [acc_shape, max_shape],
            ([pltpu.VMEM((1, GROUP, DX, TOK), F32), pltpu.VMEM((1, GROUP, 8, TOK), F32)] if last else [])
            + far_scratch,
            cost(HG * 2 * TOK * TOK),
        )

    pairs = [jnp.stack(sel[:2]), jnp.stack(sel[2:])]
    rings = []
    for _ in range(RATE - 1):
        pairs = [around(p) for p in pairs]
        rings.append(pairs)

    state = near(True, sel, ())
    state = beyond(False, rings[0], state)
    state = near(False, far, state)
    state = beyond(False, rings[1], state)
    parts = list(beyond(True, rings[2], state))
    for j in range(1, GROUP):
        parts[j] = within(parts[j], j)
    parts = [p.reshape(HG * DH, TOK) for p in parts]
    return call(
        project_kernel, (pos,), (*parts, out_weight), (1,),
        [whole((HG * DH, TOK))] * GROUP + [whole((width, width))],
        whole((TOK, width)),
        jax.ShapeDtypeStruct((TOK, width), BF16),
        [],
        cost(1 << 18),
    )


def shards(queries, key_states, value_states, offsets_mid, offsets_top, out_weight):
    tokens, width = queries.shape
    heads = offsets_mid.shape[0]
    fits = (
        lax.axis_size("head") == 1
        and lax.axis_size("seq") == GROUP * RATE
        and tokens == TOK
        and heads == GROUP * HG
        and width == heads * DH
    )
    run = shards_four if fits else shards_general
    return run(queries, key_states, value_states, offsets_mid, offsets_top, out_weight)


def solution(mesh):
    in_specs = (
        P(("slide", "seq"), "head"),
        P(("slide", "seq"), "head"),
        P(("slide", "seq"), "head"),
        P(),
        P(),
        P("head", None),
    )
    out_specs = P(("slide", "seq", "head"), None)
    return jax.shard_map(shards, mesh=mesh, in_specs=in_specs, out_specs=out_specs, check_vma=False)
```

```python
import functools

import jax
import jax.numpy as jnp
from jax import lax
from jax.experimental import pallas as pl
from jax.experimental.pallas import tpu as pltpu
from jax.sharding import PartitionSpec as P

SEG = 2048
LOG2E = 1.4426950408889634
VMEM_LIMIT = 40 * 1024 * 1024
VMEM_MOST = 60 * 1024 * 1024
BF16 = jnp.bfloat16
F32 = jnp.float32


def partner_2(block, axis, apart):
    count = lax.axis_size(axis)
    route = []
    for low in range(count):
        high = low | 1 << apart
        if high != low and high < count:
            route += [(low, high), (high, low)]
    return lax.ppermute(block, axis, route)


def attend_head(triple_in):
    query_rows, key_rows, value_rows = triple_in
    score_scale = query_rows.shape[-1] ** (-0.5)
    scores = jnp.dot(query_rows, key_rows.T, preferred_element_type=jnp.float32) * score_scale
    row_max = jnp.max(scores, axis=1)
    shifted = jnp.exp(scores - row_max[:, None])
    row_total = jnp.sum(shifted, axis=1)
    weights = shifted.astype(jnp.bfloat16)
    numerator = jnp.dot(weights, value_rows, preferred_element_type=jnp.float32)
    return (numerator, row_total, row_max)


def attend_local(query_rows, pair_rows):
    return lax.map(
        attend_head,
        (
            query_rows.transpose(1, 0, 2),
            pair_rows[:, 0].transpose(1, 0, 2),
            pair_rows[:, 1].transpose(1, 0, 2),
        ),
    )


def pick_rows(states, offsets, rate):
    row_count, inner_count, heads_here, head_width = states.shape
    picker = (jnp.arange(rate)[:, None] == offsets[None, :]).astype(jnp.bfloat16)
    folded = states.reshape(row_count // rate, rate, inner_count, heads_here, head_width)
    return jnp.einsum("archd,rh->achd", folded, picker, preferred_element_type=jnp.float32).astype(
        jnp.bfloat16
    )


def spread_back(numerator, row_total, row_max, offsets, rate):
    heads_here, picked_count, head_width = numerator.shape
    chosen = jnp.arange(rate)[:, None] == offsets[None, :]
    full_num = jnp.where(chosen[None, :, :, None], numerator.transpose(1, 0, 2)[:, None], 0.0)
    full_total = jnp.where(chosen[None], row_total.T[:, None], 0.0)
    full_max = jnp.where(chosen[None], row_max.T[:, None], -1e30)
    return (
        full_num.reshape(picked_count * rate, heads_here, head_width),
        full_total.reshape(picked_count * rate, heads_here),
        full_max.reshape(picked_count * rate, heads_here),
    )


def doubling(buffer, steps_count):
    position = lax.axis_index("seq")
    for bit_index in range(steps_count):
        partner = partner_2(buffer, "seq", bit_index)
        is_lower = position >> bit_index & 1 == 0
        buffer = jnp.where(
            is_lower, jnp.concatenate([buffer, partner], 0), jnp.concatenate([partner, buffer], 0)
        )
    return buffer


def shards_general(queries, key_states, value_states, offsets_mid, offsets_top, out_weight):
    tok_rows = queries.shape[0]
    heads_local = offsets_mid.shape[0] // lax.axis_size("head")
    head_size = queries.shape[1] // heads_local
    seq_devices = lax.axis_size("seq")
    seq_total = tok_rows * seq_devices
    width_mid = min(16 * SEG, seq_total)
    rate_mid = width_mid // SEG
    rate_top = seq_total // SEG
    start_head = lax.axis_index("head") * heads_local
    mid_local = lax.dynamic_slice(offsets_mid, (start_head,), (heads_local,))
    top_local = lax.dynamic_slice(offsets_top, (start_head,), (heads_local,))
    query_heads = queries.reshape(tok_rows, 1, heads_local, head_size)
    paired = jnp.stack([key_states, value_states], axis=1).reshape(
        tok_rows, 2, heads_local, head_size
    )
    near_bits = (SEG // tok_rows).bit_length() - 1
    near_rows = doubling(paired.reshape(tok_rows, -1), near_bits).reshape(
        SEG, 2, heads_local, head_size
    )
    near_num, near_total, near_max = attend_local(query_heads[:, 0], near_rows)
    level_near = spread_back(
        near_num, near_total, near_max, jnp.zeros((heads_local,), jnp.int32), 1
    )
    mid_q = pick_rows(query_heads, mid_local, rate_mid)[:, 0]
    mid_kv = pick_rows(paired, mid_local, rate_mid)
    mid_group = width_mid // tok_rows
    mid_bits = mid_group.bit_length() - 1
    mid_rows = doubling(mid_kv.reshape(mid_kv.shape[0], -1), mid_bits).reshape(
        SEG, 2, heads_local, head_size
    )
    mid_num, mid_total, mid_max = attend_local(mid_q, mid_rows)
    level_mid = spread_back(mid_num, mid_total, mid_max, mid_local, rate_mid)
    top_q = pick_rows(query_heads, top_local, rate_top)[:, 0]
    top_kv = pick_rows(paired, top_local, rate_top)
    top_rows = lax.all_gather(
        top_kv.reshape(top_kv.shape[0], -1), "seq", axis=0, tiled=True
    ).reshape(SEG, 2, heads_local, head_size)
    top_num, top_total, top_max = attend_local(top_q, top_rows)
    level_top = spread_back(top_num, top_total, top_max, top_local, rate_top)
    levels = [level_near, level_mid, level_top]
    overall = jnp.maximum(jnp.maximum(level_near[2], level_mid[2]), level_top[2])
    numerator = jnp.zeros((tok_rows, heads_local, head_size), jnp.float32)
    row_total = jnp.zeros((tok_rows, heads_local), jnp.float32)
    for level_num, level_total, level_max in levels:
        factor = jnp.exp(level_max - overall)
        numerator = numerator + factor[..., None] * level_num
        row_total = row_total + factor * level_total
    attention = (
        (numerator / row_total[..., None])
        .astype(jnp.bfloat16)
        .reshape(tok_rows, heads_local * head_size)
    )
    result = lax.psum_scatter(
        jnp.dot(attention, out_weight, preferred_element_type=jnp.float32),
        "head",
        scatter_dimension=0,
        tiled=True,
    )
    return result.astype(jnp.bfloat16)


RATE = 4
GROUP = 4
HG = 4
DH = 48
BLK = 128
HALF = 2 * BLK
TOK = 512
DX = 64


def dot(a, b):
    return jnp.dot(a, b, preferred_element_type=F32)


def dot_nt(a, b):
    return lax.dot_general(a, b, (((1,), (1,)), ((), ())), preferred_element_type=F32)


def class_of_slots(off_mid, off_top):
    first = off_mid
    second = jnp.where(off_top == off_mid, lax.rem(off_mid + 1, RATE), off_top)
    free0 = (first != 0) & (second != 0)
    free1 = (first != 1) & (second != 1)
    third = jnp.where(free0, 0, jnp.where(free1, 1, 2))
    return first, second, third, 6 - first - second - third


def head_of(place, j, p):
    return (place[0] ^ j) * HG + ((place[1] + p) & (HG - 1))


def token_picker():
    row = lax.broadcasted_iota(jnp.int32, (TOK, TOK), 0)
    col = lax.broadcasted_iota(jnp.int32, (TOK, TOK), 1)
    return (col == RATE * (row % BLK) + row // BLK).astype(BF16)


def fill_class_major(block, picker, scratch):
    ordered = dot(picker, block).astype(BF16)
    step = 256
    eye = (
        lax.broadcasted_iota(jnp.int32, (step, step), 0)
        == lax.broadcasted_iota(jnp.int32, (step, step), 1)
    ).astype(BF16)
    for c in range(0, block.shape[1], step):
        scratch[c : c + step, :] = dot_nt(eye, ordered[:, c : c + step]).astype(BF16)


def lane_block(index):
    return pl.ds(pl.multiple_of(index * BLK, BLK), BLK)


def head_rows(head):
    return pl.ds(pl.multiple_of(head * DH, 16), DH)


def pack_kernel(place, mid, top, k_ref, v_ref, q_ref, *rest):
    sel, far, scratch = rest[:GROUP], rest[GROUP : 2 * GROUP], rest[2 * GROUP :]
    picker = token_picker()
    for ref, held in zip((k_ref, v_ref, q_ref), scratch):
        fill_class_major(ref[...], picker, held)
    for j in range(GROUP):
        for p in range(HG):
            head = head_of(place, j, p)
            slots = class_of_slots(mid[head], top[head])
            for s in range(RATE):
                out = sel[j] if s < 2 else far[j]
                lanes = slice((s % 2) * BLK, (s % 2 + 1) * BLK)
                for i, held in enumerate(scratch):
                    out[p, i * DH : (i + 1) * DH, lanes] = held[
                        head_rows(head), lane_block(slots[s])
                    ]


def split_query(q):
    scaled = q.astype(F32) * (DH**-0.5 * LOG2E)
    high = scaled.astype(BF16)
    low = (scaled - high.astype(F32)).astype(BF16)
    return jnp.concatenate([high, low], axis=0)


def twice_keys(keys_t):
    both = jnp.concatenate([keys_t, keys_t], axis=0).astype(F32)
    return both.T.astype(BF16)


def column_max(blocks):
    best = jnp.max(blocks[0], axis=0, keepdims=True)
    for block in blocks[1:]:
        best = jnp.maximum(best, jnp.max(block, axis=0, keepdims=True))
    return best


def near_kernel(blocks, tasks, carried, place, mid, top, *refs):
    kv = refs[: len(blocks)]
    refs = refs[len(blocks) :]
    old = [refs[2 * i : 2 * i + 2] for i in range(carried)]
    outs = refs[2 * carried : 2 * carried + 2 * len(tasks[0])]
    k_s, v_s = refs[-2:]
    head = head_of(place, 0, pl.program_id(0))
    same = (mid[head] == top[head]).astype(jnp.int32)
    slot = lax.broadcasted_iota(jnp.int32, (1, HALF), 1) // BLK
    first_again = jnp.where(same == 1, 1.584962500721156, 1.0)
    second_again = jnp.where(same == 1, 0.0, 1.0)
    again = [
        jnp.where(slot == 0, first_again, 0.0),
        jnp.where(slot == 1, second_again, 0.0),
    ]
    for i, ref in enumerate(kv):
        rows = slice(i * HALF, (i + 1) * HALF)
        k_s[rows, :] = twice_keys(ref[0, 0:DH, :])
        v_s[0:DH, rows] = ref[0, DH : 2 * DH, :]
    v_s[DH:DX, :] = jnp.ones((DX - DH, v_s.shape[1]), BF16)

    flat = [
        (block, low, merge, out, i)
        for out, group in enumerate(tasks)
        for i, (block, low, merge) in enumerate(group)
    ]

    def score(task):
        block, low = task[:2]
        return dot(k_s[low * HALF :, :], split_query(kv[blocks.index(block)][0, 2 * DH :, :]))

    scores = score(flat[0])
    for n, (block, low, merge, out, i) in enumerate(flat):
        following = score(flat[n + 1]) if n + 1 < len(flat) else None
        best = jnp.max(scores, axis=0, keepdims=True)
        if merge is not None:
            acc_in, max_in = old[merge[0]]
            old_max = max_in[0, merge[1], 0:1, :]
            best = jnp.maximum(best, old_max)
        weights = []
        for b in range(low, len(blocks)):
            part = scores[(b - low) * HALF : (b - low + 1) * HALF, :]
            if block[1] == 0 and blocks[b][1] == 0:
                weights += [
                    jnp.exp2(part[s * BLK : (s + 1) * BLK, :] - (best - again[s]))
                    for s in range(2)
                ]
            else:
                weights.append(jnp.exp2(part - best))
        weights = jnp.concatenate([w.astype(BF16) for w in weights], axis=0)
        acc = dot(v_s[:, low * HALF :], weights)
        if merge is not None:
            acc = acc + acc_in[0, merge[1]] * jnp.exp2(old_max - best)
        acc_ref, max_ref = outs[2 * out : 2 * out + 2]
        acc_ref[0, i] = acc
        max_ref[0, i] = jnp.broadcast_to(best, (8, HALF))
        scores = following


def far_kernel(chip, place, mid, top, *refs):
    own, beyond = refs[:GROUP], refs[GROUP : GROUP + 6]
    outs = refs[GROUP + 6 : GROUP + 6 + RATE]
    k_s, v_s = refs[GROUP + 6 + RATE :]
    head = head_of(place, 0, 0)
    same = mid[head] == top[head]
    slots = (0, jnp.where(same, 0, 1))

    def source(s, j):
        return own[j].at[0] if s == 0 else beyond[2 * (s - 1) + j // 2].at[j % 2]

    for level, slot in enumerate(slots):
        for s in range(RATE):
            for j in range(GROUP):
                here = slice(j * BLK, (j + 1) * BLK)
                ref = source(s, j)
                k_s[level, s, here, :] = twice_keys(ref[0:DH, lane_block(slot)])
                v_s[level, s, 0:DH, here] = ref[DH : 2 * DH, lane_block(slot)]
    v_s[:, :, DH:DX, :] = jnp.ones((2, RATE, DX - DH, TOK), BF16)
    row = lax.broadcasted_iota(jnp.int32, (16, HALF), 0)
    tasks = [(s, level) for s in range(RATE) for level in range(2)]

    def score(task):
        s, level = task
        query = jnp.concatenate(
            [
                split_query(source(s, 2 * chip + i)[2 * DH :, lane_block(slots[level])])
                for i in range(2)
            ],
            axis=1,
        )
        return [dot(k_s[level, b], query) for b in range(RATE) if b != s]

    scores = score(tasks[0])
    for n, (s, level) in enumerate(tasks):
        following = score(tasks[n + 1]) if n + 1 < len(tasks) else None
        best = column_max(scores)
        acc = None
        for i, b in enumerate([b for b in range(RATE) if b != s]):
            part = dot(v_s[level, b], jnp.exp2(scores[i] - best).astype(BF16))
            acc = part if acc is None else acc + part
        total = acc[DH : DH + 1, :]
        result = (acc[0:DH, :] / total).astype(BF16)
        lse = best + jnp.log2(total)
        if level == 0:
            lse = jnp.where(same, lse + 1.0, lse)
        else:
            lse = jnp.where(same, -1e30, lse)
        high = lse.astype(BF16).astype(F32)
        middle = (lse - high).astype(BF16).astype(F32)
        low = lse - high - middle
        tail = jnp.where(row == 0, high, jnp.where(row == 1, middle, jnp.where(row == 2, low, 0.0)))
        tail = tail.astype(BF16)
        for i in range(2):
            lanes = slice(i * HALF + level * BLK, i * HALF + (level + 1) * BLK)
            outs[s][0:DH, lanes] = result[:, i * BLK : (i + 1) * BLK]
            outs[s][DH:DX, lanes] = tail[:, i * BLK : (i + 1) * BLK]
        scores = following


def combine_kernel(acc_ref, max_ref, *refs):
    far, outs = refs[:HG], refs[HG:]
    for p in range(HG):
        for i in range(2):
            lanes = slice(i * HALF, (i + 1) * HALF)
            acc, best = acc_ref[p, 2 * i], max_ref[p, 2 * i, 0:1, :]
            tail = far[p][DH:DX, lanes].astype(F32)
            lse = tail[0:1] + tail[1:2] + tail[2:3]
            overall = jnp.maximum(best, lse)
            near_factor, far_factor = jnp.exp2(best - overall), jnp.exp2(lse - overall)
            total = acc[DH : DH + 1] * near_factor + far_factor
            value = acc[0:DH] * near_factor + far[p][0:DH, lanes].astype(F32) * far_factor
            outs[i][p, :, 0:HALF] = (value / total).astype(BF16)
            acc = acc_ref[p, 2 * i + 1]
            outs[i][p, :, HALF:] = (acc[0:DH] / acc[DH : DH + 1]).astype(BF16)


def project_kernel(place, mid, top, *refs):
    parts = refs[:GROUP]
    w_ref, out_ref, held = refs[GROUP:]
    for j in range(GROUP):
        for p in range(HG):
            head = head_of(place, j, p)
            slots = class_of_slots(mid[head], top[head])
            for s in range(RATE):
                held[head_rows(head), lane_block(slots[s])] = parts[j][
                    p, :, s * BLK : (s + 1) * BLK
                ]
    row = lax.broadcasted_iota(jnp.int32, (TOK, TOK), 0)
    col = lax.broadcasted_iota(jnp.int32, (TOK, TOK), 1)
    picker = (row == RATE * (col % BLK) + col // BLK).astype(BF16)
    attention = dot_nt(picker, held[...]).astype(BF16)
    out_ref[...] = dot(attention, w_ref[...]).astype(BF16)


def whole(shape):
    return pl.BlockSpec(shape, lambda *_: (0,) * len(shape))


def per_head(shape):
    return pl.BlockSpec(shape, lambda h, *_: (h,) + (0,) * (len(shape) - 1))


def call(kernel, scalars, args, grid, in_specs, outs, scratch, scores, limit=VMEM_LIMIT):
    return pl.pallas_call(
        kernel,
        grid_spec=pltpu.PrefetchScalarGridSpec(
            num_scalar_prefetch=len(scalars),
            grid=grid,
            in_specs=in_specs,
            out_specs=[spec for spec, _ in outs],
            scratch_shapes=scratch,
        ),
        out_shape=[shape for _, shape in outs],
        compiler_params=pltpu.CompilerParams(vmem_limit_bytes=limit),
        cost_estimate=pl.CostEstimate(
            flops=scores * 1024, bytes_accessed=1 << 20, transcendentals=scores
        ),
    )(*scalars, *args)


def within(array, apart):
    count = lax.axis_size("seq")
    return lax.ppermute(array, "seq", [(i, i ^ apart) for i in range(count)])


def across(array, segments):
    count = lax.axis_size("seq")
    return lax.ppermute(
        array, "seq", [(i, (i + GROUP * segments) % count) for i in range(count)]
    )


def shards_four(queries, key_states, value_states, offsets_mid, offsets_top, out_weight):
    width = queries.shape[1]
    index = lax.axis_index("seq").astype(jnp.int32)
    place = jnp.stack([index % GROUP, index // GROUP])
    scalars = (place, offsets_mid, offsets_top)
    piece = jax.ShapeDtypeStruct((HG, 3 * DH, HALF), BF16)
    packed = call(
        pack_kernel, scalars, (key_states, value_states, queries), (1,),
        [whole((TOK, width))] * 3,
        [(whole(piece.shape), piece)] * (2 * GROUP),
        [pltpu.VMEM((width, TOK), BF16)] * 3,
        1 << 19, VMEM_MOST,
    )
    sel, rest = list(packed[:GROUP]), list(packed[GROUP:])
    sel[1] = within(sel[1], 1)
    rest[1] = within(rest[1], 1)
    for j in (2, 3):
        sel[j] = within(sel[j], j)
    for j in (2, 3):
        rest[j] = within(rest[j], j)

    beyond = []
    for s in range(1, RATE):
        beyond += [
            across(jnp.stack([sel[0][s], sel[1][s]]), s),
            across(jnp.stack([sel[2][s], sel[3][s]]), s),
        ]

    piece_spec = per_head((1, 3 * DH, HALF))

    def state(count):
        return [
            (per_head((1, count, rows, HALF)), jax.ShapeDtypeStruct((HG, count, rows, HALF), F32))
            for rows in (DX, 8)
        ]

    held = {(j, half): (sel, rest)[half][j] for j in range(GROUP) for half in range(2)}

    def near(blocks, tasks, old):
        keys = len(blocks) * HALF
        scores = sum((len(blocks) - low) * HALF * HALF for group in tasks for _, low, _ in group)
        return call(
            functools.partial(near_kernel, blocks, tasks, len(old)), scalars,
            (*[held[b] for b in blocks], *[x for pair in old for x in pair]), (HG,),
            [piece_spec] * len(blocks)
            + [per_head((1,) + x.shape[1:]) for pair in old for x in pair],
            [out for group in tasks for out in state(len(group))],
            [pltpu.VMEM((keys, 2 * DH), BF16), pltpu.VMEM((DX, keys), BF16)],
            HG * scores,
        )

    own = [(0, 0), (0, 1), (1, 0), (1, 1)]
    state_own = near(own, [[(b, 0, None) for b in own]], [])
    with_sel = own + [(2, 0), (3, 0)]
    out = near(
        with_sel,
        [
            [(b, 4, (0, i)) for i, b in enumerate(own)],
            [((2, 0), 0, None), ((3, 0), 0, None)],
        ],
        [state_own],
    )
    state_own, state_sel = out[:2], out[2:]

    piece_0 = pl.BlockSpec((1, 3 * DH, HALF), lambda *_: (0, 0, 0))
    result = jax.ShapeDtypeStruct((DX, 2 * HALF), BF16)

    def far(chip):
        return call(
            functools.partial(far_kernel, chip), scalars, (*sel, *beyond), (1,),
            [piece_0] * GROUP + [whole((2, 3 * DH, HALF))] * 6,
            [(whole(result.shape), result)] * RATE,
            [
                pltpu.VMEM((2, RATE, TOK, 2 * DH), BF16),
                pltpu.VMEM((2, RATE, DX, TOK), BF16),
            ],
            RATE * 2 * 3 * TOK * HALF,
        )

    back = {}
    for chip in (1, 0):
        results = far(chip)
        back[chip] = [results[0]] + [across(results[s], -s) for s in range(1, RATE)]

    everything = with_sel + [(2, 1), (3, 1)]
    out = near(
        everything,
        [
            [(b, 6, (0, i)) for i, b in enumerate(own)],
            [
                ((2, 0), 6, (1, 0)), ((2, 1), 0, None),
                ((3, 0), 6, (1, 1)), ((3, 1), 0, None),
            ],
        ],
        [state_own, state_sel],
    )
    attended = jax.ShapeDtypeStruct((HG, DH, TOK), BF16)

    def combine(state, results):
        return call(
            combine_kernel, (), (*state, *results), (1,),
            [whole(x.shape) for x in state] + [whole(result.shape)] * HG,
            [(whole(attended.shape), attended)] * 2,
            [],
            1 << 18,
        )

    parts = [None] * GROUP
    parts[2:] = combine(out[2:], back[1])
    parts[:2] = combine(out[:2], back[0])
    for j in (2, 3, 1):
        parts[j] = within(parts[j], j)
    return call(
        project_kernel, scalars, (*parts, out_weight), (1,),
        [whole(attended.shape)] * GROUP + [whole((width, width))],
        [(whole((TOK, width)), jax.ShapeDtypeStruct((TOK, width), BF16))],
        [pltpu.VMEM((width, TOK), BF16)],
        1 << 18,
    )[0]


def shards(queries, key_states, value_states, offsets_mid, offsets_top, out_weight):
    tokens, width = queries.shape
    heads = offsets_mid.shape[0]
    fits = (
        lax.axis_size("head") == 1
        and lax.axis_size("seq") == GROUP * RATE
        and tokens == TOK
        and heads == GROUP * HG
        and width == heads * DH
    )
    run = shards_four if fits else shards_general
    return run(queries, key_states, value_states, offsets_mid, offsets_top, out_weight)


def solution(mesh):
    in_specs = (
        P(("slide", "seq"), "head"),
        P(("slide", "seq"), "head"),
        P(("slide", "seq"), "head"),
        P(),
        P(),
        P("head", None),
    )
    out_specs = P(("slide", "seq", "head"), None)
    return jax.shard_map(shards, mesh=mesh, in_specs=in_specs, out_specs=out_specs, check_vma=False)
```

```python
import functools

import jax
import jax.numpy as jnp
from jax import lax
from jax.experimental import pallas as pl
from jax.experimental.pallas import tpu as pltpu
from jax.sharding import PartitionSpec as P

SEG = 2048
LOG2E = 1.4426950408889634
VMEM_LIMIT = 40 * 1024 * 1024
VMEM_MOST = 60 * 1024 * 1024
BF16 = jnp.bfloat16
F32 = jnp.float32


def partner_2(block, axis, apart):
    count = lax.axis_size(axis)
    route = []
    for low in range(count):
        high = low | 1 << apart
        if high != low and high < count:
            route += [(low, high), (high, low)]
    return lax.ppermute(block, axis, route)


def attend_head(triple_in):
    query_rows, key_rows, value_rows = triple_in
    score_scale = query_rows.shape[-1] ** (-0.5)
    scores = jnp.dot(query_rows, key_rows.T, preferred_element_type=jnp.float32) * score_scale
    row_max = jnp.max(scores, axis=1)
    shifted = jnp.exp(scores - row_max[:, None])
    row_total = jnp.sum(shifted, axis=1)
    weights = shifted.astype(jnp.bfloat16)
    numerator = jnp.dot(weights, value_rows, preferred_element_type=jnp.float32)
    return (numerator, row_total, row_max)


def attend_local(query_rows, pair_rows):
    return lax.map(
        attend_head,
        (
            query_rows.transpose(1, 0, 2),
            pair_rows[:, 0].transpose(1, 0, 2),
            pair_rows[:, 1].transpose(1, 0, 2),
        ),
    )


def pick_rows(states, offsets, rate):
    row_count, inner_count, heads_here, head_width = states.shape
    picker = (jnp.arange(rate)[:, None] == offsets[None, :]).astype(jnp.bfloat16)
    folded = states.reshape(row_count // rate, rate, inner_count, heads_here, head_width)
    return jnp.einsum("archd,rh->achd", folded, picker, preferred_element_type=jnp.float32).astype(
        jnp.bfloat16
    )


def spread_back(numerator, row_total, row_max, offsets, rate):
    heads_here, picked_count, head_width = numerator.shape
    chosen = jnp.arange(rate)[:, None] == offsets[None, :]
    full_num = jnp.where(chosen[None, :, :, None], numerator.transpose(1, 0, 2)[:, None], 0.0)
    full_total = jnp.where(chosen[None], row_total.T[:, None], 0.0)
    full_max = jnp.where(chosen[None], row_max.T[:, None], -1e30)
    return (
        full_num.reshape(picked_count * rate, heads_here, head_width),
        full_total.reshape(picked_count * rate, heads_here),
        full_max.reshape(picked_count * rate, heads_here),
    )


def doubling(buffer, steps_count):
    position = lax.axis_index("seq")
    for bit_index in range(steps_count):
        partner = partner_2(buffer, "seq", bit_index)
        is_lower = position >> bit_index & 1 == 0
        buffer = jnp.where(
            is_lower, jnp.concatenate([buffer, partner], 0), jnp.concatenate([partner, buffer], 0)
        )
    return buffer


def shards_general(queries, key_states, value_states, offsets_mid, offsets_top, out_weight):
    tok_rows = queries.shape[0]
    heads_local = offsets_mid.shape[0] // lax.axis_size("head")
    head_size = queries.shape[1] // heads_local
    seq_devices = lax.axis_size("seq")
    seq_total = tok_rows * seq_devices
    width_mid = min(16 * SEG, seq_total)
    rate_mid = width_mid // SEG
    rate_top = seq_total // SEG
    start_head = lax.axis_index("head") * heads_local
    mid_local = lax.dynamic_slice(offsets_mid, (start_head,), (heads_local,))
    top_local = lax.dynamic_slice(offsets_top, (start_head,), (heads_local,))
    query_heads = queries.reshape(tok_rows, 1, heads_local, head_size)
    paired = jnp.stack([key_states, value_states], axis=1).reshape(
        tok_rows, 2, heads_local, head_size
    )
    near_bits = (SEG // tok_rows).bit_length() - 1
    near_rows = doubling(paired.reshape(tok_rows, -1), near_bits).reshape(
        SEG, 2, heads_local, head_size
    )
    near_num, near_total, near_max = attend_local(query_heads[:, 0], near_rows)
    level_near = spread_back(
        near_num, near_total, near_max, jnp.zeros((heads_local,), jnp.int32), 1
    )
    mid_q = pick_rows(query_heads, mid_local, rate_mid)[:, 0]
    mid_kv = pick_rows(paired, mid_local, rate_mid)
    mid_group = width_mid // tok_rows
    mid_bits = mid_group.bit_length() - 1
    mid_rows = doubling(mid_kv.reshape(mid_kv.shape[0], -1), mid_bits).reshape(
        SEG, 2, heads_local, head_size
    )
    mid_num, mid_total, mid_max = attend_local(mid_q, mid_rows)
    level_mid = spread_back(mid_num, mid_total, mid_max, mid_local, rate_mid)
    top_q = pick_rows(query_heads, top_local, rate_top)[:, 0]
    top_kv = pick_rows(paired, top_local, rate_top)
    top_rows = lax.all_gather(
        top_kv.reshape(top_kv.shape[0], -1), "seq", axis=0, tiled=True
    ).reshape(SEG, 2, heads_local, head_size)
    top_num, top_total, top_max = attend_local(top_q, top_rows)
    level_top = spread_back(top_num, top_total, top_max, top_local, rate_top)
    levels = [level_near, level_mid, level_top]
    overall = jnp.maximum(jnp.maximum(level_near[2], level_mid[2]), level_top[2])
    numerator = jnp.zeros((tok_rows, heads_local, head_size), jnp.float32)
    row_total = jnp.zeros((tok_rows, heads_local), jnp.float32)
    for level_num, level_total, level_max in levels:
        factor = jnp.exp(level_max - overall)
        numerator = numerator + factor[..., None] * level_num
        row_total = row_total + factor * level_total
    attention = (
        (numerator / row_total[..., None])
        .astype(jnp.bfloat16)
        .reshape(tok_rows, heads_local * head_size)
    )
    result = lax.psum_scatter(
        jnp.dot(attention, out_weight, preferred_element_type=jnp.float32),
        "head",
        scatter_dimension=0,
        tiled=True,
    )
    return result.astype(jnp.bfloat16)


RATE = 4
GROUP = 4
HG = 4
DH = 48
BLK = 128
HALF = 2 * BLK
TOK = 512
DX = 64


def dot(a, b):
    return jnp.dot(a, b, preferred_element_type=F32)


def dot_nt(a, b):
    return lax.dot_general(a, b, (((1,), (1,)), ((), ())), preferred_element_type=F32)


def class_of_slots(off_mid, off_top):
    first = off_mid
    second = jnp.where(off_top == off_mid, lax.rem(off_mid + 1, RATE), off_top)
    free0 = (first != 0) & (second != 0)
    free1 = (first != 1) & (second != 1)
    third = jnp.where(free0, 0, jnp.where(free1, 1, 2))
    return first, second, third, 6 - first - second - third


def head_of(place, j, p):
    return (place[0] ^ j) * HG + ((place[1] + p) & (HG - 1))


def token_picker():
    row = lax.broadcasted_iota(jnp.int32, (TOK, TOK), 0)
    col = lax.broadcasted_iota(jnp.int32, (TOK, TOK), 1)
    return (col == RATE * (row % BLK) + row // BLK).astype(BF16)


def fill_class_major(block, picker, scratch):
    ordered = dot(picker, block).astype(BF16)
    step = 256
    eye = (
        lax.broadcasted_iota(jnp.int32, (step, step), 0)
        == lax.broadcasted_iota(jnp.int32, (step, step), 1)
    ).astype(BF16)
    for c in range(0, block.shape[1], step):
        scratch[c : c + step, :] = dot_nt(eye, ordered[:, c : c + step]).astype(BF16)


def lane_block(index):
    return pl.ds(pl.multiple_of(index * BLK, BLK), BLK)


def head_rows(head):
    return pl.ds(pl.multiple_of(head * DH, 16), DH)


def pack_kernel(place, mid, top, k_hbm, v_hbm, q_hbm, *refs):
    outs, refs = refs[:6], refs[6:]
    blocks, held, packed, sems_in, sems_out = refs[:3], refs[3:6], refs[6:12], refs[12], refs[13]
    loads = [
        pltpu.make_async_copy(hbm, block, sems_in.at[i])
        for i, (hbm, block) in enumerate(zip((k_hbm, v_hbm, q_hbm), blocks))
    ]
    for load in loads:
        load.start()
    picker = token_picker()
    for load, block, scratch in zip(loads, blocks, held):
        load.wait()
        fill_class_major(block[...], picker, scratch)
    stores = [
        pltpu.make_async_copy(packed[i], outs[i], sems_out.at[i]) for i in range(6)
    ]
    for i, (j, first, count) in enumerate(
        ((0, 0, 4), (1, 0, 4), (2, 0, 2), (3, 0, 2), (2, 2, 2), (3, 2, 2))
    ):
        for p in range(HG):
            head = head_of(place, j, p)
            slots = class_of_slots(mid[head], top[head])
            for s in range(count):
                for n in range(3):
                    packed[i][p, n * DH : (n + 1) * DH, s * BLK : (s + 1) * BLK] = held[n][
                        head_rows(head), lane_block(slots[first + s])
                    ]
        stores[i].start()
    for store in stores:
        store.wait()


def regroup_kernel(a_ref, b_ref, *refs):
    for s, out in enumerate(refs[-3:]):
        out[0] = a_ref[s + 1, :, 0:HALF]
        out[1] = b_ref[s + 1, :, 0:HALF]


def split_query(q):
    scaled = q.astype(F32) * (DH**-0.5 * LOG2E)
    high = scaled.astype(BF16)
    low = (scaled - high.astype(F32)).astype(BF16)
    return jnp.concatenate([high, low], axis=0)


def twice_keys(keys_t):
    both = jnp.concatenate([keys_t, keys_t], axis=0).astype(F32)
    return both.T.astype(BF16)


def column_max(blocks):
    best = jnp.max(blocks[0], axis=0, keepdims=True)
    for block in blocks[1:]:
        best = jnp.maximum(best, jnp.max(block, axis=0, keepdims=True))
    return best


def near_kernel(inputs, units, tasks, carried, place, mid, top, *refs):
    pieces = dict(zip(inputs, refs[: len(inputs)]))
    refs = refs[len(inputs) :]
    old = [refs[2 * i : 2 * i + 2] for i in range(carried)]
    outs = refs[2 * carried : 2 * carried + 2 * len(tasks)]
    k_s, v_s = refs[-2:]
    head = head_of(place, 0, pl.program_id(0))
    same = mid[head] == top[head]
    lane_slot = lax.broadcasted_iota(jnp.int32, (1, HALF), 1) // BLK
    again = [
        jnp.where(lane_slot == 0, jnp.where(same, 1.584962500721156, 1.0), 0.0),
        jnp.where(lane_slot == 1, jnp.where(same, 0.0, 1.0), 0.0),
    ]

    def lookup(j, slot):
        first = 0 if (j, 0) in pieces and pieces[j, 0].shape[2] > HALF else slot // 2 * 2
        return pieces[j, first], (slot - first) * BLK

    chunks = []
    row = 0
    for label, members in units:
        low = row
        for j, slot in members:
            ref, lane = lookup(j, slot)
            k_s[row : row + BLK, :] = twice_keys(ref[0, 0:DH, lane : lane + BLK])
            v_s[0:DH, row : row + BLK] = ref[0, DH : 2 * DH, lane : lane + BLK]
            row += BLK
        chunks.append((label, slice(low, row)))
    v_s[DH:DX, :] = jnp.ones((DX - DH, v_s.shape[1]), BF16)

    flat = [
        (query, low, merge, out, i)
        for out, group in enumerate(tasks)
        for i, (query, low, merge) in enumerate(group)
    ]

    def score(task):
        (j, half), low = task[:2]
        ref, lane = lookup(j, 2 * half)
        query = split_query(ref[0, 2 * DH :, lane : lane + HALF])
        return [dot(k_s[rows, :], query) for _, rows in chunks[low:]]

    scores = score(flat[0])
    for n, ((_, half), low, merge, out, i) in enumerate(flat):
        following = score(flat[n + 1]) if n + 1 < len(flat) else None
        best = column_max(scores)
        if merge is not None:
            acc_in, max_in = old[merge[0]]
            old_max = max_in[0, merge[1], 0:1, :]
            best = jnp.maximum(best, old_max)
        acc = None
        for (label, rows), block in zip(chunks[low:], scores):
            shift = best if half == 1 or label is None else best - again[label]
            part = dot(v_s[:, rows], jnp.exp2(block - shift).astype(BF16))
            acc = part if acc is None else acc + part
        if merge is not None:
            acc = acc + acc_in[0, merge[1]] * jnp.exp2(old_max - best)
        acc_ref, max_ref = outs[2 * out : 2 * out + 2]
        acc_ref[0, i] = acc
        max_ref[0, i] = jnp.broadcast_to(best, (8, HALF))
        scores = following


def far_kernel(place, mid, top, *refs):
    own, beyond = refs[:GROUP], refs[GROUP : GROUP + 6]
    outs = refs[GROUP + 6 : GROUP + 6 + RATE]
    k_s, v_s = refs[GROUP + 6 + RATE :]
    head = head_of(place, 0, 0)
    same = mid[head] == top[head]
    slots = (0, jnp.where(same, 0, 1))

    def source(s, j):
        return own[j].at[0] if s == 0 else beyond[2 * (s - 1) + j // 2].at[j % 2]

    for level, slot in enumerate(slots):
        for s in range(RATE):
            for j in range(GROUP):
                here = slice(j * BLK, (j + 1) * BLK)
                ref = source(s, j)
                k_s[level, s, here, :] = twice_keys(ref[0:DH, lane_block(slot)])
                v_s[level, s, 0:DH, here] = ref[DH : 2 * DH, lane_block(slot)]
    v_s[:, :, DH:DX, :] = jnp.ones((2, RATE, DX - DH, TOK), BF16)
    row = lax.broadcasted_iota(jnp.int32, (16, HALF), 0)
    tasks = [(s, level, chip) for s in range(RATE) for level in range(2) for chip in range(2)]

    def score(task):
        s, level, chip = task
        query = jnp.concatenate(
            [
                split_query(source(s, 2 * chip + i)[2 * DH :, lane_block(slots[level])])
                for i in range(2)
            ],
            axis=1,
        )
        return [dot(k_s[level, b], query) for b in range(RATE) if b != s]

    scores = score(tasks[0])
    for n, (s, level, chip) in enumerate(tasks):
        following = score(tasks[n + 1]) if n + 1 < len(tasks) else None
        best = column_max(scores)
        acc = None
        for i, b in enumerate([b for b in range(RATE) if b != s]):
            part = dot(v_s[level, b], jnp.exp2(scores[i] - best).astype(BF16))
            acc = part if acc is None else acc + part
        total = acc[DH : DH + 1, :]
        result = (acc[0:DH, :] / total).astype(BF16)
        lse = best + jnp.log2(total)
        if level == 0:
            lse = jnp.where(same, lse + 1.0, lse)
        else:
            lse = jnp.where(same, -1e30, lse)
        high = lse.astype(BF16).astype(F32)
        middle = (lse - high).astype(BF16).astype(F32)
        low = lse - high - middle
        tail = jnp.where(row == 0, high, jnp.where(row == 1, middle, jnp.where(row == 2, low, 0.0)))
        tail = tail.astype(BF16)
        for i in range(2):
            start = (2 * chip + i) * HALF + level * BLK
            lanes = slice(start, start + BLK)
            outs[s][0:DH, lanes] = result[:, i * BLK : (i + 1) * BLK]
            outs[s][DH:DX, lanes] = tail[:, i * BLK : (i + 1) * BLK]
        scores = following


def combine_kernel(place, *refs):
    states, far, out_ref = refs[:4], refs[4 : 4 + HG], refs[4 + HG]
    for j in range(GROUP):
        acc_ref, max_ref = states[j // 2 * 2 : j // 2 * 2 + 2]
        lanes = slice(j * HALF, (j + 1) * HALF)
        for p in range(HG):
            acc, best = acc_ref[p, j % 2 * 2], max_ref[p, j % 2 * 2, 0:1, :]
            tail = far[p][DH:DX, lanes].astype(F32)
            lse = tail[0:1] + tail[1:2] + tail[2:3]
            overall = jnp.maximum(best, lse)
            near_factor, far_factor = jnp.exp2(best - overall), jnp.exp2(lse - overall)
            total = acc[DH : DH + 1] * near_factor + far_factor
            value = acc[0:DH] * near_factor + far[p][0:DH, lanes].astype(F32) * far_factor
            out_ref[place[0] ^ j, p, :, 0:HALF] = (value / total).astype(BF16)
            acc = acc_ref[p, j % 2 * 2 + 1]
            out_ref[place[0] ^ j, p, :, HALF:] = (acc[0:DH] / acc[DH : DH + 1]).astype(BF16)


def project_kernel(place, mid, top, parts, w_ref, out_ref, held):
    for group in range(GROUP):
        for p in range(HG):
            head = group * HG + ((place[1] + p) & (HG - 1))
            slots = class_of_slots(mid[head], top[head])
            for s in range(RATE):
                held[head_rows(head), lane_block(slots[s])] = parts[
                    group, p, :, s * BLK : (s + 1) * BLK
                ]
    row = lax.broadcasted_iota(jnp.int32, (TOK, TOK), 0)
    col = lax.broadcasted_iota(jnp.int32, (TOK, TOK), 1)
    picker = (row == RATE * (col % BLK) + col // BLK).astype(BF16)
    attention = dot_nt(picker, held[...]).astype(BF16)
    out_ref[...] = dot(attention, w_ref[...]).astype(BF16)


def whole(shape):
    return pl.BlockSpec(shape, lambda *_: (0,) * len(shape))


def per_head(shape):
    return pl.BlockSpec(shape, lambda h, *_: (h,) + (0,) * (len(shape) - 1))


def call(
    kernel, scalars, args, grid, in_specs, outs, scratch, scores,
    limit=VMEM_LIMIT, aliases={}, after=(),
):
    known = len(scalars) + len(args)

    def body(*refs):
        kernel(*refs[:known], *refs[known + len(after) :])

    return pl.pallas_call(
        body if after else kernel,
        grid_spec=pltpu.PrefetchScalarGridSpec(
            num_scalar_prefetch=len(scalars),
            grid=grid,
            in_specs=list(in_specs) + [pl.BlockSpec(memory_space=pl.ANY)] * len(after),
            out_specs=[spec for spec, _ in outs],
            scratch_shapes=scratch,
        ),
        out_shape=[shape for _, shape in outs],
        input_output_aliases=aliases,
        compiler_params=pltpu.CompilerParams(vmem_limit_bytes=limit),
        cost_estimate=pl.CostEstimate(flops=scores, bytes_accessed=1024, transcendentals=0),
    )(*scalars, *args, *after)


def within(array, apart):
    count = lax.axis_size("seq")
    return lax.ppermute(array, "seq", [(i, i ^ apart) for i in range(count)])


def across(array, segments):
    count = lax.axis_size("seq")
    return lax.ppermute(
        array, "seq", [(i, (i + GROUP * segments) % count) for i in range(count)]
    )


def shards_four(queries, key_states, value_states, offsets_mid, offsets_top, out_weight):
    width = queries.shape[1]
    index = lax.axis_index("seq").astype(jnp.int32)
    place = jnp.stack([index % GROUP, index // GROUP])
    scalars = (place, offsets_mid, offsets_top)
    full = jax.ShapeDtypeStruct((HG, 3 * DH, TOK), BF16)
    piece = jax.ShapeDtypeStruct((HG, 3 * DH, HALF), BF16)
    pair = jax.ShapeDtypeStruct((2, 3 * DH, HALF), BF16)
    anywhere = pl.BlockSpec(memory_space=pl.ANY)
    shapes = [full] * 2 + [piece] * 4
    own0, own1, sel2, sel3, rest2, rest3 = call(
        pack_kernel, scalars, (key_states, value_states, queries), (1,),
        [anywhere] * 3,
        [(anywhere, shape) for shape in shapes],
        [pltpu.VMEM((TOK, width), BF16)] * 3
        + [pltpu.VMEM((width, TOK), BF16)] * 3
        + [pltpu.VMEM(shape.shape, BF16) for shape in shapes]
        + [pltpu.SemaphoreType.DMA((3,)), pltpu.SemaphoreType.DMA((6,))],
        1 << 19, VMEM_MOST,
    )
    own1 = within(own1, 1)
    sel2, sel3 = within(sel2, 2), within(sel3, 3)

    def regroup(a, b, through, after):
        shapes = [jax.ShapeDtypeStruct(x.shape, x.dtype) for x in through] + [pair] * 3
        return call(
            regroup_kernel, (), (a, b, *through), (1,),
            [whole(a.shape), whole(b.shape)] + [anywhere] * len(through),
            [(anywhere, x) for x in shapes[: len(through)]] + [(whole(pair.shape), pair)] * 3,
            [], 1 << 17,
            aliases={2 + i: i for i in range(len(through))}, after=after,
        )

    def state(count):
        return [
            (per_head((1, count, rows, HALF)), jax.ShapeDtypeStruct((HG, count, rows, HALF), F32))
            for rows in (DX, 8)
        ]

    def near(held, units, tasks, old, after=()):
        sizes = [len(members) * BLK for _, members in units]
        scores = sum(sum(sizes[low:]) * HALF for group in tasks for _, low, _ in group)
        return call(
            functools.partial(near_kernel, list(held), units, tasks, len(old)), scalars,
            (*held.values(), *[x for one in old for x in one]), (HG,),
            [per_head((1,) + x.shape[1:]) for x in held.values()]
            + [per_head((1,) + x.shape[1:]) for one in old for x in one],
            [out for group in tasks for out in state(len(group))],
            [pltpu.VMEM((sum(sizes), 2 * DH), BF16), pltpu.VMEM((DX, sum(sizes)), BF16)],
            HG * scores, after=after,
        )

    def units_of(a, b):
        return [(0, [(a, 0), (b, 0)]), (1, [(a, 1), (b, 1)])], [
            (None, [(a, 2), (a, 3), (b, 2), (b, 3)])
        ]

    own_sel, own_rest = units_of(0, 1)
    other_sel, other_rest = units_of(2, 3)
    own = [(0, 0), (0, 1), (1, 0), (1, 1)]

    ours = regroup(own0, own1, (), ())
    ours = [across(x, s + 1) for s, x in enumerate(ours)]
    held = {(0, 0): own0, (1, 0): own1}
    state_own = near(held, own_sel + own_rest, [[(q, 0, None) for q in own]], [])
    rest2, rest3, *theirs = regroup(
        sel2, sel3, (rest2, rest3), (state_own[1], *ours)
    )
    theirs = [across(x, s + 1) for s, x in enumerate(theirs)]
    rest2, rest3 = within(rest2, 2), within(rest3, 3)
    beyond = [x for both in zip(ours, theirs) for x in both]

    held.update({(2, 0): sel2, (3, 0): sel3})
    out = near(
        held, own_sel + own_rest + other_sel,
        [
            [(q, 3, (0, i)) for i, q in enumerate(own)],
            [((2, 0), 0, None), ((3, 0), 0, None)],
        ],
        [state_own],
    )
    state_own, state_sel = out[:2], out[2:]

    result = jax.ShapeDtypeStruct((DX, GROUP * HALF), BF16)
    piece_0 = pl.BlockSpec((1, 3 * DH, HALF), lambda *_: (0, 0, 0))
    results = call(
        far_kernel, scalars, (own0, own1, sel2, sel3, *beyond), (1,),
        [piece_0] * GROUP + [whole(pair.shape)] * 6,
        [(whole(result.shape), result)] * RATE,
        [
            pltpu.VMEM((2, RATE, TOK, 2 * DH), BF16),
            pltpu.VMEM((2, RATE, DX, TOK), BF16),
        ],
        RATE * 2 * 3 * TOK * TOK, after=(out[1],),
    )
    back = [results[0]] + [across(results[s], -s) for s in range(1, RATE)]

    held.update({(2, 2): rest2, (3, 2): rest3})
    out = near(
        held, own_sel + own_rest + other_sel + other_rest,
        [
            [
                ((2, 0), 5, (1, 0)), ((2, 1), 0, None),
                ((3, 0), 5, (1, 1)), ((3, 1), 0, None),
            ],
            [(q, 5, (0, i)) for i, q in enumerate(own)],
        ],
        [state_own, state_sel],
        after=results[:1],
    )
    attended = jax.ShapeDtypeStruct((GROUP, HG, DH, TOK), BF16)
    states = (*out[2:], *out[:2])
    (parts,) = call(
        combine_kernel, (place,), (*states, *back), (1,),
        [whole(x.shape) for x in states] + [whole(result.shape)] * HG,
        [(whole(attended.shape), attended)],
        [],
        1 << 18,
    )
    count = lax.axis_size("seq")
    segments = [list(range(i, i + GROUP)) for i in range(0, count, GROUP)]
    parts = lax.all_to_all(parts, "seq", 0, 0, axis_index_groups=segments, tiled=True)
    return call(
        project_kernel, scalars, (parts, out_weight), (1,),
        [whole(attended.shape), whole((width, width))],
        [(whole((TOK, width)), jax.ShapeDtypeStruct((TOK, width), BF16))],
        [pltpu.VMEM((width, TOK), BF16)],
        1 << 18,
    )[0]


def shards(queries, key_states, value_states, offsets_mid, offsets_top, out_weight):
    tokens, width = queries.shape
    heads = offsets_mid.shape[0]
    fits = (
        lax.axis_size("head") == 1
        and lax.axis_size("seq") == GROUP * RATE
        and tokens == TOK
        and heads == GROUP * HG
        and width == heads * DH
    )
    run = shards_four if fits else shards_general
    return run(queries, key_states, value_states, offsets_mid, offsets_top, out_weight)


def solution(mesh):
    in_specs = (
        P(("slide", "seq"), "head"),
        P(("slide", "seq"), "head"),
        P(("slide", "seq"), "head"),
        P(),
        P(),
        P("head", None),
    )
    out_specs = P(("slide", "seq", "head"), None)
    return jax.shard_map(shards, mesh=mesh, in_specs=in_specs, out_specs=out_specs, check_vma=False)
```

```python
import functools

import jax
import jax.numpy as jnp
from jax import lax
from jax.experimental import pallas as pl
from jax.experimental.pallas import tpu as pltpu
from jax.sharding import PartitionSpec as P

SEG = 2048
LOG2E = 1.4426950408889634
VMEM_LIMIT = 40 * 1024 * 1024
VMEM_MOST = 60 * 1024 * 1024
BF16 = jnp.bfloat16
F32 = jnp.float32


def partner_2(block, axis, apart):
    count = lax.axis_size(axis)
    route = []
    for low in range(count):
        high = low | 1 << apart
        if high != low and high < count:
            route += [(low, high), (high, low)]
    return lax.ppermute(block, axis, route)


def attend_head(triple_in):
    query_rows, key_rows, value_rows = triple_in
    score_scale = query_rows.shape[-1] ** (-0.5)
    scores = jnp.dot(query_rows, key_rows.T, preferred_element_type=jnp.float32) * score_scale
    row_max = jnp.max(scores, axis=1)
    shifted = jnp.exp(scores - row_max[:, None])
    row_total = jnp.sum(shifted, axis=1)
    weights = shifted.astype(jnp.bfloat16)
    numerator = jnp.dot(weights, value_rows, preferred_element_type=jnp.float32)
    return (numerator, row_total, row_max)


def attend_local(query_rows, pair_rows):
    return lax.map(
        attend_head,
        (
            query_rows.transpose(1, 0, 2),
            pair_rows[:, 0].transpose(1, 0, 2),
            pair_rows[:, 1].transpose(1, 0, 2),
        ),
    )


def pick_rows(states, offsets, rate):
    row_count, inner_count, heads_here, head_width = states.shape
    picker = (jnp.arange(rate)[:, None] == offsets[None, :]).astype(jnp.bfloat16)
    folded = states.reshape(row_count // rate, rate, inner_count, heads_here, head_width)
    return jnp.einsum("archd,rh->achd", folded, picker, preferred_element_type=jnp.float32).astype(
        jnp.bfloat16
    )


def spread_back(numerator, row_total, row_max, offsets, rate):
    heads_here, picked_count, head_width = numerator.shape
    chosen = jnp.arange(rate)[:, None] == offsets[None, :]
    full_num = jnp.where(chosen[None, :, :, None], numerator.transpose(1, 0, 2)[:, None], 0.0)
    full_total = jnp.where(chosen[None], row_total.T[:, None], 0.0)
    full_max = jnp.where(chosen[None], row_max.T[:, None], -1e30)
    return (
        full_num.reshape(picked_count * rate, heads_here, head_width),
        full_total.reshape(picked_count * rate, heads_here),
        full_max.reshape(picked_count * rate, heads_here),
    )


def doubling(buffer, steps_count):
    position = lax.axis_index("seq")
    for bit_index in range(steps_count):
        partner = partner_2(buffer, "seq", bit_index)
        is_lower = position >> bit_index & 1 == 0
        buffer = jnp.where(
            is_lower, jnp.concatenate([buffer, partner], 0), jnp.concatenate([partner, buffer], 0)
        )
    return buffer


def shards_general(queries, key_states, value_states, offsets_mid, offsets_top, out_weight):
    tok_rows = queries.shape[0]
    heads_local = offsets_mid.shape[0] // lax.axis_size("head")
    head_size = queries.shape[1] // heads_local
    seq_devices = lax.axis_size("seq")
    seq_total = tok_rows * seq_devices
    width_mid = min(16 * SEG, seq_total)
    rate_mid = width_mid // SEG
    rate_top = seq_total // SEG
    start_head = lax.axis_index("head") * heads_local
    mid_local = lax.dynamic_slice(offsets_mid, (start_head,), (heads_local,))
    top_local = lax.dynamic_slice(offsets_top, (start_head,), (heads_local,))
    query_heads = queries.reshape(tok_rows, 1, heads_local, head_size)
    paired = jnp.stack([key_states, value_states], axis=1).reshape(
        tok_rows, 2, heads_local, head_size
    )
    near_bits = (SEG // tok_rows).bit_length() - 1
    near_rows = doubling(paired.reshape(tok_rows, -1), near_bits).reshape(
        SEG, 2, heads_local, head_size
    )
    near_num, near_total, near_max = attend_local(query_heads[:, 0], near_rows)
    level_near = spread_back(
        near_num, near_total, near_max, jnp.zeros((heads_local,), jnp.int32), 1
    )
    mid_q = pick_rows(query_heads, mid_local, rate_mid)[:, 0]
    mid_kv = pick_rows(paired, mid_local, rate_mid)
    mid_group = width_mid // tok_rows
    mid_bits = mid_group.bit_length() - 1
    mid_rows = doubling(mid_kv.reshape(mid_kv.shape[0], -1), mid_bits).reshape(
        SEG, 2, heads_local, head_size
    )
    mid_num, mid_total, mid_max = attend_local(mid_q, mid_rows)
    level_mid = spread_back(mid_num, mid_total, mid_max, mid_local, rate_mid)
    top_q = pick_rows(query_heads, top_local, rate_top)[:, 0]
    top_kv = pick_rows(paired, top_local, rate_top)
    top_rows = lax.all_gather(
        top_kv.reshape(top_kv.shape[0], -1), "seq", axis=0, tiled=True
    ).reshape(SEG, 2, heads_local, head_size)
    top_num, top_total, top_max = attend_local(top_q, top_rows)
    level_top = spread_back(top_num, top_total, top_max, top_local, rate_top)
    levels = [level_near, level_mid, level_top]
    overall = jnp.maximum(jnp.maximum(level_near[2], level_mid[2]), level_top[2])
    numerator = jnp.zeros((tok_rows, heads_local, head_size), jnp.float32)
    row_total = jnp.zeros((tok_rows, heads_local), jnp.float32)
    for level_num, level_total, level_max in levels:
        factor = jnp.exp(level_max - overall)
        numerator = numerator + factor[..., None] * level_num
        row_total = row_total + factor * level_total
    attention = (
        (numerator / row_total[..., None])
        .astype(jnp.bfloat16)
        .reshape(tok_rows, heads_local * head_size)
    )
    result = lax.psum_scatter(
        jnp.dot(attention, out_weight, preferred_element_type=jnp.float32),
        "head",
        scatter_dimension=0,
        tiled=True,
    )
    return result.astype(jnp.bfloat16)


RATE = 4
GROUP = 4
HG = 4
STEP = 2
DH = 48
BLK = 128
HALF = 2 * BLK
TOK = 512
DX = 64


def dot(a, b):
    return jnp.dot(a, b, preferred_element_type=F32)


def dot_nt(a, b):
    return lax.dot_general(a, b, (((1,), (1,)), ((), ())), preferred_element_type=F32)


def class_of_slots(off_mid, off_top):
    first = off_mid
    second = jnp.where(off_top == off_mid, lax.rem(off_mid + 1, RATE), off_top)
    free0 = (first != 0) & (second != 0)
    free1 = (first != 1) & (second != 1)
    third = jnp.where(free0, 0, jnp.where(free1, 1, 2))
    return first, second, third, 6 - first - second - third


def head_of(place, j, p):
    return ((place[0] & (GROUP - 1)) ^ j) * HG + ((place[0] // GROUP) ^ p)


def token_picker():
    row = lax.broadcasted_iota(jnp.int32, (TOK, TOK), 0)
    col = lax.broadcasted_iota(jnp.int32, (TOK, TOK), 1)
    return (col == RATE * (row % BLK) + row // BLK).astype(BF16)


def fill_class_major(block, picker, scratch):
    ordered = dot(picker, block).astype(BF16)
    step = 256
    eye = (
        lax.broadcasted_iota(jnp.int32, (step, step), 0)
        == lax.broadcasted_iota(jnp.int32, (step, step), 1)
    ).astype(BF16)
    for c in range(0, block.shape[1], step):
        scratch[c : c + step, :] = dot_nt(eye, ordered[:, c : c + step]).astype(BF16)


def lane_block(index):
    return pl.ds(pl.multiple_of(index * BLK, BLK), BLK)


def head_rows(head):
    return pl.ds(pl.multiple_of(head * DH, 16), DH)


def pack_kernel(place, mid, top, k_hbm, v_hbm, q_hbm, *refs):
    outs, refs = refs[:6], refs[6:]
    blocks, held, packed, sems_in, sems_out = refs[:3], refs[3:6], refs[6:12], refs[12], refs[13]
    loads = [
        pltpu.make_async_copy(hbm, block, sems_in.at[i])
        for i, (hbm, block) in enumerate(zip((k_hbm, v_hbm, q_hbm), blocks))
    ]
    for load in loads:
        load.start()
    picker = token_picker()
    stores = []
    for n, (load, block, scratch) in enumerate(zip(loads, blocks, held)):
        load.wait()
        fill_class_major(block[...], picker, scratch)
        rows = slice(n * DH, (n + 1) * DH)
        for i, (j, first, count) in enumerate(
            ((0, 0, 4), (1, 0, 4), (2, 0, 2), (3, 0, 2), (2, 2, 2), (3, 2, 2))
        ):
            for p in range(HG):
                head = head_of(place, j, p)
                slots = class_of_slots(mid[head], top[head])
                for s in range(count):
                    packed[i][p, rows, s * BLK : (s + 1) * BLK] = scratch[
                        head_rows(head), lane_block(slots[first + s])
                    ]
            store = pltpu.make_async_copy(
                packed[i].at[:, rows], outs[i].at[:, rows], sems_out.at[i, n]
            )
            store.start()
            stores.append(store)
    for store in stores:
        store.wait()


def regroup_kernel(a_ref, b_ref, *refs):
    for s, out in enumerate(refs[-3:]):
        out[0] = a_ref[s + 1, :, 0:HALF]
        out[1] = b_ref[s + 1, :, 0:HALF]


def split_query(q):
    scaled = q.astype(F32) * (DH**-0.5 * LOG2E)
    high = scaled.astype(BF16)
    low = (scaled - high.astype(F32)).astype(BF16)
    return jnp.concatenate([high, low], axis=0)


def twice_keys(keys_t):
    both = jnp.concatenate([keys_t, keys_t], axis=0).astype(F32)
    return both.T.astype(BF16)


def column_max(blocks):
    best = jnp.max(blocks[0], axis=0, keepdims=True)
    for block in blocks[1:]:
        best = jnp.maximum(best, jnp.max(block, axis=0, keepdims=True))
    return best


def near_kernel(inputs, units, tasks, carried, place, mid, top, *refs):
    pieces = dict(zip(inputs, refs[: len(inputs)]))
    refs = refs[len(inputs) :]
    old = [refs[2 * i : 2 * i + 2] for i in range(carried)]
    outs = refs[2 * carried : 2 * carried + 2 * len(tasks)]
    k_s, v_s = refs[-2:]
    v_s[:, DH:DX, :] = jnp.ones((STEP, DX - DH, v_s.shape[2]), BF16)
    lane_slot = lax.broadcasted_iota(jnp.int32, (1, HALF), 1) // BLK

    def lookup(j, slot):
        first = 0 if (j, 0) in pieces and pieces[j, 0].shape[2] > HALF else slot // 2 * 2
        return pieces[j, first], (slot - first) * BLK

    chunks = []
    row = 0
    for label, members in units:
        chunks.append((label, slice(row, row + len(members) * BLK)))
        row += len(members) * BLK
    members = [member for _, group in units for member in group]

    def prepare(h):
        head = head_of(place, 0, pl.program_id(0) * STEP + h)
        same = mid[head] == top[head]
        for i, (j, slot) in enumerate(members):
            ref, lane = lookup(j, slot)
            rows = slice(i * BLK, (i + 1) * BLK)
            k_s[h, rows, :] = twice_keys(ref[h, 0:DH, lane : lane + BLK])
            v_s[h, 0:DH, rows] = ref[h, DH : 2 * DH, lane : lane + BLK]
        return [
            jnp.where(lane_slot == 0, jnp.where(same, 1.584962500721156, 1.0), 0.0),
            jnp.where(lane_slot == 1, jnp.where(same, 0.0, 1.0), 0.0),
        ]

    flat = [
        (h, query, low, merge, out, i)
        for h in range(STEP)
        for out, group in enumerate(tasks)
        for i, (query, low, merge) in enumerate(group)
    ]

    def score(task):
        h, (j, half), low = task[:3]
        ref, lane = lookup(j, 2 * half)
        query = split_query(ref[h, 2 * DH :, lane : lane + HALF])
        return [dot(k_s[h, rows, :], query) for _, rows in chunks[low:]]

    again = [prepare(h) for h in range(STEP)]
    scores = score(flat[0])
    for n, (h, (_, half), low, merge, out, i) in enumerate(flat):
        following = score(flat[n + 1]) if n + 1 < len(flat) else None
        best = column_max(scores)
        if merge is not None:
            acc_in, max_in = old[merge[0]]
            old_max = max_in[h, merge[1], 0:1, :]
            best = jnp.maximum(best, old_max)
        acc = None
        for (label, rows), block in zip(chunks[low:], scores):
            shift = best if half == 1 or label is None else best - again[h][label]
            part = dot(v_s[h, :, rows], jnp.exp2(block - shift).astype(BF16))
            acc = part if acc is None else acc + part
        if merge is not None:
            acc = acc + acc_in[h, merge[1]] * jnp.exp2(old_max - best)
        acc_ref, max_ref = outs[2 * out : 2 * out + 2]
        acc_ref[h, i] = acc
        max_ref[h, i] = jnp.broadcast_to(best, (8, HALF))
        scores = following


def far_kernel(place, mid, top, *refs):
    own, beyond = refs[:GROUP], refs[GROUP : GROUP + 6]
    outs = refs[GROUP + 6 : GROUP + 6 + RATE]
    k_s, v_s = refs[GROUP + 6 + RATE :]
    head = head_of(place, 0, 0)
    same = mid[head] == top[head]
    slots = (0, jnp.where(same, 0, 1))

    def source(s, j):
        return own[j].at[0] if s == 0 else beyond[2 * (s - 1) + j // 2].at[j % 2]

    for level, slot in enumerate(slots):
        for s in range(RATE):
            for j in range(GROUP):
                here = slice(j * BLK, (j + 1) * BLK)
                ref = source(s, j)
                k_s[level, s, here, :] = twice_keys(ref[0:DH, lane_block(slot)])
                v_s[level, s, 0:DH, here] = ref[DH : 2 * DH, lane_block(slot)]
    v_s[:, :, DH:DX, :] = jnp.ones((2, RATE, DX - DH, TOK), BF16)
    row = lax.broadcasted_iota(jnp.int32, (16, HALF), 0)
    tasks = [(s, level, chip) for s in range(RATE) for level in range(2) for chip in range(2)]

    def score(task):
        s, level, chip = task
        query = jnp.concatenate(
            [
                split_query(source(s, 2 * chip + i)[2 * DH :, lane_block(slots[level])])
                for i in range(2)
            ],
            axis=1,
        )
        return [dot(k_s[level, b], query) for b in range(RATE) if b != s]

    scores = score(tasks[0])
    for n, (s, level, chip) in enumerate(tasks):
        following = score(tasks[n + 1]) if n + 1 < len(tasks) else None
        best = column_max(scores)
        acc = None
        for i, b in enumerate([b for b in range(RATE) if b != s]):
            part = dot(v_s[level, b], jnp.exp2(scores[i] - best).astype(BF16))
            acc = part if acc is None else acc + part
        total = acc[DH : DH + 1, :]
        result = (acc[0:DH, :] / total).astype(BF16)
        lse = best + jnp.log2(total)
        if level == 0:
            lse = jnp.where(same, lse + 1.0, lse)
        else:
            lse = jnp.where(same, -1e30, lse)
        high = lse.astype(BF16).astype(F32)
        middle = (lse - high).astype(BF16).astype(F32)
        low = lse - high - middle
        tail = jnp.where(row == 0, high, jnp.where(row == 1, middle, jnp.where(row == 2, low, 0.0)))
        tail = tail.astype(BF16)
        for i in range(2):
            start = (2 * chip + i) * HALF + level * BLK
            lanes = slice(start, start + BLK)
            outs[s][0:DH, lanes] = result[:, i * BLK : (i + 1) * BLK]
            outs[s][DH:DX, lanes] = tail[:, i * BLK : (i + 1) * BLK]
        scores = following


def combine_kernel(chip, acc_ref, max_ref, *refs):
    far, outs = refs[:HG], refs[HG:]
    for i in range(2):
        lanes = slice((2 * chip + i) * HALF, (2 * chip + i + 1) * HALF)
        for p in range(HG):
            acc, best = acc_ref[p, 2 * i], max_ref[p, 2 * i, 0:1, :]
            tail = far[p][DH:DX, lanes].astype(F32)
            lse = tail[0:1] + tail[1:2] + tail[2:3]
            overall = jnp.maximum(best, lse)
            near_factor, far_factor = jnp.exp2(best - overall), jnp.exp2(lse - overall)
            total = acc[DH : DH + 1] * near_factor + far_factor
            value = acc[0:DH] * near_factor + far[p][0:DH, lanes].astype(F32) * far_factor
            outs[i][p, :, 0:HALF] = (value / total).astype(BF16)
            acc = acc_ref[p, 2 * i + 1]
            outs[i][p, :, HALF:] = (acc[0:DH] / acc[DH : DH + 1]).astype(BF16)


def project_kernel(place, mid, top, *refs):
    parts = refs[:GROUP]
    w_ref, out_ref, held = refs[GROUP:]
    for j in range(GROUP):
        for p in range(HG):
            head = head_of(place, j, p)
            slots = class_of_slots(mid[head], top[head])
            for s in range(RATE):
                held[head_rows(head), lane_block(slots[s])] = parts[j][
                    p, :, s * BLK : (s + 1) * BLK
                ]
    row = lax.broadcasted_iota(jnp.int32, (TOK, TOK), 0)
    col = lax.broadcasted_iota(jnp.int32, (TOK, TOK), 1)
    picker = (row == RATE * (col % BLK) + col // BLK).astype(BF16)
    attention = dot_nt(picker, held[...]).astype(BF16)
    out_ref[...] = dot(attention, w_ref[...]).astype(BF16)


def whole(shape):
    return pl.BlockSpec(shape, lambda *_: (0,) * len(shape))


def per_head(shape):
    return pl.BlockSpec(shape, lambda h, *_: (h,) + (0,) * (len(shape) - 1))


def call(
    kernel, scalars, args, grid, in_specs, outs, scratch, scores,
    limit=VMEM_LIMIT, aliases={}, after=(),
):
    known = len(scalars) + len(args)

    def body(*refs):
        kernel(*refs[:known], *refs[known + len(after) :])

    return pl.pallas_call(
        body if after else kernel,
        grid_spec=pltpu.PrefetchScalarGridSpec(
            num_scalar_prefetch=len(scalars),
            grid=grid,
            in_specs=list(in_specs) + [pl.BlockSpec(memory_space=pl.ANY)] * len(after),
            out_specs=[spec for spec, _ in outs],
            scratch_shapes=scratch,
        ),
        out_shape=[shape for _, shape in outs],
        input_output_aliases=aliases,
        compiler_params=pltpu.CompilerParams(vmem_limit_bytes=limit),
        cost_estimate=pl.CostEstimate(flops=0, bytes_accessed=0, transcendentals=0),
    )(*scalars, *args, *after)


def within(array, apart):
    count = lax.axis_size("seq")
    return lax.ppermute(array, "seq", [(i, i ^ apart) for i in range(count)])


def across(array, segments):
    return within(array, GROUP * segments)


def shards_four(queries, key_states, value_states, offsets_mid, offsets_top, out_weight):
    width = queries.shape[1]
    place = lax.axis_index("seq").astype(jnp.int32).reshape(1)
    scalars = (place, offsets_mid, offsets_top)
    full = jax.ShapeDtypeStruct((HG, 3 * DH, TOK), BF16)
    piece = jax.ShapeDtypeStruct((HG, 3 * DH, HALF), BF16)
    pair = jax.ShapeDtypeStruct((2, 3 * DH, HALF), BF16)
    anywhere = pl.BlockSpec(memory_space=pl.ANY)
    shapes = [full] * 2 + [piece] * 4
    own0, own1, sel2, sel3, rest2, rest3 = call(
        pack_kernel, scalars, (key_states, value_states, queries), (1,),
        [anywhere] * 3,
        [(anywhere, shape) for shape in shapes],
        [pltpu.VMEM((TOK, width), BF16)] * 3
        + [pltpu.VMEM((width, TOK), BF16)] * 3
        + [pltpu.VMEM(shape.shape, BF16) for shape in shapes]
        + [pltpu.SemaphoreType.DMA((3,)), pltpu.SemaphoreType.DMA((6, 3))],
        1 << 19, VMEM_MOST,
    )
    own1 = within(own1, 1)
    sel2, sel3 = within(sel2, 2), within(sel3, 3)

    def regroup(a, b, through, after):
        shapes = [jax.ShapeDtypeStruct(x.shape, x.dtype) for x in through] + [pair] * 3
        return call(
            regroup_kernel, (), (a, b, *through), (1,),
            [whole(a.shape), whole(b.shape)] + [anywhere] * len(through),
            [(anywhere, x) for x in shapes[: len(through)]] + [(whole(pair.shape), pair)] * 3,
            [], 1 << 17,
            aliases={2 + i: i for i in range(len(through))}, after=after,
        )

    def state(count):
        return [
            (per_head((STEP, count, rows, HALF)), jax.ShapeDtypeStruct((HG, count, rows, HALF), F32))
            for rows in (DX, 8)
        ]

    def near(held, units, tasks, old, after=()):
        sizes = [len(members) * BLK for _, members in units]
        scores = sum(sum(sizes[low:]) * HALF for group in tasks for _, low, _ in group)
        return call(
            functools.partial(near_kernel, list(held), units, tasks, len(old)), scalars,
            (*held.values(), *[x for one in old for x in one]), (HG // STEP,),
            [per_head((STEP,) + x.shape[1:]) for x in held.values()]
            + [per_head((STEP,) + x.shape[1:]) for one in old for x in one],
            [out for group in tasks for out in state(len(group))],
            [
                pltpu.VMEM((STEP, sum(sizes), 2 * DH), BF16),
                pltpu.VMEM((STEP, DX, sum(sizes)), BF16),
            ],
            HG * scores, after=after,
        )

    def units_of(a, b):
        return [(0, [(a, 0), (b, 0)]), (1, [(a, 1), (b, 1)])], [
            (None, [(a, 2), (a, 3), (b, 2), (b, 3)])
        ]

    own_sel, own_rest = units_of(0, 1)
    other_sel, other_rest = units_of(2, 3)
    own = [(0, 0), (0, 1), (1, 0), (1, 1)]

    ours = regroup(own0, own1, (), ())
    ours = [across(x, s + 1) for s, x in enumerate(ours)]
    held = {(0, 0): own0, (1, 0): own1}
    state_own = near(held, own_sel + own_rest, [[(q, 0, None) for q in own]], [])
    rest2, rest3, *theirs = regroup(
        sel2, sel3, (rest2, rest3), (state_own[1], *ours)
    )
    theirs = [across(x, s + 1) for s, x in enumerate(theirs)]
    rest2, rest3 = within(rest2, 2), within(rest3, 3)
    beyond = [x for both in zip(ours, theirs) for x in both]

    held.update({(2, 0): sel2, (3, 0): sel3})
    out = near(
        held, own_sel + own_rest + other_sel,
        [
            [(q, 3, (0, i)) for i, q in enumerate(own)],
            [((2, 0), 0, None), ((3, 0), 0, None)],
        ],
        [state_own],
    )
    state_own, state_sel = out[:2], out[2:]

    result = jax.ShapeDtypeStruct((DX, GROUP * HALF), BF16)
    piece_0 = pl.BlockSpec((1, 3 * DH, HALF), lambda *_: (0, 0, 0))
    results = call(
        far_kernel, scalars, (own0, own1, sel2, sel3, *beyond), (1,),
        [piece_0] * GROUP + [whole(pair.shape)] * 6,
        [(whole(result.shape), result)] * RATE,
        [
            pltpu.VMEM((2, RATE, TOK, 2 * DH), BF16),
            pltpu.VMEM((2, RATE, DX, TOK), BF16),
        ],
        RATE * 2 * 3 * TOK * TOK, after=(out[1],),
    )
    back = [results[0]] + [across(results[s], s) for s in range(1, RATE)]

    held.update({(2, 2): rest2, (3, 2): rest3})
    units = own_sel + own_rest + other_sel + other_rest
    attended = jax.ShapeDtypeStruct((HG, DH, TOK), BF16)

    def combine(chip, state):
        return call(
            functools.partial(combine_kernel, chip), (), (*state, *back), (1,),
            [whole(x.shape) for x in state] + [whole(result.shape)] * HG,
            [(whole(attended.shape), attended)] * 2,
            [],
            1 << 18,
        )

    state_other = near(
        held, units,
        [
            [
                ((2, 0), 5, (0, 0)), ((2, 1), 0, None),
                ((3, 0), 5, (0, 1)), ((3, 1), 0, None),
            ]
        ],
        [state_sel],
        after=results[:1],
    )
    part2, part3 = combine(1, state_other)
    state_own = near(
        {(2, 2): rest2, (3, 2): rest3, **{q: held[q] for q in ((0, 0), (1, 0))}},
        other_rest,
        [[(q, 0, (0, i)) for i, q in enumerate(own)]],
        [state_own],
        after=(part2,),
    )
    part0, part1 = combine(0, state_own)
    parts = [part0, within(part1, 1), within(part2, 2), within(part3, 3)]
    return call(
        project_kernel, scalars, (*parts, out_weight), (1,),
        [whole(attended.shape)] * GROUP + [whole((width, width))],
        [(whole((TOK, width)), jax.ShapeDtypeStruct((TOK, width), BF16))],
        [pltpu.VMEM((width, TOK), BF16)],
        1 << 18,
    )[0]


def shards(queries, key_states, value_states, offsets_mid, offsets_top, out_weight):
    tokens, width = queries.shape
    heads = offsets_mid.shape[0]
    fits = (
        lax.axis_size("head") == 1
        and lax.axis_size("seq") == GROUP * RATE
        and tokens == TOK
        and heads == GROUP * HG
        and width == heads * DH
    )
    run = shards_four if fits else shards_general
    return run(queries, key_states, value_states, offsets_mid, offsets_top, out_weight)


def solution(mesh):
    in_specs = (
        P(("slide", "seq"), "head"),
        P(("slide", "seq"), "head"),
        P(("slide", "seq"), "head"),
        P(),
        P(),
        P("head", None),
    )
    out_specs = P(("slide", "seq", "head"), None)
    return jax.shard_map(shards, mesh=mesh, in_specs=in_specs, out_specs=out_specs, check_vma=False)
```

```python
import functools

import jax
import jax.numpy as jnp
from jax import lax
from jax.experimental import pallas as pl
from jax.experimental.pallas import tpu as pltpu
from jax.sharding import PartitionSpec as P

SEG = 2048
LOG2E = 1.4426950408889634
VMEM_LIMIT = 40 * 1024 * 1024
VMEM_MOST = 60 * 1024 * 1024
BF16 = jnp.bfloat16
F32 = jnp.float32


def partner_2(block, axis, apart):
    count = lax.axis_size(axis)
    route = []
    for low in range(count):
        high = low | 1 << apart
        if high != low and high < count:
            route += [(low, high), (high, low)]
    return lax.ppermute(block, axis, route)


def attend_head(triple_in):
    query_rows, key_rows, value_rows = triple_in
    score_scale = query_rows.shape[-1] ** (-0.5)
    scores = jnp.dot(query_rows, key_rows.T, preferred_element_type=jnp.float32) * score_scale
    row_max = jnp.max(scores, axis=1)
    shifted = jnp.exp(scores - row_max[:, None])
    row_total = jnp.sum(shifted, axis=1)
    weights = shifted.astype(jnp.bfloat16)
    numerator = jnp.dot(weights, value_rows, preferred_element_type=jnp.float32)
    return (numerator, row_total, row_max)


def attend_local(query_rows, pair_rows):
    return lax.map(
        attend_head,
        (
            query_rows.transpose(1, 0, 2),
            pair_rows[:, 0].transpose(1, 0, 2),
            pair_rows[:, 1].transpose(1, 0, 2),
        ),
    )


def pick_rows(states, offsets, rate):
    row_count, inner_count, heads_here, head_width = states.shape
    picker = (jnp.arange(rate)[:, None] == offsets[None, :]).astype(jnp.bfloat16)
    folded = states.reshape(row_count // rate, rate, inner_count, heads_here, head_width)
    return jnp.einsum("archd,rh->achd", folded, picker, preferred_element_type=jnp.float32).astype(
        jnp.bfloat16
    )


def spread_back(numerator, row_total, row_max, offsets, rate):
    heads_here, picked_count, head_width = numerator.shape
    chosen = jnp.arange(rate)[:, None] == offsets[None, :]
    full_num = jnp.where(chosen[None, :, :, None], numerator.transpose(1, 0, 2)[:, None], 0.0)
    full_total = jnp.where(chosen[None], row_total.T[:, None], 0.0)
    full_max = jnp.where(chosen[None], row_max.T[:, None], -1e30)
    return (
        full_num.reshape(picked_count * rate, heads_here, head_width),
        full_total.reshape(picked_count * rate, heads_here),
        full_max.reshape(picked_count * rate, heads_here),
    )


def doubling(buffer, steps_count):
    position = lax.axis_index("seq")
    for bit_index in range(steps_count):
        partner = partner_2(buffer, "seq", bit_index)
        is_lower = position >> bit_index & 1 == 0
        buffer = jnp.where(
            is_lower, jnp.concatenate([buffer, partner], 0), jnp.concatenate([partner, buffer], 0)
        )
    return buffer


def shards_general(queries, key_states, value_states, offsets_mid, offsets_top, out_weight):
    tok_rows = queries.shape[0]
    heads_local = offsets_mid.shape[0] // lax.axis_size("head")
    head_size = queries.shape[1] // heads_local
    seq_devices = lax.axis_size("seq")
    seq_total = tok_rows * seq_devices
    width_mid = min(16 * SEG, seq_total)
    rate_mid = width_mid // SEG
    rate_top = seq_total // SEG
    start_head = lax.axis_index("head") * heads_local
    mid_local = lax.dynamic_slice(offsets_mid, (start_head,), (heads_local,))
    top_local = lax.dynamic_slice(offsets_top, (start_head,), (heads_local,))
    query_heads = queries.reshape(tok_rows, 1, heads_local, head_size)
    paired = jnp.stack([key_states, value_states], axis=1).reshape(
        tok_rows, 2, heads_local, head_size
    )
    near_bits = (SEG // tok_rows).bit_length() - 1
    near_rows = doubling(paired.reshape(tok_rows, -1), near_bits).reshape(
        SEG, 2, heads_local, head_size
    )
    near_num, near_total, near_max = attend_local(query_heads[:, 0], near_rows)
    level_near = spread_back(
        near_num, near_total, near_max, jnp.zeros((heads_local,), jnp.int32), 1
    )
    mid_q = pick_rows(query_heads, mid_local, rate_mid)[:, 0]
    mid_kv = pick_rows(paired, mid_local, rate_mid)
    mid_group = width_mid // tok_rows
    mid_bits = mid_group.bit_length() - 1
    mid_rows = doubling(mid_kv.reshape(mid_kv.shape[0], -1), mid_bits).reshape(
        SEG, 2, heads_local, head_size
    )
    mid_num, mid_total, mid_max = attend_local(mid_q, mid_rows)
    level_mid = spread_back(mid_num, mid_total, mid_max, mid_local, rate_mid)
    top_q = pick_rows(query_heads, top_local, rate_top)[:, 0]
    top_kv = pick_rows(paired, top_local, rate_top)
    top_rows = lax.all_gather(
        top_kv.reshape(top_kv.shape[0], -1), "seq", axis=0, tiled=True
    ).reshape(SEG, 2, heads_local, head_size)
    top_num, top_total, top_max = attend_local(top_q, top_rows)
    level_top = spread_back(top_num, top_total, top_max, top_local, rate_top)
    levels = [level_near, level_mid, level_top]
    overall = jnp.maximum(jnp.maximum(level_near[2], level_mid[2]), level_top[2])
    numerator = jnp.zeros((tok_rows, heads_local, head_size), jnp.float32)
    row_total = jnp.zeros((tok_rows, heads_local), jnp.float32)
    for level_num, level_total, level_max in levels:
        factor = jnp.exp(level_max - overall)
        numerator = numerator + factor[..., None] * level_num
        row_total = row_total + factor * level_total
    attention = (
        (numerator / row_total[..., None])
        .astype(jnp.bfloat16)
        .reshape(tok_rows, heads_local * head_size)
    )
    result = lax.psum_scatter(
        jnp.dot(attention, out_weight, preferred_element_type=jnp.float32),
        "head",
        scatter_dimension=0,
        tiled=True,
    )
    return result.astype(jnp.bfloat16)


RATE = 4
GROUP = 4
HG = 4
STEP = 2
DH = 48
BLK = 128
HALF = 2 * BLK
TOK = 512
DX = 64


def dot(a, b):
    return jnp.dot(a, b, preferred_element_type=F32)


def dot_nt(a, b):
    return lax.dot_general(a, b, (((1,), (1,)), ((), ())), preferred_element_type=F32)


def class_of_slots(off_mid, off_top):
    first = off_mid
    second = jnp.where(off_top == off_mid, lax.rem(off_mid + 1, RATE), off_top)
    free0 = (first != 0) & (second != 0)
    free1 = (first != 1) & (second != 1)
    third = jnp.where(free0, 0, jnp.where(free1, 1, 2))
    return first, second, third, 6 - first - second - third


def head_of(place, j, p):
    return ((place[0] & (GROUP - 1)) ^ j) * HG + ((place[0] // GROUP) ^ p)


def token_picker():
    row = lax.broadcasted_iota(jnp.int32, (TOK, TOK), 0)
    col = lax.broadcasted_iota(jnp.int32, (TOK, TOK), 1)
    return (col == RATE * (row % BLK) + row // BLK).astype(BF16)


def fill_class_major(block, picker, scratch):
    scratch[...] = lax.dot_general(
        block, picker, (((0,), (1,)), ((), ())), preferred_element_type=F32
    ).astype(BF16)


def lane_block(index):
    return pl.ds(pl.multiple_of(index * BLK, BLK), BLK)


def head_rows(head):
    return pl.ds(pl.multiple_of(head * DH, 16), DH)


def pack_kernel(place, mid, top, k_hbm, v_hbm, q_hbm, *refs):
    outs, refs = refs[:6], refs[6:]
    blocks, held, packed, sems_in, sems_out = refs[:3], refs[3:6], refs[6:12], refs[12], refs[13]
    loads = [
        pltpu.make_async_copy(hbm, block, sems_in.at[i])
        for i, (hbm, block) in enumerate(zip((k_hbm, v_hbm, q_hbm), blocks))
    ]
    for load in loads:
        load.start()
    picker = token_picker()
    stores = []
    for n, (load, block, scratch) in enumerate(zip(loads, blocks, held)):
        load.wait()
        fill_class_major(block[...], picker, scratch)
        rows = slice(n * DH, (n + 1) * DH)
        for i, (j, first, count) in enumerate(
            ((0, 0, 4), (1, 0, 4), (2, 0, 2), (3, 0, 2), (2, 2, 2), (3, 2, 2))
        ):
            for p in range(HG):
                head = head_of(place, j, p)
                slots = class_of_slots(mid[head], top[head])
                for s in range(count):
                    packed[i][p, rows, s * BLK : (s + 1) * BLK] = scratch[
                        head_rows(head), lane_block(slots[first + s])
                    ]
            store = pltpu.make_async_copy(
                packed[i].at[:, rows], outs[i].at[:, rows], sems_out.at[i, n]
            )
            store.start()
            stores.append(store)
    for store in stores:
        store.wait()


def regroup_kernel(a_ref, b_ref, *refs):
    for s, out in enumerate(refs[-3:]):
        out[0] = a_ref[s + 1, :, 0:HALF]
        out[1] = b_ref[s + 1, :, 0:HALF]


def split_query(q):
    scaled = q.astype(F32) * (DH**-0.5 * LOG2E)
    high = scaled.astype(BF16)
    low = (scaled - high.astype(F32)).astype(BF16)
    return jnp.concatenate([high, low], axis=0)


def twice_keys(keys_t):
    both = jnp.concatenate([keys_t, keys_t], axis=0).astype(F32)
    return both.T.astype(BF16)


def column_max(blocks):
    best = jnp.max(blocks[0], axis=0, keepdims=True)
    for block in blocks[1:]:
        best = jnp.maximum(best, jnp.max(block, axis=0, keepdims=True))
    return best


def near_kernel(inputs, units, tasks, carried, place, mid, top, *refs):
    pieces = dict(zip(inputs, refs[: len(inputs)]))
    refs = refs[len(inputs) :]
    old = [refs[2 * i : 2 * i + 2] for i in range(carried)]
    outs = refs[2 * carried : 2 * carried + 2 * len(tasks)]
    k_s, v_s = refs[-2:]
    v_s[:, DH:DX, :] = jnp.ones((STEP, DX - DH, v_s.shape[2]), BF16)
    lane_slot = lax.broadcasted_iota(jnp.int32, (1, HALF), 1) // BLK

    def lookup(j, slot):
        first = 0 if (j, 0) in pieces and pieces[j, 0].shape[2] > HALF else slot // 2 * 2
        return pieces[j, first], (slot - first) * BLK

    chunks = []
    row = 0
    for label, members in units:
        chunks.append((label, slice(row, row + len(members) * BLK)))
        row += len(members) * BLK
    members = [member for _, group in units for member in group]

    def prepare(h):
        head = head_of(place, 0, pl.program_id(0) * STEP + h)
        same = mid[head] == top[head]
        for i, (j, slot) in enumerate(members):
            ref, lane = lookup(j, slot)
            rows = slice(i * BLK, (i + 1) * BLK)
            k_s[h, rows, :] = twice_keys(ref[h, 0:DH, lane : lane + BLK])
            v_s[h, 0:DH, rows] = ref[h, DH : 2 * DH, lane : lane + BLK]
        return [
            jnp.where(lane_slot == 0, jnp.where(same, 1.584962500721156, 1.0), 0.0),
            jnp.where(lane_slot == 1, jnp.where(same, 0.0, 1.0), 0.0),
        ]

    flat = [
        (h, query, low, merge, out, i)
        for h in range(STEP)
        for out, group in enumerate(tasks)
        for i, (query, low, merge) in enumerate(group)
    ]

    def score(task):
        h, (j, half), low = task[:3]
        ref, lane = lookup(j, 2 * half)
        query = split_query(ref[h, 2 * DH :, lane : lane + HALF])
        return [dot(k_s[h, rows, :], query) for _, rows in chunks[low:]]

    again = [prepare(h) for h in range(STEP)]
    scores = score(flat[0])
    for n, (h, (_, half), low, merge, out, i) in enumerate(flat):
        following = score(flat[n + 1]) if n + 1 < len(flat) else None
        best = column_max(scores)
        if merge is not None:
            acc_in, max_in = old[merge[0]]
            old_max = max_in[h, merge[1], 0:1, :]
            best = jnp.maximum(best, old_max)
        acc = None
        for (label, rows), block in zip(chunks[low:], scores):
            shift = best if half == 1 or label is None else best - again[h][label]
            part = dot(v_s[h, :, rows], jnp.exp2(block - shift).astype(BF16))
            acc = part if acc is None else acc + part
        if merge is not None:
            acc = acc + acc_in[h, merge[1]] * jnp.exp2(old_max - best)
        acc_ref, max_ref = outs[2 * out : 2 * out + 2]
        acc_ref[h, i] = acc
        max_ref[h, i] = jnp.broadcast_to(best, (8, HALF))
        scores = following


def far_kernel(place, mid, top, *refs):
    own, beyond = refs[:GROUP], refs[GROUP : GROUP + 6]
    outs = refs[GROUP + 6 : GROUP + 6 + RATE]
    k_s, v_s, tail_s = refs[GROUP + 6 + RATE :]
    tail_s[...] = jnp.zeros(tail_s.shape, F32)
    head = head_of(place, 0, 0)
    same = mid[head] == top[head]
    slots = (0, jnp.where(same, 0, 1))

    def source(s, j):
        return own[j].at[0] if s == 0 else beyond[2 * (s - 1) + j // 2].at[j % 2]

    for level, slot in enumerate(slots):
        for s in range(RATE):
            for j in range(GROUP):
                here = slice(j * BLK, (j + 1) * BLK)
                ref = source(s, j)
                k_s[level, s, here, :] = twice_keys(ref[0:DH, lane_block(slot)])
                v_s[level, s, 0:DH, here] = ref[DH : 2 * DH, lane_block(slot)]
    v_s[:, :, DH:DX, :] = jnp.ones((2, RATE, DX - DH, TOK), BF16)
    tasks = [(s, level, chip) for s in range(RATE) for level in range(2) for chip in range(2)]

    def score(task):
        s, level, chip = task
        query = jnp.concatenate(
            [
                split_query(source(s, 2 * chip + i)[2 * DH :, lane_block(slots[level])])
                for i in range(2)
            ],
            axis=1,
        )
        return [dot(k_s[level, b], query) for b in range(RATE) if b != s]

    scores = score(tasks[0])
    for n, (s, level, chip) in enumerate(tasks):
        following = score(tasks[n + 1]) if n + 1 < len(tasks) else None
        best = column_max(scores)
        acc = None
        for i, b in enumerate([b for b in range(RATE) if b != s]):
            part = dot(v_s[level, b], jnp.exp2(scores[i] - best).astype(BF16))
            acc = part if acc is None else acc + part
        total = acc[DH : DH + 1, :]
        result = (acc[0:DH, :] / total).astype(BF16)
        lse = best + jnp.log2(total)
        if level == 0:
            lse = jnp.where(same, lse + 1.0, lse)
        else:
            lse = jnp.where(same, -1e30, lse)
        high = lse.astype(BF16).astype(F32)
        middle = (lse - high).astype(BF16).astype(F32)
        low = lse - high - middle
        for i in range(2):
            n = 2 * (2 * chip + i) + level
            outs[s][:, n * BLK : (n + 1) * BLK] = result[:, i * BLK : (i + 1) * BLK]
            for k, part in enumerate((high, middle, low)):
                tail_s[s, 3 * n + k : 3 * n + k + 1, :] = part[:, i * BLK : (i + 1) * BLK]
        scores = following
    for s in range(RATE):
        outs[s][:, GROUP * HALF :] = tail_s[s].astype(BF16)


def join(acc, best, far, j):
    tail = far[:, GROUP * HALF :].astype(F32)
    lse = jnp.concatenate(
        [
            tail[3 * n : 3 * n + 1] + tail[3 * n + 1 : 3 * n + 2] + tail[3 * n + 2 : 3 * n + 3]
            for n in (2 * j, 2 * j + 1)
        ],
        axis=1,
    )
    overall = jnp.maximum(best, lse)
    near_factor, far_factor = jnp.exp2(best - overall), jnp.exp2(lse - overall)
    total = acc[DH : DH + 1] * near_factor + far_factor
    value = far[:, j * HALF : (j + 1) * HALF].astype(F32) * far_factor
    return ((acc[0:DH] * near_factor + value) / total).astype(BF16)


def combine_kernel(chip, acc_ref, max_ref, *refs):
    far, outs = refs[:HG], refs[HG:]
    for i in range(2):
        for p in range(HG):
            outs[i][p, :, 0:HALF] = join(
                acc_ref[p, 2 * i], max_ref[p, 2 * i, 0:1, :], far[p], 2 * chip + i
            )
            acc = acc_ref[p, 2 * i + 1]
            outs[i][p, :, HALF:] = (acc[0:DH] / acc[DH : DH + 1]).astype(BF16)


def project_kernel(place, mid, top, *refs):
    parts = refs[:GROUP]
    w_ref, out_ref, held, attention = refs[GROUP:]

    @pl.when(pl.program_id(0) == 0)
    def _():
        for j in range(GROUP):
            for p in range(HG):
                head = head_of(place, j, p)
                slots = class_of_slots(mid[head], top[head])
                for s in range(RATE):
                    held[head_rows(head), lane_block(slots[s])] = parts[j][
                        p, :, s * BLK : (s + 1) * BLK
                    ]
        row = lax.broadcasted_iota(jnp.int32, (TOK, TOK), 0)
        col = lax.broadcasted_iota(jnp.int32, (TOK, TOK), 1)
        picker = (row == RATE * (col % BLK) + col // BLK).astype(BF16)
        attention[...] = dot_nt(picker, held[...]).astype(BF16)

    out_ref[...] = dot(attention[...], w_ref[...]).astype(BF16)


def whole(shape):
    return pl.BlockSpec(shape, lambda *_: (0,) * len(shape))


def per_head(shape):
    return pl.BlockSpec(shape, lambda h, *_: (h,) + (0,) * (len(shape) - 1))


def call(
    kernel, scalars, args, grid, in_specs, outs, scratch, scores,
    limit=VMEM_LIMIT, after=(), through=(),
):
    known = len(scalars) + len(args)
    extra = (*after, *through)
    count = len(outs)
    anywhere = pl.BlockSpec(memory_space=pl.ANY)

    def body(*refs):
        results = refs[known + len(extra) :]
        kernel(*refs[:known], *results[:count], *results[count + len(through) :])

    return pl.pallas_call(
        body if extra else kernel,
        grid_spec=pltpu.PrefetchScalarGridSpec(
            num_scalar_prefetch=len(scalars),
            grid=grid,
            in_specs=list(in_specs) + [anywhere] * len(extra),
            out_specs=[spec for spec, _ in outs] + [anywhere] * len(through),
            scratch_shapes=scratch,
        ),
        out_shape=[shape for _, shape in outs]
        + [jax.ShapeDtypeStruct(x.shape, x.dtype) for x in through],
        input_output_aliases={known + len(after) + i: count + i for i in range(len(through))},
        compiler_params=pltpu.CompilerParams(vmem_limit_bytes=limit),
        cost_estimate=pl.CostEstimate(flops=0, bytes_accessed=0, transcendentals=0),
    )(*scalars, *args, *extra)


def within(array, apart):
    count = lax.axis_size("seq")
    return lax.ppermute(array, "seq", [(i, i ^ apart) for i in range(count)])


def across(array, segments):
    return within(array, GROUP * segments)


def shards_four(queries, key_states, value_states, offsets_mid, offsets_top, out_weight):
    width = queries.shape[1]
    place = lax.axis_index("seq").astype(jnp.int32).reshape(1)
    scalars = (place, offsets_mid, offsets_top)
    full = jax.ShapeDtypeStruct((HG, 3 * DH, TOK), BF16)
    piece = jax.ShapeDtypeStruct((HG, 3 * DH, HALF), BF16)
    pair = jax.ShapeDtypeStruct((2, 3 * DH, HALF), BF16)
    anywhere = pl.BlockSpec(memory_space=pl.ANY)
    shapes = [full] * 2 + [piece] * 4
    own0, own1, sel2, sel3, rest2, rest3 = call(
        pack_kernel, scalars, (key_states, value_states, queries), (1,),
        [anywhere] * 3,
        [(anywhere, shape) for shape in shapes],
        [pltpu.VMEM((TOK, width), BF16)] * 3
        + [pltpu.VMEM((width, TOK), BF16)] * 3
        + [pltpu.VMEM(shape.shape, BF16) for shape in shapes]
        + [pltpu.SemaphoreType.DMA((3,)), pltpu.SemaphoreType.DMA((6, 3))],
        1 << 19, VMEM_MOST,
    )
    own1 = within(own1, 1)
    sel2, sel3 = within(sel2, 2), within(sel3, 3)

    def regroup(a, b, **order):
        return call(
            regroup_kernel, (), (a, b), (1,),
            [whole(a.shape), whole(b.shape)], [(whole(pair.shape), pair)] * 3,
            [], 1 << 17, **order,
        )

    def state(count):
        return [
            (per_head((STEP, count, rows, HALF)), jax.ShapeDtypeStruct((HG, count, rows, HALF), F32))
            for rows in (DX, 8)
        ]

    def near(held, units, tasks, old, **order):
        sizes = [len(members) * BLK for _, members in units]
        scores = sum(sum(sizes[low:]) * HALF for group in tasks for _, low, _ in group)
        return call(
            functools.partial(near_kernel, list(held), units, tasks, len(old)), scalars,
            (*held.values(), *[x for one in old for x in one]), (HG // STEP,),
            [per_head((STEP,) + x.shape[1:]) for x in held.values()]
            + [per_head((STEP,) + x.shape[1:]) for one in old for x in one],
            [out for group in tasks for out in state(len(group))],
            [
                pltpu.VMEM((STEP, sum(sizes), 2 * DH), BF16),
                pltpu.VMEM((STEP, DX, sum(sizes)), BF16),
            ],
            HG * scores, **order,
        )

    def units_of(a, b):
        return [(0, [(a, 0), (b, 0)]), (1, [(a, 1), (b, 1)])], [
            (None, [(a, 2), (a, 3), (b, 2), (b, 3)])
        ]

    own_sel, own_rest = units_of(0, 1)
    other_sel, other_rest = units_of(2, 3)
    own = [(0, 0), (0, 1), (1, 0), (1, 1)]

    ours = regroup(own0, own1)
    ours = [across(x, s + 1) for s, x in enumerate(ours)]
    held = {(0, 0): own0, (1, 0): own1}
    state_own = near(held, own_sel + own_rest, [[(q, 0, None) for q in own]], [])
    *theirs, rest2, rest3 = regroup(sel2, sel3, after=state_own[1:], through=(rest2, rest3))
    theirs = [across(x, s + 1) for s, x in enumerate(theirs)]
    rest2, rest3 = within(rest2, 2), within(rest3, 3)
    beyond = [x for both in zip(ours, theirs) for x in both]

    held.update({(2, 0): sel2, (3, 0): sel3})
    out = near(
        held, own_sel + own_rest + other_sel,
        [
            [(q, 3, (0, i)) for i, q in enumerate(own)],
            [((2, 0), 0, None), ((3, 0), 0, None)],
        ],
        [state_own],
        after=ours,
    )
    state_own, state_sel = out[:2], out[2:]

    result = jax.ShapeDtypeStruct((DH, GROUP * HALF + BLK), BF16)
    piece_0 = pl.BlockSpec((1, 3 * DH, HALF), lambda *_: (0, 0, 0))
    results = call(
        far_kernel, scalars, (own0, own1, sel2, sel3, *beyond), (1,),
        [piece_0] * GROUP + [whole(pair.shape)] * 6,
        [(whole(result.shape), result)] * RATE,
        [
            pltpu.VMEM((2, RATE, TOK, 2 * DH), BF16),
            pltpu.VMEM((2, RATE, DX, TOK), BF16),
            pltpu.VMEM((RATE, DH, BLK), F32),
        ],
        RATE * 2 * 3 * TOK * TOK, after=(out[1],),
    )
    back = [results[0]] + [across(results[s], s) for s in range(1, RATE)]

    held.update({(2, 2): rest2, (3, 2): rest3})
    units = own_sel + own_rest + other_sel + other_rest
    attended = jax.ShapeDtypeStruct((HG, DH, TOK), BF16)

    def combine(chip, state):
        return call(
            functools.partial(combine_kernel, chip), (), (*state, *back), (1,),
            [whole(x.shape) for x in state] + [whole(result.shape)] * HG,
            [(whole(attended.shape), attended)] * 2,
            [],
            1 << 18,
        )

    state_other = near(
        held, units,
        [
            [
                ((2, 0), 5, (0, 0)), ((2, 1), 0, None),
                ((3, 0), 5, (0, 1)), ((3, 1), 0, None),
            ]
        ],
        [state_sel],
        after=results[:1],
    )
    part2, part3 = combine(1, state_other)
    state_own = near(
        {(2, 2): rest2, (3, 2): rest3, **{q: held[q] for q in ((0, 0), (1, 0))}},
        other_rest,
        [[(q, 0, (0, i)) for i, q in enumerate(own)]],
        [state_own],
        after=(part2,),
    )
    part0, part1 = combine(0, state_own)
    parts = [part0, within(part1, 1), within(part2, 2), within(part3, 3)]
    return call(
        project_kernel, scalars, (*parts, out_weight), (width // 256,),
        [whole(attended.shape)] * GROUP + [pl.BlockSpec((width, 256), lambda n, *_: (0, n))],
        [
            (
                pl.BlockSpec((TOK, 256), lambda n, *_: (0, n)),
                jax.ShapeDtypeStruct((TOK, width), BF16),
            )
        ],
        [pltpu.VMEM((width, TOK), BF16), pltpu.VMEM((TOK, width), BF16)],
        1 << 18,
    )[0]


def shards(queries, key_states, value_states, offsets_mid, offsets_top, out_weight):
    tokens, width = queries.shape
    heads = offsets_mid.shape[0]
    fits = (
        lax.axis_size("head") == 1
        and lax.axis_size("seq") == GROUP * RATE
        and tokens == TOK
        and heads == GROUP * HG
        and width == heads * DH
    )
    run = shards_four if fits else shards_general
    return run(queries, key_states, value_states, offsets_mid, offsets_top, out_weight)


def solution(mesh):
    in_specs = (
        P(("slide", "seq"), "head"),
        P(("slide", "seq"), "head"),
        P(("slide", "seq"), "head"),
        P(),
        P(),
        P("head", None),
    )
    out_specs = P(("slide", "seq", "head"), None)
    return jax.shard_map(shards, mesh=mesh, in_specs=in_specs, out_specs=out_specs, check_vma=False)
```

```python
import functools

import jax
import jax.numpy as jnp
from jax import lax
from jax.experimental import pallas as pl
from jax.experimental.pallas import tpu as pltpu
from jax.sharding import PartitionSpec as P

SEG = 2048
LOG2E = 1.4426950408889634
VMEM_LIMIT = 40 * 1024 * 1024
VMEM_MOST = 60 * 1024 * 1024
BF16 = jnp.bfloat16
F32 = jnp.float32


def partner_2(block, axis, apart):
    count = lax.axis_size(axis)
    route = []
    for low in range(count):
        high = low | 1 << apart
        if high != low and high < count:
            route += [(low, high), (high, low)]
    return lax.ppermute(block, axis, route)


def attend_head(triple_in):
    query_rows, key_rows, value_rows = triple_in
    score_scale = query_rows.shape[-1] ** (-0.5)
    scores = jnp.dot(query_rows, key_rows.T, preferred_element_type=jnp.float32) * score_scale
    row_max = jnp.max(scores, axis=1)
    shifted = jnp.exp(scores - row_max[:, None])
    row_total = jnp.sum(shifted, axis=1)
    weights = shifted.astype(jnp.bfloat16)
    numerator = jnp.dot(weights, value_rows, preferred_element_type=jnp.float32)
    return (numerator, row_total, row_max)


def attend_local(query_rows, pair_rows):
    return lax.map(
        attend_head,
        (
            query_rows.transpose(1, 0, 2),
            pair_rows[:, 0].transpose(1, 0, 2),
            pair_rows[:, 1].transpose(1, 0, 2),
        ),
    )


def pick_rows(states, offsets, rate):
    row_count, inner_count, heads_here, head_width = states.shape
    picker = (jnp.arange(rate)[:, None] == offsets[None, :]).astype(jnp.bfloat16)
    folded = states.reshape(row_count // rate, rate, inner_count, heads_here, head_width)
    return jnp.einsum("archd,rh->achd", folded, picker, preferred_element_type=jnp.float32).astype(
        jnp.bfloat16
    )


def spread_back(numerator, row_total, row_max, offsets, rate):
    heads_here, picked_count, head_width = numerator.shape
    chosen = jnp.arange(rate)[:, None] == offsets[None, :]
    full_num = jnp.where(chosen[None, :, :, None], numerator.transpose(1, 0, 2)[:, None], 0.0)
    full_total = jnp.where(chosen[None], row_total.T[:, None], 0.0)
    full_max = jnp.where(chosen[None], row_max.T[:, None], -1e30)
    return (
        full_num.reshape(picked_count * rate, heads_here, head_width),
        full_total.reshape(picked_count * rate, heads_here),
        full_max.reshape(picked_count * rate, heads_here),
    )


def doubling(buffer, steps_count):
    position = lax.axis_index("seq")
    for bit_index in range(steps_count):
        partner = partner_2(buffer, "seq", bit_index)
        is_lower = position >> bit_index & 1 == 0
        buffer = jnp.where(
            is_lower, jnp.concatenate([buffer, partner], 0), jnp.concatenate([partner, buffer], 0)
        )
    return buffer


def shards_general(queries, key_states, value_states, offsets_mid, offsets_top, out_weight):
    tok_rows = queries.shape[0]
    heads_local = offsets_mid.shape[0] // lax.axis_size("head")
    head_size = queries.shape[1] // heads_local
    seq_devices = lax.axis_size("seq")
    seq_total = tok_rows * seq_devices
    width_mid = min(16 * SEG, seq_total)
    rate_mid = width_mid // SEG
    rate_top = seq_total // SEG
    start_head = lax.axis_index("head") * heads_local
    mid_local = lax.dynamic_slice(offsets_mid, (start_head,), (heads_local,))
    top_local = lax.dynamic_slice(offsets_top, (start_head,), (heads_local,))
    query_heads = queries.reshape(tok_rows, 1, heads_local, head_size)
    paired = jnp.stack([key_states, value_states], axis=1).reshape(
        tok_rows, 2, heads_local, head_size
    )
    near_bits = (SEG // tok_rows).bit_length() - 1
    near_rows = doubling(paired.reshape(tok_rows, -1), near_bits).reshape(
        SEG, 2, heads_local, head_size
    )
    near_num, near_total, near_max = attend_local(query_heads[:, 0], near_rows)
    level_near = spread_back(
        near_num, near_total, near_max, jnp.zeros((heads_local,), jnp.int32), 1
    )
    mid_q = pick_rows(query_heads, mid_local, rate_mid)[:, 0]
    mid_kv = pick_rows(paired, mid_local, rate_mid)
    mid_group = width_mid // tok_rows
    mid_bits = mid_group.bit_length() - 1
    mid_rows = doubling(mid_kv.reshape(mid_kv.shape[0], -1), mid_bits).reshape(
        SEG, 2, heads_local, head_size
    )
    mid_num, mid_total, mid_max = attend_local(mid_q, mid_rows)
    level_mid = spread_back(mid_num, mid_total, mid_max, mid_local, rate_mid)
    top_q = pick_rows(query_heads, top_local, rate_top)[:, 0]
    top_kv = pick_rows(paired, top_local, rate_top)
    top_rows = lax.all_gather(
        top_kv.reshape(top_kv.shape[0], -1), "seq", axis=0, tiled=True
    ).reshape(SEG, 2, heads_local, head_size)
    top_num, top_total, top_max = attend_local(top_q, top_rows)
    level_top = spread_back(top_num, top_total, top_max, top_local, rate_top)
    levels = [level_near, level_mid, level_top]
    overall = jnp.maximum(jnp.maximum(level_near[2], level_mid[2]), level_top[2])
    numerator = jnp.zeros((tok_rows, heads_local, head_size), jnp.float32)
    row_total = jnp.zeros((tok_rows, heads_local), jnp.float32)
    for level_num, level_total, level_max in levels:
        factor = jnp.exp(level_max - overall)
        numerator = numerator + factor[..., None] * level_num
        row_total = row_total + factor * level_total
    attention = (
        (numerator / row_total[..., None])
        .astype(jnp.bfloat16)
        .reshape(tok_rows, heads_local * head_size)
    )
    result = lax.psum_scatter(
        jnp.dot(attention, out_weight, preferred_element_type=jnp.float32),
        "head",
        scatter_dimension=0,
        tiled=True,
    )
    return result.astype(jnp.bfloat16)


RATE = 4
GROUP = 4
HG = 4
STEP = 2
DH = 48
BLK = 128
HALF = 2 * BLK
TOK = 512
SAFE = 96.0
DX = 64


def dot(a, b):
    return jnp.dot(a, b, preferred_element_type=F32)


def dot_nt(a, b):
    return lax.dot_general(a, b, (((1,), (1,)), ((), ())), preferred_element_type=F32)


def class_of_slots(off_mid, off_top):
    first = off_mid
    second = jnp.where(off_top == off_mid, lax.rem(off_mid + 1, RATE), off_top)
    free0 = (first != 0) & (second != 0)
    free1 = (first != 1) & (second != 1)
    third = jnp.where(free0, 0, jnp.where(free1, 1, 2))
    return first, second, third, 6 - first - second - third


def head_of(place, j, p):
    return ((place[0] & (GROUP - 1)) ^ j) * HG + ((place[0] // GROUP) ^ p)


def token_picker():
    row = lax.broadcasted_iota(jnp.int32, (TOK, TOK), 0)
    col = lax.broadcasted_iota(jnp.int32, (TOK, TOK), 1)
    return (col == RATE * (row % BLK) + row // BLK).astype(BF16)


def fill_class_major(block, picker, scratch):
    scratch[...] = lax.dot_general(
        block, picker, (((0,), (1,)), ((), ())), preferred_element_type=F32
    ).astype(BF16)


def lane_block(index):
    return pl.ds(pl.multiple_of(index * BLK, BLK), BLK)


def head_rows(head):
    return pl.ds(pl.multiple_of(head * DH, 16), DH)


def pack_kernel(place, mid, top, k_hbm, v_hbm, q_hbm, *refs):
    outs, refs = refs[:6], refs[6:]
    blocks, held, packed, sems_in, sems_out = refs[:3], refs[3:6], refs[6:12], refs[12], refs[13]
    loads = [
        pltpu.make_async_copy(hbm, block, sems_in.at[i])
        for i, (hbm, block) in enumerate(zip((k_hbm, v_hbm, q_hbm), blocks))
    ]
    for load in loads:
        load.start()
    picker = token_picker()
    stores = []
    for n, (load, block, scratch) in enumerate(zip(loads, blocks, held)):
        load.wait()
        fill_class_major(block[...], picker, scratch)
        rows = slice(n * DH, (n + 1) * DH)
        for i, (j, first, count) in enumerate(
            ((0, 0, 4), (1, 0, 4), (2, 0, 2), (3, 0, 2), (2, 2, 2), (3, 2, 2))
        ):
            for p in range(HG):
                head = head_of(place, j, p)
                slots = class_of_slots(mid[head], top[head])
                for s in range(count):
                    packed[i][p, rows, s * BLK : (s + 1) * BLK] = scratch[
                        head_rows(head), lane_block(slots[first + s])
                    ]
            store = pltpu.make_async_copy(
                packed[i].at[:, rows], outs[i].at[:, rows], sems_out.at[i, n]
            )
            store.start()
            stores.append(store)
    for store in stores:
        store.wait()


def regroup_kernel(a_ref, b_ref, *refs):
    for s, out in enumerate(refs[-3:]):
        out[0] = a_ref[s + 1, :, 0:HALF]
        out[1] = b_ref[s + 1, :, 0:HALF]


def split_query(q):
    scaled = q.astype(F32) * (DH**-0.5 * LOG2E)
    high = scaled.astype(BF16)
    low = (scaled - high.astype(F32)).astype(BF16)
    return jnp.concatenate([high, low], axis=0)


def twice_keys(keys_t):
    both = jnp.concatenate([keys_t, keys_t], axis=0).astype(F32)
    return both.T.astype(BF16)


def largest(blocks):
    best = None
    for block in blocks:
        wide = block.astype(F32)
        length = jnp.sum(wide * wide, axis=0, keepdims=True)
        for low in range(0, block.shape[1], HALF):
            part = length[:, low : low + HALF]
            best = part if best is None else jnp.maximum(best, part)
    return jnp.max(best)


def is_small(queries, keys):
    scale = DH**-0.5 * LOG2E
    return largest(queries) * largest(keys) * (scale * scale) < SAFE * SAFE


def column_max(blocks):
    best = jnp.max(blocks[0], axis=0, keepdims=True)
    for block in blocks[1:]:
        best = jnp.maximum(best, jnp.max(block, axis=0, keepdims=True))
    return best


def near_kernel(inputs, units, tasks, carried, place, mid, top, *refs):
    pieces = dict(zip(inputs, refs[: len(inputs)]))
    refs = refs[len(inputs) :]
    old = [refs[2 * i : 2 * i + 2] for i in range(carried)]
    outs = refs[2 * carried : 2 * carried + 2 * len(tasks)]
    k_s, v_s = refs[-2:]
    v_s[:, DH:DX, :] = jnp.ones((STEP, DX - DH, v_s.shape[2]), BF16)
    lane_slot = lax.broadcasted_iota(jnp.int32, (1, HALF), 1) // BLK

    def lookup(j, slot):
        first = 0 if (j, 0) in pieces and pieces[j, 0].shape[2] > HALF else slot // 2 * 2
        return pieces[j, first], (slot - first) * BLK

    chunks = []
    row = 0
    for label, members in units:
        chunks.append((label, slice(row, row + len(members) * BLK)))
        row += len(members) * BLK
    members = [member for _, group in units for member in group]

    def prepare(h):
        head = head_of(place, 0, pl.program_id(0) * STEP + h)
        same = mid[head] == top[head]
        for i, (j, slot) in enumerate(members):
            ref, lane = lookup(j, slot)
            rows = slice(i * BLK, (i + 1) * BLK)
            k_s[h, rows, :] = twice_keys(ref[h, 0:DH, lane : lane + BLK])
            v_s[h, 0:DH, rows] = ref[h, DH : 2 * DH, lane : lane + BLK]
        return [
            jnp.where(lane_slot == 0, jnp.where(same, 1.584962500721156, 1.0), 0.0),
            jnp.where(lane_slot == 1, jnp.where(same, 0.0, 1.0), 0.0),
        ]

    flat = [
        (h, query, low, merge, out, i)
        for h in range(STEP)
        for out, group in enumerate(tasks)
        for i, (query, low, merge) in enumerate(group)
    ]

    def score(task):
        h, (j, half), low = task[:3]
        ref, lane = lookup(j, 2 * half)
        query = split_query(ref[h, 2 * DH :, lane : lane + HALF])
        return [dot(k_s[h, rows, :], query) for _, rows in chunks[low:]]

    again = [prepare(h) for h in range(STEP)]

    def run(plain):
        scores = score(flat[0])
        for n, (h, (_, half), low, merge, out, i) in enumerate(flat):
            following = score(flat[n + 1]) if n + 1 < len(flat) else None
            best = jnp.zeros((1, HALF), F32) if plain else column_max(scores)
            if merge is not None:
                acc_in, max_in = old[merge[0]]
                old_max = max_in[h, merge[1], 0:1, :]
                best = best if plain else jnp.maximum(best, old_max)
            acc = None
            for (label, rows), block in zip(chunks[low:], scores):
                if half == 0 and label is not None:
                    block = block - (best - again[h][label])
                elif not plain:
                    block = block - best
                part = dot(v_s[h, :, rows], jnp.exp2(block).astype(BF16))
                acc = part if acc is None else acc + part
            if merge is not None:
                before = acc_in[h, merge[1]]
                acc = acc + (before if plain else before * jnp.exp2(old_max - best))
            acc_ref, max_ref = outs[2 * out : 2 * out + 2]
            acc_ref[h, i] = acc
            max_ref[h, i] = jnp.broadcast_to(best, (8, HALF))
            scores = following

    plain = is_small(
        [ref[h, 2 * DH :, :] for ref in pieces.values() for h in range(STEP)],
        [ref[h, 0:DH, :] for ref in pieces.values() for h in range(STEP)],
    )
    for _, max_in in old:
        plain = plain & (jnp.max(jnp.abs(max_in[...])) == 0.0)
    pl.when(plain)(lambda: run(True))
    pl.when(jnp.logical_not(plain))(lambda: run(False))


def far_kernel(place, mid, top, *refs):
    own, beyond = refs[:GROUP], refs[GROUP : GROUP + 6]
    outs = refs[GROUP + 6 : GROUP + 6 + RATE]
    k_s, v_s, tail_s = refs[GROUP + 6 + RATE :]
    tail_s[...] = jnp.zeros(tail_s.shape, F32)
    head = head_of(place, 0, 0)
    same = mid[head] == top[head]
    slots = (0, jnp.where(same, 0, 1))

    def source(s, j):
        return own[j].at[0] if s == 0 else beyond[2 * (s - 1) + j // 2].at[j % 2]

    for level, slot in enumerate(slots):
        for s in range(RATE):
            for j in range(GROUP):
                here = slice(j * BLK, (j + 1) * BLK)
                ref = source(s, j)
                k_s[level, s, here, :] = twice_keys(ref[0:DH, lane_block(slot)])
                v_s[level, s, 0:DH, here] = ref[DH : 2 * DH, lane_block(slot)]
    v_s[:, :, DH:DX, :] = jnp.ones((2, RATE, DX - DH, TOK), BF16)
    tasks = [(s, level, chip) for s in range(RATE) for level in range(2) for chip in range(2)]

    def score(task):
        s, level, chip = task
        query = jnp.concatenate(
            [
                split_query(source(s, 2 * chip + i)[2 * DH :, lane_block(slots[level])])
                for i in range(2)
            ],
            axis=1,
        )
        return [dot(k_s[level, b], query) for b in range(RATE) if b != s]

    def run(plain):
        scores = score(tasks[0])
        for n, (s, level, chip) in enumerate(tasks):
            following = score(tasks[n + 1]) if n + 1 < len(tasks) else None
            best = jnp.zeros((1, HALF), F32) if plain else column_max(scores)
            acc = None
            for i, b in enumerate([b for b in range(RATE) if b != s]):
                block = scores[i] if plain else scores[i] - best
                part = dot(v_s[level, b], jnp.exp2(block).astype(BF16))
                acc = part if acc is None else acc + part
            total = acc[DH : DH + 1, :]
            result = (acc[0:DH, :] / total).astype(BF16)
            lse = best + jnp.log2(total)
            if level == 0:
                lse = jnp.where(same, lse + 1.0, lse)
            else:
                lse = jnp.where(same, -1e30, lse)
            high = lse.astype(BF16).astype(F32)
            middle = (lse - high).astype(BF16).astype(F32)
            low = lse - high - middle
            for i in range(2):
                n = 2 * (2 * chip + i) + level
                outs[s][:, n * BLK : (n + 1) * BLK] = result[:, i * BLK : (i + 1) * BLK]
                for k, part in enumerate((high, middle, low)):
                    tail_s[s, 3 * n + k : 3 * n + k + 1, :] = part[:, i * BLK : (i + 1) * BLK]
            scores = following

    every = [source(s, j) for s in range(RATE) for j in range(GROUP)]
    plain = is_small(
        [ref[2 * DH : 3 * DH, 0:HALF] for ref in every], [ref[0:DH, 0:HALF] for ref in every]
    )
    pl.when(plain)(lambda: run(True))
    pl.when(jnp.logical_not(plain))(lambda: run(False))
    for s in range(RATE):
        outs[s][:, GROUP * HALF :] = tail_s[s].astype(BF16)


def join(acc, best, far, j):
    tail = far[:, GROUP * HALF :].astype(F32)
    lse = jnp.concatenate(
        [
            tail[3 * n : 3 * n + 1] + tail[3 * n + 1 : 3 * n + 2] + tail[3 * n + 2 : 3 * n + 3]
            for n in (2 * j, 2 * j + 1)
        ],
        axis=1,
    )
    overall = jnp.maximum(best, lse)
    near_factor, far_factor = jnp.exp2(best - overall), jnp.exp2(lse - overall)
    total = acc[DH : DH + 1] * near_factor + far_factor
    value = far[:, j * HALF : (j + 1) * HALF].astype(F32) * far_factor
    return ((acc[0:DH] * near_factor + value) / total).astype(BF16)


def combine_kernel(chip, acc_ref, max_ref, *refs):
    far, outs = refs[:HG], refs[HG:]
    for i in range(2):
        for p in range(HG):
            outs[i][p, :, 0:HALF] = join(
                acc_ref[p, 2 * i], max_ref[p, 2 * i, 0:1, :], far[p], 2 * chip + i
            )
            acc = acc_ref[p, 2 * i + 1]
            outs[i][p, :, HALF:] = (acc[0:DH] / acc[DH : DH + 1]).astype(BF16)


def project_kernel(place, mid, top, *refs):
    parts = refs[:GROUP]
    w_ref, out_ref, held = refs[GROUP:]
    for j in range(GROUP):
        for p in range(HG):
            head = head_of(place, j, p)
            slots = class_of_slots(mid[head], top[head])
            for s in range(RATE):
                held[head_rows(head), lane_block(slots[s])] = parts[j][
                    p, :, s * BLK : (s + 1) * BLK
                ]
    row = lax.broadcasted_iota(jnp.int32, (TOK, TOK), 0)
    col = lax.broadcasted_iota(jnp.int32, (TOK, TOK), 1)
    picker = (row == RATE * (col % BLK) + col // BLK).astype(BF16)
    attention = dot_nt(picker, held[...]).astype(BF16)
    out_ref[...] = dot(attention, w_ref[...]).astype(BF16)


def whole(shape):
    return pl.BlockSpec(shape, lambda *_: (0,) * len(shape))


def per_head(shape):
    return pl.BlockSpec(shape, lambda h, *_: (h,) + (0,) * (len(shape) - 1))


def call(
    kernel, scalars, args, grid, in_specs, outs, scratch, scores,
    limit=VMEM_LIMIT, after=(), through=(),
):
    known = len(scalars) + len(args)
    extra = (*after, *through)
    count = len(outs)
    anywhere = pl.BlockSpec(memory_space=pl.ANY)

    def body(*refs):
        results = refs[known + len(extra) :]
        kernel(*refs[:known], *results[:count], *results[count + len(through) :])

    return pl.pallas_call(
        body if extra else kernel,
        grid_spec=pltpu.PrefetchScalarGridSpec(
            num_scalar_prefetch=len(scalars),
            grid=grid,
            in_specs=list(in_specs) + [anywhere] * len(extra),
            out_specs=[spec for spec, _ in outs] + [anywhere] * len(through),
            scratch_shapes=scratch,
        ),
        out_shape=[shape for _, shape in outs]
        + [jax.ShapeDtypeStruct(x.shape, x.dtype) for x in through],
        input_output_aliases={known + len(after) + i: count + i for i in range(len(through))},
        compiler_params=pltpu.CompilerParams(vmem_limit_bytes=limit),
        cost_estimate=pl.CostEstimate(flops=0, bytes_accessed=0, transcendentals=0),
    )(*scalars, *args, *extra)


def within(array, apart):
    count = lax.axis_size("seq")
    return lax.ppermute(array, "seq", [(i, i ^ apart) for i in range(count)])


def across(array, segments):
    return within(array, GROUP * segments)


def shards_four(queries, key_states, value_states, offsets_mid, offsets_top, out_weight):
    width = queries.shape[1]
    place = lax.axis_index("seq").astype(jnp.int32).reshape(1)
    scalars = (place, offsets_mid, offsets_top)
    full = jax.ShapeDtypeStruct((HG, 3 * DH, TOK), BF16)
    piece = jax.ShapeDtypeStruct((HG, 3 * DH, HALF), BF16)
    pair = jax.ShapeDtypeStruct((2, 3 * DH, HALF), BF16)
    anywhere = pl.BlockSpec(memory_space=pl.ANY)
    shapes = [full] * 2 + [piece] * 4
    own0, own1, sel2, sel3, rest2, rest3 = call(
        pack_kernel, scalars, (key_states, value_states, queries), (1,),
        [anywhere] * 3,
        [(anywhere, shape) for shape in shapes],
        [pltpu.VMEM((TOK, width), BF16)] * 3
        + [pltpu.VMEM((width, TOK), BF16)] * 3
        + [pltpu.VMEM(shape.shape, BF16) for shape in shapes]
        + [pltpu.SemaphoreType.DMA((3,)), pltpu.SemaphoreType.DMA((6, 3))],
        1 << 19, VMEM_MOST,
    )
    own1 = within(own1, 1)
    sel2, sel3 = within(sel2, 2), within(sel3, 3)

    def regroup(a, b, **order):
        return call(
            regroup_kernel, (), (a, b), (1,),
            [whole(a.shape), whole(b.shape)], [(whole(pair.shape), pair)] * 3,
            [], 1 << 17, **order,
        )

    def state(count):
        return [
            (per_head((STEP, count, rows, HALF)), jax.ShapeDtypeStruct((HG, count, rows, HALF), F32))
            for rows in (DX, 8)
        ]

    def near(held, units, tasks, old, **order):
        sizes = [len(members) * BLK for _, members in units]
        scores = sum(sum(sizes[low:]) * HALF for group in tasks for _, low, _ in group)
        return call(
            functools.partial(near_kernel, list(held), units, tasks, len(old)), scalars,
            (*held.values(), *[x for one in old for x in one]), (HG // STEP,),
            [per_head((STEP,) + x.shape[1:]) for x in held.values()]
            + [per_head((STEP,) + x.shape[1:]) for one in old for x in one],
            [out for group in tasks for out in state(len(group))],
            [
                pltpu.VMEM((STEP, sum(sizes), 2 * DH), BF16),
                pltpu.VMEM((STEP, DX, sum(sizes)), BF16),
            ],
            HG * scores, **order,
        )

    def units_of(a, b):
        return [(0, [(a, 0), (b, 0)]), (1, [(a, 1), (b, 1)])], [
            (None, [(a, 2), (a, 3), (b, 2), (b, 3)])
        ]

    own_sel, own_rest = units_of(0, 1)
    other_sel, other_rest = units_of(2, 3)
    own = [(0, 0), (0, 1), (1, 0), (1, 1)]

    ours = regroup(own0, own1)
    ours = [across(x, s + 1) for s, x in enumerate(ours)]
    held = {(0, 0): own0, (1, 0): own1}
    state_own = near(held, own_sel + own_rest, [[(q, 0, None) for q in own]], [])
    *theirs, rest2, rest3 = regroup(sel2, sel3, after=state_own[1:], through=(rest2, rest3))
    theirs = [across(x, s + 1) for s, x in enumerate(theirs)]
    rest2, rest3 = within(rest2, 2), within(rest3, 3)
    beyond = [x for both in zip(ours, theirs) for x in both]

    held.update({(2, 0): sel2, (3, 0): sel3})
    out = near(
        held, own_sel + own_rest + other_sel,
        [
            [(q, 3, (0, i)) for i, q in enumerate(own)],
            [((2, 0), 0, None), ((3, 0), 0, None)],
        ],
        [state_own],
        after=ours,
    )
    state_own, state_sel = out[:2], out[2:]

    result = jax.ShapeDtypeStruct((DH, GROUP * HALF + BLK), BF16)
    piece_0 = pl.BlockSpec((1, 3 * DH, HALF), lambda *_: (0, 0, 0))
    results = call(
        far_kernel, scalars, (own0, own1, sel2, sel3, *beyond), (1,),
        [piece_0] * GROUP + [whole(pair.shape)] * 6,
        [(whole(result.shape), result)] * RATE,
        [
            pltpu.VMEM((2, RATE, TOK, 2 * DH), BF16),
            pltpu.VMEM((2, RATE, DX, TOK), BF16),
            pltpu.VMEM((RATE, DH, BLK), F32),
        ],
        RATE * 2 * 3 * TOK * TOK, after=(out[1],),
    )
    back = [results[0]] + [across(results[s], s) for s in range(1, RATE)]

    held.update({(2, 2): rest2, (3, 2): rest3})
    units = own_sel + own_rest + other_sel + other_rest
    attended = jax.ShapeDtypeStruct((HG, DH, TOK), BF16)

    def combine(chip, state):
        return call(
            functools.partial(combine_kernel, chip), (), (*state, *back), (1,),
            [whole(x.shape) for x in state] + [whole(result.shape)] * HG,
            [(whole(attended.shape), attended)] * 2,
            [],
            1 << 18,
        )

    state_other = near(
        held, units,
        [
            [
                ((2, 0), 5, (0, 0)), ((2, 1), 0, None),
                ((3, 0), 5, (0, 1)), ((3, 1), 0, None),
            ]
        ],
        [state_sel],
        after=results[:1],
    )
    part2, part3 = combine(1, state_other)
    state_own = near(
        {(2, 2): rest2, (3, 2): rest3, **{q: held[q] for q in ((0, 0), (1, 0))}},
        other_rest,
        [[(q, 0, (0, i)) for i, q in enumerate(own)]],
        [state_own],
        after=(part2,),
    )
    part0, part1 = combine(0, state_own)
    parts = [part0, within(part1, 1), within(part2, 2), within(part3, 3)]
    return call(
        project_kernel, scalars, (*parts, out_weight), (1,),
        [whole(attended.shape)] * GROUP + [whole((width, width))],
        [(whole((TOK, width)), jax.ShapeDtypeStruct((TOK, width), BF16))],
        [pltpu.VMEM((width, TOK), BF16)],
        1 << 18,
    )[0]


def shards(queries, key_states, value_states, offsets_mid, offsets_top, out_weight):
    tokens, width = queries.shape
    heads = offsets_mid.shape[0]
    fits = (
        lax.axis_size("head") == 1
        and lax.axis_size("seq") == GROUP * RATE
        and tokens == TOK
        and heads == GROUP * HG
        and width == heads * DH
    )
    run = shards_four if fits else shards_general
    return run(queries, key_states, value_states, offsets_mid, offsets_top, out_weight)


def solution(mesh):
    in_specs = (
        P(("slide", "seq"), "head"),
        P(("slide", "seq"), "head"),
        P(("slide", "seq"), "head"),
        P(),
        P(),
        P("head", None),
    )
    out_specs = P(("slide", "seq", "head"), None)
    return jax.shard_map(shards, mesh=mesh, in_specs=in_specs, out_specs=out_specs, check_vma=False)
```

```python
import functools

import jax
import jax.numpy as jnp
from jax import lax
from jax.experimental import pallas as pl
from jax.experimental.pallas import tpu as pltpu
from jax.sharding import PartitionSpec as P

SEG = 2048
LOG2E = 1.4426950408889634
VMEM_LIMIT = 40 * 1024 * 1024
VMEM_MOST = 60 * 1024 * 1024
BF16 = jnp.bfloat16
F32 = jnp.float32


def partner_2(block, axis, apart):
    count = lax.axis_size(axis)
    route = []
    for low in range(count):
        high = low | 1 << apart
        if high != low and high < count:
            route += [(low, high), (high, low)]
    return lax.ppermute(block, axis, route)


def attend_head(triple_in):
    query_rows, key_rows, value_rows = triple_in
    score_scale = query_rows.shape[-1] ** (-0.5)
    scores = jnp.dot(query_rows, key_rows.T, preferred_element_type=jnp.float32) * score_scale
    row_max = jnp.max(scores, axis=1)
    shifted = jnp.exp(scores - row_max[:, None])
    row_total = jnp.sum(shifted, axis=1)
    weights = shifted.astype(jnp.bfloat16)
    numerator = jnp.dot(weights, value_rows, preferred_element_type=jnp.float32)
    return (numerator, row_total, row_max)


def attend_local(query_rows, pair_rows):
    return lax.map(
        attend_head,
        (
            query_rows.transpose(1, 0, 2),
            pair_rows[:, 0].transpose(1, 0, 2),
            pair_rows[:, 1].transpose(1, 0, 2),
        ),
    )


def pick_rows(states, offsets, rate):
    row_count, inner_count, heads_here, head_width = states.shape
    picker = (jnp.arange(rate)[:, None] == offsets[None, :]).astype(jnp.bfloat16)
    folded = states.reshape(row_count // rate, rate, inner_count, heads_here, head_width)
    return jnp.einsum("archd,rh->achd", folded, picker, preferred_element_type=jnp.float32).astype(
        jnp.bfloat16
    )


def spread_back(numerator, row_total, row_max, offsets, rate):
    heads_here, picked_count, head_width = numerator.shape
    chosen = jnp.arange(rate)[:, None] == offsets[None, :]
    full_num = jnp.where(chosen[None, :, :, None], numerator.transpose(1, 0, 2)[:, None], 0.0)
    full_total = jnp.where(chosen[None], row_total.T[:, None], 0.0)
    full_max = jnp.where(chosen[None], row_max.T[:, None], -1e30)
    return (
        full_num.reshape(picked_count * rate, heads_here, head_width),
        full_total.reshape(picked_count * rate, heads_here),
        full_max.reshape(picked_count * rate, heads_here),
    )


def doubling(buffer, steps_count):
    position = lax.axis_index("seq")
    for bit_index in range(steps_count):
        partner = partner_2(buffer, "seq", bit_index)
        is_lower = position >> bit_index & 1 == 0
        buffer = jnp.where(
            is_lower, jnp.concatenate([buffer, partner], 0), jnp.concatenate([partner, buffer], 0)
        )
    return buffer


def shards_general(queries, key_states, value_states, offsets_mid, offsets_top, out_weight):
    tok_rows = queries.shape[0]
    heads_local = offsets_mid.shape[0] // lax.axis_size("head")
    head_size = queries.shape[1] // heads_local
    seq_devices = lax.axis_size("seq")
    seq_total = tok_rows * seq_devices
    width_mid = min(16 * SEG, seq_total)
    rate_mid = width_mid // SEG
    rate_top = seq_total // SEG
    start_head = lax.axis_index("head") * heads_local
    mid_local = lax.dynamic_slice(offsets_mid, (start_head,), (heads_local,))
    top_local = lax.dynamic_slice(offsets_top, (start_head,), (heads_local,))
    query_heads = queries.reshape(tok_rows, 1, heads_local, head_size)
    paired = jnp.stack([key_states, value_states], axis=1).reshape(
        tok_rows, 2, heads_local, head_size
    )
    near_bits = (SEG // tok_rows).bit_length() - 1
    near_rows = doubling(paired.reshape(tok_rows, -1), near_bits).reshape(
        SEG, 2, heads_local, head_size
    )
    near_num, near_total, near_max = attend_local(query_heads[:, 0], near_rows)
    level_near = spread_back(
        near_num, near_total, near_max, jnp.zeros((heads_local,), jnp.int32), 1
    )
    mid_q = pick_rows(query_heads, mid_local, rate_mid)[:, 0]
    mid_kv = pick_rows(paired, mid_local, rate_mid)
    mid_group = width_mid // tok_rows
    mid_bits = mid_group.bit_length() - 1
    mid_rows = doubling(mid_kv.reshape(mid_kv.shape[0], -1), mid_bits).reshape(
        SEG, 2, heads_local, head_size
    )
    mid_num, mid_total, mid_max = attend_local(mid_q, mid_rows)
    level_mid = spread_back(mid_num, mid_total, mid_max, mid_local, rate_mid)
    top_q = pick_rows(query_heads, top_local, rate_top)[:, 0]
    top_kv = pick_rows(paired, top_local, rate_top)
    top_rows = lax.all_gather(
        top_kv.reshape(top_kv.shape[0], -1), "seq", axis=0, tiled=True
    ).reshape(SEG, 2, heads_local, head_size)
    top_num, top_total, top_max = attend_local(top_q, top_rows)
    level_top = spread_back(top_num, top_total, top_max, top_local, rate_top)
    levels = [level_near, level_mid, level_top]
    overall = jnp.maximum(jnp.maximum(level_near[2], level_mid[2]), level_top[2])
    numerator = jnp.zeros((tok_rows, heads_local, head_size), jnp.float32)
    row_total = jnp.zeros((tok_rows, heads_local), jnp.float32)
    for level_num, level_total, level_max in levels:
        factor = jnp.exp(level_max - overall)
        numerator = numerator + factor[..., None] * level_num
        row_total = row_total + factor * level_total
    attention = (
        (numerator / row_total[..., None])
        .astype(jnp.bfloat16)
        .reshape(tok_rows, heads_local * head_size)
    )
    result = lax.psum_scatter(
        jnp.dot(attention, out_weight, preferred_element_type=jnp.float32),
        "head",
        scatter_dimension=0,
        tiled=True,
    )
    return result.astype(jnp.bfloat16)


RATE = 4
GROUP = 4
HG = 4
STEP = 2
DH = 48
BLK = 128
HALF = 2 * BLK
TOK = 512
SAFE = 96.0
DX = 64


def dot(a, b):
    return jnp.dot(a, b, preferred_element_type=F32)


def dot_nt(a, b):
    return lax.dot_general(a, b, (((1,), (1,)), ((), ())), preferred_element_type=F32)


def class_of_slots(off_mid, off_top):
    first = off_mid
    second = jnp.where(off_top == off_mid, lax.rem(off_mid + 1, RATE), off_top)
    free0 = (first != 0) & (second != 0)
    free1 = (first != 1) & (second != 1)
    third = jnp.where(free0, 0, jnp.where(free1, 1, 2))
    return first, second, third, 6 - first - second - third


def head_of(place, j, p):
    return ((place[0] & (GROUP - 1)) ^ j) * HG + ((place[0] // GROUP) ^ p)


def token_picker():
    row = lax.broadcasted_iota(jnp.int32, (TOK, TOK), 0)
    col = lax.broadcasted_iota(jnp.int32, (TOK, TOK), 1)
    return (col == RATE * (row % BLK) + row // BLK).astype(BF16)


def fill_class_major(block, picker, scratch):
    scratch[...] = lax.dot_general(
        block, picker, (((0,), (1,)), ((), ())), preferred_element_type=F32
    ).astype(BF16)


def lane_block(index):
    return pl.ds(pl.multiple_of(index * BLK, BLK), BLK)


def head_rows(head):
    return pl.ds(pl.multiple_of(head * DH, 16), DH)


def pack_kernel(place, mid, top, k_hbm, v_hbm, q_hbm, *refs):
    outs, refs = refs[:6], refs[6:]
    blocks, held, packed, sems_in, sems_out = refs[:3], refs[3:6], refs[6:12], refs[12], refs[13]
    loads = [
        pltpu.make_async_copy(hbm, block, sems_in.at[i])
        for i, (hbm, block) in enumerate(zip((k_hbm, v_hbm, q_hbm), blocks))
    ]
    for load in loads:
        load.start()
    picker = token_picker()
    stores = []
    for n, (load, block, scratch) in enumerate(zip(loads, blocks, held)):
        load.wait()
        fill_class_major(block[...], picker, scratch)
        rows = slice(n * DH, (n + 1) * DH)
        for i, (j, first, count) in enumerate(
            ((0, 0, 4), (1, 0, 4), (2, 0, 2), (3, 0, 2), (2, 2, 2), (3, 2, 2))
        ):
            for p in range(HG):
                head = head_of(place, j, p)
                slots = class_of_slots(mid[head], top[head])
                for s in range(count):
                    packed[i][p, rows, s * BLK : (s + 1) * BLK] = scratch[
                        head_rows(head), lane_block(slots[first + s])
                    ]
            store = pltpu.make_async_copy(
                packed[i].at[:, rows], outs[i].at[:, rows], sems_out.at[i, n]
            )
            store.start()
            stores.append(store)
    for store in stores:
        store.wait()


def regroup_kernel(a_ref, b_ref, *refs):
    for s, out in enumerate(refs[-3:]):
        out[0] = a_ref[s + 1, :, 0:HALF]
        out[1] = b_ref[s + 1, :, 0:HALF]


def split_query(q):
    scaled = q.astype(F32) * (DH**-0.5 * LOG2E)
    high = scaled.astype(BF16)
    low = (scaled - high.astype(F32)).astype(BF16)
    return jnp.concatenate([high, low], axis=0)


def twice_keys(keys_t):
    both = jnp.concatenate([keys_t, keys_t], axis=0).astype(F32)
    return both.T.astype(BF16)


def largest(blocks):
    best = None
    for block in blocks:
        wide = block.astype(F32)
        length = jnp.sum(wide * wide, axis=0, keepdims=True)
        for low in range(0, block.shape[1], HALF):
            part = length[:, low : low + HALF]
            best = part if best is None else jnp.maximum(best, part)
    return jnp.max(best)


def is_small(queries, keys):
    scale = DH**-0.5 * LOG2E
    return largest(queries) * largest(keys) * (scale * scale) < SAFE * SAFE


def column_max(blocks):
    best = jnp.max(blocks[0], axis=0, keepdims=True)
    for block in blocks[1:]:
        best = jnp.maximum(best, jnp.max(block, axis=0, keepdims=True))
    return best


def near_kernel(inputs, units, tasks, carried, place, mid, top, *refs):
    pieces = dict(zip(inputs, refs[: len(inputs)]))
    refs = refs[len(inputs) :]
    old = [refs[2 * i : 2 * i + 2] for i in range(carried)]
    outs = refs[2 * carried : 2 * carried + 2 * len(tasks)]
    k_s, v_s = refs[-2:]
    v_s[:, DH:DX, :] = jnp.ones((STEP, DX - DH, v_s.shape[2]), BF16)
    lane_slot = lax.broadcasted_iota(jnp.int32, (1, HALF), 1) // BLK

    def lookup(j, slot):
        first = 0 if (j, 0) in pieces and pieces[j, 0].shape[2] > HALF else slot // 2 * 2
        return pieces[j, first], (slot - first) * BLK

    chunks = []
    row = 0
    for label, members in units:
        chunks.append((label, slice(row, row + len(members) * BLK)))
        row += len(members) * BLK
    members = [member for _, group in units for member in group]

    def prepare(h):
        for i, (j, slot) in enumerate(members):
            ref, lane = lookup(j, slot)
            rows = slice(i * BLK, (i + 1) * BLK)
            k_s[h, rows, :] = twice_keys(ref[h, 0:DH, lane : lane + BLK])
            v_s[h, 0:DH, rows] = ref[h, DH : 2 * DH, lane : lane + BLK]

    def counted_again(h):
        head = head_of(place, 0, pl.program_id(0) * STEP + h)
        same = mid[head] == top[head]
        return [
            jnp.where(lane_slot == 0, jnp.where(same, 1.584962500721156, 1.0), 0.0),
            jnp.where(lane_slot == 1, jnp.where(same, 0.0, 1.0), 0.0),
        ]

    def run(plain, heads):
        again = [counted_again(h) for h in heads]
        flat = [
            (h, again_h, query, low, merge, out, i)
            for h, again_h in zip(heads, again)
            for out, group in enumerate(tasks)
            for i, (query, low, merge) in enumerate(group)
        ]

        def score(task):
            h, _, (j, half), low = task[:4]
            ref, lane = lookup(j, 2 * half)
            query = split_query(ref[h, 2 * DH :, lane : lane + HALF])
            return [dot(k_s[h, rows, :], query) for _, rows in chunks[low:]]

        scores = score(flat[0])
        for n, (h, again_h, (_, half), low, merge, out, i) in enumerate(flat):
            following = score(flat[n + 1]) if n + 1 < len(flat) else None
            best = jnp.zeros((1, HALF), F32) if plain else column_max(scores)
            if merge is not None:
                acc_in, max_in = old[merge[0]]
                old_max = max_in[h, merge[1], 0:1, :]
                best = best if plain else jnp.maximum(best, old_max)
            acc = None
            for (label, rows), block in zip(chunks[low:], scores):
                if half == 0 and label is not None:
                    block = block - (best - again_h[label])
                elif not plain:
                    block = block - best
                part = dot(v_s[h, :, rows], jnp.exp2(block).astype(BF16))
                acc = part if acc is None else acc + part
            if merge is not None:
                before = acc_in[h, merge[1]]
                acc = acc + (before if plain else before * jnp.exp2(old_max - best))
            acc_ref, max_ref = outs[2 * out : 2 * out + 2]
            acc_ref[h, i] = acc
            max_ref[h, i] = jnp.broadcast_to(best, (8, HALF))
            scores = following

    for h in range(STEP):
        prepare(h)
    plain = is_small(
        [ref[h, 2 * DH :, :] for ref in pieces.values() for h in range(STEP)],
        [ref[h, 0:DH, :] for ref in pieces.values() for h in range(STEP)],
    )
    for _, max_in in old:
        plain = plain & (jnp.max(jnp.abs(max_in[...])) == 0.0)

    @pl.when(plain)
    def _():
        run(True, list(range(STEP)))

    @pl.when(jnp.logical_not(plain))
    def _():
        @pl.loop(0, STEP)
        def _(h):
            run(False, [h])


def far_kernel(place, mid, top, *refs):
    own, beyond = refs[:GROUP], refs[GROUP : GROUP + 6]
    outs = refs[GROUP + 6 : GROUP + 6 + RATE]
    k_s, v_s, q_s, result_s, tail_s = refs[GROUP + 6 + RATE :]
    head = head_of(place, 0, 0)
    same = mid[head] == top[head]
    slots = (0, jnp.where(same, 0, 1))

    def source(s, j):
        return own[j].at[0] if s == 0 else beyond[2 * (s - 1) + j // 2].at[j % 2]

    for s in range(RATE):
        for j in range(GROUP):
            ref = source(s, j)
            for level, slot in enumerate(slots):
                here = slice(j * BLK, (j + 1) * BLK)
                k_s[level, s, here, :] = twice_keys(ref[0:DH, lane_block(slot)])
                v_s[level, s, 0:DH, here] = ref[DH : 2 * DH, lane_block(slot)]
                q_s[level, s, :, here] = split_query(ref[2 * DH : 3 * DH, lane_block(slot)])
    v_s[:, :, DH:DX, :] = jnp.ones((2, RATE, DX - DH, TOK), BF16)
    tail_s[...] = jnp.zeros(tail_s.shape, F32)

    def run(plain):
        tasks = [(level, chip) for level in range(2) for chip in range(2)]

        def segment(s, carry):
            def score(task):
                level, chip = task
                query = q_s[level, s, :, chip * HALF : (chip + 1) * HALF]
                return [dot(k_s[level, s ^ d], query) for d in range(1, RATE)]

            scores = score(tasks[0])
            for n, (level, chip) in enumerate(tasks):
                following = score(tasks[n + 1]) if n + 1 < len(tasks) else None
                best = jnp.zeros((1, HALF), F32) if plain else column_max(scores)
                acc = None
                for d in range(1, RATE):
                    block = scores[d - 1] if plain else scores[d - 1] - best
                    part = dot(v_s[level, s ^ d], jnp.exp2(block).astype(BF16))
                    acc = part if acc is None else acc + part
                total = acc[DH : DH + 1, :]
                result = (acc[0:DH, :] / total).astype(BF16)
                lse = best + jnp.log2(total)
                if level == 0:
                    lse = jnp.where(same, lse + 1.0, lse)
                else:
                    lse = jnp.where(same, -1e30, lse)
                high = lse.astype(BF16).astype(F32)
                middle = (lse - high).astype(BF16).astype(F32)
                low = lse - high - middle
                for i in range(2):
                    n = 2 * (2 * chip + i) + level
                    mine = slice(i * BLK, (i + 1) * BLK)
                    result_s[s, :, n * BLK : (n + 1) * BLK] = result[:, mine]
                    for k, part in enumerate((high, middle, low)):
                        tail_s[s, 3 * n + k : 3 * n + k + 1, :] = part[:, mine]
                scores = following
            return carry

        lax.fori_loop(0, RATE, segment, 0, unroll=2 if plain else 1)

    every = [source(s, j) for s in range(RATE) for j in range(GROUP)]
    plain = is_small(
        [ref[2 * DH : 3 * DH, 0:HALF] for ref in every], [ref[0:DH, 0:HALF] for ref in every]
    )
    pl.when(plain)(lambda: run(True))
    pl.when(jnp.logical_not(plain))(lambda: run(False))
    for s in range(RATE):
        outs[s][:, : GROUP * HALF] = result_s[s]
        outs[s][:, GROUP * HALF :] = tail_s[s].astype(BF16)


def join(acc, best, far, j):
    tail = far[:, GROUP * HALF :].astype(F32)
    lse = jnp.concatenate(
        [
            tail[3 * n : 3 * n + 1] + tail[3 * n + 1 : 3 * n + 2] + tail[3 * n + 2 : 3 * n + 3]
            for n in (2 * j, 2 * j + 1)
        ],
        axis=1,
    )
    overall = jnp.maximum(best, lse)
    near_factor, far_factor = jnp.exp2(best - overall), jnp.exp2(lse - overall)
    total = acc[DH : DH + 1] * near_factor + far_factor
    value = far[:, j * HALF : (j + 1) * HALF].astype(F32) * far_factor
    return ((acc[0:DH] * near_factor + value) / total).astype(BF16)


def combine_kernel(chip, acc_ref, max_ref, *refs):
    far, outs = refs[:HG], refs[HG:]
    for i in range(2):
        for p in range(HG):
            outs[i][p, :, 0:HALF] = join(
                acc_ref[p, 2 * i], max_ref[p, 2 * i, 0:1, :], far[p], 2 * chip + i
            )
            acc = acc_ref[p, 2 * i + 1]
            outs[i][p, :, HALF:] = (acc[0:DH] / acc[DH : DH + 1]).astype(BF16)


def project_kernel(place, mid, top, *refs):
    parts = refs[:GROUP]
    w_ref, out_ref, held = refs[GROUP:]
    for j in range(GROUP):
        for p in range(HG):
            head = head_of(place, j, p)
            slots = class_of_slots(mid[head], top[head])
            for s in range(RATE):
                held[head_rows(head), lane_block(slots[s])] = parts[j][
                    p, :, s * BLK : (s + 1) * BLK
                ]
    row = lax.broadcasted_iota(jnp.int32, (TOK, TOK), 0)
    col = lax.broadcasted_iota(jnp.int32, (TOK, TOK), 1)
    picker = (row == RATE * (col % BLK) + col // BLK).astype(BF16)
    attention = dot_nt(picker, held[...]).astype(BF16)
    out_ref[...] = dot(attention, w_ref[...]).astype(BF16)


def whole(shape):
    return pl.BlockSpec(shape, lambda *_: (0,) * len(shape))


def per_head(shape):
    return pl.BlockSpec(shape, lambda h, *_: (h,) + (0,) * (len(shape) - 1))


def call(
    kernel, scalars, args, grid, in_specs, outs, scratch, scores,
    limit=VMEM_LIMIT, after=(), through=(),
):
    known = len(scalars) + len(args)
    extra = (*after, *through)
    count = len(outs)
    anywhere = pl.BlockSpec(memory_space=pl.ANY)

    def body(*refs):
        results = refs[known + len(extra) :]
        kernel(*refs[:known], *results[:count], *results[count + len(through) :])

    return pl.pallas_call(
        body if extra else kernel,
        grid_spec=pltpu.PrefetchScalarGridSpec(
            num_scalar_prefetch=len(scalars),
            grid=grid,
            in_specs=list(in_specs) + [anywhere] * len(extra),
            out_specs=[spec for spec, _ in outs] + [anywhere] * len(through),
            scratch_shapes=scratch,
        ),
        out_shape=[shape for _, shape in outs]
        + [jax.ShapeDtypeStruct(x.shape, x.dtype) for x in through],
        input_output_aliases={known + len(after) + i: count + i for i in range(len(through))},
        compiler_params=pltpu.CompilerParams(vmem_limit_bytes=limit),
        cost_estimate=pl.CostEstimate(flops=0, bytes_accessed=0, transcendentals=0),
    )(*scalars, *args, *extra)


def within(array, apart):
    count = lax.axis_size("seq")
    return lax.ppermute(array, "seq", [(i, i ^ apart) for i in range(count)])


def across(array, segments):
    return within(array, GROUP * segments)


def shards_four(queries, key_states, value_states, offsets_mid, offsets_top, out_weight):
    width = queries.shape[1]
    place = lax.axis_index("seq").astype(jnp.int32).reshape(1)
    scalars = (place, offsets_mid, offsets_top)
    full = jax.ShapeDtypeStruct((HG, 3 * DH, TOK), BF16)
    piece = jax.ShapeDtypeStruct((HG, 3 * DH, HALF), BF16)
    pair = jax.ShapeDtypeStruct((2, 3 * DH, HALF), BF16)
    anywhere = pl.BlockSpec(memory_space=pl.ANY)
    shapes = [full] * 2 + [piece] * 4
    own0, own1, sel2, sel3, rest2, rest3 = call(
        pack_kernel, scalars, (key_states, value_states, queries), (1,),
        [anywhere] * 3,
        [(anywhere, shape) for shape in shapes],
        [pltpu.VMEM((TOK, width), BF16)] * 3
        + [pltpu.VMEM((width, TOK), BF16)] * 3
        + [pltpu.VMEM(shape.shape, BF16) for shape in shapes]
        + [pltpu.SemaphoreType.DMA((3,)), pltpu.SemaphoreType.DMA((6, 3))],
        1 << 19, VMEM_MOST,
    )
    own1 = within(own1, 1)
    sel2, sel3 = within(sel2, 2), within(sel3, 3)

    def regroup(a, b, **order):
        return call(
            regroup_kernel, (), (a, b), (1,),
            [whole(a.shape), whole(b.shape)], [(whole(pair.shape), pair)] * 3,
            [], 1 << 17, **order,
        )

    def state(count):
        return [
            (per_head((STEP, count, rows, HALF)), jax.ShapeDtypeStruct((HG, count, rows, HALF), F32))
            for rows in (DX, 8)
        ]

    def near(held, units, tasks, old, **order):
        sizes = [len(members) * BLK for _, members in units]
        scores = sum(sum(sizes[low:]) * HALF for group in tasks for _, low, _ in group)
        return call(
            functools.partial(near_kernel, list(held), units, tasks, len(old)), scalars,
            (*held.values(), *[x for one in old for x in one]), (HG // STEP,),
            [per_head((STEP,) + x.shape[1:]) for x in held.values()]
            + [per_head((STEP,) + x.shape[1:]) for one in old for x in one],
            [out for group in tasks for out in state(len(group))],
            [
                pltpu.VMEM((STEP, sum(sizes), 2 * DH), BF16),
                pltpu.VMEM((STEP, DX, sum(sizes)), BF16),
            ],
            HG * scores, **order,
        )

    def units_of(a, b):
        return [(0, [(a, 0), (b, 0)]), (1, [(a, 1), (b, 1)])], [
            (None, [(a, 2), (a, 3), (b, 2), (b, 3)])
        ]

    own_sel, own_rest = units_of(0, 1)
    other_sel, other_rest = units_of(2, 3)
    own = [(0, 0), (0, 1), (1, 0), (1, 1)]

    ours = regroup(own0, own1)
    ours = [across(x, s + 1) for s, x in enumerate(ours)]
    held = {(0, 0): own0, (1, 0): own1}
    state_own = near(held, own_sel + own_rest, [[(q, 0, None) for q in own]], [])
    *theirs, rest2, rest3 = regroup(sel2, sel3, after=state_own[1:], through=(rest2, rest3))
    theirs = [across(x, s + 1) for s, x in enumerate(theirs)]
    rest2, rest3 = within(rest2, 2), within(rest3, 3)
    beyond = [x for both in zip(ours, theirs) for x in both]

    held.update({(2, 0): sel2, (3, 0): sel3})
    out = near(
        held, own_sel + own_rest + other_sel,
        [
            [(q, 3, (0, i)) for i, q in enumerate(own)],
            [((2, 0), 0, None), ((3, 0), 0, None)],
        ],
        [state_own],
        after=ours,
    )
    state_own, state_sel = out[:2], out[2:]

    result = jax.ShapeDtypeStruct((DH, GROUP * HALF + BLK), BF16)
    piece_0 = pl.BlockSpec((1, 3 * DH, HALF), lambda *_: (0, 0, 0))
    results = call(
        far_kernel, scalars, (own0, own1, sel2, sel3, *beyond), (1,),
        [piece_0] * GROUP + [whole(pair.shape)] * 6,
        [(whole(result.shape), result)] * RATE,
        [
            pltpu.VMEM((2, RATE, TOK, 2 * DH), BF16),
            pltpu.VMEM((2, RATE, DX, TOK), BF16),
            pltpu.VMEM((2, RATE, 2 * DH, TOK), BF16),
            pltpu.VMEM((RATE, DH, GROUP * HALF), BF16),
            pltpu.VMEM((RATE, DH, BLK), F32),
        ],
        RATE * 2 * 3 * TOK * TOK, after=(out[1],),
    )
    back = [results[0]] + [across(results[s], s) for s in range(1, RATE)]

    held.update({(2, 2): rest2, (3, 2): rest3})
    units = own_sel + own_rest + other_sel + other_rest
    attended = jax.ShapeDtypeStruct((HG, DH, TOK), BF16)

    def combine(chip, state):
        return call(
            functools.partial(combine_kernel, chip), (), (*state, *back), (1,),
            [whole(x.shape) for x in state] + [whole(result.shape)] * HG,
            [(whole(attended.shape), attended)] * 2,
            [],
            1 << 18,
        )

    state_other = near(
        held, units,
        [
            [
                ((2, 0), 5, (0, 0)), ((2, 1), 0, None),
                ((3, 0), 5, (0, 1)), ((3, 1), 0, None),
            ]
        ],
        [state_sel],
        after=results[:1],
    )
    part2, part3 = combine(1, state_other)
    state_own = near(
        {(2, 2): rest2, (3, 2): rest3, **{q: held[q] for q in ((0, 0), (1, 0))}},
        other_rest,
        [[(q, 0, (0, i)) for i, q in enumerate(own)]],
        [state_own],
        after=(part2,),
    )
    part0, part1 = combine(0, state_own)
    parts = [part0, within(part1, 1), within(part2, 2), within(part3, 3)]
    return call(
        project_kernel, scalars, (*parts, out_weight), (1,),
        [whole(attended.shape)] * GROUP + [whole((width, width))],
        [(whole((TOK, width)), jax.ShapeDtypeStruct((TOK, width), BF16))],
        [pltpu.VMEM((width, TOK), BF16)],
        1 << 18,
    )[0]


def shards(queries, key_states, value_states, offsets_mid, offsets_top, out_weight):
    tokens, width = queries.shape
    heads = offsets_mid.shape[0]
    fits = (
        lax.axis_size("head") == 1
        and lax.axis_size("seq") == GROUP * RATE
        and tokens == TOK
        and heads == GROUP * HG
        and width == heads * DH
    )
    run = shards_four if fits else shards_general
    return run(queries, key_states, value_states, offsets_mid, offsets_top, out_weight)


def solution(mesh):
    in_specs = (
        P(("slide", "seq"), "head"),
        P(("slide", "seq"), "head"),
        P(("slide", "seq"), "head"),
        P(),
        P(),
        P("head", None),
    )
    out_specs = P(("slide", "seq", "head"), None)
    return jax.shard_map(shards, mesh=mesh, in_specs=in_specs, out_specs=out_specs, check_vma=False)
```

```python
import functools

import jax
import jax.numpy as jnp
from jax import lax
from jax.experimental import pallas as pl
from jax.experimental.pallas import tpu as pltpu
from jax.sharding import PartitionSpec as P

SEG = 2048
LOG2E = 1.4426950408889634
VMEM_LIMIT = 40 * 1024 * 1024
VMEM_MOST = 51 * 1024 * 1024
BF16 = jnp.bfloat16
F32 = jnp.float32


def partner_2(block, axis, apart):
    count = lax.axis_size(axis)
    route = []
    for low in range(count):
        high = low | 1 << apart
        if high != low and high < count:
            route += [(low, high), (high, low)]
    return lax.ppermute(block, axis, route)


def attend_head(triple_in):
    query_rows, key_rows, value_rows = triple_in
    score_scale = query_rows.shape[-1] ** (-0.5)
    scores = jnp.dot(query_rows, key_rows.T, preferred_element_type=jnp.float32) * score_scale
    row_max = jnp.max(scores, axis=1)
    shifted = jnp.exp(scores - row_max[:, None])
    row_total = jnp.sum(shifted, axis=1)
    weights = shifted.astype(jnp.bfloat16)
    numerator = jnp.dot(weights, value_rows, preferred_element_type=jnp.float32)
    return (numerator, row_total, row_max)


def attend_local(query_rows, pair_rows):
    return lax.map(
        attend_head,
        (
            query_rows.transpose(1, 0, 2),
            pair_rows[:, 0].transpose(1, 0, 2),
            pair_rows[:, 1].transpose(1, 0, 2),
        ),
    )


def pick_rows(states, offsets, rate):
    row_count, inner_count, heads_here, head_width = states.shape
    picker = (jnp.arange(rate)[:, None] == offsets[None, :]).astype(jnp.bfloat16)
    folded = states.reshape(row_count // rate, rate, inner_count, heads_here, head_width)
    return jnp.einsum("archd,rh->achd", folded, picker, preferred_element_type=jnp.float32).astype(
        jnp.bfloat16
    )


def spread_back(numerator, row_total, row_max, offsets, rate):
    heads_here, picked_count, head_width = numerator.shape
    chosen = jnp.arange(rate)[:, None] == offsets[None, :]
    full_num = jnp.where(chosen[None, :, :, None], numerator.transpose(1, 0, 2)[:, None], 0.0)
    full_total = jnp.where(chosen[None], row_total.T[:, None], 0.0)
    full_max = jnp.where(chosen[None], row_max.T[:, None], -1e30)
    return (
        full_num.reshape(picked_count * rate, heads_here, head_width),
        full_total.reshape(picked_count * rate, heads_here),
        full_max.reshape(picked_count * rate, heads_here),
    )


def doubling(buffer, steps_count):
    position = lax.axis_index("seq")
    for bit_index in range(steps_count):
        partner = partner_2(buffer, "seq", bit_index)
        is_lower = position >> bit_index & 1 == 0
        buffer = jnp.where(
            is_lower, jnp.concatenate([buffer, partner], 0), jnp.concatenate([partner, buffer], 0)
        )
    return buffer


def shards_general(queries, key_states, value_states, offsets_mid, offsets_top, out_weight):
    tok_rows = queries.shape[0]
    heads_local = offsets_mid.shape[0] // lax.axis_size("head")
    head_size = queries.shape[1] // heads_local
    seq_devices = lax.axis_size("seq")
    seq_total = tok_rows * seq_devices
    width_mid = min(16 * SEG, seq_total)
    rate_mid = width_mid // SEG
    rate_top = seq_total // SEG
    start_head = lax.axis_index("head") * heads_local
    mid_local = lax.dynamic_slice(offsets_mid, (start_head,), (heads_local,))
    top_local = lax.dynamic_slice(offsets_top, (start_head,), (heads_local,))
    query_heads = queries.reshape(tok_rows, 1, heads_local, head_size)
    paired = jnp.stack([key_states, value_states], axis=1).reshape(
        tok_rows, 2, heads_local, head_size
    )
    near_bits = (SEG // tok_rows).bit_length() - 1
    near_rows = doubling(paired.reshape(tok_rows, -1), near_bits).reshape(
        SEG, 2, heads_local, head_size
    )
    near_num, near_total, near_max = attend_local(query_heads[:, 0], near_rows)
    level_near = spread_back(
        near_num, near_total, near_max, jnp.zeros((heads_local,), jnp.int32), 1
    )
    mid_q = pick_rows(query_heads, mid_local, rate_mid)[:, 0]
    mid_kv = pick_rows(paired, mid_local, rate_mid)
    mid_group = width_mid // tok_rows
    mid_bits = mid_group.bit_length() - 1
    mid_rows = doubling(mid_kv.reshape(mid_kv.shape[0], -1), mid_bits).reshape(
        SEG, 2, heads_local, head_size
    )
    mid_num, mid_total, mid_max = attend_local(mid_q, mid_rows)
    level_mid = spread_back(mid_num, mid_total, mid_max, mid_local, rate_mid)
    top_q = pick_rows(query_heads, top_local, rate_top)[:, 0]
    top_kv = pick_rows(paired, top_local, rate_top)
    top_rows = lax.all_gather(
        top_kv.reshape(top_kv.shape[0], -1), "seq", axis=0, tiled=True
    ).reshape(SEG, 2, heads_local, head_size)
    top_num, top_total, top_max = attend_local(top_q, top_rows)
    level_top = spread_back(top_num, top_total, top_max, top_local, rate_top)
    levels = [level_near, level_mid, level_top]
    overall = jnp.maximum(jnp.maximum(level_near[2], level_mid[2]), level_top[2])
    numerator = jnp.zeros((tok_rows, heads_local, head_size), jnp.float32)
    row_total = jnp.zeros((tok_rows, heads_local), jnp.float32)
    for level_num, level_total, level_max in levels:
        factor = jnp.exp(level_max - overall)
        numerator = numerator + factor[..., None] * level_num
        row_total = row_total + factor * level_total
    attention = (
        (numerator / row_total[..., None])
        .astype(jnp.bfloat16)
        .reshape(tok_rows, heads_local * head_size)
    )
    result = lax.psum_scatter(
        jnp.dot(attention, out_weight, preferred_element_type=jnp.float32),
        "head",
        scatter_dimension=0,
        tiled=True,
    )
    return result.astype(jnp.bfloat16)


RATE = 4
GROUP = 4
HG = 4
STEP = 2
DH = 48
BLK = 128
HALF = 2 * BLK
TOK = 512
SAFE = 96.0
FAR_ORDER = (2, 1, 3)
PART_ORDER = (0, 1, 2, 3)
DX = 64


def dot(a, b):
    return jnp.dot(a, b, preferred_element_type=F32)


def dot_nt(a, b):
    return lax.dot_general(a, b, (((1,), (1,)), ((), ())), preferred_element_type=F32)


def class_of_slots(off_mid, off_top):
    first = off_mid
    second = jnp.where(off_top == off_mid, lax.rem(off_mid + 1, RATE), off_top)
    free0 = (first != 0) & (second != 0)
    free1 = (first != 1) & (second != 1)
    third = jnp.where(free0, 0, jnp.where(free1, 1, 2))
    return first, second, third, 6 - first - second - third


def head_of(place, j, p):
    index = place[2 * GROUP * HG]
    return ((index & (GROUP - 1)) ^ j) * HG + ((index // GROUP) ^ p)


def offsets_of(place, head):
    return place[head], place[GROUP * HG + head]


def token_picker():
    row = lax.broadcasted_iota(jnp.int32, (TOK, TOK), 0)
    col = lax.broadcasted_iota(jnp.int32, (TOK, TOK), 1)
    return (col == RATE * (row % BLK) + row // BLK).astype(BF16)


def fill_class_major(block, picker, scratch):
    scratch[...] = lax.dot_general(
        block, picker, (((0,), (1,)), ((), ())), preferred_element_type=F32
    ).astype(BF16)


def lane_block(index):
    return pl.ds(pl.multiple_of(index * BLK, BLK), BLK)


def head_rows(head):
    return pl.ds(pl.multiple_of(head * DH, 16), DH)


def pack_kernel(place, k_hbm, v_hbm, q_hbm, *refs):
    outs, refs = refs[:6], refs[6:]
    blocks, held, packed = refs[:3], refs[3:6], refs[6:12]
    sems_in, sems_out = refs[12:]
    loads = [
        pltpu.make_async_copy(hbm, block, sems_in.at[i])
        for i, (hbm, block) in enumerate(zip((k_hbm, v_hbm, q_hbm), blocks))
    ]
    for load in loads:
        load.start()
    picker = token_picker()
    stores = []
    for n, (load, block, scratch) in enumerate(zip(loads, blocks, held)):
        load.wait()
        fill_class_major(block[...], picker, scratch)
        rows = slice(n * DH, (n + 1) * DH)
        for i, (j, first, count) in enumerate(
            ((0, 0, 4), (1, 0, 4), (2, 0, 2), (3, 0, 2), (2, 2, 2), (3, 2, 2))
        ):
            for p in range(HG):
                head = head_of(place, j, p)
                slots = class_of_slots(*offsets_of(place, head))
                for s in range(count):
                    packed[i][p, rows, s * BLK : (s + 1) * BLK] = scratch[
                        head_rows(head), lane_block(slots[first + s])
                    ]
            store = pltpu.make_async_copy(
                packed[i].at[:, rows], outs[i].at[:, rows], sems_out.at[i, n]
            )
            store.start()
            stores.append(store)
    for store in stores:
        store.wait()


def regroup_kernel(a_ref, b_ref, *refs):
    for s, out in enumerate(refs[-3:]):
        out[0] = a_ref[s + 1, :, 0:HALF]
        out[1] = b_ref[s + 1, :, 0:HALF]


def split_query(q):
    scaled = q.astype(F32) * (DH**-0.5 * LOG2E)
    high = scaled.astype(BF16)
    low = (scaled - high.astype(F32)).astype(BF16)
    return jnp.concatenate([high, low], axis=0)


def twice_keys(keys_t):
    both = jnp.concatenate([keys_t, keys_t], axis=0).astype(F32)
    return both.T.astype(BF16)


def largest(blocks):
    best = None
    for block in blocks:
        wide = block.astype(F32)
        length = jnp.sum(wide * wide, axis=0, keepdims=True)
        for low in range(0, block.shape[1], HALF):
            part = length[:, low : low + HALF]
            best = part if best is None else jnp.maximum(best, part)
    return jnp.max(best)


def is_small(queries, keys):
    scale = DH**-0.5 * LOG2E
    return largest(queries) * largest(keys) * (scale * scale) < SAFE * SAFE


def column_max(blocks):
    best = jnp.max(blocks[0], axis=0, keepdims=True)
    for block in blocks[1:]:
        best = jnp.maximum(best, jnp.max(block, axis=0, keepdims=True))
    return best


def near_kernel(inputs, units, tasks, carried, place, *refs):
    pieces = dict(zip(inputs, refs[: len(inputs)]))
    refs = refs[len(inputs) :]
    old = [refs[2 * i : 2 * i + 2] for i in range(carried)]
    outs = refs[2 * carried : 2 * carried + 2 * len(tasks)]
    k_s, v_s = refs[-2:]
    v_s[:, DH:DX, :] = jnp.ones((STEP, DX - DH, v_s.shape[2]), BF16)
    lane_slot = lax.broadcasted_iota(jnp.int32, (1, HALF), 1) // BLK

    def lookup(j, slot):
        first = 0 if (j, 0) in pieces and pieces[j, 0].shape[2] > HALF else slot // 2 * 2
        return pieces[j, first], (slot - first) * BLK

    chunks = []
    row = 0
    for label, members in units:
        chunks.append((label, slice(row, row + len(members) * BLK)))
        row += len(members) * BLK
    members = [member for _, group in units for member in group]

    def prepare(h):
        for i, (j, slot) in enumerate(members):
            ref, lane = lookup(j, slot)
            rows = slice(i * BLK, (i + 1) * BLK)
            k_s[h, rows, :] = twice_keys(ref[h, 0:DH, lane : lane + BLK])
            v_s[h, 0:DH, rows] = ref[h, DH : 2 * DH, lane : lane + BLK]

    def counted_again(h):
        off_mid, off_top = offsets_of(place, head_of(place, 0, pl.program_id(0) * STEP + h))
        same = off_mid == off_top
        return [
            jnp.where(lane_slot == 0, jnp.where(same, 1.584962500721156, 1.0), 0.0),
            jnp.where(lane_slot == 1, jnp.where(same, 0.0, 1.0), 0.0),
        ]

    def run(plain, heads):
        again = [counted_again(h) for h in heads]
        flat = [
            (h, again_h, query, low, merge, out, i)
            for h, again_h in zip(heads, again)
            for out, group in enumerate(tasks)
            for i, (query, low, merge) in enumerate(group)
        ]

        def score(task):
            h, _, (j, half), low = task[:4]
            ref, lane = lookup(j, 2 * half)
            query = split_query(ref[h, 2 * DH :, lane : lane + HALF])
            return [dot(k_s[h, rows, :], query) for _, rows in chunks[low:]]

        scores = score(flat[0])
        for n, (h, again_h, (_, half), low, merge, out, i) in enumerate(flat):
            following = score(flat[n + 1]) if n + 1 < len(flat) else None
            best = jnp.zeros((1, HALF), F32) if plain else column_max(scores)
            if merge is not None:
                acc_in, max_in = old[merge[0]]
                old_max = max_in[h, merge[1], 0:1, :]
                best = best if plain else jnp.maximum(best, old_max)
            acc = None
            for (label, rows), block in zip(chunks[low:], scores):
                if half == 0 and label is not None:
                    block = block - (best - again_h[label])
                elif not plain:
                    block = block - best
                part = dot(v_s[h, :, rows], jnp.exp2(block).astype(BF16))
                acc = part if acc is None else acc + part
            if merge is not None:
                before = acc_in[h, merge[1]]
                acc = acc + (before if plain else before * jnp.exp2(old_max - best))
            acc_ref, max_ref = outs[2 * out : 2 * out + 2]
            acc_ref[h, i] = acc
            max_ref[h, i] = jnp.broadcast_to(best, (8, HALF))
            scores = following

    for h in range(STEP):
        prepare(h)
    plain = is_small(
        [ref[h, 2 * DH :, :] for ref in pieces.values() for h in range(STEP)],
        [ref[h, 0:DH, :] for ref in pieces.values() for h in range(STEP)],
    )
    for _, max_in in old:
        plain = plain & (jnp.max(jnp.abs(max_in[...])) == 0.0)

    @pl.when(plain)
    def _():
        run(True, list(range(STEP)))

    @pl.when(jnp.logical_not(plain))
    def _():
        @pl.loop(0, STEP)
        def _(h):
            run(False, [h])


def far_kernel(place, *refs):
    own, beyond = refs[:GROUP], refs[GROUP : GROUP + 6]
    outs = refs[GROUP + 6 : GROUP + 6 + RATE]
    k_s, v_s, q_s, result_s, tail_s = refs[GROUP + 6 + RATE :]
    off_mid, off_top = offsets_of(place, head_of(place, 0, 0))
    same = off_mid == off_top
    slots = (0, jnp.where(same, 0, 1))

    def source(s, j):
        return own[j].at[0] if s == 0 else beyond[2 * FAR_ORDER.index(s) + j // 2].at[j % 2]

    for s in range(RATE):
        for j in range(GROUP):
            ref = source(s, j)
            for level, slot in enumerate(slots):
                here = slice(j * BLK, (j + 1) * BLK)
                k_s[level, s, here, :] = twice_keys(ref[0:DH, lane_block(slot)])
                v_s[level, s, 0:DH, here] = ref[DH : 2 * DH, lane_block(slot)]
                q_s[level, s, :, here] = split_query(ref[2 * DH : 3 * DH, lane_block(slot)])
    v_s[:, :, DH:DX, :] = jnp.ones((2, RATE, DX - DH, TOK), BF16)
    tail_s[...] = jnp.zeros(tail_s.shape, F32)

    def run(plain):
        tasks = [(level, chip) for level in range(2) for chip in range(2)]

        def segment(s, carry):
            def score(task):
                level, chip = task
                query = q_s[level, s, :, chip * HALF : (chip + 1) * HALF]
                return [dot(k_s[level, s ^ d], query) for d in range(1, RATE)]

            scores = score(tasks[0])
            for n, (level, chip) in enumerate(tasks):
                following = score(tasks[n + 1]) if n + 1 < len(tasks) else None
                best = jnp.zeros((1, HALF), F32) if plain else column_max(scores)
                acc = None
                for d in range(1, RATE):
                    block = scores[d - 1] if plain else scores[d - 1] - best
                    part = dot(v_s[level, s ^ d], jnp.exp2(block).astype(BF16))
                    acc = part if acc is None else acc + part
                total = acc[DH : DH + 1, :]
                result = (acc[0:DH, :] / total).astype(BF16)
                lse = best + jnp.log2(total)
                if level == 0:
                    lse = jnp.where(same, lse + 1.0, lse)
                else:
                    lse = jnp.where(same, -1e30, lse)
                high = lse.astype(BF16).astype(F32)
                middle = (lse - high).astype(BF16).astype(F32)
                low = lse - high - middle
                for i in range(2):
                    n = 2 * (2 * chip + i) + level
                    mine = slice(i * BLK, (i + 1) * BLK)
                    result_s[s, :, n * BLK : (n + 1) * BLK] = result[:, mine]
                    for k, part in enumerate((high, middle, low)):
                        tail_s[s, 3 * n + k : 3 * n + k + 1, :] = part[:, mine]
                scores = following
            return carry

        lax.fori_loop(0, RATE, segment, 0, unroll=2 if plain else 1)

    every = [source(s, j) for s in range(RATE) for j in range(GROUP)]
    plain = is_small(
        [ref[2 * DH : 3 * DH, 0:HALF] for ref in every], [ref[0:DH, 0:HALF] for ref in every]
    )
    pl.when(plain)(lambda: run(True))
    pl.when(jnp.logical_not(plain))(lambda: run(False))
    for s in range(RATE):
        outs[s][:, : GROUP * HALF] = result_s[s]
        outs[s][:, GROUP * HALF :] = tail_s[s].astype(BF16)


def join(acc, best, far, j):
    tail = far[:, GROUP * HALF :].astype(F32)
    lse = jnp.concatenate(
        [
            tail[3 * n : 3 * n + 1] + tail[3 * n + 1 : 3 * n + 2] + tail[3 * n + 2 : 3 * n + 3]
            for n in (2 * j, 2 * j + 1)
        ],
        axis=1,
    )
    overall = jnp.maximum(best, lse)
    near_factor, far_factor = jnp.exp2(best - overall), jnp.exp2(lse - overall)
    total = acc[DH : DH + 1] * near_factor + far_factor
    value = far[:, j * HALF : (j + 1) * HALF].astype(F32) * far_factor
    return ((acc[0:DH] * near_factor + value) / total).astype(BF16)


def combine_kernel(chip, acc_ref, max_ref, *refs):
    far, outs = refs[:HG][::-1], refs[HG:]
    for i in range(2):
        for p in range(HG):
            outs[i][p, :, 0:HALF] = join(
                acc_ref[p, 2 * i], max_ref[p, 2 * i, 0:1, :], far[p], 2 * chip + i
            )
            acc = acc_ref[p, 2 * i + 1]
            outs[i][p, :, HALF:] = (acc[0:DH] / acc[DH : DH + 1]).astype(BF16)


def project_kernel(place, *refs):
    parts = refs[:GROUP]
    w_ref, out_ref, held = refs[GROUP:]
    for n, j in enumerate(PART_ORDER):
        for p in range(HG):
            head = head_of(place, j, p)
            slots = class_of_slots(*offsets_of(place, head))
            for s in range(RATE):
                held[head_rows(head), lane_block(slots[s])] = parts[n][
                    p, :, s * BLK : (s + 1) * BLK
                ]
    row = lax.broadcasted_iota(jnp.int32, (TOK, TOK), 0)
    col = lax.broadcasted_iota(jnp.int32, (TOK, TOK), 1)
    picker = (row == RATE * (col % BLK) + col // BLK).astype(BF16)
    attention = dot_nt(picker, held[...]).astype(BF16)
    out_ref[...] = dot(attention, w_ref[...]).astype(BF16)


def whole(shape):
    return pl.BlockSpec(shape, lambda *_: (0,) * len(shape))


def per_head(shape):
    return pl.BlockSpec(shape, lambda h, *_: (h,) + (0,) * (len(shape) - 1))


def call(
    kernel, scalars, args, grid, in_specs, outs, scratch, scores,
    limit=VMEM_LIMIT, after=(), through=(),
):
    known = len(scalars) + len(args)
    extra = (*after, *through)
    count = len(outs)
    anywhere = pl.BlockSpec(memory_space=pl.ANY)

    def body(*refs):
        results = refs[known + len(extra) :]
        kernel(*refs[:known], *results[:count], *results[count + len(through) :])

    return pl.pallas_call(
        body if extra else kernel,
        grid_spec=pltpu.PrefetchScalarGridSpec(
            num_scalar_prefetch=len(scalars),
            grid=grid,
            in_specs=list(in_specs) + [anywhere] * len(extra),
            out_specs=[spec for spec, _ in outs] + [anywhere] * len(through),
            scratch_shapes=scratch,
        ),
        out_shape=[shape for _, shape in outs]
        + [jax.ShapeDtypeStruct(x.shape, x.dtype) for x in through],
        input_output_aliases={known + len(after) + i: count + i for i in range(len(through))},
        compiler_params=pltpu.CompilerParams(vmem_limit_bytes=limit),
        cost_estimate=pl.CostEstimate(flops=0, bytes_accessed=0, transcendentals=0),
    )(*scalars, *args, *extra)


def within(array, apart):
    count = lax.axis_size("seq")
    return lax.ppermute(array, "seq", [(i, i ^ apart) for i in range(count)])


def swap_segments(arrays):
    moved = {s: within(arrays[s - 1], GROUP * s) for s in (3, 2, 1)}
    return [moved[s] for s in (1, 2, 3)]


def shards_four(queries, key_states, value_states, offsets_mid, offsets_top, out_weight):
    width = queries.shape[1]
    index = lax.axis_index("seq").astype(jnp.int32).reshape(1)
    place = jnp.concatenate([offsets_mid, offsets_top, index])
    full = jax.ShapeDtypeStruct((HG, 3 * DH, TOK), BF16)
    piece = jax.ShapeDtypeStruct((HG, 3 * DH, HALF), BF16)
    pair = jax.ShapeDtypeStruct((2, 3 * DH, HALF), BF16)
    anywhere = pl.BlockSpec(memory_space=pl.ANY)
    shapes = [full] * 2 + [piece] * 4
    own0, own1, sel2, sel3, rest2, rest3 = call(
        pack_kernel, (place,), (key_states, value_states, queries), (1,),
        [anywhere] * 3,
        [(anywhere, shape) for shape in shapes],
        [pltpu.VMEM((TOK, width), BF16)] * 3
        + [pltpu.VMEM((width, TOK), BF16)] * 3
        + [pltpu.VMEM(shape.shape, BF16) for shape in shapes]
        + [pltpu.SemaphoreType.DMA((3,)), pltpu.SemaphoreType.DMA((6, 3))],
        1 << 19, VMEM_MOST,
    )
    own1 = within(own1, 1)
    sel2, sel3 = within(sel2, 2), within(sel3, 3)

    def regroup(a, b, **order):
        return call(
            regroup_kernel, (), (a, b), (1,),
            [whole(a.shape), whole(b.shape)], [(whole(pair.shape), pair)] * 3,
            [], 1 << 17, **order,
        )

    def state(count):
        return [
            (per_head((STEP, count, rows, HALF)), jax.ShapeDtypeStruct((HG, count, rows, HALF), F32))
            for rows in (DX, 8)
        ]

    def near(held, units, tasks, old, **order):
        sizes = [len(members) * BLK for _, members in units]
        scores = sum(sum(sizes[low:]) * HALF for group in tasks for _, low, _ in group)
        return call(
            functools.partial(near_kernel, list(held), units, tasks, len(old)), (place,),
            (*held.values(), *[x for one in old for x in one]), (HG // STEP,),
            [per_head((STEP,) + x.shape[1:]) for x in held.values()]
            + [per_head((STEP,) + x.shape[1:]) for one in old for x in one],
            [out for group in tasks for out in state(len(group))],
            [
                pltpu.VMEM((STEP, sum(sizes), 2 * DH), BF16),
                pltpu.VMEM((STEP, DX, sum(sizes)), BF16),
            ],
            HG * scores, **order,
        )

    def units_of(a, b):
        return [(0, [(a, 0), (b, 0)]), (1, [(a, 1), (b, 1)])], [
            (None, [(a, 2), (a, 3), (b, 2), (b, 3)])
        ]

    own_sel, own_rest = units_of(0, 1)
    other_sel, other_rest = units_of(2, 3)
    own = [(0, 0), (0, 1), (1, 0), (1, 1)]

    ours = regroup(own0, own1)
    ours = swap_segments(ours)
    held = {(0, 0): own0, (1, 0): own1}
    state_own = near(held, own_sel + own_rest, [[(q, 0, None) for q in own]], [])
    *theirs, rest2, rest3 = regroup(sel2, sel3, after=state_own[1:], through=(rest2, rest3))
    theirs = swap_segments(theirs)
    rest2, rest3 = within(rest2, 2), within(rest3, 3)
    beyond = [x for s in FAR_ORDER for x in (ours[s - 1], theirs[s - 1])]

    held.update({(2, 0): sel2, (3, 0): sel3})
    out = near(
        held, own_sel + own_rest + other_sel,
        [
            [(q, 3, (0, i)) for i, q in enumerate(own)],
            [((2, 0), 0, None), ((3, 0), 0, None)],
        ],
        [state_own],
        after=ours[::-1],
    )
    state_own, state_sel = out[:2], out[2:]

    result = jax.ShapeDtypeStruct((DH, GROUP * HALF + BLK), BF16)
    piece_0 = pl.BlockSpec((1, 3 * DH, HALF), lambda *_: (0, 0, 0))
    results = call(
        far_kernel, (place,), (own0, own1, sel2, sel3, *beyond), (1,),
        [piece_0] * GROUP + [whole(pair.shape)] * 6,
        [(whole(result.shape), result)] * RATE,
        [
            pltpu.VMEM((2, RATE, TOK, 2 * DH), BF16),
            pltpu.VMEM((2, RATE, DX, TOK), BF16),
            pltpu.VMEM((2, RATE, 2 * DH, TOK), BF16),
            pltpu.VMEM((RATE, DH, GROUP * HALF), BF16),
            pltpu.VMEM((RATE, DH, BLK), F32),
        ],
        RATE * 2 * 3 * TOK * TOK, after=(out[1],),
    )
    back = [results[0]] + swap_segments(results[1:])

    held.update({(2, 2): rest2, (3, 2): rest3})
    units = own_sel + own_rest + other_sel + other_rest
    attended = jax.ShapeDtypeStruct((HG, DH, TOK), BF16)

    def combine(chip, state):
        return call(
            functools.partial(combine_kernel, chip), (), (*state, *back[::-1]), (1,),
            [whole(x.shape) for x in state] + [whole(result.shape)] * HG,
            [(whole(attended.shape), attended)] * 2,
            [],
            1 << 18,
        )

    state_other = near(
        held, units,
        [
            [
                ((2, 0), 5, (0, 0)), ((2, 1), 0, None),
                ((3, 0), 5, (0, 1)), ((3, 1), 0, None),
            ]
        ],
        [state_sel],
        after=results[:1],
    )
    part2, part3 = combine(1, state_other)
    state_own = near(
        {(2, 2): rest2, (3, 2): rest3, **{q: held[q] for q in ((0, 0), (1, 0))}},
        other_rest,
        [[(q, 0, (0, i)) for i, q in enumerate(own)]],
        [state_own],
        after=(part2,),
    )
    part0, part1 = combine(0, state_own)
    parts = {0: part0, 1: within(part1, 1), 2: within(part2, 2), 3: within(part3, 3)}
    return call(
        project_kernel, (place,), (*[parts[j] for j in PART_ORDER], out_weight), (1,),
        [whole(attended.shape)] * GROUP + [whole((width, width))],
        [(whole((TOK, width)), jax.ShapeDtypeStruct((TOK, width), BF16))],
        [pltpu.VMEM((width, TOK), BF16)],
        1 << 18,
    )[0]


def shards(queries, key_states, value_states, offsets_mid, offsets_top, out_weight):
    tokens, width = queries.shape
    heads = offsets_mid.shape[0]
    fits = (
        lax.axis_size("head") == 1
        and lax.axis_size("seq") == GROUP * RATE
        and tokens == TOK
        and heads == GROUP * HG
        and width == heads * DH
    )
    run = shards_four if fits else shards_general
    return run(queries, key_states, value_states, offsets_mid, offsets_top, out_weight)


def solution(mesh):
    in_specs = (
        P(("slide", "seq"), "head"),
        P(("slide", "seq"), "head"),
        P(("slide", "seq"), "head"),
        P(),
        P(),
        P("head", None),
    )
    out_specs = P(("slide", "seq", "head"), None)
    return jax.shard_map(shards, mesh=mesh, in_specs=in_specs, out_specs=out_specs, check_vma=False)
```

```python
import functools

import jax
import jax.numpy as jnp
from jax import lax
from jax.experimental import pallas as pl
from jax.experimental.pallas import tpu as pltpu
from jax.sharding import PartitionSpec as P

SEG = 2048
LOG2E = 1.4426950408889634
VMEM_LIMIT = 40 * 1024 * 1024
VMEM_MOST = 60 * 1024 * 1024
BF16 = jnp.bfloat16
F32 = jnp.float32


def partner_2(block, axis, apart):
    count = lax.axis_size(axis)
    route = []
    for low in range(count):
        high = low | 1 << apart
        if high != low and high < count:
            route += [(low, high), (high, low)]
    return lax.ppermute(block, axis, route)


def attend_head(triple_in):
    query_rows, key_rows, value_rows = triple_in
    score_scale = query_rows.shape[-1] ** (-0.5)
    scores = jnp.dot(query_rows, key_rows.T, preferred_element_type=jnp.float32) * score_scale
    row_max = jnp.max(scores, axis=1)
    shifted = jnp.exp(scores - row_max[:, None])
    row_total = jnp.sum(shifted, axis=1)
    weights = shifted.astype(jnp.bfloat16)
    numerator = jnp.dot(weights, value_rows, preferred_element_type=jnp.float32)
    return (numerator, row_total, row_max)


def attend_local(query_rows, pair_rows):
    return lax.map(
        attend_head,
        (
            query_rows.transpose(1, 0, 2),
            pair_rows[:, 0].transpose(1, 0, 2),
            pair_rows[:, 1].transpose(1, 0, 2),
        ),
    )


def pick_rows(states, offsets, rate):
    row_count, inner_count, heads_here, head_width = states.shape
    picker = (jnp.arange(rate)[:, None] == offsets[None, :]).astype(jnp.bfloat16)
    folded = states.reshape(row_count // rate, rate, inner_count, heads_here, head_width)
    return jnp.einsum("archd,rh->achd", folded, picker, preferred_element_type=jnp.float32).astype(
        jnp.bfloat16
    )


def spread_back(numerator, row_total, row_max, offsets, rate):
    heads_here, picked_count, head_width = numerator.shape
    chosen = jnp.arange(rate)[:, None] == offsets[None, :]
    full_num = jnp.where(chosen[None, :, :, None], numerator.transpose(1, 0, 2)[:, None], 0.0)
    full_total = jnp.where(chosen[None], row_total.T[:, None], 0.0)
    full_max = jnp.where(chosen[None], row_max.T[:, None], -1e30)
    return (
        full_num.reshape(picked_count * rate, heads_here, head_width),
        full_total.reshape(picked_count * rate, heads_here),
        full_max.reshape(picked_count * rate, heads_here),
    )


def doubling(buffer, steps_count):
    position = lax.axis_index("seq")
    for bit_index in range(steps_count):
        partner = partner_2(buffer, "seq", bit_index)
        is_lower = position >> bit_index & 1 == 0
        buffer = jnp.where(
            is_lower, jnp.concatenate([buffer, partner], 0), jnp.concatenate([partner, buffer], 0)
        )
    return buffer


def shards_general(queries, key_states, value_states, offsets_mid, offsets_top, out_weight):
    tok_rows = queries.shape[0]
    heads_local = offsets_mid.shape[0] // lax.axis_size("head")
    head_size = queries.shape[1] // heads_local
    seq_devices = lax.axis_size("seq")
    seq_total = tok_rows * seq_devices
    width_mid = min(16 * SEG, seq_total)
    rate_mid = width_mid // SEG
    rate_top = seq_total // SEG
    start_head = lax.axis_index("head") * heads_local
    mid_local = lax.dynamic_slice(offsets_mid, (start_head,), (heads_local,))
    top_local = lax.dynamic_slice(offsets_top, (start_head,), (heads_local,))
    query_heads = queries.reshape(tok_rows, 1, heads_local, head_size)
    paired = jnp.stack([key_states, value_states], axis=1).reshape(
        tok_rows, 2, heads_local, head_size
    )
    near_bits = (SEG // tok_rows).bit_length() - 1
    near_rows = doubling(paired.reshape(tok_rows, -1), near_bits).reshape(
        SEG, 2, heads_local, head_size
    )
    near_num, near_total, near_max = attend_local(query_heads[:, 0], near_rows)
    level_near = spread_back(
        near_num, near_total, near_max, jnp.zeros((heads_local,), jnp.int32), 1
    )
    mid_q = pick_rows(query_heads, mid_local, rate_mid)[:, 0]
    mid_kv = pick_rows(paired, mid_local, rate_mid)
    mid_group = width_mid // tok_rows
    mid_bits = mid_group.bit_length() - 1
    mid_rows = doubling(mid_kv.reshape(mid_kv.shape[0], -1), mid_bits).reshape(
        SEG, 2, heads_local, head_size
    )
    mid_num, mid_total, mid_max = attend_local(mid_q, mid_rows)
    level_mid = spread_back(mid_num, mid_total, mid_max, mid_local, rate_mid)
    top_q = pick_rows(query_heads, top_local, rate_top)[:, 0]
    top_kv = pick_rows(paired, top_local, rate_top)
    top_rows = lax.all_gather(
        top_kv.reshape(top_kv.shape[0], -1), "seq", axis=0, tiled=True
    ).reshape(SEG, 2, heads_local, head_size)
    top_num, top_total, top_max = attend_local(top_q, top_rows)
    level_top = spread_back(top_num, top_total, top_max, top_local, rate_top)
    levels = [level_near, level_mid, level_top]
    overall = jnp.maximum(jnp.maximum(level_near[2], level_mid[2]), level_top[2])
    numerator = jnp.zeros((tok_rows, heads_local, head_size), jnp.float32)
    row_total = jnp.zeros((tok_rows, heads_local), jnp.float32)
    for level_num, level_total, level_max in levels:
        factor = jnp.exp(level_max - overall)
        numerator = numerator + factor[..., None] * level_num
        row_total = row_total + factor * level_total
    attention = (
        (numerator / row_total[..., None])
        .astype(jnp.bfloat16)
        .reshape(tok_rows, heads_local * head_size)
    )
    result = lax.psum_scatter(
        jnp.dot(attention, out_weight, preferred_element_type=jnp.float32),
        "head",
        scatter_dimension=0,
        tiled=True,
    )
    return result.astype(jnp.bfloat16)


RATE = 4
GROUP = 4
HG = 4
DH = 48
BLK = 128
HALF = 2 * BLK
TOK = 512
SAFE = 96.0
FAR_ORDER = (2, 1, 3)
CHUNKS = ((0, 4),)
DX = 64


def dot(a, b):
    return jnp.dot(a, b, preferred_element_type=F32)


def dot_nt(a, b):
    return lax.dot_general(a, b, (((1,), (1,)), ((), ())), preferred_element_type=F32)


def class_of_slots(off_mid, off_top):
    first = off_mid
    second = jnp.where(off_top == off_mid, lax.rem(off_mid + 1, RATE), off_top)
    free0 = (first != 0) & (second != 0)
    free1 = (first != 1) & (second != 1)
    third = jnp.where(free0, 0, jnp.where(free1, 1, 2))
    return first, second, third, 6 - first - second - third


def head_of(place, j, p):
    index = place[0][0]
    return ((index & (GROUP - 1)) ^ j) * HG + ((index // GROUP) ^ p)


def offsets_of(place, head):
    return place[1][head], place[2][head]


def token_picker():
    row = lax.broadcasted_iota(jnp.int32, (TOK, TOK), 0)
    col = lax.broadcasted_iota(jnp.int32, (TOK, TOK), 1)
    return (col == RATE * (row % BLK) + row // BLK).astype(BF16)


def fill_class_major(block, picker, scratch):
    scratch[...] = lax.dot_general(
        block, picker, (((0,), (1,)), ((), ())), preferred_element_type=F32
    ).astype(BF16)


def lane_block(index):
    return pl.ds(pl.multiple_of(index * BLK, BLK), BLK)


def head_rows(head):
    return pl.ds(pl.multiple_of(head * DH, 16), DH)


def pack_kernel(index, mid, top, k_hbm, v_hbm, q_hbm, *refs):
    place = (index, mid, top)
    outs, refs = refs[:6], refs[6:]
    blocks, held, packed = refs[:3], refs[3:6], refs[6:12]
    sems_in, sems_out = refs[12:]
    loads = [
        pltpu.make_async_copy(hbm, block, sems_in.at[i])
        for i, (hbm, block) in enumerate(zip((k_hbm, v_hbm, q_hbm), blocks))
    ]
    for load in loads:
        load.start()
    picker = token_picker()
    stores = []
    for n, (load, block, scratch) in enumerate(zip(loads, blocks, held)):
        load.wait()
        fill_class_major(block[...], picker, scratch)
        rows = slice(n * DH, (n + 1) * DH)
        for i, (j, first, count) in enumerate(
            ((0, 0, 4), (1, 0, 4), (2, 0, 2), (3, 0, 2), (2, 2, 2), (3, 2, 2))
        ):
            for p in range(HG):
                head = head_of(place, j, p)
                slots = class_of_slots(*offsets_of(place, head))
                for s in range(count):
                    packed[i][p, rows, s * BLK : (s + 1) * BLK] = scratch[
                        head_rows(head), lane_block(slots[first + s])
                    ]
            store = pltpu.make_async_copy(
                packed[i].at[:, rows], outs[i].at[:, rows], sems_out.at[i, n]
            )
            store.start()
            stores.append(store)
    for store in stores:
        store.wait()


def regroup_kernel(a_ref, b_ref, *refs):
    for s, out in enumerate(refs[-3:]):
        out[0] = a_ref[s + 1, :, 0:HALF]
        out[1] = b_ref[s + 1, :, 0:HALF]


def split_query(q):
    scaled = q.astype(F32) * (DH**-0.5 * LOG2E)
    high = scaled.astype(BF16)
    low = (scaled - high.astype(F32)).astype(BF16)
    return jnp.concatenate([high, low], axis=0)


def twice_keys(keys_t):
    both = jnp.concatenate([keys_t, keys_t], axis=0).astype(F32)
    return both.T.astype(BF16)


def largest(blocks):
    best = None
    for block in blocks:
        wide = block.astype(F32)
        length = jnp.sum(wide * wide, axis=0, keepdims=True)
        for low in range(0, block.shape[1], HALF):
            part = length[:, low : low + HALF]
            best = part if best is None else jnp.maximum(best, part)
    return jnp.max(best)


def is_small(queries, keys):
    scale = DH**-0.5 * LOG2E
    return largest(queries) * largest(keys) * (scale * scale) < SAFE * SAFE


def column_max(blocks):
    best = jnp.max(blocks[0], axis=0, keepdims=True)
    for block in blocks[1:]:
        best = jnp.maximum(best, jnp.max(block, axis=0, keepdims=True))
    return best


def near_kernel(inputs, units, tasks, carried, first, step, index, mid, top, *refs):
    place = (index, mid, top)
    pieces = dict(zip(inputs, refs[: len(inputs)]))
    refs = refs[len(inputs) :]
    old = [refs[2 * i : 2 * i + 2] for i in range(carried)]
    outs = refs[2 * carried : 2 * carried + 2 * len(tasks)]
    k_s, v_s = refs[-2:]
    v_s[:, DH:DX, :] = jnp.ones((step, DX - DH, v_s.shape[2]), BF16)
    lane_slot = lax.broadcasted_iota(jnp.int32, (1, HALF), 1) // BLK

    def lookup(j, slot):
        first = 0 if (j, 0) in pieces and pieces[j, 0].shape[2] > HALF else slot // 2 * 2
        return pieces[j, first], (slot - first) * BLK

    chunks = []
    row = 0
    for label, members in units:
        chunks.append((label, slice(row, row + len(members) * BLK)))
        row += len(members) * BLK
    members = [member for _, group in units for member in group]

    def prepare(h):
        for i, (j, slot) in enumerate(members):
            ref, lane = lookup(j, slot)
            rows = slice(i * BLK, (i + 1) * BLK)
            k_s[h, rows, :] = twice_keys(ref[h, 0:DH, lane : lane + BLK])
            v_s[h, 0:DH, rows] = ref[h, DH : 2 * DH, lane : lane + BLK]

    def counted_again(h):
        off_mid, off_top = offsets_of(place, head_of(place, 0, first + pl.program_id(0) * step + h))
        same = off_mid == off_top
        return [
            jnp.where(lane_slot == 0, jnp.where(same, 1.584962500721156, 1.0), 0.0),
            jnp.where(lane_slot == 1, jnp.where(same, 0.0, 1.0), 0.0),
        ]

    def run(plain, heads):
        again = [counted_again(h) for h in heads]
        flat = [
            (h, again_h, query, low, merge, out, i)
            for h, again_h in zip(heads, again)
            for out, group in enumerate(tasks)
            for i, (query, low, merge) in enumerate(group)
        ]

        def score(task):
            h, _, (j, half), low = task[:4]
            ref, lane = lookup(j, 2 * half)
            query = split_query(ref[h, 2 * DH :, lane : lane + HALF])
            return [dot(k_s[h, rows, :], query) for _, rows in chunks[low:]]

        scores = score(flat[0])
        for n, (h, again_h, (_, half), low, merge, out, i) in enumerate(flat):
            following = score(flat[n + 1]) if n + 1 < len(flat) else None
            best = jnp.zeros((1, HALF), F32) if plain else column_max(scores)
            if merge is not None:
                acc_in, max_in = old[merge[0]]
                old_max = max_in[h, merge[1], 0:1, :]
                best = best if plain else jnp.maximum(best, old_max)
            acc = None
            for (label, rows), block in zip(chunks[low:], scores):
                if half == 0 and label is not None:
                    block = block - (best - again_h[label])
                elif not plain:
                    block = block - best
                part = dot(v_s[h, :, rows], jnp.exp2(block).astype(BF16))
                acc = part if acc is None else acc + part
            if merge is not None:
                before = acc_in[h, merge[1]]
                acc = acc + (before if plain else before * jnp.exp2(old_max - best))
            acc_ref, max_ref = outs[2 * out : 2 * out + 2]
            acc_ref[h, i] = acc
            max_ref[h, i] = jnp.broadcast_to(best, (8, HALF))
            scores = following

    for h in range(step):
        prepare(h)
    plain = is_small(
        [ref[h, 2 * DH :, :] for ref in pieces.values() for h in range(step)],
        [ref[h, 0:DH, :] for ref in pieces.values() for h in range(step)],
    )
    for _, max_in in old:
        plain = plain & (jnp.max(jnp.abs(max_in[...])) == 0.0)

    @pl.when(plain)
    def _():
        run(True, list(range(step)))

    @pl.when(jnp.logical_not(plain))
    def _():
        @pl.loop(0, step)
        def _(h):
            run(False, [h])


def far_kernel(index, mid, top, *refs):
    place = (index, mid, top)
    own, beyond = refs[:GROUP], refs[GROUP : GROUP + 6]
    outs = refs[GROUP + 6 : GROUP + 6 + RATE]
    k_s, v_s, q_s, result_s, tail_s = refs[GROUP + 6 + RATE :]
    off_mid, off_top = offsets_of(place, head_of(place, 0, 0))
    same = off_mid == off_top
    slots = (0, jnp.where(same, 0, 1))

    def source(s, j):
        return own[j].at[0] if s == 0 else beyond[2 * FAR_ORDER.index(s) + j // 2].at[j % 2]

    for s in range(RATE):
        for j in range(GROUP):
            ref = source(s, j)
            for level, slot in enumerate(slots):
                here = slice(j * BLK, (j + 1) * BLK)
                k_s[level, s, here, :] = twice_keys(ref[0:DH, lane_block(slot)])
                v_s[level, s, 0:DH, here] = ref[DH : 2 * DH, lane_block(slot)]
                q_s[level, s, :, here] = split_query(ref[2 * DH : 3 * DH, lane_block(slot)])
    v_s[:, :, DH:DX, :] = jnp.ones((2, RATE, DX - DH, TOK), BF16)
    tail_s[...] = jnp.zeros(tail_s.shape, F32)

    def run(plain):
        tasks = [(level, chip) for level in range(2) for chip in range(2)]

        def segment(s, carry):
            def score(task):
                level, chip = task
                query = q_s[level, s, :, chip * HALF : (chip + 1) * HALF]
                return [dot(k_s[level, s ^ d], query) for d in range(1, RATE)]

            scores = score(tasks[0])
            for n, (level, chip) in enumerate(tasks):
                following = score(tasks[n + 1]) if n + 1 < len(tasks) else None
                best = jnp.zeros((1, HALF), F32) if plain else column_max(scores)
                acc = None
                for d in range(1, RATE):
                    block = scores[d - 1] if plain else scores[d - 1] - best
                    part = dot(v_s[level, s ^ d], jnp.exp2(block).astype(BF16))
                    acc = part if acc is None else acc + part
                total = acc[DH : DH + 1, :]
                result = (acc[0:DH, :] / total).astype(BF16)
                lse = best + jnp.log2(total)
                if level == 0:
                    lse = jnp.where(same, lse + 1.0, lse)
                else:
                    lse = jnp.where(same, -1e30, lse)
                high = lse.astype(BF16).astype(F32)
                middle = (lse - high).astype(BF16).astype(F32)
                low = lse - high - middle
                for i in range(2):
                    n = 2 * (2 * chip + i) + level
                    mine = slice(i * BLK, (i + 1) * BLK)
                    result_s[s, :, n * BLK : (n + 1) * BLK] = result[:, mine]
                    for k, part in enumerate((high, middle, low)):
                        tail_s[s, 3 * n + k : 3 * n + k + 1, :] = part[:, mine]
                scores = following
            return carry

        lax.fori_loop(0, RATE, segment, 0, unroll=2 if plain else 1)

    every = [source(s, j) for s in range(RATE) for j in range(GROUP)]
    plain = is_small(
        [ref[2 * DH : 3 * DH, 0:HALF] for ref in every], [ref[0:DH, 0:HALF] for ref in every]
    )
    pl.when(plain)(lambda: run(True))
    pl.when(jnp.logical_not(plain))(lambda: run(False))
    for s in range(RATE):
        outs[s][:, : GROUP * HALF] = result_s[s]
        outs[s][:, GROUP * HALF :] = tail_s[s].astype(BF16)


def join(acc, best, far, j):
    tail = far[:, GROUP * HALF :].astype(F32)
    lse = jnp.concatenate(
        [
            tail[3 * n : 3 * n + 1] + tail[3 * n + 1 : 3 * n + 2] + tail[3 * n + 2 : 3 * n + 3]
            for n in (2 * j, 2 * j + 1)
        ],
        axis=1,
    )
    overall = jnp.maximum(best, lse)
    near_factor, far_factor = jnp.exp2(best - overall), jnp.exp2(lse - overall)
    total = acc[DH : DH + 1] * near_factor + far_factor
    value = far[:, j * HALF : (j + 1) * HALF].astype(F32) * far_factor
    return ((acc[0:DH] * near_factor + value) / total).astype(BF16)


def combine_kernel(chip, acc_ref, max_ref, *refs):
    far, outs = refs[:-2][::-1], refs[-2:]
    for i in range(2):
        for p, results in enumerate(far):
            outs[i][p, :, 0:HALF] = join(
                acc_ref[p, 2 * i], max_ref[p, 2 * i, 0:1, :], results, 2 * chip + i
            )
            acc = acc_ref[p, 2 * i + 1]
            outs[i][p, :, HALF:] = (acc[0:DH] / acc[DH : DH + 1]).astype(BF16)


def project_kernel(sources, index, mid, top, *refs):
    place = (index, mid, top)
    parts, (w_ref, out_ref, held) = refs[:-3], refs[-3:]
    for (j, first), part in zip(sources, parts):
        for p in range(part.shape[0]):
            head = head_of(place, j, first + p)
            slots = class_of_slots(*offsets_of(place, head))
            for s in range(RATE):
                held[head_rows(head), lane_block(slots[s])] = part[
                    p, :, s * BLK : (s + 1) * BLK
                ]
    row = lax.broadcasted_iota(jnp.int32, (TOK, TOK), 0)
    col = lax.broadcasted_iota(jnp.int32, (TOK, TOK), 1)
    picker = (row == RATE * (col % BLK) + col // BLK).astype(BF16)
    attention = dot_nt(picker, held[...]).astype(BF16)
    out_ref[...] = dot(attention, w_ref[...]).astype(BF16)


def whole(shape):
    return pl.BlockSpec(shape, lambda *_: (0,) * len(shape))


def per_head(shape, skip=0):
    return pl.BlockSpec(shape, lambda h, *_: (h + skip,) + (0,) * (len(shape) - 1))


def call(
    kernel, scalars, args, grid, in_specs, outs, scratch, scores,
    limit=VMEM_LIMIT, after=(), through=(),
):
    known = len(scalars) + len(args)
    extra = (*after, *through)
    count = len(outs)
    anywhere = pl.BlockSpec(memory_space=pl.ANY)

    def body(*refs):
        results = refs[known + len(extra) :]
        kernel(*refs[:known], *results[:count], *results[count + len(through) :])

    return pl.pallas_call(
        body if extra else kernel,
        grid_spec=pltpu.PrefetchScalarGridSpec(
            num_scalar_prefetch=len(scalars),
            grid=grid,
            in_specs=list(in_specs) + [anywhere] * len(extra),
            out_specs=[spec for spec, _ in outs] + [anywhere] * len(through),
            scratch_shapes=scratch,
        ),
        out_shape=[shape for _, shape in outs]
        + [jax.ShapeDtypeStruct(x.shape, x.dtype) for x in through],
        input_output_aliases={known + len(after) + i: count + i for i in range(len(through))},
        compiler_params=pltpu.CompilerParams(vmem_limit_bytes=limit),
        cost_estimate=pl.CostEstimate(flops=0, bytes_accessed=0, transcendentals=0),
    )(*scalars, *args, *extra)


def handed_on(arrays):
    return call(lambda: None, (), (), (1,), [], [], [], 0, through=tuple(arrays))


def within(array, apart):
    count = lax.axis_size("seq")
    return lax.ppermute(array, "seq", [(i, i ^ apart) for i in range(count)])


def swap_segments(arrays):
    moved = {s: within(arrays[s - 1], GROUP * s) for s in (3, 2, 1)}
    return [moved[s] for s in (1, 2, 3)]


def shards_four(queries, key_states, value_states, offsets_mid, offsets_top, out_weight):
    width = queries.shape[1]
    place = (lax.axis_index("seq").astype(jnp.int32).reshape(1), offsets_mid, offsets_top)
    full = jax.ShapeDtypeStruct((HG, 3 * DH, TOK), BF16)
    piece = jax.ShapeDtypeStruct((HG, 3 * DH, HALF), BF16)
    pair = jax.ShapeDtypeStruct((2, 3 * DH, HALF), BF16)
    anywhere = pl.BlockSpec(memory_space=pl.ANY)
    shapes = [full] * 2 + [piece] * 4
    own0, own1, sel2, sel3, rest2, rest3 = call(
        pack_kernel, place, (key_states, value_states, queries), (1,),
        [anywhere] * 3,
        [(anywhere, shape) for shape in shapes],
        [pltpu.VMEM((TOK, width), BF16)] * 3
        + [pltpu.VMEM((width, TOK), BF16)] * 3
        + [pltpu.VMEM(shape.shape, BF16) for shape in shapes]
        + [pltpu.SemaphoreType.DMA((3,)), pltpu.SemaphoreType.DMA((6, 3))],
        1 << 19, VMEM_MOST,
    )
    own1 = within(own1, 1)
    sel2, sel3 = within(sel2, 2), within(sel3, 3)

    def regroup(a, b, **order):
        return call(
            regroup_kernel, (), (a, b), (1,),
            [whole(a.shape), whole(b.shape)], [(whole(pair.shape), pair)] * 3,
            [], 1 << 17, **order,
        )

    def near(held, units, tasks, old, first=0, heads=HG, step=2, **order):
        sizes = [len(members) * BLK for _, members in units]
        scores = sum(sum(sizes[low:]) * HALF for group in tasks for _, low, _ in group)
        arrays = [*held.values(), *[x for one in old for x in one]]
        shapes = [
            jax.ShapeDtypeStruct((heads, len(group), rows, HALF), F32)
            for group in tasks
            for rows in (DX, 8)
        ]
        return call(
            functools.partial(near_kernel, list(held), units, tasks, len(old), first, step),
            place, arrays, (heads // step,),
            [per_head((step,) + x.shape[1:], first // step) for x in arrays],
            [(per_head((step,) + x.shape[1:]), x) for x in shapes],
            [
                pltpu.VMEM((step, sum(sizes), 2 * DH), BF16),
                pltpu.VMEM((step, DX, sum(sizes)), BF16),
            ],
            heads * scores, **order,
        )

    def units_of(a, b):
        return [(0, [(a, 0), (b, 0)]), (1, [(a, 1), (b, 1)])], [
            (None, [(a, 2), (a, 3), (b, 2), (b, 3)])
        ]

    own_sel, own_rest = units_of(0, 1)
    other_sel, other_rest = units_of(2, 3)
    own = [(0, 0), (0, 1), (1, 0), (1, 1)]

    ours = regroup(own0, own1)
    ours = swap_segments(ours)
    held = {(0, 0): own0, (1, 0): own1}
    state_own = near(held, own_sel + own_rest, [[(q, 0, None) for q in own]], [])
    *theirs, rest2, rest3 = regroup(sel2, sel3, after=state_own[1:], through=(rest2, rest3))
    theirs = swap_segments(theirs)
    rest2, rest3 = within(rest2, 2), within(rest3, 3)
    beyond = [x for s in FAR_ORDER for x in (ours[s - 1], theirs[s - 1])]

    held.update({(2, 0): sel2, (3, 0): sel3})
    out = near(
        held, own_sel + own_rest + other_sel,
        [
            [(q, 3, (0, i)) for i, q in enumerate(own)],
            [((2, 0), 0, None), ((3, 0), 0, None)],
        ],
        [state_own],
        after=ours[::-1],
    )
    state_own, state_sel = out[:2], out[2:]

    result = jax.ShapeDtypeStruct((DH, GROUP * HALF + BLK), BF16)
    piece_0 = pl.BlockSpec((1, 3 * DH, HALF), lambda *_: (0, 0, 0))
    results = call(
        far_kernel, place, (own0, own1, sel2, sel3, *beyond), (1,),
        [piece_0] * GROUP + [whole(pair.shape)] * 6,
        [(whole(result.shape), result)] * RATE,
        [
            pltpu.VMEM((2, RATE, TOK, 2 * DH), BF16),
            pltpu.VMEM((2, RATE, DX, TOK), BF16),
            pltpu.VMEM((2, RATE, 2 * DH, TOK), BF16),
            pltpu.VMEM((RATE, DH, GROUP * HALF), BF16),
            pltpu.VMEM((RATE, DH, BLK), F32),
        ],
        RATE * 2 * 3 * TOK * TOK, after=(state_sel[1],),
    )
    back = [results[0]] + swap_segments(results[1:])

    held.update({(2, 2): rest2, (3, 2): rest3})
    units = own_sel + own_rest + other_sel + other_rest

    def combine(chip, state, far, **order):
        heads = state[0].shape[0]
        attended = jax.ShapeDtypeStruct((heads, DH, TOK), BF16)
        return call(
            functools.partial(combine_kernel, chip), (), (*state, *far[::-1]), (1,),
            [whole(x.shape) for x in state] + [whole(result.shape)] * heads,
            [(whole(attended.shape), attended)] * 2,
            [],
            1 << 18, **order,
        )

    parts = {}
    last = results[0]
    for first, heads in CHUNKS:
        state_other = near(
            held, units,
            [
                [
                    ((2, 0), 5, (0, 0)), ((2, 1), 0, None),
                    ((3, 0), 5, (0, 1)), ((3, 1), 0, None),
                ]
            ],
            [state_sel],
            first, heads, 2, after=(last,),
        )
        part2, part3 = combine(1, state_other, back[first : first + heads])
        parts[2, first], parts[3, first] = within(part2, 2), within(part3, 3)
        last = part3
    state_own = near(
        {(2, 2): rest2, (3, 2): rest3, **{q: held[q] for q in ((0, 0), (1, 0))}},
        other_rest,
        [[(q, 0, (0, i)) for i, q in enumerate(own)]],
        [state_own],
        after=(last,),
    )
    early = [parts[j, first] for first, _ in CHUNKS[:-1] for j in (2, 3)]
    part0, part1 = combine(0, state_own, back, after=early)
    parts = dict(zip(parts, handed_on(parts.values())))
    parts[0, 0], parts[1, 0] = part0, within(part1, 1)
    return call(
        functools.partial(project_kernel, list(parts)), place, (*parts.values(), out_weight), (1,),
        [whole(x.shape) for x in parts.values()] + [whole((width, width))],
        [(whole((TOK, width)), jax.ShapeDtypeStruct((TOK, width), BF16))],
        [pltpu.VMEM((width, TOK), BF16)],
        1 << 18,
    )[0]


def shards(queries, key_states, value_states, offsets_mid, offsets_top, out_weight):
    tokens, width = queries.shape
    heads = offsets_mid.shape[0]
    fits = (
        lax.axis_size("head") == 1
        and lax.axis_size("seq") == GROUP * RATE
        and tokens == TOK
        and heads == GROUP * HG
        and width == heads * DH
    )
    run = shards_four if fits else shards_general
    return run(queries, key_states, value_states, offsets_mid, offsets_top, out_weight)


def solution(mesh):
    in_specs = (
        P(("slide", "seq"), "head"),
        P(("slide", "seq"), "head"),
        P(("slide", "seq"), "head"),
        P(),
        P(),
        P("head", None),
    )
    out_specs = P(("slide", "seq", "head"), None)
    return jax.shard_map(shards, mesh=mesh, in_specs=in_specs, out_specs=out_specs, check_vma=False)
```

```python
import functools

import jax
import jax.numpy as jnp
from jax import lax
from jax.experimental import pallas as pl
from jax.experimental.pallas import tpu as pltpu
from jax.sharding import PartitionSpec as P

SEG = 2048
LOG2E = 1.4426950408889634
VMEM_LIMIT = 40 * 1024 * 1024
VMEM_MOST = 60 * 1024 * 1024
BF16 = jnp.bfloat16
F32 = jnp.float32


def partner_2(block, axis, apart):
    count = lax.axis_size(axis)
    route = []
    for low in range(count):
        high = low | 1 << apart
        if high != low and high < count:
            route += [(low, high), (high, low)]
    return lax.ppermute(block, axis, route)


def attend_head(triple_in):
    query_rows, key_rows, value_rows = triple_in
    score_scale = query_rows.shape[-1] ** (-0.5)
    scores = jnp.dot(query_rows, key_rows.T, preferred_element_type=jnp.float32) * score_scale
    row_max = jnp.max(scores, axis=1)
    shifted = jnp.exp(scores - row_max[:, None])
    row_total = jnp.sum(shifted, axis=1)
    weights = shifted.astype(jnp.bfloat16)
    numerator = jnp.dot(weights, value_rows, preferred_element_type=jnp.float32)
    return (numerator, row_total, row_max)


def attend_local(query_rows, pair_rows):
    return lax.map(
        attend_head,
        (
            query_rows.transpose(1, 0, 2),
            pair_rows[:, 0].transpose(1, 0, 2),
            pair_rows[:, 1].transpose(1, 0, 2),
        ),
    )


def pick_rows(states, offsets, rate):
    row_count, inner_count, heads_here, head_width = states.shape
    picker = (jnp.arange(rate)[:, None] == offsets[None, :]).astype(jnp.bfloat16)
    folded = states.reshape(row_count // rate, rate, inner_count, heads_here, head_width)
    return jnp.einsum("archd,rh->achd", folded, picker, preferred_element_type=jnp.float32).astype(
        jnp.bfloat16
    )


def spread_back(numerator, row_total, row_max, offsets, rate):
    heads_here, picked_count, head_width = numerator.shape
    chosen = jnp.arange(rate)[:, None] == offsets[None, :]
    full_num = jnp.where(chosen[None, :, :, None], numerator.transpose(1, 0, 2)[:, None], 0.0)
    full_total = jnp.where(chosen[None], row_total.T[:, None], 0.0)
    full_max = jnp.where(chosen[None], row_max.T[:, None], -1e30)
    return (
        full_num.reshape(picked_count * rate, heads_here, head_width),
        full_total.reshape(picked_count * rate, heads_here),
        full_max.reshape(picked_count * rate, heads_here),
    )


def doubling(buffer, steps_count):
    position = lax.axis_index("seq")
    for bit_index in range(steps_count):
        partner = partner_2(buffer, "seq", bit_index)
        is_lower = position >> bit_index & 1 == 0
        buffer = jnp.where(
            is_lower, jnp.concatenate([buffer, partner], 0), jnp.concatenate([partner, buffer], 0)
        )
    return buffer


def shards_general(queries, key_states, value_states, offsets_mid, offsets_top, out_weight):
    tok_rows = queries.shape[0]
    heads_local = offsets_mid.shape[0] // lax.axis_size("head")
    head_size = queries.shape[1] // heads_local
    seq_devices = lax.axis_size("seq")
    seq_total = tok_rows * seq_devices
    width_mid = min(16 * SEG, seq_total)
    rate_mid = width_mid // SEG
    rate_top = seq_total // SEG
    start_head = lax.axis_index("head") * heads_local
    mid_local = lax.dynamic_slice(offsets_mid, (start_head,), (heads_local,))
    top_local = lax.dynamic_slice(offsets_top, (start_head,), (heads_local,))
    query_heads = queries.reshape(tok_rows, 1, heads_local, head_size)
    paired = jnp.stack([key_states, value_states], axis=1).reshape(
        tok_rows, 2, heads_local, head_size
    )
    near_bits = (SEG // tok_rows).bit_length() - 1
    near_rows = doubling(paired.reshape(tok_rows, -1), near_bits).reshape(
        SEG, 2, heads_local, head_size
    )
    near_num, near_total, near_max = attend_local(query_heads[:, 0], near_rows)
    level_near = spread_back(
        near_num, near_total, near_max, jnp.zeros((heads_local,), jnp.int32), 1
    )
    mid_q = pick_rows(query_heads, mid_local, rate_mid)[:, 0]
    mid_kv = pick_rows(paired, mid_local, rate_mid)
    mid_group = width_mid // tok_rows
    mid_bits = mid_group.bit_length() - 1
    mid_rows = doubling(mid_kv.reshape(mid_kv.shape[0], -1), mid_bits).reshape(
        SEG, 2, heads_local, head_size
    )
    mid_num, mid_total, mid_max = attend_local(mid_q, mid_rows)
    level_mid = spread_back(mid_num, mid_total, mid_max, mid_local, rate_mid)
    top_q = pick_rows(query_heads, top_local, rate_top)[:, 0]
    top_kv = pick_rows(paired, top_local, rate_top)
    top_rows = lax.all_gather(
        top_kv.reshape(top_kv.shape[0], -1), "seq", axis=0, tiled=True
    ).reshape(SEG, 2, heads_local, head_size)
    top_num, top_total, top_max = attend_local(top_q, top_rows)
    level_top = spread_back(top_num, top_total, top_max, top_local, rate_top)
    levels = [level_near, level_mid, level_top]
    overall = jnp.maximum(jnp.maximum(level_near[2], level_mid[2]), level_top[2])
    numerator = jnp.zeros((tok_rows, heads_local, head_size), jnp.float32)
    row_total = jnp.zeros((tok_rows, heads_local), jnp.float32)
    for level_num, level_total, level_max in levels:
        factor = jnp.exp(level_max - overall)
        numerator = numerator + factor[..., None] * level_num
        row_total = row_total + factor * level_total
    attention = (
        (numerator / row_total[..., None])
        .astype(jnp.bfloat16)
        .reshape(tok_rows, heads_local * head_size)
    )
    result = lax.psum_scatter(
        jnp.dot(attention, out_weight, preferred_element_type=jnp.float32),
        "head",
        scatter_dimension=0,
        tiled=True,
    )
    return result.astype(jnp.bfloat16)


RATE = 4
GROUP = 4
HG = 4
DH = 48
BLK = 128
HALF = 2 * BLK
TOK = 512
SAFE = 96.0
CHUNKS = ((0, 4),)
DX = 64


def dot(a, b):
    return jnp.dot(a, b, preferred_element_type=F32)


def dot_nt(a, b):
    return lax.dot_general(a, b, (((1,), (1,)), ((), ())), preferred_element_type=F32)


def class_of_slots(off_mid, off_top):
    first = off_mid
    second = jnp.where(off_top == off_mid, lax.rem(off_mid + 1, RATE), off_top)
    free0 = (first != 0) & (second != 0)
    free1 = (first != 1) & (second != 1)
    third = jnp.where(free0, 0, jnp.where(free1, 1, 2))
    return first, second, third, 6 - first - second - third


def head_of(place, j, p):
    index = place[0][0]
    return ((index & (GROUP - 1)) ^ j) * HG + ((index // GROUP) ^ p)


def offsets_of(place, head):
    return place[1][head], place[2][head]


def token_picker():
    row = lax.broadcasted_iota(jnp.int32, (TOK, TOK), 0)
    col = lax.broadcasted_iota(jnp.int32, (TOK, TOK), 1)
    return (col == RATE * (row % BLK) + row // BLK).astype(BF16)


def fill_class_major(block, picker, scratch):
    scratch[...] = lax.dot_general(
        block, picker, (((0,), (1,)), ((), ())), preferred_element_type=F32
    ).astype(BF16)


def lane_block(index):
    return pl.ds(pl.multiple_of(index * BLK, BLK), BLK)


def head_rows(head):
    return pl.ds(pl.multiple_of(head * DH, 16), DH)


def pack_kernel(index, mid, top, k_hbm, v_hbm, q_hbm, *refs):
    place = (index, mid, top)
    outs, refs = refs[:6], refs[6:]
    blocks, held, packed = refs[:3], refs[3:6], refs[6:12]
    sems_in, sems_out = refs[12:]
    loads = [
        pltpu.make_async_copy(hbm, block, sems_in.at[i])
        for i, (hbm, block) in enumerate(zip((k_hbm, v_hbm, q_hbm), blocks))
    ]
    for load in loads:
        load.start()
    picker = token_picker()
    stores = []
    for n, (load, block, scratch) in enumerate(zip(loads, blocks, held)):
        load.wait()
        fill_class_major(block[...], picker, scratch)
        rows = slice(n * DH, (n + 1) * DH)
        for i, (j, first, count) in enumerate(
            ((0, 0, 4), (1, 0, 4), (2, 0, 2), (3, 0, 2), (2, 2, 2), (3, 2, 2))
        ):
            for p in range(HG):
                head = head_of(place, j, p)
                slots = class_of_slots(*offsets_of(place, head))
                for s in range(count):
                    packed[i][p, rows, s * BLK : (s + 1) * BLK] = scratch[
                        head_rows(head), lane_block(slots[first + s])
                    ]
            store = pltpu.make_async_copy(
                packed[i].at[:, rows], outs[i].at[:, rows], sems_out.at[i, n]
            )
            store.start()
            stores.append(store)
    for store in stores:
        store.wait()


def regroup_kernel(a_ref, b_ref, *refs):
    for s, out in enumerate(refs[-3:]):
        out[0] = a_ref[s + 1, :, 0:HALF]
        out[1] = b_ref[s + 1, :, 0:HALF]


def split_query(q):
    scaled = q.astype(F32) * (DH**-0.5 * LOG2E)
    high = scaled.astype(BF16)
    low = (scaled - high.astype(F32)).astype(BF16)
    return jnp.concatenate([high, low], axis=0)


def twice_keys(keys_t):
    both = jnp.concatenate([keys_t, keys_t], axis=0).astype(F32)
    return both.T.astype(BF16)


def largest(blocks):
    best = None
    for block in blocks:
        wide = block.astype(F32)
        length = jnp.sum(wide * wide, axis=0, keepdims=True)
        for low in range(0, block.shape[1], HALF):
            part = length[:, low : low + HALF]
            best = part if best is None else jnp.maximum(best, part)
    return jnp.max(best)


def is_small(query_length, key_length):
    scale = DH**-0.5 * LOG2E
    return query_length * key_length * (scale * scale) < SAFE * SAFE


def column_max(blocks):
    best = jnp.max(blocks[0], axis=0, keepdims=True)
    for block in blocks[1:]:
        best = jnp.maximum(best, jnp.max(block, axis=0, keepdims=True))
    return best


def near_kernel(inputs, units, tasks, carried, first, step, index, mid, top, *refs):
    place = (index, mid, top)
    pieces = dict(zip(inputs, refs[: len(inputs)]))
    refs = refs[len(inputs) :]
    old = [refs[2 * i : 2 * i + 2] for i in range(carried)]
    outs = refs[2 * carried : 2 * carried + 2 * len(tasks)]
    k_s, v_s = refs[-2:]
    v_s[:, DH:DX, :] = jnp.ones((step, DX - DH, v_s.shape[2]), BF16)
    lane_slot = lax.broadcasted_iota(jnp.int32, (1, HALF), 1) // BLK

    def lookup(j, slot):
        first = 0 if (j, 0) in pieces and pieces[j, 0].shape[2] > HALF else slot // 2 * 2
        return pieces[j, first], (slot - first) * BLK

    chunks = []
    row = 0
    for label, members in units:
        chunks.append((label, slice(row, row + len(members) * BLK)))
        row += len(members) * BLK
    members = [member for _, group in units for member in group]

    def prepare(h):
        for i, (j, slot) in enumerate(members):
            ref, lane = lookup(j, slot)
            rows = slice(i * BLK, (i + 1) * BLK)
            k_s[h, rows, :] = twice_keys(ref[h, 0:DH, lane : lane + BLK])
            v_s[h, 0:DH, rows] = ref[h, DH : 2 * DH, lane : lane + BLK]

    def counted_again(h):
        off_mid, off_top = offsets_of(place, head_of(place, 0, first + pl.program_id(0) * step + h))
        same = off_mid == off_top
        return [
            jnp.where(lane_slot == 0, jnp.where(same, 1.584962500721156, 1.0), 0.0),
            jnp.where(lane_slot == 1, jnp.where(same, 0.0, 1.0), 0.0),
        ]

    def run(plain, heads):
        again = [counted_again(h) for h in heads]
        flat = [
            (h, again_h, query, low, merge, out, i)
            for h, again_h in zip(heads, again)
            for out, group in enumerate(tasks)
            for i, (query, low, merge) in enumerate(group)
        ]

        def score(task):
            h, _, (j, half), low = task[:4]
            ref, lane = lookup(j, 2 * half)
            query = split_query(ref[h, 2 * DH :, lane : lane + HALF])
            return [dot(k_s[h, rows, :], query) for _, rows in chunks[low:]]

        scores = score(flat[0])
        for n, (h, again_h, (_, half), low, merge, out, i) in enumerate(flat):
            following = score(flat[n + 1]) if n + 1 < len(flat) else None
            best = jnp.zeros((1, HALF), F32) if plain else column_max(scores)
            if merge is not None:
                acc_in, max_in = old[merge[0]]
                old_max = max_in[h, merge[1], 0:1, :]
                best = best if plain else jnp.maximum(best, old_max)
            acc = None
            for (label, rows), block in zip(chunks[low:], scores):
                if half == 0 and label is not None:
                    block = block - (best - again_h[label])
                elif not plain:
                    block = block - best
                part = dot(v_s[h, :, rows], jnp.exp2(block).astype(BF16))
                acc = part if acc is None else acc + part
            if merge is not None:
                before = acc_in[h, merge[1]]
                acc = acc + (before if plain else before * jnp.exp2(old_max - best))
            acc_ref, max_ref = outs[2 * out : 2 * out + 2]
            acc_ref[h, i] = acc
            max_ref[h, i] = jnp.broadcast_to(best, (8, HALF))
            scores = following

    for h in range(step):
        prepare(h)
    plain = is_small(
        largest([ref[h, 2 * DH :, :] for ref in pieces.values() for h in range(step)]),
        largest([ref[h, 0:DH, :] for ref in pieces.values() for h in range(step)]),
    )
    for _, max_in in old:
        plain = plain & (jnp.max(jnp.abs(max_in[...])) == 0.0)

    @pl.when(plain)
    def _():
        run(True, list(range(step)))

    @pl.when(jnp.logical_not(plain))
    def _():
        @pl.loop(0, step)
        def _(h):
            run(False, [h])


def far_slots(place):
    off_mid, off_top = offsets_of(place, head_of(place, 0, 0))
    same = off_mid == off_top
    return same, (0, jnp.where(same, 0, 1))


def far_pieces(place, sources, k_s, v_s, q_s):
    _, slots = far_slots(place)
    for s, pair in enumerate(sources):
        for i, ref in enumerate(pair):
            here = slice(i * BLK, (i + 1) * BLK)
            for level, slot in enumerate(slots):
                k_s[level, s, here, :] = twice_keys(ref[0:DH, lane_block(slot)])
                v_s[level, s, 0:DH, here] = ref[DH : 2 * DH, lane_block(slot)]
                q_s[level, s, :, here] = split_query(ref[2 * DH : 3 * DH, lane_block(slot)])
    v_s[:, :, DH:DX, :] = jnp.ones((2, RATE, DX - DH, HALF), BF16)


def far_lengths(sources):
    every = [ref for pair in sources for ref in pair]
    return (
        largest([ref[2 * DH : 3 * DH, 0:HALF] for ref in every]),
        largest([ref[0:DH, 0:HALF] for ref in every]),
    )


def far_own_kernel(index, mid, top, own0, own1, beyond1, beyond2, beyond3, *refs):
    k_s, v_s, q_s, acc_ref, max_ref, length_ref = refs
    sources = [(own0.at[0], own1.at[0])] + [
        (ref.at[0], ref.at[1]) for ref in (beyond1, beyond2, beyond3)
    ]
    far_pieces((index, mid, top), sources, k_s, v_s, q_s)

    def run(plain):
        def segment(s, carry):
            def score(level):
                return [dot(k_s[level, s ^ d], q_s[level, s]) for d in range(1, RATE)]

            scores = score(0)
            for level in range(2):
                following = score(1) if level == 0 else None
                best = jnp.zeros((1, HALF), F32) if plain else column_max(scores)
                acc = None
                for d in range(1, RATE):
                    block = scores[d - 1] if plain else scores[d - 1] - best
                    part = dot(v_s[level, s ^ d], jnp.exp2(block).astype(BF16))
                    acc = part if acc is None else acc + part
                acc_ref[level, s] = acc
                max_ref[level, s] = jnp.broadcast_to(best, (8, HALF))
                scores = following
            return carry

        lax.fori_loop(0, RATE, segment, 0, unroll=2 if plain else 1)

    query_length, key_length = far_lengths(sources)
    length_ref[0] = query_length
    length_ref[1] = key_length
    plain = is_small(query_length, key_length)
    pl.when(plain)(lambda: run(True))
    pl.when(jnp.logical_not(plain))(lambda: run(False))


def far_kernel(index, mid, top, *refs):
    place = (index, mid, top)
    sel2, sel3, beyond3, beyond2, beyond1, k_own, v_own, q_own, acc_in, max_in, length_in = refs[
        :11
    ]
    outs = refs[11 : 11 + RATE]
    k_s, v_s, q_s, result_s, tail_s = refs[11 + RATE :]
    same, _ = far_slots(place)
    sources = [(sel2.at[0], sel3.at[0])] + [
        (ref.at[0], ref.at[1]) for ref in (beyond1, beyond2, beyond3)
    ]
    far_pieces(place, sources, k_s, v_s, q_s)
    tail_s[...] = jnp.zeros(tail_s.shape, F32)

    def run(plain):
        tasks = [(level, chip) for level in range(2) for chip in range(2)]
        held = ((k_own, v_own, q_own), (k_s, v_s, q_s))

        def segment(s, carry):
            def blocks(chip):
                return [(held[c], s ^ d) for d in range(1, RATE) for c in ((1,), (0, 1))[chip]]

            def score(task):
                level, chip = task
                query = held[chip][2][level, s]
                return [dot(keys[0][level, b], query) for keys, b in blocks(chip)]

            scores = score(tasks[0])
            for n, (level, chip) in enumerate(tasks):
                following = score(tasks[n + 1]) if n + 1 < len(tasks) else None
                best = jnp.zeros((1, HALF), F32) if plain else column_max(scores)
                acc = None
                if chip == 0:
                    acc = acc_in[level, s]
                    if not plain:
                        old_max = max_in[level, s, 0:1, :]
                        best = jnp.maximum(best, old_max)
                        acc = acc * jnp.exp2(old_max - best)
                for block, (keys, b) in zip(scores, blocks(chip)):
                    block = block if plain else block - best
                    part = dot(keys[1][level, b], jnp.exp2(block).astype(BF16))
                    acc = part if acc is None else acc + part
                total = acc[DH : DH + 1, :]
                result = (acc[0:DH, :] / total).astype(BF16)
                lse = best + jnp.log2(total)
                if level == 0:
                    lse = jnp.where(same, lse + 1.0, lse)
                else:
                    lse = jnp.where(same, -1e30, lse)
                high = lse.astype(BF16).astype(F32)
                middle = (lse - high).astype(BF16).astype(F32)
                low = lse - high - middle
                for i in range(2):
                    n = 2 * (2 * chip + i) + level
                    mine = slice(i * BLK, (i + 1) * BLK)
                    result_s[s, :, n * BLK : (n + 1) * BLK] = result[:, mine]
                    for k, part in enumerate((high, middle, low)):
                        tail_s[s, 3 * n + k : 3 * n + k + 1, :] = part[:, mine]
                scores = following
            return carry

        lax.fori_loop(0, RATE, segment, 0, unroll=2 if plain else 1)

    query_length, key_length = far_lengths(sources)
    plain = is_small(
        jnp.maximum(query_length, length_in[0]), jnp.maximum(key_length, length_in[1])
    )
    pl.when(plain)(lambda: run(True))
    pl.when(jnp.logical_not(plain))(lambda: run(False))
    for s in range(RATE):
        outs[s][:, : GROUP * HALF] = result_s[s]
        outs[s][:, GROUP * HALF :] = tail_s[s].astype(BF16)


def join(acc, best, far, j):
    tail = far[:, GROUP * HALF :].astype(F32)
    lse = jnp.concatenate(
        [
            tail[3 * n : 3 * n + 1] + tail[3 * n + 1 : 3 * n + 2] + tail[3 * n + 2 : 3 * n + 3]
            for n in (2 * j, 2 * j + 1)
        ],
        axis=1,
    )
    overall = jnp.maximum(best, lse)
    near_factor, far_factor = jnp.exp2(best - overall), jnp.exp2(lse - overall)
    total = acc[DH : DH + 1] * near_factor + far_factor
    value = far[:, j * HALF : (j + 1) * HALF].astype(F32) * far_factor
    return ((acc[0:DH] * near_factor + value) / total).astype(BF16)


def combine_kernel(chip, acc_ref, max_ref, *refs):
    far, outs = refs[:-2][::-1], refs[-2:]
    for i in range(2):
        for p, results in enumerate(far):
            outs[i][p, :, 0:HALF] = join(
                acc_ref[p, 2 * i], max_ref[p, 2 * i, 0:1, :], results, 2 * chip + i
            )
            acc = acc_ref[p, 2 * i + 1]
            outs[i][p, :, HALF:] = (acc[0:DH] / acc[DH : DH + 1]).astype(BF16)


def project_kernel(sources, index, mid, top, *refs):
    place = (index, mid, top)
    parts, (w_hbm, out_hbm, held, w_ref, out_ref, sems) = refs[:-6], refs[-6:]
    load = pltpu.make_async_copy(w_hbm, w_ref, sems.at[0])
    load.start()
    for (j, first), part in zip(sources, parts):
        for p in range(part.shape[0]):
            head = head_of(place, j, first + p)
            slots = class_of_slots(*offsets_of(place, head))
            for s in range(RATE):
                held[head_rows(head), lane_block(slots[s])] = part[
                    p, :, s * BLK : (s + 1) * BLK
                ]
    row = lax.broadcasted_iota(jnp.int32, (HALF, TOK), 0)
    col = lax.broadcasted_iota(jnp.int32, (HALF, TOK), 1)
    stores = []
    for n in range(2):
        rows = slice(n * HALF, (n + 1) * HALF)
        picker = (row + n * HALF == RATE * (col % BLK) + col // BLK).astype(BF16)
        attention = dot_nt(picker, held[...]).astype(BF16)
        if n == 0:
            load.wait()
        out_ref[rows, :] = dot(attention, w_ref[...]).astype(BF16)
        stores.append(pltpu.make_async_copy(out_ref.at[rows], out_hbm.at[rows], sems.at[1 + n]))
        stores[n].start()
    for store in stores:
        store.wait()


def whole(shape):
    return pl.BlockSpec(shape, lambda *_: (0,) * len(shape))


def per_head(shape, skip=0):
    return pl.BlockSpec(shape, lambda h, *_: (h + skip,) + (0,) * (len(shape) - 1))


def call(
    kernel, scalars, args, grid, in_specs, outs, scratch, scores,
    limit=VMEM_LIMIT, after=(), through=(),
):
    known = len(scalars) + len(args)
    extra = (*after, *through)
    count = len(outs)
    anywhere = pl.BlockSpec(memory_space=pl.ANY)

    def body(*refs):
        results = refs[known + len(extra) :]
        kernel(*refs[:known], *results[:count], *results[count + len(through) :])

    return pl.pallas_call(
        body if extra else kernel,
        grid_spec=pltpu.PrefetchScalarGridSpec(
            num_scalar_prefetch=len(scalars),
            grid=grid,
            in_specs=list(in_specs) + [anywhere] * len(extra),
            out_specs=[spec for spec, _ in outs] + [anywhere] * len(through),
            scratch_shapes=scratch,
        ),
        out_shape=[shape for _, shape in outs]
        + [jax.ShapeDtypeStruct(x.shape, x.dtype) for x in through],
        input_output_aliases={known + len(after) + i: count + i for i in range(len(through))},
        compiler_params=pltpu.CompilerParams(vmem_limit_bytes=limit),
        cost_estimate=pl.CostEstimate(flops=0, bytes_accessed=0, transcendentals=0),
    )(*scalars, *args, *extra)


def handed_on(arrays):
    return call(lambda: None, (), (), (1,), [], [], [], 0, through=tuple(arrays))


def within(array, apart):
    count = lax.axis_size("seq")
    return lax.ppermute(array, "seq", [(i, i ^ apart) for i in range(count)])


def swap_segments(arrays):
    moved = {s: within(arrays[s - 1], GROUP * s) for s in (3, 2, 1)}
    return [moved[s] for s in (1, 2, 3)]


def shards_four(queries, key_states, value_states, offsets_mid, offsets_top, out_weight):
    width = queries.shape[1]
    place = (lax.axis_index("seq").astype(jnp.int32).reshape(1), offsets_mid, offsets_top)
    full = jax.ShapeDtypeStruct((HG, 3 * DH, TOK), BF16)
    piece = jax.ShapeDtypeStruct((HG, 3 * DH, HALF), BF16)
    pair = jax.ShapeDtypeStruct((2, 3 * DH, HALF), BF16)
    anywhere = pl.BlockSpec(memory_space=pl.ANY)
    shapes = [full] * 2 + [piece] * 4
    own0, own1, sel2, sel3, rest2, rest3 = call(
        pack_kernel, place, (key_states, value_states, queries), (1,),
        [anywhere] * 3,
        [(anywhere, shape) for shape in shapes],
        [pltpu.VMEM((TOK, width), BF16)] * 3
        + [pltpu.VMEM((width, TOK), BF16)] * 3
        + [pltpu.VMEM(shape.shape, BF16) for shape in shapes]
        + [pltpu.SemaphoreType.DMA((3,)), pltpu.SemaphoreType.DMA((6, 3))],
        1 << 19, VMEM_MOST,
    )
    own1 = within(own1, 1)
    sel2, sel3 = within(sel2, 2), within(sel3, 3)

    def regroup(a, b, **order):
        return call(
            regroup_kernel, (), (a, b), (1,),
            [whole(a.shape), whole(b.shape)], [(whole(pair.shape), pair)] * 3,
            [], 1 << 17, **order,
        )

    def near(held, units, tasks, old, first=0, heads=HG, step=2, **order):
        sizes = [len(members) * BLK for _, members in units]
        scores = sum(sum(sizes[low:]) * HALF for group in tasks for _, low, _ in group)
        arrays = [*held.values(), *[x for one in old for x in one]]
        shapes = [
            jax.ShapeDtypeStruct((heads, len(group), rows, HALF), F32)
            for group in tasks
            for rows in (DX, 8)
        ]
        return call(
            functools.partial(near_kernel, list(held), units, tasks, len(old), first, step),
            place, arrays, (heads // step,),
            [per_head((step,) + x.shape[1:], first // step) for x in arrays],
            [(per_head((step,) + x.shape[1:]), x) for x in shapes],
            [
                pltpu.VMEM((step, sum(sizes), 2 * DH), BF16),
                pltpu.VMEM((step, DX, sum(sizes)), BF16),
            ],
            heads * scores, **order,
        )

    def units_of(a, b):
        return [(0, [(a, 0), (b, 0)]), (1, [(a, 1), (b, 1)])], [
            (None, [(a, 2), (a, 3), (b, 2), (b, 3)])
        ]

    own_sel, own_rest = units_of(0, 1)
    other_sel, other_rest = units_of(2, 3)
    own = [(0, 0), (0, 1), (1, 0), (1, 1)]

    ours = regroup(own0, own1)
    ours = swap_segments(ours)
    held = {(0, 0): own0, (1, 0): own1}
    state_own = near(held, own_sel + own_rest, [[(q, 0, None) for q in own]], [])
    *theirs, rest2, rest3 = regroup(sel2, sel3, after=state_own[1:], through=(rest2, rest3))
    theirs = swap_segments(theirs)
    rest2, rest3 = within(rest2, 2), within(rest3, 3)

    held.update({(2, 0): sel2, (3, 0): sel3})
    out = near(
        held, own_sel + own_rest + other_sel,
        [
            [(q, 3, (0, i)) for i, q in enumerate(own)],
            [((2, 0), 0, None), ((3, 0), 0, None)],
        ],
        [state_own],
        after=ours[::-1],
    )
    state_own, state_sel = out[:2], out[2:]

    result = jax.ShapeDtypeStruct((DH, GROUP * HALF + BLK), BF16)
    piece_0 = pl.BlockSpec((1, 3 * DH, HALF), lambda *_: (0, 0, 0))
    pieces_shapes = [
        jax.ShapeDtypeStruct((2, RATE, HALF, 2 * DH), BF16),
        jax.ShapeDtypeStruct((2, RATE, DX, HALF), BF16),
        jax.ShapeDtypeStruct((2, RATE, 2 * DH, HALF), BF16),
    ]
    sums_shapes = [
        jax.ShapeDtypeStruct((2, RATE, DX, HALF), F32),
        jax.ShapeDtypeStruct((2, RATE, 8, HALF), F32),
    ]
    in_scalars = pl.BlockSpec(memory_space=pltpu.SMEM)
    far_own = call(
        far_own_kernel, place, (own0, own1, *ours), (1,),
        [piece_0] * 2 + [whole(pair.shape)] * 3,
        [(whole(x.shape), x) for x in pieces_shapes + sums_shapes]
        + [(in_scalars, jax.ShapeDtypeStruct((2,), F32))],
        [], RATE * 2 * 3 * HALF * HALF, after=(state_sel[1],),
    )
    results = call(
        far_kernel, place, (sel2, sel3, *theirs[::-1], *far_own), (1,),
        [piece_0] * 2 + [whole(pair.shape)] * 3
        + [whole(x.shape) for x in far_own[:-1]] + [in_scalars],
        [(whole(result.shape), result)] * RATE,
        [pltpu.VMEM(x.shape, BF16) for x in pieces_shapes]
        + [
            pltpu.VMEM((RATE, DH, GROUP * HALF), BF16),
            pltpu.VMEM((RATE, DH, BLK), F32),
        ],
        RATE * 2 * 3 * 3 * HALF * HALF,
    )
    back = [results[0]] + swap_segments(results[1:])

    held.update({(2, 2): rest2, (3, 2): rest3})
    units = own_sel + own_rest + other_sel + other_rest

    def combine(chip, state, far, **order):
        heads = state[0].shape[0]
        attended = jax.ShapeDtypeStruct((heads, DH, TOK), BF16)
        return call(
            functools.partial(combine_kernel, chip), (), (*state, *far[::-1]), (1,),
            [whole(x.shape) for x in state] + [whole(result.shape)] * heads,
            [(whole(attended.shape), attended)] * 2,
            [],
            1 << 18, **order,
        )

    parts = {}
    last = results[0]
    for first, heads in CHUNKS:
        state_other = near(
            held, units,
            [
                [
                    ((2, 0), 5, (0, 0)), ((2, 1), 0, None),
                    ((3, 0), 5, (0, 1)), ((3, 1), 0, None),
                ]
            ],
            [state_sel],
            first, heads, 2, after=(last,),
        )
        part2, part3 = combine(1, state_other, back[first : first + heads])
        parts[2, first], parts[3, first] = within(part2, 2), within(part3, 3)
        last = part3
    state_own = near(
        {(2, 2): rest2, (3, 2): rest3, **{q: held[q] for q in ((0, 0), (1, 0))}},
        other_rest,
        [[(q, 0, (0, i)) for i, q in enumerate(own)]],
        [state_own],
        after=(last,),
    )
    early = [parts[j, first] for first, _ in CHUNKS[:-1] for j in (2, 3)]
    part0, part1 = combine(0, state_own, back, after=early)
    parts = dict(zip(parts, handed_on(parts.values())))
    parts[0, 0], parts[1, 0] = part0, within(part1, 1)
    return call(
        functools.partial(project_kernel, list(parts)), place, (*parts.values(), out_weight), (1,),
        [whole(x.shape) for x in parts.values()] + [anywhere],
        [(anywhere, jax.ShapeDtypeStruct((TOK, width), BF16))],
        [
            pltpu.VMEM((width, TOK), BF16),
            pltpu.VMEM((width, width), BF16),
            pltpu.VMEM((TOK, width), BF16),
            pltpu.SemaphoreType.DMA((3,)),
        ],
        1 << 18,
    )[0]


def shards(queries, key_states, value_states, offsets_mid, offsets_top, out_weight):
    tokens, width = queries.shape
    heads = offsets_mid.shape[0]
    fits = (
        lax.axis_size("head") == 1
        and lax.axis_size("seq") == GROUP * RATE
        and tokens == TOK
        and heads == GROUP * HG
        and width == heads * DH
    )
    run = shards_four if fits else shards_general
    return run(queries, key_states, value_states, offsets_mid, offsets_top, out_weight)


def solution(mesh):
    in_specs = (
        P(("slide", "seq"), "head"),
        P(("slide", "seq"), "head"),
        P(("slide", "seq"), "head"),
        P(),
        P(),
        P("head", None),
    )
    out_specs = P(("slide", "seq", "head"), None)
    return jax.shard_map(shards, mesh=mesh, in_specs=in_specs, out_specs=out_specs, check_vma=False)
```

```python
import functools

import jax
import jax.numpy as jnp
from jax import lax
from jax.experimental import pallas as pl
from jax.experimental.pallas import tpu as pltpu
from jax.sharding import PartitionSpec as P

SEG = 2048
LOG2E = 1.4426950408889634
VMEM_LIMIT = 40 * 1024 * 1024
VMEM_MOST = 60 * 1024 * 1024
BF16 = jnp.bfloat16
F32 = jnp.float32


def partner_2(block, axis, apart):
    count = lax.axis_size(axis)
    route = []
    for low in range(count):
        high = low | 1 << apart
        if high != low and high < count:
            route += [(low, high), (high, low)]
    return lax.ppermute(block, axis, route)


def attend_head(triple_in):
    query_rows, key_rows, value_rows = triple_in
    score_scale = query_rows.shape[-1] ** (-0.5)
    scores = jnp.dot(query_rows, key_rows.T, preferred_element_type=jnp.float32) * score_scale
    row_max = jnp.max(scores, axis=1)
    shifted = jnp.exp(scores - row_max[:, None])
    row_total = jnp.sum(shifted, axis=1)
    weights = shifted.astype(jnp.bfloat16)
    numerator = jnp.dot(weights, value_rows, preferred_element_type=jnp.float32)
    return (numerator, row_total, row_max)


def attend_local(query_rows, pair_rows):
    return lax.map(
        attend_head,
        (
            query_rows.transpose(1, 0, 2),
            pair_rows[:, 0].transpose(1, 0, 2),
            pair_rows[:, 1].transpose(1, 0, 2),
        ),
    )


def pick_rows(states, offsets, rate):
    row_count, inner_count, heads_here, head_width = states.shape
    picker = (jnp.arange(rate)[:, None] == offsets[None, :]).astype(jnp.bfloat16)
    folded = states.reshape(row_count // rate, rate, inner_count, heads_here, head_width)
    return jnp.einsum("archd,rh->achd", folded, picker, preferred_element_type=jnp.float32).astype(
        jnp.bfloat16
    )


def spread_back(numerator, row_total, row_max, offsets, rate):
    heads_here, picked_count, head_width = numerator.shape
    chosen = jnp.arange(rate)[:, None] == offsets[None, :]
    full_num = jnp.where(chosen[None, :, :, None], numerator.transpose(1, 0, 2)[:, None], 0.0)
    full_total = jnp.where(chosen[None], row_total.T[:, None], 0.0)
    full_max = jnp.where(chosen[None], row_max.T[:, None], -1e30)
    return (
        full_num.reshape(picked_count * rate, heads_here, head_width),
        full_total.reshape(picked_count * rate, heads_here),
        full_max.reshape(picked_count * rate, heads_here),
    )


def doubling(buffer, steps_count):
    position = lax.axis_index("seq")
    for bit_index in range(steps_count):
        partner = partner_2(buffer, "seq", bit_index)
        is_lower = position >> bit_index & 1 == 0
        buffer = jnp.where(
            is_lower, jnp.concatenate([buffer, partner], 0), jnp.concatenate([partner, buffer], 0)
        )
    return buffer


def shards_general(queries, key_states, value_states, offsets_mid, offsets_top, out_weight):
    tok_rows = queries.shape[0]
    heads_local = offsets_mid.shape[0] // lax.axis_size("head")
    head_size = queries.shape[1] // heads_local
    seq_devices = lax.axis_size("seq")
    seq_total = tok_rows * seq_devices
    width_mid = min(16 * SEG, seq_total)
    rate_mid = width_mid // SEG
    rate_top = seq_total // SEG
    start_head = lax.axis_index("head") * heads_local
    mid_local = lax.dynamic_slice(offsets_mid, (start_head,), (heads_local,))
    top_local = lax.dynamic_slice(offsets_top, (start_head,), (heads_local,))
    query_heads = queries.reshape(tok_rows, 1, heads_local, head_size)
    paired = jnp.stack([key_states, value_states], axis=1).reshape(
        tok_rows, 2, heads_local, head_size
    )
    near_bits = (SEG // tok_rows).bit_length() - 1
    near_rows = doubling(paired.reshape(tok_rows, -1), near_bits).reshape(
        SEG, 2, heads_local, head_size
    )
    near_num, near_total, near_max = attend_local(query_heads[:, 0], near_rows)
    level_near = spread_back(
        near_num, near_total, near_max, jnp.zeros((heads_local,), jnp.int32), 1
    )
    mid_q = pick_rows(query_heads, mid_local, rate_mid)[:, 0]
    mid_kv = pick_rows(paired, mid_local, rate_mid)
    mid_group = width_mid // tok_rows
    mid_bits = mid_group.bit_length() - 1
    mid_rows = doubling(mid_kv.reshape(mid_kv.shape[0], -1), mid_bits).reshape(
        SEG, 2, heads_local, head_size
    )
    mid_num, mid_total, mid_max = attend_local(mid_q, mid_rows)
    level_mid = spread_back(mid_num, mid_total, mid_max, mid_local, rate_mid)
    top_q = pick_rows(query_heads, top_local, rate_top)[:, 0]
    top_kv = pick_rows(paired, top_local, rate_top)
    top_rows = lax.all_gather(
        top_kv.reshape(top_kv.shape[0], -1), "seq", axis=0, tiled=True
    ).reshape(SEG, 2, heads_local, head_size)
    top_num, top_total, top_max = attend_local(top_q, top_rows)
    level_top = spread_back(top_num, top_total, top_max, top_local, rate_top)
    levels = [level_near, level_mid, level_top]
    overall = jnp.maximum(jnp.maximum(level_near[2], level_mid[2]), level_top[2])
    numerator = jnp.zeros((tok_rows, heads_local, head_size), jnp.float32)
    row_total = jnp.zeros((tok_rows, heads_local), jnp.float32)
    for level_num, level_total, level_max in levels:
        factor = jnp.exp(level_max - overall)
        numerator = numerator + factor[..., None] * level_num
        row_total = row_total + factor * level_total
    attention = (
        (numerator / row_total[..., None])
        .astype(jnp.bfloat16)
        .reshape(tok_rows, heads_local * head_size)
    )
    result = lax.psum_scatter(
        jnp.dot(attention, out_weight, preferred_element_type=jnp.float32),
        "head",
        scatter_dimension=0,
        tiled=True,
    )
    return result.astype(jnp.bfloat16)


RATE = 4
GROUP = 4
HG = 4
DH = 48
BLK = 128
HALF = 2 * BLK
TOK = 512
SCALE = DH**-0.5 * LOG2E
SAFE = 96.0
CHUNKS = ((0, 4),)
DX = 64


def dot(a, b):
    return jnp.dot(a, b, preferred_element_type=F32)


def dot_nt(a, b):
    return lax.dot_general(a, b, (((1,), (1,)), ((), ())), preferred_element_type=F32)


def class_of_slots(off_mid, off_top):
    first = off_mid
    second = jnp.where(off_top == off_mid, lax.rem(off_mid + 1, RATE), off_top)
    free0 = (first != 0) & (second != 0)
    free1 = (first != 1) & (second != 1)
    third = jnp.where(free0, 0, jnp.where(free1, 1, 2))
    return first, second, third, 6 - first - second - third


def head_of(place, j, p):
    index = place[0][0]
    return ((index & (GROUP - 1)) ^ j) * HG + ((index // GROUP) ^ p)


def offsets_of(place, head):
    return place[1][head], place[2][head]


def token_picker():
    row = lax.broadcasted_iota(jnp.int32, (TOK, TOK), 0)
    col = lax.broadcasted_iota(jnp.int32, (TOK, TOK), 1)
    return (col == RATE * (row % BLK) + row // BLK).astype(BF16)


def fill_class_major(block, picker, scratch):
    scratch[...] = lax.dot_general(
        block, picker, (((0,), (1,)), ((), ())), preferred_element_type=F32
    ).astype(BF16)


def lane_block(index):
    return pl.ds(pl.multiple_of(index * BLK, BLK), BLK)


def head_rows(head):
    return pl.ds(pl.multiple_of(head * DH, 16), DH)


def pack_kernel(index, mid, top, k_hbm, v_hbm, q_hbm, *refs):
    place = (index, mid, top)
    outs, refs = refs[:6], refs[6:]
    blocks, held, packed = refs[:3], refs[3:6], refs[6:12]
    sems_in, sems_out = refs[12:]
    loads = [
        pltpu.make_async_copy(hbm, block, sems_in.at[i])
        for i, (hbm, block) in enumerate(zip((k_hbm, v_hbm, q_hbm), blocks))
    ]
    for load in loads:
        load.start()
    picker = token_picker()
    stores = []
    for n, (load, block, scratch) in enumerate(zip(loads, blocks, held)):
        load.wait()
        fill_class_major(block[...], picker, scratch)
        rows = slice(n * DH, (n + 1) * DH)
        for i, (j, first, count) in enumerate(
            ((0, 0, 4), (1, 0, 4), (2, 0, 2), (3, 0, 2), (2, 2, 2), (3, 2, 2))
        ):
            for p in range(HG):
                head = head_of(place, j, p)
                slots = class_of_slots(*offsets_of(place, head))
                for s in range(count):
                    packed[i][p, rows, s * BLK : (s + 1) * BLK] = scratch[
                        head_rows(head), lane_block(slots[first + s])
                    ]
            store = pltpu.make_async_copy(
                packed[i].at[:, rows], outs[i].at[:, rows], sems_out.at[i, n]
            )
            store.start()
            stores.append(store)
    for store in stores:
        store.wait()


def regroup_kernel(a_ref, b_ref, *refs):
    for s, out in enumerate(refs[-3:]):
        out[0] = a_ref[s + 1, :, 0:HALF]
        out[1] = b_ref[s + 1, :, 0:HALF]


def upright(keys_t):
    return keys_t.T


def largest(blocks):
    best = None
    for block in blocks:
        wide = block.astype(F32)
        length = jnp.sum(wide * wide, axis=0, keepdims=True)
        for low in range(0, block.shape[1], HALF):
            part = length[:, low : low + HALF]
            best = part if best is None else jnp.maximum(best, part)
    return jnp.max(best)


def is_small(query_length, key_length):
    return query_length * key_length * (SCALE * SCALE) < SAFE * SAFE


def column_max(blocks):
    best = jnp.max(blocks[0], axis=0, keepdims=True)
    for block in blocks[1:]:
        best = jnp.maximum(best, jnp.max(block, axis=0, keepdims=True))
    return best * SCALE


def near_kernel(inputs, units, tasks, carried, first, step, index, mid, top, *refs):
    place = (index, mid, top)
    pieces = dict(zip(inputs, refs[: len(inputs)]))
    refs = refs[len(inputs) :]
    old = [refs[2 * i : 2 * i + 2] for i in range(carried)]
    outs = refs[2 * carried : 2 * carried + 2 * len(tasks)]
    k_s, v_s = refs[-2:]
    v_s[:, DH:DX, :] = jnp.ones((step, DX - DH, v_s.shape[2]), BF16)
    lane_slot = lax.broadcasted_iota(jnp.int32, (1, HALF), 1) // BLK

    def lookup(j, slot):
        first = 0 if (j, 0) in pieces and pieces[j, 0].shape[2] > HALF else slot // 2 * 2
        return pieces[j, first], (slot - first) * BLK

    chunks = []
    row = 0
    for label, members in units:
        chunks.append((label, slice(row, row + len(members) * BLK)))
        row += len(members) * BLK
    members = [member for _, group in units for member in group]

    def prepare(h):
        for i, (j, slot) in enumerate(members):
            ref, lane = lookup(j, slot)
            rows = slice(i * BLK, (i + 1) * BLK)
            k_s[h, rows, :] = upright(ref[h, 0:DH, lane : lane + BLK])
            v_s[h, 0:DH, rows] = ref[h, DH : 2 * DH, lane : lane + BLK]

    def counted_again(h):
        off_mid, off_top = offsets_of(place, head_of(place, 0, first + pl.program_id(0) * step + h))
        same = off_mid == off_top
        return [
            jnp.where(lane_slot == 0, jnp.where(same, 1.584962500721156, 1.0), 0.0),
            jnp.where(lane_slot == 1, jnp.where(same, 0.0, 1.0), 0.0),
        ]

    def run(plain, heads):
        again = [counted_again(h) for h in heads]
        flat = [
            (h, again_h, query, low, merge, out, i)
            for h, again_h in zip(heads, again)
            for out, group in enumerate(tasks)
            for i, (query, low, merge) in enumerate(group)
        ]

        def score(task):
            h, _, (j, half), low = task[:4]
            ref, lane = lookup(j, 2 * half)
            query = ref[h, 2 * DH :, lane : lane + HALF]
            return [dot(k_s[h, rows, :], query) for _, rows in chunks[low:]]

        scores = score(flat[0])
        for n, (h, again_h, (_, half), low, merge, out, i) in enumerate(flat):
            following = score(flat[n + 1]) if n + 1 < len(flat) else None
            best = jnp.zeros((1, HALF), F32) if plain else column_max(scores)
            if merge is not None:
                acc_in, max_in = old[merge[0]]
                old_max = max_in[h, merge[1], 0:1, :]
                best = best if plain else jnp.maximum(best, old_max)
            acc = None
            for (label, rows), block in zip(chunks[low:], scores):
                block = block * SCALE
                if half == 0 and label is not None:
                    block = block - (best - again_h[label])
                elif not plain:
                    block = block - best
                part = dot(v_s[h, :, rows], jnp.exp2(block).astype(BF16))
                acc = part if acc is None else acc + part
            if merge is not None:
                before = acc_in[h, merge[1]]
                acc = acc + (before if plain else before * jnp.exp2(old_max - best))
            acc_ref, max_ref = outs[2 * out : 2 * out + 2]
            acc_ref[h, i] = acc
            max_ref[h, i] = jnp.broadcast_to(best, (8, HALF))
            scores = following

    for h in range(step):
        prepare(h)
    plain = is_small(
        largest([ref[h, 2 * DH :, :] for ref in pieces.values() for h in range(step)]),
        largest([ref[h, 0:DH, :] for ref in pieces.values() for h in range(step)]),
    )
    for _, max_in in old:
        plain = plain & (jnp.max(jnp.abs(max_in[...])) == 0.0)

    @pl.when(plain)
    def _():
        run(True, list(range(step)))

    @pl.when(jnp.logical_not(plain))
    def _():
        @pl.loop(0, step)
        def _(h):
            run(False, [h])


def far_slots(place):
    off_mid, off_top = offsets_of(place, head_of(place, 0, 0))
    same = off_mid == off_top
    return same, (0, jnp.where(same, 0, 1))


def far_pieces(place, sources, k_s, v_s, q_s):
    _, slots = far_slots(place)
    for s, pair in enumerate(sources):
        for i, ref in enumerate(pair):
            here = slice(i * BLK, (i + 1) * BLK)
            for level, slot in enumerate(slots):
                k_s[level, s, here, :] = upright(ref[0:DH, lane_block(slot)])
                v_s[level, s, 0:DH, here] = ref[DH : 2 * DH, lane_block(slot)]
                q_s[level, s, :, here] = ref[2 * DH : 3 * DH, lane_block(slot)]
    v_s[:, :, DH:DX, :] = jnp.ones((2, RATE, DX - DH, HALF), BF16)


def far_lengths(sources):
    every = [ref for pair in sources for ref in pair]
    return (
        largest([ref[2 * DH : 3 * DH, 0:HALF] for ref in every]),
        largest([ref[0:DH, 0:HALF] for ref in every]),
    )


def far_own_kernel(index, mid, top, own0, own1, beyond1, beyond2, beyond3, *refs):
    k_s, v_s, q_s, acc_ref, max_ref, length_ref = refs
    sources = [(own0.at[0], own1.at[0])] + [
        (ref.at[0], ref.at[1]) for ref in (beyond1, beyond2, beyond3)
    ]
    far_pieces((index, mid, top), sources, k_s, v_s, q_s)

    def run(plain):
        def segment(s, carry):
            def score(level):
                return [dot(k_s[level, s ^ d], q_s[level, s]) for d in range(1, RATE)]

            scores = score(0)
            for level in range(2):
                following = score(1) if level == 0 else None
                best = jnp.zeros((1, HALF), F32) if plain else column_max(scores)
                acc = None
                for d in range(1, RATE):
                    block = scores[d - 1] * SCALE
                    block = block if plain else block - best
                    part = dot(v_s[level, s ^ d], jnp.exp2(block).astype(BF16))
                    acc = part if acc is None else acc + part
                acc_ref[level, s] = acc
                max_ref[level, s] = jnp.broadcast_to(best, (8, HALF))
                scores = following
            return carry

        lax.fori_loop(0, RATE, segment, 0, unroll=2 if plain else 1)

    query_length, key_length = far_lengths(sources)
    length_ref[0] = query_length
    length_ref[1] = key_length
    plain = is_small(query_length, key_length)
    pl.when(plain)(lambda: run(True))
    pl.when(jnp.logical_not(plain))(lambda: run(False))


def far_kernel(index, mid, top, *refs):
    place = (index, mid, top)
    sel2, sel3, beyond3, beyond2, beyond1, k_own, v_own, q_own, acc_in, max_in, length_in = refs[
        :11
    ]
    outs = refs[11 : 11 + RATE]
    k_s, v_s, q_s, result_s, tail_s = refs[11 + RATE :]
    same, _ = far_slots(place)
    sources = [(sel2.at[0], sel3.at[0])] + [
        (ref.at[0], ref.at[1]) for ref in (beyond1, beyond2, beyond3)
    ]
    far_pieces(place, sources, k_s, v_s, q_s)
    tail_s[...] = jnp.zeros(tail_s.shape, F32)

    def run(plain):
        tasks = [(level, chip) for level in range(2) for chip in range(2)]
        held = ((k_own, v_own, q_own), (k_s, v_s, q_s))

        def segment(s, carry):
            def blocks(chip):
                return [(held[c], s ^ d) for d in range(1, RATE) for c in ((1,), (0, 1))[chip]]

            def score(task):
                level, chip = task
                query = held[chip][2][level, s]
                return [dot(keys[0][level, b], query) for keys, b in blocks(chip)]

            scores = score(tasks[0])
            for n, (level, chip) in enumerate(tasks):
                following = score(tasks[n + 1]) if n + 1 < len(tasks) else None
                best = jnp.zeros((1, HALF), F32) if plain else column_max(scores)
                acc = None
                if chip == 0:
                    acc = acc_in[level, s]
                    if not plain:
                        old_max = max_in[level, s, 0:1, :]
                        best = jnp.maximum(best, old_max)
                        acc = acc * jnp.exp2(old_max - best)
                for block, (keys, b) in zip(scores, blocks(chip)):
                    block = block * SCALE if plain else block * SCALE - best
                    part = dot(keys[1][level, b], jnp.exp2(block).astype(BF16))
                    acc = part if acc is None else acc + part
                total = acc[DH : DH + 1, :]
                result = (acc[0:DH, :] / total).astype(BF16)
                lse = best + jnp.log2(total)
                if level == 0:
                    lse = jnp.where(same, lse + 1.0, lse)
                else:
                    lse = jnp.where(same, -1e30, lse)
                high = lse.astype(BF16).astype(F32)
                middle = (lse - high).astype(BF16).astype(F32)
                low = lse - high - middle
                for i in range(2):
                    n = 2 * (2 * chip + i) + level
                    mine = slice(i * BLK, (i + 1) * BLK)
                    result_s[s, :, n * BLK : (n + 1) * BLK] = result[:, mine]
                    for k, part in enumerate((high, middle, low)):
                        tail_s[s, 3 * n + k : 3 * n + k + 1, :] = part[:, mine]
                scores = following
            return carry

        lax.fori_loop(0, RATE, segment, 0, unroll=2 if plain else 1)

    query_length, key_length = far_lengths(sources)
    plain = is_small(
        jnp.maximum(query_length, length_in[0]), jnp.maximum(key_length, length_in[1])
    )
    pl.when(plain)(lambda: run(True))
    pl.when(jnp.logical_not(plain))(lambda: run(False))
    for s in range(RATE):
        outs[s][:, : GROUP * HALF] = result_s[s]
        outs[s][:, GROUP * HALF :] = tail_s[s].astype(BF16)


def join(acc, best, far, j):
    tail = far[:, GROUP * HALF :].astype(F32)
    lse = jnp.concatenate(
        [
            tail[3 * n : 3 * n + 1] + tail[3 * n + 1 : 3 * n + 2] + tail[3 * n + 2 : 3 * n + 3]
            for n in (2 * j, 2 * j + 1)
        ],
        axis=1,
    )
    overall = jnp.maximum(best, lse)
    near_factor, far_factor = jnp.exp2(best - overall), jnp.exp2(lse - overall)
    total = acc[DH : DH + 1] * near_factor + far_factor
    value = far[:, j * HALF : (j + 1) * HALF].astype(F32) * far_factor
    return ((acc[0:DH] * near_factor + value) / total).astype(BF16)


def combine_kernel(chip, acc_ref, max_ref, *refs):
    far, outs = refs[:-2][::-1], refs[-2:]
    for i in range(2):
        for p, results in enumerate(far):
            outs[i][p, :, 0:HALF] = join(
                acc_ref[p, 2 * i], max_ref[p, 2 * i, 0:1, :], results, 2 * chip + i
            )
            acc = acc_ref[p, 2 * i + 1]
            outs[i][p, :, HALF:] = (acc[0:DH] / acc[DH : DH + 1]).astype(BF16)


def project_kernel(sources, index, mid, top, *refs):
    place = (index, mid, top)
    parts, (w_ref, out_ref, held) = refs[:-3], refs[-3:]
    for (j, first), part in zip(sources, parts):
        for p in range(part.shape[0]):
            head = head_of(place, j, first + p)
            slots = class_of_slots(*offsets_of(place, head))
            for s in range(RATE):
                held[head_rows(head), lane_block(slots[s])] = part[
                    p, :, s * BLK : (s + 1) * BLK
                ]
    row = lax.broadcasted_iota(jnp.int32, (TOK, TOK), 0)
    col = lax.broadcasted_iota(jnp.int32, (TOK, TOK), 1)
    picker = (row == RATE * (col % BLK) + col // BLK).astype(BF16)
    attention = dot_nt(picker, held[...]).astype(BF16)
    out_ref[...] = dot(attention, w_ref[...]).astype(BF16)


def whole(shape):
    return pl.BlockSpec(shape, lambda *_: (0,) * len(shape))


def per_head(shape, skip=0):
    return pl.BlockSpec(shape, lambda h, *_: (h + skip,) + (0,) * (len(shape) - 1))


def call(
    kernel, scalars, args, grid, in_specs, outs, scratch, scores,
    limit=VMEM_LIMIT, after=(), through=(),
):
    known = len(scalars) + len(args)
    extra = (*after, *through)
    count = len(outs)
    anywhere = pl.BlockSpec(memory_space=pl.ANY)

    def body(*refs):
        results = refs[known + len(extra) :]
        kernel(*refs[:known], *results[:count], *results[count + len(through) :])

    return pl.pallas_call(
        body if extra else kernel,
        grid_spec=pltpu.PrefetchScalarGridSpec(
            num_scalar_prefetch=len(scalars),
            grid=grid,
            in_specs=list(in_specs) + [anywhere] * len(extra),
            out_specs=[spec for spec, _ in outs] + [anywhere] * len(through),
            scratch_shapes=scratch,
        ),
        out_shape=[shape for _, shape in outs]
        + [jax.ShapeDtypeStruct(x.shape, x.dtype) for x in through],
        input_output_aliases={known + len(after) + i: count + i for i in range(len(through))},
        compiler_params=pltpu.CompilerParams(vmem_limit_bytes=limit),
        cost_estimate=pl.CostEstimate(flops=0, bytes_accessed=0, transcendentals=0),
    )(*scalars, *args, *extra)


def handed_on(arrays):
    return call(lambda: None, (), (), (1,), [], [], [], 0, through=tuple(arrays))


def within(array, apart):
    count = lax.axis_size("seq")
    return lax.ppermute(array, "seq", [(i, i ^ apart) for i in range(count)])


def swap_segments(arrays):
    moved = {s: within(arrays[s - 1], GROUP * s) for s in (3, 2, 1)}
    return [moved[s] for s in (1, 2, 3)]


def shards_four(queries, key_states, value_states, offsets_mid, offsets_top, out_weight):
    width = queries.shape[1]
    place = (lax.axis_index("seq").astype(jnp.int32).reshape(1), offsets_mid, offsets_top)
    full = jax.ShapeDtypeStruct((HG, 3 * DH, TOK), BF16)
    piece = jax.ShapeDtypeStruct((HG, 3 * DH, HALF), BF16)
    pair = jax.ShapeDtypeStruct((2, 3 * DH, HALF), BF16)
    anywhere = pl.BlockSpec(memory_space=pl.ANY)
    shapes = [full] * 2 + [piece] * 4
    own0, own1, sel2, sel3, rest2, rest3 = call(
        pack_kernel, place, (key_states, value_states, queries), (1,),
        [anywhere] * 3,
        [(anywhere, shape) for shape in shapes],
        [pltpu.VMEM((TOK, width), BF16)] * 3
        + [pltpu.VMEM((width, TOK), BF16)] * 3
        + [pltpu.VMEM(shape.shape, BF16) for shape in shapes]
        + [pltpu.SemaphoreType.DMA((3,)), pltpu.SemaphoreType.DMA((6, 3))],
        1 << 19, VMEM_MOST,
    )
    own1 = within(own1, 1)
    sel2, sel3 = within(sel2, 2), within(sel3, 3)

    def regroup(a, b, **order):
        return call(
            regroup_kernel, (), (a, b), (1,),
            [whole(a.shape), whole(b.shape)], [(whole(pair.shape), pair)] * 3,
            [], 1 << 17, **order,
        )

    def near(held, units, tasks, old, first=0, heads=HG, step=2, **order):
        sizes = [len(members) * BLK for _, members in units]
        scores = sum(sum(sizes[low:]) * HALF for group in tasks for _, low, _ in group)
        arrays = [*held.values(), *[x for one in old for x in one]]
        shapes = [
            jax.ShapeDtypeStruct((heads, len(group), rows, HALF), F32)
            for group in tasks
            for rows in (DX, 8)
        ]
        return call(
            functools.partial(near_kernel, list(held), units, tasks, len(old), first, step),
            place, arrays, (heads // step,),
            [per_head((step,) + x.shape[1:], first // step) for x in arrays],
            [(per_head((step,) + x.shape[1:]), x) for x in shapes],
            [
                pltpu.VMEM((step, sum(sizes), DH), BF16),
                pltpu.VMEM((step, DX, sum(sizes)), BF16),
            ],
            heads * scores, **order,
        )

    def units_of(a, b):
        return [(0, [(a, 0), (b, 0)]), (1, [(a, 1), (b, 1)])], [
            (None, [(a, 2), (a, 3), (b, 2), (b, 3)])
        ]

    own_sel, own_rest = units_of(0, 1)
    other_sel, other_rest = units_of(2, 3)
    own = [(0, 0), (0, 1), (1, 0), (1, 1)]

    ours = regroup(own0, own1)
    ours = swap_segments(ours)
    held = {(0, 0): own0, (1, 0): own1}
    state_own = near(held, own_sel + own_rest, [[(q, 0, None) for q in own]], [])
    *theirs, rest2, rest3 = regroup(sel2, sel3, after=state_own[1:], through=(rest2, rest3))
    theirs = swap_segments(theirs)
    rest2, rest3 = within(rest2, 2), within(rest3, 3)

    held.update({(2, 0): sel2, (3, 0): sel3})
    out = near(
        held, own_sel + own_rest + other_sel,
        [
            [(q, 3, (0, i)) for i, q in enumerate(own)],
            [((2, 0), 0, None), ((3, 0), 0, None)],
        ],
        [state_own],
        after=ours[::-1],
    )
    state_own, state_sel = out[:2], out[2:]

    result = jax.ShapeDtypeStruct((DH, GROUP * HALF + BLK), BF16)
    piece_0 = pl.BlockSpec((1, 3 * DH, HALF), lambda *_: (0, 0, 0))
    pieces_shapes = [
        jax.ShapeDtypeStruct((2, RATE, HALF, DH), BF16),
        jax.ShapeDtypeStruct((2, RATE, DX, HALF), BF16),
        jax.ShapeDtypeStruct((2, RATE, DH, HALF), BF16),
    ]
    sums_shapes = [
        jax.ShapeDtypeStruct((2, RATE, DX, HALF), F32),
        jax.ShapeDtypeStruct((2, RATE, 8, HALF), F32),
    ]
    in_scalars = pl.BlockSpec(memory_space=pltpu.SMEM)
    far_own = call(
        far_own_kernel, place, (own0, own1, *ours), (1,),
        [piece_0] * 2 + [whole(pair.shape)] * 3,
        [(whole(x.shape), x) for x in pieces_shapes + sums_shapes]
        + [(in_scalars, jax.ShapeDtypeStruct((2,), F32))],
        [], RATE * 2 * 3 * HALF * HALF, after=(state_sel[1],),
    )
    results = call(
        far_kernel, place, (sel2, sel3, *theirs[::-1], *far_own), (1,),
        [piece_0] * 2 + [whole(pair.shape)] * 3
        + [whole(x.shape) for x in far_own[:-1]] + [in_scalars],
        [(whole(result.shape), result)] * RATE,
        [pltpu.VMEM(x.shape, BF16) for x in pieces_shapes]
        + [
            pltpu.VMEM((RATE, DH, GROUP * HALF), BF16),
            pltpu.VMEM((RATE, DH, BLK), F32),
        ],
        RATE * 2 * 3 * 3 * HALF * HALF,
    )
    back = [results[0]] + swap_segments(results[1:])

    held.update({(2, 2): rest2, (3, 2): rest3})
    units = own_sel + own_rest + other_sel + other_rest

    def combine(chip, state, far, **order):
        heads = state[0].shape[0]
        attended = jax.ShapeDtypeStruct((heads, DH, TOK), BF16)
        return call(
            functools.partial(combine_kernel, chip), (), (*state, *far[::-1]), (1,),
            [whole(x.shape) for x in state] + [whole(result.shape)] * heads,
            [(whole(attended.shape), attended)] * 2,
            [],
            1 << 18, **order,
        )

    parts = {}
    last = results[0]
    for first, heads in CHUNKS:
        state_other = near(
            held, units,
            [
                [
                    ((2, 0), 5, (0, 0)), ((2, 1), 0, None),
                    ((3, 0), 5, (0, 1)), ((3, 1), 0, None),
                ]
            ],
            [state_sel],
            first, heads, 2, after=(last,),
        )
        part2, part3 = combine(1, state_other, back[first : first + heads])
        parts[2, first], parts[3, first] = within(part2, 2), within(part3, 3)
        last = part3
    state_own = near(
        {(2, 2): rest2, (3, 2): rest3, **{q: held[q] for q in ((0, 0), (1, 0))}},
        other_rest,
        [[(q, 0, (0, i)) for i, q in enumerate(own)]],
        [state_own],
        after=(last,),
    )
    early = [parts[j, first] for first, _ in CHUNKS[:-1] for j in (2, 3)]
    part0, part1 = combine(0, state_own, back, after=early)
    parts = dict(zip(parts, handed_on(parts.values())))
    parts[0, 0], parts[1, 0] = part0, within(part1, 1)
    return call(
        functools.partial(project_kernel, list(parts)), place, (*parts.values(), out_weight), (1,),
        [whole(x.shape) for x in parts.values()] + [whole((width, width))],
        [(whole((TOK, width)), jax.ShapeDtypeStruct((TOK, width), BF16))],
        [pltpu.VMEM((width, TOK), BF16)],
        1 << 18,
    )[0]


def shards(queries, key_states, value_states, offsets_mid, offsets_top, out_weight):
    tokens, width = queries.shape
    heads = offsets_mid.shape[0]
    fits = (
        lax.axis_size("head") == 1
        and lax.axis_size("seq") == GROUP * RATE
        and tokens == TOK
        and heads == GROUP * HG
        and width == heads * DH
    )
    run = shards_four if fits else shards_general
    return run(queries, key_states, value_states, offsets_mid, offsets_top, out_weight)


def solution(mesh):
    in_specs = (
        P(("slide", "seq"), "head"),
        P(("slide", "seq"), "head"),
        P(("slide", "seq"), "head"),
        P(),
        P(),
        P("head", None),
    )
    out_specs = P(("slide", "seq", "head"), None)
    return jax.shard_map(shards, mesh=mesh, in_specs=in_specs, out_specs=out_specs, check_vma=False)
```

```python
import functools

import jax
import jax.numpy as jnp
from jax import lax
from jax.experimental import pallas as pl
from jax.experimental.pallas import tpu as pltpu
from jax.sharding import PartitionSpec as P

SEG = 2048
LOG2E = 1.4426950408889634
VMEM_LIMIT = 40 * 1024 * 1024
VMEM_MOST = 60 * 1024 * 1024
BF16 = jnp.bfloat16
F32 = jnp.float32


def partner_2(block, axis, apart):
    count = lax.axis_size(axis)
    route = []
    for low in range(count):
        high = low | 1 << apart
        if high != low and high < count:
            route += [(low, high), (high, low)]
    return lax.ppermute(block, axis, route)


def attend_head(triple_in):
    query_rows, key_rows, value_rows = triple_in
    score_scale = query_rows.shape[-1] ** (-0.5)
    scores = jnp.dot(query_rows, key_rows.T, preferred_element_type=jnp.float32) * score_scale
    row_max = jnp.max(scores, axis=1)
    shifted = jnp.exp(scores - row_max[:, None])
    row_total = jnp.sum(shifted, axis=1)
    weights = shifted.astype(jnp.bfloat16)
    numerator = jnp.dot(weights, value_rows, preferred_element_type=jnp.float32)
    return (numerator, row_total, row_max)


def attend_local(query_rows, pair_rows):
    return lax.map(
        attend_head,
        (
            query_rows.transpose(1, 0, 2),
            pair_rows[:, 0].transpose(1, 0, 2),
            pair_rows[:, 1].transpose(1, 0, 2),
        ),
    )


def pick_rows(states, offsets, rate):
    row_count, inner_count, heads_here, head_width = states.shape
    picker = (jnp.arange(rate)[:, None] == offsets[None, :]).astype(jnp.bfloat16)
    folded = states.reshape(row_count // rate, rate, inner_count, heads_here, head_width)
    return jnp.einsum("archd,rh->achd", folded, picker, preferred_element_type=jnp.float32).astype(
        jnp.bfloat16
    )


def spread_back(numerator, row_total, row_max, offsets, rate):
    heads_here, picked_count, head_width = numerator.shape
    chosen = jnp.arange(rate)[:, None] == offsets[None, :]
    full_num = jnp.where(chosen[None, :, :, None], numerator.transpose(1, 0, 2)[:, None], 0.0)
    full_total = jnp.where(chosen[None], row_total.T[:, None], 0.0)
    full_max = jnp.where(chosen[None], row_max.T[:, None], -1e30)
    return (
        full_num.reshape(picked_count * rate, heads_here, head_width),
        full_total.reshape(picked_count * rate, heads_here),
        full_max.reshape(picked_count * rate, heads_here),
    )


def doubling(buffer, steps_count):
    position = lax.axis_index("seq")
    for bit_index in range(steps_count):
        partner = partner_2(buffer, "seq", bit_index)
        is_lower = position >> bit_index & 1 == 0
        buffer = jnp.where(
            is_lower, jnp.concatenate([buffer, partner], 0), jnp.concatenate([partner, buffer], 0)
        )
    return buffer


def shards_general(queries, key_states, value_states, offsets_mid, offsets_top, out_weight):
    tok_rows = queries.shape[0]
    heads_local = offsets_mid.shape[0] // lax.axis_size("head")
    head_size = queries.shape[1] // heads_local
    seq_devices = lax.axis_size("seq")
    seq_total = tok_rows * seq_devices
    width_mid = min(16 * SEG, seq_total)
    rate_mid = width_mid // SEG
    rate_top = seq_total // SEG
    start_head = lax.axis_index("head") * heads_local
    mid_local = lax.dynamic_slice(offsets_mid, (start_head,), (heads_local,))
    top_local = lax.dynamic_slice(offsets_top, (start_head,), (heads_local,))
    query_heads = queries.reshape(tok_rows, 1, heads_local, head_size)
    paired = jnp.stack([key_states, value_states], axis=1).reshape(
        tok_rows, 2, heads_local, head_size
    )
    near_bits = (SEG // tok_rows).bit_length() - 1
    near_rows = doubling(paired.reshape(tok_rows, -1), near_bits).reshape(
        SEG, 2, heads_local, head_size
    )
    near_num, near_total, near_max = attend_local(query_heads[:, 0], near_rows)
    level_near = spread_back(
        near_num, near_total, near_max, jnp.zeros((heads_local,), jnp.int32), 1
    )
    mid_q = pick_rows(query_heads, mid_local, rate_mid)[:, 0]
    mid_kv = pick_rows(paired, mid_local, rate_mid)
    mid_group = width_mid // tok_rows
    mid_bits = mid_group.bit_length() - 1
    mid_rows = doubling(mid_kv.reshape(mid_kv.shape[0], -1), mid_bits).reshape(
        SEG, 2, heads_local, head_size
    )
    mid_num, mid_total, mid_max = attend_local(mid_q, mid_rows)
    level_mid = spread_back(mid_num, mid_total, mid_max, mid_local, rate_mid)
    top_q = pick_rows(query_heads, top_local, rate_top)[:, 0]
    top_kv = pick_rows(paired, top_local, rate_top)
    top_rows = lax.all_gather(
        top_kv.reshape(top_kv.shape[0], -1), "seq", axis=0, tiled=True
    ).reshape(SEG, 2, heads_local, head_size)
    top_num, top_total, top_max = attend_local(top_q, top_rows)
    level_top = spread_back(top_num, top_total, top_max, top_local, rate_top)
    levels = [level_near, level_mid, level_top]
    overall = jnp.maximum(jnp.maximum(level_near[2], level_mid[2]), level_top[2])
    numerator = jnp.zeros((tok_rows, heads_local, head_size), jnp.float32)
    row_total = jnp.zeros((tok_rows, heads_local), jnp.float32)
    for level_num, level_total, level_max in levels:
        factor = jnp.exp(level_max - overall)
        numerator = numerator + factor[..., None] * level_num
        row_total = row_total + factor * level_total
    attention = (
        (numerator / row_total[..., None])
        .astype(jnp.bfloat16)
        .reshape(tok_rows, heads_local * head_size)
    )
    result = lax.psum_scatter(
        jnp.dot(attention, out_weight, preferred_element_type=jnp.float32),
        "head",
        scatter_dimension=0,
        tiled=True,
    )
    return result.astype(jnp.bfloat16)


RATE = 4
GROUP = 4
HG = 4
DH = 48
BLK = 128
HALF = 2 * BLK
TOK = 512
SCALE = DH**-0.5 * LOG2E
SAFE = 96.0
CHUNKS = ((0, 4),)
DX = 64


def dot(a, b):
    return jnp.dot(a, b, preferred_element_type=F32)


def dot_nt(a, b):
    return lax.dot_general(a, b, (((1,), (1,)), ((), ())), preferred_element_type=F32)


def class_of_slots(off_mid, off_top):
    first = off_mid
    second = jnp.where(off_top == off_mid, lax.rem(off_mid + 1, RATE), off_top)
    free0 = (first != 0) & (second != 0)
    free1 = (first != 1) & (second != 1)
    third = jnp.where(free0, 0, jnp.where(free1, 1, 2))
    return first, second, third, 6 - first - second - third


def head_of(place, j, p):
    index = place[0][0]
    return ((index & (GROUP - 1)) ^ j) * HG + ((index // GROUP) ^ p)


def offsets_of(place, head):
    return place[1][head], place[2][head]


def token_picker():
    row = lax.broadcasted_iota(jnp.int32, (TOK, TOK), 0)
    col = lax.broadcasted_iota(jnp.int32, (TOK, TOK), 1)
    return (col == RATE * (row % BLK) + row // BLK).astype(BF16)


def fill_class_major(block, picker, scratch):
    scratch[...] = lax.dot_general(
        block, picker, (((0,), (1,)), ((), ())), preferred_element_type=F32
    ).astype(BF16)


def lane_block(index):
    return pl.ds(pl.multiple_of(index * BLK, BLK), BLK)


def head_rows(head):
    return pl.ds(pl.multiple_of(head * DH, 16), DH)


def pack_kernel(index, mid, top, k_hbm, v_hbm, q_hbm, *refs):
    place = (index, mid, top)
    outs, refs = refs[:6], refs[6:]
    blocks, held, packed = refs[:3], refs[3:6], refs[6:12]
    sems_in, sems_out = refs[12:]
    loads = [
        pltpu.make_async_copy(hbm, block, sems_in.at[i])
        for i, (hbm, block) in enumerate(zip((k_hbm, v_hbm, q_hbm), blocks))
    ]
    for load in loads:
        load.start()
    picker = token_picker()
    stores = []
    for n, (load, block, scratch) in enumerate(zip(loads, blocks, held)):
        load.wait()
        fill_class_major(block[...], picker, scratch)
        rows = slice(n * DH, (n + 1) * DH)
        for i, (j, first, count) in enumerate(
            ((0, 0, 4), (1, 0, 4), (2, 0, 2), (3, 0, 2), (2, 2, 2), (3, 2, 2))
        ):
            for p in range(HG):
                head = head_of(place, j, p)
                slots = class_of_slots(*offsets_of(place, head))
                for s in range(count):
                    packed[i][p, rows, s * BLK : (s + 1) * BLK] = scratch[
                        head_rows(head), lane_block(slots[first + s])
                    ]
            store = pltpu.make_async_copy(
                packed[i].at[:, rows], outs[i].at[:, rows], sems_out.at[i, n]
            )
            store.start()
            stores.append(store)
    for store in stores:
        store.wait()


def regroup_kernel(a_ref, b_ref, *refs):
    for s, out in enumerate(refs[-3:]):
        out[0] = a_ref[s + 1, :, 0:HALF]
        out[1] = b_ref[s + 1, :, 0:HALF]


def upright(keys_t):
    return keys_t.T


def largest(blocks):
    best = None
    for block in blocks:
        wide = block.astype(F32)
        length = jnp.sum(wide * wide, axis=0, keepdims=True)
        for low in range(0, block.shape[1], HALF):
            part = length[:, low : low + HALF]
            best = part if best is None else jnp.maximum(best, part)
    return jnp.max(best)


def is_small(query_length, key_length):
    return query_length * key_length * (SCALE * SCALE) < SAFE * SAFE


def column_max(blocks):
    best = jnp.max(blocks[0], axis=0, keepdims=True)
    for block in blocks[1:]:
        best = jnp.maximum(best, jnp.max(block, axis=0, keepdims=True))
    return best * SCALE


def near_kernel(inputs, units, tasks, carried, first, step, index, mid, top, *refs):
    place = (index, mid, top)
    pieces = dict(zip(inputs, refs[: len(inputs)]))
    refs = refs[len(inputs) :]
    old = [refs[2 * i : 2 * i + 2] for i in range(carried)]
    outs = refs[2 * carried : 2 * carried + 2 * len(tasks)]
    k_s, v_s = refs[-2:]
    v_s[:, DH:DX, :] = jnp.ones((step, DX - DH, v_s.shape[2]), BF16)
    lane_slot = lax.broadcasted_iota(jnp.int32, (1, HALF), 1) // BLK

    def lookup(j, slot):
        first = 0 if (j, 0) in pieces and pieces[j, 0].shape[2] > HALF else slot // 2 * 2
        return pieces[j, first], (slot - first) * BLK

    chunks = []
    row = 0
    for label, members in units:
        chunks.append((label, slice(row, row + len(members) * BLK)))
        row += len(members) * BLK
    members = [member for _, group in units for member in group]

    def prepare(h):
        for i, (j, slot) in enumerate(members):
            ref, lane = lookup(j, slot)
            rows = slice(i * BLK, (i + 1) * BLK)
            k_s[h, rows, :] = upright(ref[h, 0:DH, lane : lane + BLK])
            v_s[h, 0:DH, rows] = ref[h, DH : 2 * DH, lane : lane + BLK]

    def counted_again(h):
        off_mid, off_top = offsets_of(place, head_of(place, 0, first + pl.program_id(0) * step + h))
        same = off_mid == off_top
        return [
            jnp.where(lane_slot == 0, jnp.where(same, 1.584962500721156, 1.0), 0.0),
            jnp.where(lane_slot == 1, jnp.where(same, 0.0, 1.0), 0.0),
        ]

    def run(heads):
        again = [counted_again(h) for h in heads]
        flat = [
            (h, again_h, query, low, merge, out, i)
            for h, again_h in zip(heads, again)
            for out, group in enumerate(tasks)
            for i, (query, low, merge) in enumerate(group)
        ]

        def score(task):
            h, _, (j, half), low = task[:4]
            ref, lane = lookup(j, 2 * half)
            query = ref[h, 2 * DH :, lane : lane + HALF]
            return [dot(k_s[h, rows, :], query) for _, rows in chunks[low:]]

        scores = score(flat[0])
        for n, (h, again_h, (_, half), low, merge, out, i) in enumerate(flat):
            following = score(flat[n + 1]) if n + 1 < len(flat) else None
            best = column_max(scores)
            if merge is not None:
                acc_in, max_in = old[merge[0]]
                old_max = max_in[h, merge[1], 0:1, :]
                best = jnp.maximum(best, old_max)
            acc = None
            for (label, rows), block in zip(chunks[low:], scores):
                block = block * SCALE
                if half == 0 and label is not None:
                    block = block - (best - again_h[label])
                else:
                    block = block - best
                part = dot(v_s[h, :, rows], jnp.exp2(block).astype(BF16))
                acc = part if acc is None else acc + part
            if merge is not None:
                acc = acc + acc_in[h, merge[1]] * jnp.exp2(old_max - best)
            acc_ref, max_ref = outs[2 * out : 2 * out + 2]
            acc_ref[h, i] = acc
            max_ref[h, i] = jnp.broadcast_to(best, (8, HALF))
            scores = following

    def run_plain():
        again = [counted_again(h) for h in range(step)]
        steps = [
            (h, query, merge, out, i, c, c == low, c == len(chunks) - 1)
            for h in range(step)
            for out, group in enumerate(tasks)
            for i, (query, low, merge) in enumerate(group)
            for c in range(low, len(chunks))
        ]

        def score(item):
            h, (j, half), c = item[0], item[1], item[5]
            ref, lane = lookup(j, 2 * half)
            return dot(k_s[h, chunks[c][1], :], ref[h, 2 * DH :, lane : lane + HALF])

        block = score(steps[0])
        acc = None
        for n, (h, (_, half), merge, out, i, c, begins, ends) in enumerate(steps):
            following = score(steps[n + 1]) if n + 1 < len(steps) else None
            label, rows = chunks[c]
            block = block * SCALE
            if half == 0 and label is not None:
                block = block + again[h][label]
            part = dot(v_s[h, :, rows], jnp.exp2(block).astype(BF16))
            acc = part if begins else acc + part
            if ends:
                if merge is not None:
                    acc = acc + old[merge[0]][0][h, merge[1]]
                acc_ref, max_ref = outs[2 * out : 2 * out + 2]
                acc_ref[h, i] = acc
                max_ref[h, i] = jnp.zeros((8, HALF), F32)
            block = following

    for h in range(step):
        prepare(h)
    plain = is_small(
        largest([ref[h, 2 * DH :, :] for ref in pieces.values() for h in range(step)]),
        largest([ref[h, 0:DH, :] for ref in pieces.values() for h in range(step)]),
    )
    for _, max_in in old:
        plain = plain & (jnp.max(jnp.abs(max_in[...])) == 0.0)

    @pl.when(plain)
    def _():
        run_plain()

    @pl.when(jnp.logical_not(plain))
    def _():
        @pl.loop(0, step)
        def _(h):
            run([h])


def far_slots(place):
    off_mid, off_top = offsets_of(place, head_of(place, 0, 0))
    same = off_mid == off_top
    return same, (0, jnp.where(same, 0, 1))


def far_pieces(place, sources, k_s, v_s, q_s):
    _, slots = far_slots(place)
    for s, pair in enumerate(sources):
        for i, ref in enumerate(pair):
            here = slice(i * BLK, (i + 1) * BLK)
            for level, slot in enumerate(slots):
                k_s[level, s, here, :] = upright(ref[0:DH, lane_block(slot)])
                v_s[level, s, 0:DH, here] = ref[DH : 2 * DH, lane_block(slot)]
                q_s[level, s, :, here] = ref[2 * DH : 3 * DH, lane_block(slot)]
    v_s[:, :, DH:DX, :] = jnp.ones((2, RATE, DX - DH, HALF), BF16)


def far_lengths(sources):
    every = [ref for pair in sources for ref in pair]
    return (
        largest([ref[2 * DH : 3 * DH, 0:HALF] for ref in every]),
        largest([ref[0:DH, 0:HALF] for ref in every]),
    )


def far_own_kernel(index, mid, top, own0, own1, beyond1, beyond2, beyond3, *refs):
    k_s, v_s, q_s, acc_ref, max_ref, length_ref = refs
    sources = [(own0.at[0], own1.at[0])] + [
        (ref.at[0], ref.at[1]) for ref in (beyond1, beyond2, beyond3)
    ]
    far_pieces((index, mid, top), sources, k_s, v_s, q_s)

    def run_plain():
        steps = [(level, d) for level in range(2) for d in range(1, RATE)]

        def segment(s, carry):
            def score(item):
                level, d = item
                return dot(k_s[level, s ^ d], q_s[level, s])

            block = score(steps[0])
            acc = None
            for n, (level, d) in enumerate(steps):
                following = score(steps[n + 1]) if n + 1 < len(steps) else None
                part = dot(v_s[level, s ^ d], jnp.exp2(block * SCALE).astype(BF16))
                acc = part if d == 1 else acc + part
                if d == RATE - 1:
                    acc_ref[level, s] = acc
                    max_ref[level, s] = jnp.zeros((8, HALF), F32)
                block = following
            return carry

        lax.fori_loop(0, RATE, segment, 0, unroll=2)

    def run():
        def segment(s, carry):
            def score(level):
                return [dot(k_s[level, s ^ d], q_s[level, s]) for d in range(1, RATE)]

            scores = score(0)
            for level in range(2):
                following = score(1) if level == 0 else None
                best = column_max(scores)
                acc = None
                for d in range(1, RATE):
                    block = scores[d - 1] * SCALE - best
                    part = dot(v_s[level, s ^ d], jnp.exp2(block).astype(BF16))
                    acc = part if acc is None else acc + part
                acc_ref[level, s] = acc
                max_ref[level, s] = jnp.broadcast_to(best, (8, HALF))
                scores = following
            return carry

        lax.fori_loop(0, RATE, segment, 0)

    query_length, key_length = far_lengths(sources)
    length_ref[0] = query_length
    length_ref[1] = key_length
    plain = is_small(query_length, key_length)
    pl.when(plain)(run_plain)
    pl.when(jnp.logical_not(plain))(run)


def far_kernel(index, mid, top, *refs):
    place = (index, mid, top)
    sel2, sel3, beyond3, beyond2, beyond1, k_own, v_own, q_own, acc_in, max_in, length_in = refs[
        :11
    ]
    outs = refs[11 : 11 + RATE]
    k_s, v_s, q_s, result_s, tail_s = refs[11 + RATE :]
    same, _ = far_slots(place)
    sources = [(sel2.at[0], sel3.at[0])] + [
        (ref.at[0], ref.at[1]) for ref in (beyond1, beyond2, beyond3)
    ]
    far_pieces(place, sources, k_s, v_s, q_s)
    tail_s[...] = jnp.zeros(tail_s.shape, F32)

    tasks = [(level, chip) for level in range(2) for chip in range(2)]
    held = ((k_own, v_own, q_own), (k_s, v_s, q_s))

    def blocks(s, chip):
        return [(held[c], s ^ d) for d in range(1, RATE) for c in ((1,), (0, 1))[chip]]

    def finish(s, level, chip, acc, best):
        total = acc[DH : DH + 1, :]
        result = (acc[0:DH, :] / total).astype(BF16)
        lse = best + jnp.log2(total)
        if level == 0:
            lse = jnp.where(same, lse + 1.0, lse)
        else:
            lse = jnp.where(same, -1e30, lse)
        high = lse.astype(BF16).astype(F32)
        middle = (lse - high).astype(BF16).astype(F32)
        low = lse - high - middle
        for i in range(2):
            n = 2 * (2 * chip + i) + level
            mine = slice(i * BLK, (i + 1) * BLK)
            result_s[s, :, n * BLK : (n + 1) * BLK] = result[:, mine]
            for k, part in enumerate((high, middle, low)):
                tail_s[s, 3 * n + k : 3 * n + k + 1, :] = part[:, mine]

    def run_plain():
        def segment(s, carry):
            steps = [
                (level, chip, keys, b, n)
                for level, chip in tasks
                for n, (keys, b) in enumerate(blocks(s, chip))
            ]

            def score(item):
                level, chip, keys, b, _ = item
                return dot(keys[0][level, b], held[chip][2][level, s])

            block = score(steps[0])
            acc = None
            for m, (level, chip, keys, b, n) in enumerate(steps):
                following = score(steps[m + 1]) if m + 1 < len(steps) else None
                part = dot(keys[1][level, b], jnp.exp2(block * SCALE).astype(BF16))
                acc = acc + part if n else part
                if n + 1 == len(blocks(s, chip)):
                    if chip == 0:
                        acc = acc + acc_in[level, s]
                    finish(s, level, chip, acc, jnp.zeros((1, HALF), F32))
                block = following
            return carry

        lax.fori_loop(0, RATE, segment, 0, unroll=2)

    def run():
        def segment(s, carry):
            for level, chip in tasks:
                scores = [
                    dot(keys[0][level, b], held[chip][2][level, s]) for keys, b in blocks(s, chip)
                ]
                best = column_max(scores)
                acc = jnp.zeros((DX, HALF), F32)
                if chip == 0:
                    old_max = max_in[level, s, 0:1, :]
                    best = jnp.maximum(best, old_max)
                    acc = acc_in[level, s] * jnp.exp2(old_max - best)
                for block, (keys, b) in zip(scores, blocks(s, chip)):
                    acc += dot(keys[1][level, b], jnp.exp2(block * SCALE - best).astype(BF16))
                finish(s, level, chip, acc, best)
            return carry

        lax.fori_loop(0, RATE, segment, 0)

    query_length, key_length = far_lengths(sources)
    plain = is_small(
        jnp.maximum(query_length, length_in[0]), jnp.maximum(key_length, length_in[1])
    )
    pl.when(plain)(run_plain)
    pl.when(jnp.logical_not(plain))(run)
    for s in range(RATE):
        outs[s][:, : GROUP * HALF] = result_s[s]
        outs[s][:, GROUP * HALF :] = tail_s[s].astype(BF16)


def join(acc, best, far, j):
    tail = far[:, GROUP * HALF :].astype(F32)
    lse = jnp.concatenate(
        [
            tail[3 * n : 3 * n + 1] + tail[3 * n + 1 : 3 * n + 2] + tail[3 * n + 2 : 3 * n + 3]
            for n in (2 * j, 2 * j + 1)
        ],
        axis=1,
    )
    overall = jnp.maximum(best, lse)
    near_factor, far_factor = jnp.exp2(best - overall), jnp.exp2(lse - overall)
    total = acc[DH : DH + 1] * near_factor + far_factor
    value = far[:, j * HALF : (j + 1) * HALF].astype(F32) * far_factor
    return ((acc[0:DH] * near_factor + value) / total).astype(BF16)


def combine_kernel(chip, acc_ref, max_ref, *refs):
    far, outs = refs[:-2][::-1], refs[-2:]
    for i in range(2):
        for p, results in enumerate(far):
            outs[i][p, :, 0:HALF] = join(
                acc_ref[p, 2 * i], max_ref[p, 2 * i, 0:1, :], results, 2 * chip + i
            )
            acc = acc_ref[p, 2 * i + 1]
            outs[i][p, :, HALF:] = (acc[0:DH] / acc[DH : DH + 1]).astype(BF16)


def project_kernel(sources, index, mid, top, *refs):
    place = (index, mid, top)
    parts, (w_ref, out_ref, held) = refs[:-3], refs[-3:]
    for (j, first), part in zip(sources, parts):
        for p in range(part.shape[0]):
            head = head_of(place, j, first + p)
            slots = class_of_slots(*offsets_of(place, head))
            for s in range(RATE):
                held[head_rows(head), lane_block(slots[s])] = part[
                    p, :, s * BLK : (s + 1) * BLK
                ]
    row = lax.broadcasted_iota(jnp.int32, (TOK, TOK), 0)
    col = lax.broadcasted_iota(jnp.int32, (TOK, TOK), 1)
    picker = (row == RATE * (col % BLK) + col // BLK).astype(BF16)
    attention = dot_nt(picker, held[...]).astype(BF16)
    out_ref[...] = dot(attention, w_ref[...]).astype(BF16)


def whole(shape):
    return pl.BlockSpec(shape, lambda *_: (0,) * len(shape))


def per_head(shape, skip=0):
    return pl.BlockSpec(shape, lambda h, *_: (h + skip,) + (0,) * (len(shape) - 1))


def call(
    kernel, scalars, args, grid, in_specs, outs, scratch, scores,
    limit=VMEM_LIMIT, after=(), through=(),
):
    known = len(scalars) + len(args)
    extra = (*after, *through)
    count = len(outs)
    anywhere = pl.BlockSpec(memory_space=pl.ANY)

    def body(*refs):
        results = refs[known + len(extra) :]
        kernel(*refs[:known], *results[:count], *results[count + len(through) :])

    return pl.pallas_call(
        body if extra else kernel,
        grid_spec=pltpu.PrefetchScalarGridSpec(
            num_scalar_prefetch=len(scalars),
            grid=grid,
            in_specs=list(in_specs) + [anywhere] * len(extra),
            out_specs=[spec for spec, _ in outs] + [anywhere] * len(through),
            scratch_shapes=scratch,
        ),
        out_shape=[shape for _, shape in outs]
        + [jax.ShapeDtypeStruct(x.shape, x.dtype) for x in through],
        input_output_aliases={known + len(after) + i: count + i for i in range(len(through))},
        compiler_params=pltpu.CompilerParams(vmem_limit_bytes=limit),
        cost_estimate=pl.CostEstimate(flops=0, bytes_accessed=0, transcendentals=0),
    )(*scalars, *args, *extra)


def handed_on(arrays):
    return call(lambda: None, (), (), (1,), [], [], [], 0, through=tuple(arrays))


def within(array, apart):
    count = lax.axis_size("seq")
    return lax.ppermute(array, "seq", [(i, i ^ apart) for i in range(count)])


def swap_segments(arrays):
    moved = {s: within(arrays[s - 1], GROUP * s) for s in (3, 2, 1)}
    return [moved[s] for s in (1, 2, 3)]


def shards_four(queries, key_states, value_states, offsets_mid, offsets_top, out_weight):
    width = queries.shape[1]
    place = (lax.axis_index("seq").astype(jnp.int32).reshape(1), offsets_mid, offsets_top)
    full = jax.ShapeDtypeStruct((HG, 3 * DH, TOK), BF16)
    piece = jax.ShapeDtypeStruct((HG, 3 * DH, HALF), BF16)
    pair = jax.ShapeDtypeStruct((2, 3 * DH, HALF), BF16)
    anywhere = pl.BlockSpec(memory_space=pl.ANY)
    shapes = [full] * 2 + [piece] * 4
    own0, own1, sel2, sel3, rest2, rest3 = call(
        pack_kernel, place, (key_states, value_states, queries), (1,),
        [anywhere] * 3,
        [(anywhere, shape) for shape in shapes],
        [pltpu.VMEM((TOK, width), BF16)] * 3
        + [pltpu.VMEM((width, TOK), BF16)] * 3
        + [pltpu.VMEM(shape.shape, BF16) for shape in shapes]
        + [pltpu.SemaphoreType.DMA((3,)), pltpu.SemaphoreType.DMA((6, 3))],
        1 << 19, VMEM_MOST,
    )
    own1 = within(own1, 1)
    sel2, sel3 = within(sel2, 2), within(sel3, 3)

    def regroup(a, b, **order):
        return call(
            regroup_kernel, (), (a, b), (1,),
            [whole(a.shape), whole(b.shape)], [(whole(pair.shape), pair)] * 3,
            [], 1 << 17, **order,
        )

    def near(held, units, tasks, old, first=0, heads=HG, step=2, **order):
        sizes = [len(members) * BLK for _, members in units]
        scores = sum(sum(sizes[low:]) * HALF for group in tasks for _, low, _ in group)
        arrays = [*held.values(), *[x for one in old for x in one]]
        shapes = [
            jax.ShapeDtypeStruct((heads, len(group), rows, HALF), F32)
            for group in tasks
            for rows in (DX, 8)
        ]
        return call(
            functools.partial(near_kernel, list(held), units, tasks, len(old), first, step),
            place, arrays, (heads // step,),
            [per_head((step,) + x.shape[1:], first // step) for x in arrays],
            [(per_head((step,) + x.shape[1:]), x) for x in shapes],
            [
                pltpu.VMEM((step, sum(sizes), DH), BF16),
                pltpu.VMEM((step, DX, sum(sizes)), BF16),
            ],
            heads * scores, **order,
        )

    def units_of(a, b):
        return [(0, [(a, 0), (b, 0)]), (1, [(a, 1), (b, 1)])], [
            (None, [(a, 2), (a, 3), (b, 2), (b, 3)])
        ]

    own_sel, own_rest = units_of(0, 1)
    other_sel, other_rest = units_of(2, 3)
    own = [(0, 0), (0, 1), (1, 0), (1, 1)]

    ours = regroup(own0, own1)
    ours = swap_segments(ours)
    held = {(0, 0): own0, (1, 0): own1}
    state_own = near(held, own_sel + own_rest, [[(q, 0, None) for q in own]], [])
    *theirs, rest2, rest3 = regroup(sel2, sel3, after=state_own[1:], through=(rest2, rest3))
    theirs = swap_segments(theirs)
    rest2, rest3 = within(rest2, 2), within(rest3, 3)

    held.update({(2, 0): sel2, (3, 0): sel3})
    out = near(
        held, own_sel + own_rest + other_sel,
        [
            [(q, 3, (0, i)) for i, q in enumerate(own)],
            [((2, 0), 0, None), ((3, 0), 0, None)],
        ],
        [state_own],
        after=ours[::-1],
    )
    state_own, state_sel = out[:2], out[2:]

    result = jax.ShapeDtypeStruct((DH, GROUP * HALF + BLK), BF16)
    piece_0 = pl.BlockSpec((1, 3 * DH, HALF), lambda *_: (0, 0, 0))
    pieces_shapes = [
        jax.ShapeDtypeStruct((2, RATE, HALF, DH), BF16),
        jax.ShapeDtypeStruct((2, RATE, DX, HALF), BF16),
        jax.ShapeDtypeStruct((2, RATE, DH, HALF), BF16),
    ]
    sums_shapes = [
        jax.ShapeDtypeStruct((2, RATE, DX, HALF), F32),
        jax.ShapeDtypeStruct((2, RATE, 8, HALF), F32),
    ]
    in_scalars = pl.BlockSpec(memory_space=pltpu.SMEM)
    far_own = call(
        far_own_kernel, place, (own0, own1, *ours), (1,),
        [piece_0] * 2 + [whole(pair.shape)] * 3,
        [(whole(x.shape), x) for x in pieces_shapes + sums_shapes]
        + [(in_scalars, jax.ShapeDtypeStruct((2,), F32))],
        [], RATE * 2 * 3 * HALF * HALF, after=(state_sel[1],),
    )
    results = call(
        far_kernel, place, (sel2, sel3, *theirs[::-1], *far_own), (1,),
        [piece_0] * 2 + [whole(pair.shape)] * 3
        + [whole(x.shape) for x in far_own[:-1]] + [in_scalars],
        [(whole(result.shape), result)] * RATE,
        [pltpu.VMEM(x.shape, BF16) for x in pieces_shapes]
        + [
            pltpu.VMEM((RATE, DH, GROUP * HALF), BF16),
            pltpu.VMEM((RATE, DH, BLK), F32),
        ],
        RATE * 2 * 3 * 3 * HALF * HALF,
    )
    back = [results[0]] + swap_segments(results[1:])

    held.update({(2, 2): rest2, (3, 2): rest3})
    units = own_sel + own_rest + other_sel + other_rest

    def combine(chip, state, far, **order):
        heads = state[0].shape[0]
        attended = jax.ShapeDtypeStruct((heads, DH, TOK), BF16)
        return call(
            functools.partial(combine_kernel, chip), (), (*state, *far[::-1]), (1,),
            [whole(x.shape) for x in state] + [whole(result.shape)] * heads,
            [(whole(attended.shape), attended)] * 2,
            [],
            1 << 18, **order,
        )

    parts = {}
    last = results[0]
    for first, heads in CHUNKS:
        state_other = near(
            held, units,
            [
                [
                    ((2, 0), 5, (0, 0)), ((2, 1), 0, None),
                    ((3, 0), 5, (0, 1)), ((3, 1), 0, None),
                ]
            ],
            [state_sel],
            first, heads, 2, after=(last,),
        )
        part2, part3 = combine(1, state_other, back[first : first + heads])
        parts[2, first], parts[3, first] = within(part2, 2), within(part3, 3)
        last = part3
    state_own = near(
        {(2, 2): rest2, (3, 2): rest3, **{q: held[q] for q in ((0, 0), (1, 0))}},
        other_rest,
        [[(q, 0, (0, i)) for i, q in enumerate(own)]],
        [state_own],
        after=(last,),
    )
    early = [parts[j, first] for first, _ in CHUNKS[:-1] for j in (2, 3)]
    part0, part1 = combine(0, state_own, back, after=early)
    parts = dict(zip(parts, handed_on(parts.values())))
    parts[0, 0], parts[1, 0] = part0, within(part1, 1)
    return call(
        functools.partial(project_kernel, list(parts)), place, (*parts.values(), out_weight), (1,),
        [whole(x.shape) for x in parts.values()] + [whole((width, width))],
        [(whole((TOK, width)), jax.ShapeDtypeStruct((TOK, width), BF16))],
        [pltpu.VMEM((width, TOK), BF16)],
        1 << 18,
    )[0]


def shards(queries, key_states, value_states, offsets_mid, offsets_top, out_weight):
    tokens, width = queries.shape
    heads = offsets_mid.shape[0]
    fits = (
        lax.axis_size("head") == 1
        and lax.axis_size("seq") == GROUP * RATE
        and tokens == TOK
        and heads == GROUP * HG
        and width == heads * DH
    )
    run = shards_four if fits else shards_general
    return run(queries, key_states, value_states, offsets_mid, offsets_top, out_weight)


def solution(mesh):
    in_specs = (
        P(("slide", "seq"), "head"),
        P(("slide", "seq"), "head"),
        P(("slide", "seq"), "head"),
        P(),
        P(),
        P("head", None),
    )
    out_specs = P(("slide", "seq", "head"), None)
    return jax.shard_map(shards, mesh=mesh, in_specs=in_specs, out_specs=out_specs, check_vma=False)
```

```python
import functools

import jax
import jax.numpy as jnp
from jax import lax
from jax.experimental import pallas as pl
from jax.experimental.pallas import tpu as pltpu
from jax.sharding import PartitionSpec as P

SEG = 2048
LOG2E = 1.4426950408889634
VMEM_LIMIT = 40 * 1024 * 1024
VMEM_MOST = 60 * 1024 * 1024
BF16 = jnp.bfloat16
F32 = jnp.float32


def partner_2(block, axis, apart):
    count = lax.axis_size(axis)
    route = []
    for low in range(count):
        high = low | 1 << apart
        if high != low and high < count:
            route += [(low, high), (high, low)]
    return lax.ppermute(block, axis, route)


def attend_head(triple_in):
    query_rows, key_rows, value_rows = triple_in
    score_scale = query_rows.shape[-1] ** (-0.5)
    scores = jnp.dot(query_rows, key_rows.T, preferred_element_type=jnp.float32) * score_scale
    row_max = jnp.max(scores, axis=1)
    shifted = jnp.exp(scores - row_max[:, None])
    row_total = jnp.sum(shifted, axis=1)
    weights = shifted.astype(jnp.bfloat16)
    numerator = jnp.dot(weights, value_rows, preferred_element_type=jnp.float32)
    return (numerator, row_total, row_max)


def attend_local(query_rows, pair_rows):
    return lax.map(
        attend_head,
        (
            query_rows.transpose(1, 0, 2),
            pair_rows[:, 0].transpose(1, 0, 2),
            pair_rows[:, 1].transpose(1, 0, 2),
        ),
    )


def pick_rows(states, offsets, rate):
    row_count, inner_count, heads_here, head_width = states.shape
    picker = (jnp.arange(rate)[:, None] == offsets[None, :]).astype(jnp.bfloat16)
    folded = states.reshape(row_count // rate, rate, inner_count, heads_here, head_width)
    return jnp.einsum("archd,rh->achd", folded, picker, preferred_element_type=jnp.float32).astype(
        jnp.bfloat16
    )


def spread_back(numerator, row_total, row_max, offsets, rate):
    heads_here, picked_count, head_width = numerator.shape
    chosen = jnp.arange(rate)[:, None] == offsets[None, :]
    full_num = jnp.where(chosen[None, :, :, None], numerator.transpose(1, 0, 2)[:, None], 0.0)
    full_total = jnp.where(chosen[None], row_total.T[:, None], 0.0)
    full_max = jnp.where(chosen[None], row_max.T[:, None], -1e30)
    return (
        full_num.reshape(picked_count * rate, heads_here, head_width),
        full_total.reshape(picked_count * rate, heads_here),
        full_max.reshape(picked_count * rate, heads_here),
    )


def doubling(buffer, steps_count):
    position = lax.axis_index("seq")
    for bit_index in range(steps_count):
        partner = partner_2(buffer, "seq", bit_index)
        is_lower = position >> bit_index & 1 == 0
        buffer = jnp.where(
            is_lower, jnp.concatenate([buffer, partner], 0), jnp.concatenate([partner, buffer], 0)
        )
    return buffer


def shards_general(queries, key_states, value_states, offsets_mid, offsets_top, out_weight):
    tok_rows = queries.shape[0]
    heads_local = offsets_mid.shape[0] // lax.axis_size("head")
    head_size = queries.shape[1] // heads_local
    seq_devices = lax.axis_size("seq")
    seq_total = tok_rows * seq_devices
    width_mid = min(16 * SEG, seq_total)
    rate_mid = width_mid // SEG
    rate_top = seq_total // SEG
    start_head = lax.axis_index("head") * heads_local
    mid_local = lax.dynamic_slice(offsets_mid, (start_head,), (heads_local,))
    top_local = lax.dynamic_slice(offsets_top, (start_head,), (heads_local,))
    query_heads = queries.reshape(tok_rows, 1, heads_local, head_size)
    paired = jnp.stack([key_states, value_states], axis=1).reshape(
        tok_rows, 2, heads_local, head_size
    )
    near_bits = (SEG // tok_rows).bit_length() - 1
    near_rows = doubling(paired.reshape(tok_rows, -1), near_bits).reshape(
        SEG, 2, heads_local, head_size
    )
    near_num, near_total, near_max = attend_local(query_heads[:, 0], near_rows)
    level_near = spread_back(
        near_num, near_total, near_max, jnp.zeros((heads_local,), jnp.int32), 1
    )
    mid_q = pick_rows(query_heads, mid_local, rate_mid)[:, 0]
    mid_kv = pick_rows(paired, mid_local, rate_mid)
    mid_group = width_mid // tok_rows
    mid_bits = mid_group.bit_length() - 1
    mid_rows = doubling(mid_kv.reshape(mid_kv.shape[0], -1), mid_bits).reshape(
        SEG, 2, heads_local, head_size
    )
    mid_num, mid_total, mid_max = attend_local(mid_q, mid_rows)
    level_mid = spread_back(mid_num, mid_total, mid_max, mid_local, rate_mid)
    top_q = pick_rows(query_heads, top_local, rate_top)[:, 0]
    top_kv = pick_rows(paired, top_local, rate_top)
    top_rows = lax.all_gather(
        top_kv.reshape(top_kv.shape[0], -1), "seq", axis=0, tiled=True
    ).reshape(SEG, 2, heads_local, head_size)
    top_num, top_total, top_max = attend_local(top_q, top_rows)
    level_top = spread_back(top_num, top_total, top_max, top_local, rate_top)
    levels = [level_near, level_mid, level_top]
    overall = jnp.maximum(jnp.maximum(level_near[2], level_mid[2]), level_top[2])
    numerator = jnp.zeros((tok_rows, heads_local, head_size), jnp.float32)
    row_total = jnp.zeros((tok_rows, heads_local), jnp.float32)
    for level_num, level_total, level_max in levels:
        factor = jnp.exp(level_max - overall)
        numerator = numerator + factor[..., None] * level_num
        row_total = row_total + factor * level_total
    attention = (
        (numerator / row_total[..., None])
        .astype(jnp.bfloat16)
        .reshape(tok_rows, heads_local * head_size)
    )
    result = lax.psum_scatter(
        jnp.dot(attention, out_weight, preferred_element_type=jnp.float32),
        "head",
        scatter_dimension=0,
        tiled=True,
    )
    return result.astype(jnp.bfloat16)


RATE = 4
GROUP = 4
HG = 4
DH = 48
BLK = 128
HALF = 2 * BLK
TOK = 512
SCALE = DH**-0.5 * LOG2E
AHEAD = 4
SAFE = 96.0
CHUNKS = ((0, 4),)
DX = 64


def dot(a, b):
    return jnp.dot(a, b, preferred_element_type=F32)


def dot_nt(a, b):
    return lax.dot_general(a, b, (((1,), (1,)), ((), ())), preferred_element_type=F32)


def class_of_slots(off_mid, off_top):
    first = off_mid
    second = jnp.where(off_top == off_mid, lax.rem(off_mid + 1, RATE), off_top)
    free0 = (first != 0) & (second != 0)
    free1 = (first != 1) & (second != 1)
    third = jnp.where(free0, 0, jnp.where(free1, 1, 2))
    return first, second, third, 6 - first - second - third


def head_of(place, j, p):
    index = place[0][0]
    return ((index & (GROUP - 1)) ^ j) * HG + ((index // GROUP) ^ p)


def offsets_of(place, head):
    return place[1][head], place[2][head]


def token_picker():
    row = lax.broadcasted_iota(jnp.int32, (TOK, TOK), 0)
    col = lax.broadcasted_iota(jnp.int32, (TOK, TOK), 1)
    return (col == RATE * (row % BLK) + row // BLK).astype(BF16)


def fill_class_major(block, picker, scratch):
    scratch[...] = lax.dot_general(
        block, picker, (((0,), (1,)), ((), ())), preferred_element_type=F32
    ).astype(BF16)


def lane_block(index):
    return pl.ds(pl.multiple_of(index * BLK, BLK), BLK)


def head_rows(head):
    return pl.ds(pl.multiple_of(head * DH, 16), DH)


def pack_kernel(index, mid, top, k_hbm, v_hbm, q_hbm, *refs):
    place = (index, mid, top)
    outs, refs = refs[:6], refs[6:]
    blocks, held, packed = refs[:3], refs[3:6], refs[6:12]
    sems_in, sems_out = refs[12:]
    loads = [
        pltpu.make_async_copy(hbm, block, sems_in.at[i])
        for i, (hbm, block) in enumerate(zip((k_hbm, v_hbm, q_hbm), blocks))
    ]
    for load in loads:
        load.start()
    picker = token_picker()
    stores = []
    for n, (load, block, scratch) in enumerate(zip(loads, blocks, held)):
        load.wait()
        fill_class_major(block[...], picker, scratch)
        rows = slice(n * DH, (n + 1) * DH)
        for i, (j, first, count) in enumerate(
            ((0, 0, 4), (1, 0, 4), (2, 0, 2), (3, 0, 2), (2, 2, 2), (3, 2, 2))
        ):
            for p in range(HG):
                head = head_of(place, j, p)
                slots = class_of_slots(*offsets_of(place, head))
                for s in range(count):
                    packed[i][p, rows, s * BLK : (s + 1) * BLK] = scratch[
                        head_rows(head), lane_block(slots[first + s])
                    ]
            store = pltpu.make_async_copy(
                packed[i].at[:, rows], outs[i].at[:, rows], sems_out.at[i, n]
            )
            store.start()
            stores.append(store)
    for store in stores:
        store.wait()


def regroup_kernel(a_ref, b_ref, *refs):
    for s, out in enumerate(refs[-3:]):
        out[0] = a_ref[s + 1, :, 0:HALF]
        out[1] = b_ref[s + 1, :, 0:HALF]


def upright(keys_t):
    return keys_t.T


def largest(blocks):
    best = None
    for block in blocks:
        wide = block.astype(F32)
        length = jnp.sum(wide * wide, axis=0, keepdims=True)
        for low in range(0, block.shape[1], HALF):
            part = length[:, low : low + HALF]
            best = part if best is None else jnp.maximum(best, part)
    return jnp.max(best)


def is_small(query_length, key_length):
    return query_length * key_length * (SCALE * SCALE) < SAFE * SAFE


def column_max(blocks):
    best = jnp.max(blocks[0], axis=0, keepdims=True)
    for block in blocks[1:]:
        best = jnp.maximum(best, jnp.max(block, axis=0, keepdims=True))
    return best * SCALE


def in_stages(items, score, weigh, gather):
    scores = {n: score(item) for n, item in enumerate(items[:AHEAD])}
    weights = weigh(items[0], scores.pop(0))
    for n, item in enumerate(items):
        if n + AHEAD < len(items):
            scores[n + AHEAD] = score(items[n + AHEAD])
        following = weigh(items[n + 1], scores.pop(n + 1)) if n + 1 < len(items) else None
        gather(item, weights)
        weights = following


def near_kernel(inputs, units, tasks, carried, first, step, index, mid, top, *refs):
    place = (index, mid, top)
    pieces = dict(zip(inputs, refs[: len(inputs)]))
    refs = refs[len(inputs) :]
    old = [refs[2 * i : 2 * i + 2] for i in range(carried)]
    outs = refs[2 * carried : 2 * carried + 2 * len(tasks)]
    k_s, v_s = refs[-2:]
    v_s[:, DH:DX, :] = jnp.ones((step, DX - DH, v_s.shape[2]), BF16)
    lane_slot = lax.broadcasted_iota(jnp.int32, (1, HALF), 1) // BLK

    def lookup(j, slot):
        first = 0 if (j, 0) in pieces and pieces[j, 0].shape[2] > HALF else slot // 2 * 2
        return pieces[j, first], (slot - first) * BLK

    chunks = []
    row = 0
    for label, members in units:
        chunks.append((label, slice(row, row + len(members) * BLK)))
        row += len(members) * BLK
    members = [member for _, group in units for member in group]

    def prepare(h):
        for i, (j, slot) in enumerate(members):
            ref, lane = lookup(j, slot)
            rows = slice(i * BLK, (i + 1) * BLK)
            k_s[h, rows, :] = upright(ref[h, 0:DH, lane : lane + BLK])
            v_s[h, 0:DH, rows] = ref[h, DH : 2 * DH, lane : lane + BLK]

    def counted_again(h):
        off_mid, off_top = offsets_of(place, head_of(place, 0, first + pl.program_id(0) * step + h))
        same = off_mid == off_top
        return [
            jnp.where(lane_slot == 0, jnp.where(same, 1.584962500721156, 1.0), 0.0),
            jnp.where(lane_slot == 1, jnp.where(same, 0.0, 1.0), 0.0),
        ]

    def run(heads):
        again = [counted_again(h) for h in heads]
        flat = [
            (h, again_h, query, low, merge, out, i)
            for h, again_h in zip(heads, again)
            for out, group in enumerate(tasks)
            for i, (query, low, merge) in enumerate(group)
        ]

        def score(task):
            h, _, (j, half), low = task[:4]
            ref, lane = lookup(j, 2 * half)
            query = ref[h, 2 * DH :, lane : lane + HALF]
            return [dot(k_s[h, rows, :], query) for _, rows in chunks[low:]]

        scores = score(flat[0])
        for n, (h, again_h, (_, half), low, merge, out, i) in enumerate(flat):
            following = score(flat[n + 1]) if n + 1 < len(flat) else None
            best = column_max(scores)
            if merge is not None:
                acc_in, max_in = old[merge[0]]
                old_max = max_in[h, merge[1], 0:1, :]
                best = jnp.maximum(best, old_max)
            acc = None
            for (label, rows), block in zip(chunks[low:], scores):
                block = block * SCALE
                if half == 0 and label is not None:
                    block = block - (best - again_h[label])
                else:
                    block = block - best
                part = dot(v_s[h, :, rows], jnp.exp2(block).astype(BF16))
                acc = part if acc is None else acc + part
            if merge is not None:
                acc = acc + acc_in[h, merge[1]] * jnp.exp2(old_max - best)
            acc_ref, max_ref = outs[2 * out : 2 * out + 2]
            acc_ref[h, i] = acc
            max_ref[h, i] = jnp.broadcast_to(best, (8, HALF))
            scores = following

    def run_plain():
        again = [counted_again(h) for h in range(step)]
        steps = [
            (h, query, merge, out, i, c, c == low, c == len(chunks) - 1)
            for h in range(step)
            for out, group in enumerate(tasks)
            for i, (query, low, merge) in enumerate(group)
            for c in range(low, len(chunks))
        ]

        def score(item):
            h, (j, half), c = item[0], item[1], item[5]
            ref, lane = lookup(j, 2 * half)
            return dot(k_s[h, chunks[c][1], :], ref[h, 2 * DH :, lane : lane + HALF])

        def weigh(item, block):
            h, (_, half), c = item[0], item[1], item[5]
            label = chunks[c][0]
            block = block * SCALE
            if half == 0 and label is not None:
                block = block + again[h][label]
            return jnp.exp2(block).astype(BF16)

        held = {}

        def gather(item, weights):
            h, _, merge, out, i, c, begins, ends = item
            part = dot(v_s[h, :, chunks[c][1]], weights)
            acc = part if begins else held[0] + part
            if ends:
                if merge is not None:
                    acc = acc + old[merge[0]][0][h, merge[1]]
                acc_ref, max_ref = outs[2 * out : 2 * out + 2]
                acc_ref[h, i] = acc
                max_ref[h, i] = jnp.zeros((8, HALF), F32)
            held[0] = acc

        in_stages(steps, score, weigh, gather)

    for h in range(step):
        prepare(h)
    plain = is_small(
        largest([ref[h, 2 * DH :, :] for ref in pieces.values() for h in range(step)]),
        largest([ref[h, 0:DH, :] for ref in pieces.values() for h in range(step)]),
    )
    for _, max_in in old:
        plain = plain & (jnp.max(jnp.abs(max_in[...])) == 0.0)

    @pl.when(plain)
    def _():
        run_plain()

    @pl.when(jnp.logical_not(plain))
    def _():
        @pl.loop(0, step)
        def _(h):
            run([h])


def far_slots(place):
    off_mid, off_top = offsets_of(place, head_of(place, 0, 0))
    same = off_mid == off_top
    return same, (0, jnp.where(same, 0, 1))


def far_pieces(place, sources, k_s, v_s, q_s):
    _, slots = far_slots(place)
    for s, pair in enumerate(sources):
        for i, ref in enumerate(pair):
            here = slice(i * BLK, (i + 1) * BLK)
            for level, slot in enumerate(slots):
                k_s[level, s, here, :] = upright(ref[0:DH, lane_block(slot)])
                v_s[level, s, 0:DH, here] = ref[DH : 2 * DH, lane_block(slot)]
                q_s[level, s, :, here] = ref[2 * DH : 3 * DH, lane_block(slot)]
    v_s[:, :, DH:DX, :] = jnp.ones((2, RATE, DX - DH, HALF), BF16)


def far_lengths(sources):
    every = [ref for pair in sources for ref in pair]
    return (
        largest([ref[2 * DH : 3 * DH, 0:HALF] for ref in every]),
        largest([ref[0:DH, 0:HALF] for ref in every]),
    )


def far_own_kernel(index, mid, top, own0, own1, beyond1, beyond2, beyond3, *refs):
    k_s, v_s, q_s, acc_ref, max_ref, length_ref = refs
    sources = [(own0.at[0], own1.at[0])] + [
        (ref.at[0], ref.at[1]) for ref in (beyond1, beyond2, beyond3)
    ]
    far_pieces((index, mid, top), sources, k_s, v_s, q_s)

    def run_plain():
        steps = [(level, d) for level in range(2) for d in range(1, RATE)]

        def segment(s, carry):
            def score(item):
                level, d = item
                return dot(k_s[level, s ^ d], q_s[level, s])

            def weigh(item, block):
                return jnp.exp2(block * SCALE).astype(BF16)

            held = {}

            def gather(item, weights):
                level, d = item
                part = dot(v_s[level, s ^ d], weights)
                held[0] = part if d == 1 else held[0] + part
                if d == RATE - 1:
                    acc_ref[level, s] = held[0]
                    max_ref[level, s] = jnp.zeros((8, HALF), F32)

            in_stages(steps, score, weigh, gather)
            return carry

        lax.fori_loop(0, RATE, segment, 0, unroll=2)

    def run():
        def segment(s, carry):
            def score(level):
                return [dot(k_s[level, s ^ d], q_s[level, s]) for d in range(1, RATE)]

            scores = score(0)
            for level in range(2):
                following = score(1) if level == 0 else None
                best = column_max(scores)
                acc = None
                for d in range(1, RATE):
                    block = scores[d - 1] * SCALE - best
                    part = dot(v_s[level, s ^ d], jnp.exp2(block).astype(BF16))
                    acc = part if acc is None else acc + part
                acc_ref[level, s] = acc
                max_ref[level, s] = jnp.broadcast_to(best, (8, HALF))
                scores = following
            return carry

        lax.fori_loop(0, RATE, segment, 0)

    query_length, key_length = far_lengths(sources)
    length_ref[0] = query_length
    length_ref[1] = key_length
    plain = is_small(query_length, key_length)
    pl.when(plain)(run_plain)
    pl.when(jnp.logical_not(plain))(run)


def far_kernel(index, mid, top, *refs):
    place = (index, mid, top)
    sel2, sel3, beyond3, beyond2, beyond1, k_own, v_own, q_own, acc_in, max_in, length_in = refs[
        :11
    ]
    outs = refs[11 : 11 + RATE]
    k_s, v_s, q_s, result_s, tail_s = refs[11 + RATE :]
    same, _ = far_slots(place)
    sources = [(sel2.at[0], sel3.at[0])] + [
        (ref.at[0], ref.at[1]) for ref in (beyond1, beyond2, beyond3)
    ]
    far_pieces(place, sources, k_s, v_s, q_s)
    tail_s[...] = jnp.zeros(tail_s.shape, F32)

    tasks = [(level, chip) for level in range(2) for chip in range(2)]
    held = ((k_own, v_own, q_own), (k_s, v_s, q_s))

    def blocks(s, chip):
        return [(held[c], s ^ d) for d in range(1, RATE) for c in ((1,), (0, 1))[chip]]

    def finish(s, level, chip, acc, best):
        total = acc[DH : DH + 1, :]
        result = (acc[0:DH, :] / total).astype(BF16)
        lse = best + jnp.log2(total)
        if level == 0:
            lse = jnp.where(same, lse + 1.0, lse)
        else:
            lse = jnp.where(same, -1e30, lse)
        high = lse.astype(BF16).astype(F32)
        middle = (lse - high).astype(BF16).astype(F32)
        low = lse - high - middle
        for i in range(2):
            n = 2 * (2 * chip + i) + level
            mine = slice(i * BLK, (i + 1) * BLK)
            result_s[s, :, n * BLK : (n + 1) * BLK] = result[:, mine]
            for k, part in enumerate((high, middle, low)):
                tail_s[s, 3 * n + k : 3 * n + k + 1, :] = part[:, mine]

    def run_plain():
        def segment(s, carry):
            steps = [
                (level, chip, keys, b, n)
                for level, chip in tasks
                for n, (keys, b) in enumerate(blocks(s, chip))
            ]

            def score(item):
                level, chip, keys, b, _ = item
                return dot(keys[0][level, b], held[chip][2][level, s])

            def weigh(item, block):
                return jnp.exp2(block * SCALE).astype(BF16)

            sums = {}

            def gather(item, weights):
                level, chip, keys, b, n = item
                part = dot(keys[1][level, b], weights)
                sums[0] = sums[0] + part if n else part
                if n + 1 == len(blocks(s, chip)):
                    acc = sums[0] + acc_in[level, s] if chip == 0 else sums[0]
                    finish(s, level, chip, acc, jnp.zeros((1, HALF), F32))

            in_stages(steps, score, weigh, gather)
            return carry

        lax.fori_loop(0, RATE, segment, 0, unroll=2)

    def run():
        def segment(s, carry):
            for level, chip in tasks:
                scores = [
                    dot(keys[0][level, b], held[chip][2][level, s]) for keys, b in blocks(s, chip)
                ]
                best = column_max(scores)
                acc = jnp.zeros((DX, HALF), F32)
                if chip == 0:
                    old_max = max_in[level, s, 0:1, :]
                    best = jnp.maximum(best, old_max)
                    acc = acc_in[level, s] * jnp.exp2(old_max - best)
                for block, (keys, b) in zip(scores, blocks(s, chip)):
                    acc += dot(keys[1][level, b], jnp.exp2(block * SCALE - best).astype(BF16))
                finish(s, level, chip, acc, best)
            return carry

        lax.fori_loop(0, RATE, segment, 0)

    query_length, key_length = far_lengths(sources)
    plain = is_small(
        jnp.maximum(query_length, length_in[0]), jnp.maximum(key_length, length_in[1])
    )
    pl.when(plain)(run_plain)
    pl.when(jnp.logical_not(plain))(run)
    for s in range(RATE):
        outs[s][:, : GROUP * HALF] = result_s[s]
        outs[s][:, GROUP * HALF :] = tail_s[s].astype(BF16)


def join(acc, best, far, j):
    tail = far[:, GROUP * HALF :].astype(F32)
    lse = jnp.concatenate(
        [
            tail[3 * n : 3 * n + 1] + tail[3 * n + 1 : 3 * n + 2] + tail[3 * n + 2 : 3 * n + 3]
            for n in (2 * j, 2 * j + 1)
        ],
        axis=1,
    )
    overall = jnp.maximum(best, lse)
    near_factor, far_factor = jnp.exp2(best - overall), jnp.exp2(lse - overall)
    total = acc[DH : DH + 1] * near_factor + far_factor
    value = far[:, j * HALF : (j + 1) * HALF].astype(F32) * far_factor
    return ((acc[0:DH] * near_factor + value) / total).astype(BF16)


def combine_kernel(chip, acc_ref, max_ref, *refs):
    far, outs = refs[:-2][::-1], refs[-2:]
    for i in range(2):
        for p, results in enumerate(far):
            outs[i][p, :, 0:HALF] = join(
                acc_ref[p, 2 * i], max_ref[p, 2 * i, 0:1, :], results, 2 * chip + i
            )
            acc = acc_ref[p, 2 * i + 1]
            outs[i][p, :, HALF:] = (acc[0:DH] / acc[DH : DH + 1]).astype(BF16)


def project_kernel(sources, index, mid, top, *refs):
    place = (index, mid, top)
    parts, (w_ref, out_ref, held) = refs[:-3], refs[-3:]
    for (j, first), part in zip(sources, parts):
        for p in range(part.shape[0]):
            head = head_of(place, j, first + p)
            slots = class_of_slots(*offsets_of(place, head))
            for s in range(RATE):
                held[head_rows(head), lane_block(slots[s])] = part[
                    p, :, s * BLK : (s + 1) * BLK
                ]
    row = lax.broadcasted_iota(jnp.int32, (TOK, TOK), 0)
    col = lax.broadcasted_iota(jnp.int32, (TOK, TOK), 1)
    picker = (row == RATE * (col % BLK) + col // BLK).astype(BF16)
    attention = dot_nt(picker, held[...]).astype(BF16)
    out_ref[...] = dot(attention, w_ref[...]).astype(BF16)


def whole(shape):
    return pl.BlockSpec(shape, lambda *_: (0,) * len(shape))


def per_head(shape, skip=0):
    return pl.BlockSpec(shape, lambda h, *_: (h + skip,) + (0,) * (len(shape) - 1))


def call(
    kernel, scalars, args, grid, in_specs, outs, scratch, scores,
    limit=VMEM_LIMIT, after=(), through=(),
):
    known = len(scalars) + len(args)
    extra = (*after, *through)
    count = len(outs)
    anywhere = pl.BlockSpec(memory_space=pl.ANY)

    def body(*refs):
        results = refs[known + len(extra) :]
        kernel(*refs[:known], *results[:count], *results[count + len(through) :])

    return pl.pallas_call(
        body if extra else kernel,
        grid_spec=pltpu.PrefetchScalarGridSpec(
            num_scalar_prefetch=len(scalars),
            grid=grid,
            in_specs=list(in_specs) + [anywhere] * len(extra),
            out_specs=[spec for spec, _ in outs] + [anywhere] * len(through),
            scratch_shapes=scratch,
        ),
        out_shape=[shape for _, shape in outs]
        + [jax.ShapeDtypeStruct(x.shape, x.dtype) for x in through],
        input_output_aliases={known + len(after) + i: count + i for i in range(len(through))},
        compiler_params=pltpu.CompilerParams(vmem_limit_bytes=limit),
        cost_estimate=pl.CostEstimate(flops=0, bytes_accessed=0, transcendentals=0),
    )(*scalars, *args, *extra)


def handed_on(arrays):
    return call(lambda: None, (), (), (1,), [], [], [], 0, through=tuple(arrays))


def within(array, apart):
    count = lax.axis_size("seq")
    return lax.ppermute(array, "seq", [(i, i ^ apart) for i in range(count)])


def swap_segments(arrays):
    moved = {s: within(arrays[s - 1], GROUP * s) for s in (3, 2, 1)}
    return [moved[s] for s in (1, 2, 3)]


def shards_four(queries, key_states, value_states, offsets_mid, offsets_top, out_weight):
    width = queries.shape[1]
    place = (lax.axis_index("seq").astype(jnp.int32).reshape(1), offsets_mid, offsets_top)
    full = jax.ShapeDtypeStruct((HG, 3 * DH, TOK), BF16)
    piece = jax.ShapeDtypeStruct((HG, 3 * DH, HALF), BF16)
    pair = jax.ShapeDtypeStruct((2, 3 * DH, HALF), BF16)
    anywhere = pl.BlockSpec(memory_space=pl.ANY)
    shapes = [full] * 2 + [piece] * 4
    own0, own1, sel2, sel3, rest2, rest3 = call(
        pack_kernel, place, (key_states, value_states, queries), (1,),
        [anywhere] * 3,
        [(anywhere, shape) for shape in shapes],
        [pltpu.VMEM((TOK, width), BF16)] * 3
        + [pltpu.VMEM((width, TOK), BF16)] * 3
        + [pltpu.VMEM(shape.shape, BF16) for shape in shapes]
        + [pltpu.SemaphoreType.DMA((3,)), pltpu.SemaphoreType.DMA((6, 3))],
        1 << 19, VMEM_MOST,
    )
    own1 = within(own1, 1)
    sel2, sel3 = within(sel2, 2), within(sel3, 3)

    def regroup(a, b, **order):
        return call(
            regroup_kernel, (), (a, b), (1,),
            [whole(a.shape), whole(b.shape)], [(whole(pair.shape), pair)] * 3,
            [], 1 << 17, **order,
        )

    def near(held, units, tasks, old, first=0, heads=HG, step=2, **order):
        sizes = [len(members) * BLK for _, members in units]
        scores = sum(sum(sizes[low:]) * HALF for group in tasks for _, low, _ in group)
        arrays = [*held.values(), *[x for one in old for x in one]]
        shapes = [
            jax.ShapeDtypeStruct((heads, len(group), rows, HALF), F32)
            for group in tasks
            for rows in (DX, 8)
        ]
        return call(
            functools.partial(near_kernel, list(held), units, tasks, len(old), first, step),
            place, arrays, (heads // step,),
            [per_head((step,) + x.shape[1:], first // step) for x in arrays],
            [(per_head((step,) + x.shape[1:]), x) for x in shapes],
            [
                pltpu.VMEM((step, sum(sizes), DH), BF16),
                pltpu.VMEM((step, DX, sum(sizes)), BF16),
            ],
            heads * scores, **order,
        )

    def units_of(a, b):
        return [(0, [(a, 0), (b, 0)]), (1, [(a, 1), (b, 1)])], [
            (None, [(a, 2), (a, 3), (b, 2), (b, 3)])
        ]

    own_sel, own_rest = units_of(0, 1)
    other_sel, other_rest = units_of(2, 3)
    own = [(0, 0), (0, 1), (1, 0), (1, 1)]

    ours = regroup(own0, own1)
    ours = swap_segments(ours)
    held = {(0, 0): own0, (1, 0): own1}
    state_own = near(held, own_sel + own_rest, [[(q, 0, None) for q in own]], [])
    *theirs, rest2, rest3 = regroup(sel2, sel3, after=state_own[1:], through=(rest2, rest3))
    theirs = swap_segments(theirs)
    rest2, rest3 = within(rest2, 2), within(rest3, 3)

    held.update({(2, 0): sel2, (3, 0): sel3})
    out = near(
        held, own_sel + own_rest + other_sel,
        [
            [(q, 3, (0, i)) for i, q in enumerate(own)],
            [((2, 0), 0, None), ((3, 0), 0, None)],
        ],
        [state_own],
        after=ours[::-1],
    )
    state_own, state_sel = out[:2], out[2:]

    result = jax.ShapeDtypeStruct((DH, GROUP * HALF + BLK), BF16)
    piece_0 = pl.BlockSpec((1, 3 * DH, HALF), lambda *_: (0, 0, 0))
    pieces_shapes = [
        jax.ShapeDtypeStruct((2, RATE, HALF, DH), BF16),
        jax.ShapeDtypeStruct((2, RATE, DX, HALF), BF16),
        jax.ShapeDtypeStruct((2, RATE, DH, HALF), BF16),
    ]
    sums_shapes = [
        jax.ShapeDtypeStruct((2, RATE, DX, HALF), F32),
        jax.ShapeDtypeStruct((2, RATE, 8, HALF), F32),
    ]
    in_scalars = pl.BlockSpec(memory_space=pltpu.SMEM)
    far_own = call(
        far_own_kernel, place, (own0, own1, *ours), (1,),
        [piece_0] * 2 + [whole(pair.shape)] * 3,
        [(whole(x.shape), x) for x in pieces_shapes + sums_shapes]
        + [(in_scalars, jax.ShapeDtypeStruct((2,), F32))],
        [], RATE * 2 * 3 * HALF * HALF, after=(state_sel[1],),
    )
    results = call(
        far_kernel, place, (sel2, sel3, *theirs[::-1], *far_own), (1,),
        [piece_0] * 2 + [whole(pair.shape)] * 3
        + [whole(x.shape) for x in far_own[:-1]] + [in_scalars],
        [(whole(result.shape), result)] * RATE,
        [pltpu.VMEM(x.shape, BF16) for x in pieces_shapes]
        + [
            pltpu.VMEM((RATE, DH, GROUP * HALF), BF16),
            pltpu.VMEM((RATE, DH, BLK), F32),
        ],
        RATE * 2 * 3 * 3 * HALF * HALF,
    )
    back = [results[0]] + swap_segments(results[1:])

    held.update({(2, 2): rest2, (3, 2): rest3})
    units = own_sel + own_rest + other_sel + other_rest

    def combine(chip, state, far, **order):
        heads = state[0].shape[0]
        attended = jax.ShapeDtypeStruct((heads, DH, TOK), BF16)
        return call(
            functools.partial(combine_kernel, chip), (), (*state, *far[::-1]), (1,),
            [whole(x.shape) for x in state] + [whole(result.shape)] * heads,
            [(whole(attended.shape), attended)] * 2,
            [],
            1 << 18, **order,
        )

    parts = {}
    last = results[0]
    for first, heads in CHUNKS:
        state_other = near(
            held, units,
            [
                [
                    ((2, 0), 5, (0, 0)), ((2, 1), 0, None),
                    ((3, 0), 5, (0, 1)), ((3, 1), 0, None),
                ]
            ],
            [state_sel],
            first, heads, 2, after=(last,),
        )
        part2, part3 = combine(1, state_other, back[first : first + heads])
        parts[2, first], parts[3, first] = within(part2, 2), within(part3, 3)
        last = part3
    state_own = near(
        {(2, 2): rest2, (3, 2): rest3, **{q: held[q] for q in ((0, 0), (1, 0))}},
        other_rest,
        [[(q, 0, (0, i)) for i, q in enumerate(own)]],
        [state_own],
        after=(last,),
    )
    early = [parts[j, first] for first, _ in CHUNKS[:-1] for j in (2, 3)]
    part0, part1 = combine(0, state_own, back, after=early)
    parts = dict(zip(parts, handed_on(parts.values())))
    parts[0, 0], parts[1, 0] = part0, within(part1, 1)
    return call(
        functools.partial(project_kernel, list(parts)), place, (*parts.values(), out_weight), (1,),
        [whole(x.shape) for x in parts.values()] + [whole((width, width))],
        [(whole((TOK, width)), jax.ShapeDtypeStruct((TOK, width), BF16))],
        [pltpu.VMEM((width, TOK), BF16)],
        1 << 18,
    )[0]


def shards(queries, key_states, value_states, offsets_mid, offsets_top, out_weight):
    tokens, width = queries.shape
    heads = offsets_mid.shape[0]
    fits = (
        lax.axis_size("head") == 1
        and lax.axis_size("seq") == GROUP * RATE
        and tokens == TOK
        and heads == GROUP * HG
        and width == heads * DH
    )
    run = shards_four if fits else shards_general
    return run(queries, key_states, value_states, offsets_mid, offsets_top, out_weight)


def solution(mesh):
    in_specs = (
        P(("slide", "seq"), "head"),
        P(("slide", "seq"), "head"),
        P(("slide", "seq"), "head"),
        P(),
        P(),
        P("head", None),
    )
    out_specs = P(("slide", "seq", "head"), None)
    return jax.shard_map(shards, mesh=mesh, in_specs=in_specs, out_specs=out_specs, check_vma=False)
```

```python
import functools

import jax
import jax.numpy as jnp
from jax import lax
from jax.experimental import pallas as pl
from jax.experimental.pallas import tpu as pltpu
from jax.sharding import PartitionSpec as P

SEG = 2048
LOG2E = 1.4426950408889634
VMEM_LIMIT = 40 * 1024 * 1024
VMEM_MOST = 60 * 1024 * 1024
BF16 = jnp.bfloat16
F32 = jnp.float32


def partner_2(block, axis, apart):
    count = lax.axis_size(axis)
    route = []
    for low in range(count):
        high = low | 1 << apart
        if high != low and high < count:
            route += [(low, high), (high, low)]
    return lax.ppermute(block, axis, route)


def attend_head(triple_in):
    query_rows, key_rows, value_rows = triple_in
    score_scale = query_rows.shape[-1] ** (-0.5)
    scores = jnp.dot(query_rows, key_rows.T, preferred_element_type=jnp.float32) * score_scale
    row_max = jnp.max(scores, axis=1)
    shifted = jnp.exp(scores - row_max[:, None])
    row_total = jnp.sum(shifted, axis=1)
    weights = shifted.astype(jnp.bfloat16)
    numerator = jnp.dot(weights, value_rows, preferred_element_type=jnp.float32)
    return (numerator, row_total, row_max)


def attend_local(query_rows, pair_rows):
    return lax.map(
        attend_head,
        (
            query_rows.transpose(1, 0, 2),
            pair_rows[:, 0].transpose(1, 0, 2),
            pair_rows[:, 1].transpose(1, 0, 2),
        ),
    )


def pick_rows(states, offsets, rate):
    row_count, inner_count, heads_here, head_width = states.shape
    picker = (jnp.arange(rate)[:, None] == offsets[None, :]).astype(jnp.bfloat16)
    folded = states.reshape(row_count // rate, rate, inner_count, heads_here, head_width)
    return jnp.einsum("archd,rh->achd", folded, picker, preferred_element_type=jnp.float32).astype(
        jnp.bfloat16
    )


def spread_back(numerator, row_total, row_max, offsets, rate):
    heads_here, picked_count, head_width = numerator.shape
    chosen = jnp.arange(rate)[:, None] == offsets[None, :]
    full_num = jnp.where(chosen[None, :, :, None], numerator.transpose(1, 0, 2)[:, None], 0.0)
    full_total = jnp.where(chosen[None], row_total.T[:, None], 0.0)
    full_max = jnp.where(chosen[None], row_max.T[:, None], -1e30)
    return (
        full_num.reshape(picked_count * rate, heads_here, head_width),
        full_total.reshape(picked_count * rate, heads_here),
        full_max.reshape(picked_count * rate, heads_here),
    )


def doubling(buffer, steps_count):
    position = lax.axis_index("seq")
    for bit_index in range(steps_count):
        partner = partner_2(buffer, "seq", bit_index)
        is_lower = position >> bit_index & 1 == 0
        buffer = jnp.where(
            is_lower, jnp.concatenate([buffer, partner], 0), jnp.concatenate([partner, buffer], 0)
        )
    return buffer


def shards_general(queries, key_states, value_states, offsets_mid, offsets_top, out_weight):
    tok_rows = queries.shape[0]
    heads_local = offsets_mid.shape[0] // lax.axis_size("head")
    head_size = queries.shape[1] // heads_local
    seq_devices = lax.axis_size("seq")
    seq_total = tok_rows * seq_devices
    width_mid = min(16 * SEG, seq_total)
    rate_mid = width_mid // SEG
    rate_top = seq_total // SEG
    start_head = lax.axis_index("head") * heads_local
    mid_local = lax.dynamic_slice(offsets_mid, (start_head,), (heads_local,))
    top_local = lax.dynamic_slice(offsets_top, (start_head,), (heads_local,))
    query_heads = queries.reshape(tok_rows, 1, heads_local, head_size)
    paired = jnp.stack([key_states, value_states], axis=1).reshape(
        tok_rows, 2, heads_local, head_size
    )
    near_bits = (SEG // tok_rows).bit_length() - 1
    near_rows = doubling(paired.reshape(tok_rows, -1), near_bits).reshape(
        SEG, 2, heads_local, head_size
    )
    near_num, near_total, near_max = attend_local(query_heads[:, 0], near_rows)
    level_near = spread_back(
        near_num, near_total, near_max, jnp.zeros((heads_local,), jnp.int32), 1
    )
    mid_q = pick_rows(query_heads, mid_local, rate_mid)[:, 0]
    mid_kv = pick_rows(paired, mid_local, rate_mid)
    mid_group = width_mid // tok_rows
    mid_bits = mid_group.bit_length() - 1
    mid_rows = doubling(mid_kv.reshape(mid_kv.shape[0], -1), mid_bits).reshape(
        SEG, 2, heads_local, head_size
    )
    mid_num, mid_total, mid_max = attend_local(mid_q, mid_rows)
    level_mid = spread_back(mid_num, mid_total, mid_max, mid_local, rate_mid)
    top_q = pick_rows(query_heads, top_local, rate_top)[:, 0]
    top_kv = pick_rows(paired, top_local, rate_top)
    top_rows = lax.all_gather(
        top_kv.reshape(top_kv.shape[0], -1), "seq", axis=0, tiled=True
    ).reshape(SEG, 2, heads_local, head_size)
    top_num, top_total, top_max = attend_local(top_q, top_rows)
    level_top = spread_back(top_num, top_total, top_max, top_local, rate_top)
    levels = [level_near, level_mid, level_top]
    overall = jnp.maximum(jnp.maximum(level_near[2], level_mid[2]), level_top[2])
    numerator = jnp.zeros((tok_rows, heads_local, head_size), jnp.float32)
    row_total = jnp.zeros((tok_rows, heads_local), jnp.float32)
    for level_num, level_total, level_max in levels:
        factor = jnp.exp(level_max - overall)
        numerator = numerator + factor[..., None] * level_num
        row_total = row_total + factor * level_total
    attention = (
        (numerator / row_total[..., None])
        .astype(jnp.bfloat16)
        .reshape(tok_rows, heads_local * head_size)
    )
    result = lax.psum_scatter(
        jnp.dot(attention, out_weight, preferred_element_type=jnp.float32),
        "head",
        scatter_dimension=0,
        tiled=True,
    )
    return result.astype(jnp.bfloat16)


RATE = 4
GROUP = 4
HG = 4
DH = 48
BLK = 128
HALF = 2 * BLK
TOK = 512
SCALE = DH**-0.5 * LOG2E
BUSY = 1 << 33
AHEAD = 4
SAFE = 96.0
CHUNKS = ((0, 4),)
DX = 64


def dot(a, b):
    return jnp.dot(a, b, preferred_element_type=F32)


def dot_nt(a, b):
    return lax.dot_general(a, b, (((1,), (1,)), ((), ())), preferred_element_type=F32)


def class_of_slots(off_mid, off_top):
    first = off_mid
    second = jnp.where(off_top == off_mid, lax.rem(off_mid + 1, RATE), off_top)
    free0 = (first != 0) & (second != 0)
    free1 = (first != 1) & (second != 1)
    third = jnp.where(free0, 0, jnp.where(free1, 1, 2))
    return first, second, third, 6 - first - second - third


def head_of(place, j, p):
    index = place[0][0]
    return ((index & (GROUP - 1)) ^ j) * HG + ((index // GROUP) ^ p)


def offsets_of(place, head):
    return place[1][head], place[2][head]


def token_picker():
    row = lax.broadcasted_iota(jnp.int32, (TOK, TOK), 0)
    col = lax.broadcasted_iota(jnp.int32, (TOK, TOK), 1)
    return (col == RATE * (row % BLK) + row // BLK).astype(BF16)


def fill_class_major(block, picker, scratch):
    scratch[...] = lax.dot_general(
        block, picker, (((0,), (1,)), ((), ())), preferred_element_type=F32
    ).astype(BF16)


def lane_block(index):
    return pl.ds(pl.multiple_of(index * BLK, BLK), BLK)


def head_rows(head):
    return pl.ds(pl.multiple_of(head * DH, 16), DH)


def pack_kernel(index, mid, top, k_hbm, v_hbm, q_hbm, *refs):
    place = (index, mid, top)
    outs, refs = refs[:6], refs[6:]
    blocks, held, packed = refs[:3], refs[3:6], refs[6:12]
    sems_in, sems_out = refs[12:]
    loads = [
        pltpu.make_async_copy(hbm, block, sems_in.at[i])
        for i, (hbm, block) in enumerate(zip((k_hbm, v_hbm, q_hbm), blocks))
    ]
    for load in loads:
        load.start()
    picker = token_picker()
    stores = []
    for n, (load, block, scratch) in enumerate(zip(loads, blocks, held)):
        load.wait()
        fill_class_major(block[...], picker, scratch)
        rows = slice(n * DH, (n + 1) * DH)
        for i, (j, first, count) in enumerate(
            ((0, 0, 4), (1, 0, 4), (2, 0, 2), (3, 0, 2), (2, 2, 2), (3, 2, 2))
        ):
            for p in range(HG):
                head = head_of(place, j, p)
                slots = class_of_slots(*offsets_of(place, head))
                for s in range(count):
                    packed[i][p, rows, s * BLK : (s + 1) * BLK] = scratch[
                        head_rows(head), lane_block(slots[first + s])
                    ]
            store = pltpu.make_async_copy(
                packed[i].at[:, rows], outs[i].at[:, rows], sems_out.at[i, n]
            )
            store.start()
            stores.append(store)
    for store in stores:
        store.wait()


def regroup_kernel(a_ref, b_ref, *refs):
    for s, out in enumerate(refs[-3:]):
        out[0] = a_ref[s + 1, :, 0:HALF]
        out[1] = b_ref[s + 1, :, 0:HALF]


def upright(keys_t):
    return keys_t.T


def largest(blocks):
    best = None
    for block in blocks:
        wide = block.astype(F32)
        length = jnp.sum(wide * wide, axis=0, keepdims=True)
        for low in range(0, block.shape[1], HALF):
            part = length[:, low : low + HALF]
            best = part if best is None else jnp.maximum(best, part)
    return jnp.max(best)


def is_small(query_length, key_length):
    return query_length * key_length * (SCALE * SCALE) < SAFE * SAFE


def column_max(blocks):
    best = jnp.max(blocks[0], axis=0, keepdims=True)
    for block in blocks[1:]:
        best = jnp.maximum(best, jnp.max(block, axis=0, keepdims=True))
    return best * SCALE


def in_stages(items, score, weigh, gather):
    scores = {n: score(item) for n, item in enumerate(items[:AHEAD])}
    weights = weigh(items[0], scores.pop(0))
    for n, item in enumerate(items):
        if n + AHEAD < len(items):
            scores[n + AHEAD] = score(items[n + AHEAD])
        following = weigh(items[n + 1], scores.pop(n + 1)) if n + 1 < len(items) else None
        gather(item, weights)
        weights = following


def near_kernel(inputs, units, tasks, carried, first, step, index, mid, top, *refs):
    place = (index, mid, top)
    pieces = dict(zip(inputs, refs[: len(inputs)]))
    refs = refs[len(inputs) :]
    old = [refs[2 * i : 2 * i + 2] for i in range(carried)]
    outs = refs[2 * carried : 2 * carried + 2 * len(tasks)]
    k_s, v_s = refs[-2:]
    v_s[:, DH:DX, :] = jnp.ones((step, DX - DH, v_s.shape[2]), BF16)
    lane_slot = lax.broadcasted_iota(jnp.int32, (1, HALF), 1) // BLK

    def lookup(j, slot):
        first = 0 if (j, 0) in pieces and pieces[j, 0].shape[2] > HALF else slot // 2 * 2
        return pieces[j, first], (slot - first) * BLK

    chunks = []
    row = 0
    for label, members in units:
        chunks.append((label, slice(row, row + len(members) * BLK)))
        row += len(members) * BLK
    members = [member for _, group in units for member in group]

    def prepare(h):
        for i, (j, slot) in enumerate(members):
            ref, lane = lookup(j, slot)
            rows = slice(i * BLK, (i + 1) * BLK)
            k_s[h, rows, :] = upright(ref[h, 0:DH, lane : lane + BLK])
            v_s[h, 0:DH, rows] = ref[h, DH : 2 * DH, lane : lane + BLK]

    def counted_again(h):
        off_mid, off_top = offsets_of(place, head_of(place, 0, first + pl.program_id(0) * step + h))
        same = off_mid == off_top
        return [
            jnp.where(lane_slot == 0, jnp.where(same, 1.584962500721156, 1.0), 0.0),
            jnp.where(lane_slot == 1, jnp.where(same, 0.0, 1.0), 0.0),
        ]

    def run(heads):
        again = [counted_again(h) for h in heads]
        flat = [
            (h, again_h, query, low, merge, out, i)
            for h, again_h in zip(heads, again)
            for out, group in enumerate(tasks)
            for i, (query, low, merge) in enumerate(group)
        ]

        def score(task):
            h, _, (j, half), low = task[:4]
            ref, lane = lookup(j, 2 * half)
            query = ref[h, 2 * DH :, lane : lane + HALF]
            return [dot(k_s[h, rows, :], query) for _, rows in chunks[low:]]

        scores = score(flat[0])
        for n, (h, again_h, (_, half), low, merge, out, i) in enumerate(flat):
            following = score(flat[n + 1]) if n + 1 < len(flat) else None
            best = column_max(scores)
            if merge is not None:
                acc_in, max_in = old[merge[0]]
                old_max = max_in[h, merge[1], 0:1, :]
                best = jnp.maximum(best, old_max)
            acc = None
            for (label, rows), block in zip(chunks[low:], scores):
                block = block * SCALE
                if half == 0 and label is not None:
                    block = block - (best - again_h[label])
                else:
                    block = block - best
                part = dot(v_s[h, :, rows], jnp.exp2(block).astype(BF16))
                acc = part if acc is None else acc + part
            if merge is not None:
                acc = acc + acc_in[h, merge[1]] * jnp.exp2(old_max - best)
            acc_ref, max_ref = outs[2 * out : 2 * out + 2]
            acc_ref[h, i] = acc
            max_ref[h, i] = jnp.broadcast_to(best, (8, HALF))
            scores = following

    def run_plain():
        again = [counted_again(h) for h in range(step)]
        steps = [
            (h, query, merge, out, i, c, c == low, c == len(chunks) - 1)
            for h in range(step)
            for out, group in enumerate(tasks)
            for i, (query, low, merge) in enumerate(group)
            for c in range(low, len(chunks))
        ]

        def score(item):
            h, (j, half), c = item[0], item[1], item[5]
            ref, lane = lookup(j, 2 * half)
            return dot(k_s[h, chunks[c][1], :], ref[h, 2 * DH :, lane : lane + HALF])

        def weigh(item, block):
            h, (_, half), c = item[0], item[1], item[5]
            label = chunks[c][0]
            block = block * SCALE
            if half == 0 and label is not None:
                block = block + again[h][label]
            return jnp.exp2(block).astype(BF16)

        held = {}

        def gather(item, weights):
            h, _, merge, out, i, c, begins, ends = item
            part = dot(v_s[h, :, chunks[c][1]], weights)
            acc = part if begins else held[0] + part
            if ends:
                if merge is not None:
                    acc = acc + old[merge[0]][0][h, merge[1]]
                acc_ref, max_ref = outs[2 * out : 2 * out + 2]
                acc_ref[h, i] = acc
                max_ref[h, i] = jnp.zeros((8, HALF), F32)
            held[0] = acc

        in_stages(steps, score, weigh, gather)

    for h in range(step):
        prepare(h)
    plain = is_small(
        largest([ref[h, 2 * DH :, :] for ref in pieces.values() for h in range(step)]),
        largest([ref[h, 0:DH, :] for ref in pieces.values() for h in range(step)]),
    )
    for _, max_in in old:
        plain = plain & (jnp.max(jnp.abs(max_in[...])) == 0.0)

    @pl.when(plain)
    def _():
        run_plain()

    @pl.when(jnp.logical_not(plain))
    def _():
        @pl.loop(0, step)
        def _(h):
            run([h])


def far_slots(place):
    off_mid, off_top = offsets_of(place, head_of(place, 0, 0))
    same = off_mid == off_top
    return same, (0, jnp.where(same, 0, 1))


def far_pieces(place, sources, k_s, v_s, q_s):
    _, slots = far_slots(place)
    for s, pair in enumerate(sources):
        for i, ref in enumerate(pair):
            here = slice(i * BLK, (i + 1) * BLK)
            for level, slot in enumerate(slots):
                k_s[level, s, here, :] = upright(ref[0:DH, lane_block(slot)])
                v_s[level, s, 0:DH, here] = ref[DH : 2 * DH, lane_block(slot)]
                q_s[level, s, :, here] = ref[2 * DH : 3 * DH, lane_block(slot)]
    v_s[:, :, DH:DX, :] = jnp.ones((2, RATE, DX - DH, HALF), BF16)


def far_lengths(sources):
    every = [ref for pair in sources for ref in pair]
    return (
        largest([ref[2 * DH : 3 * DH, 0:HALF] for ref in every]),
        largest([ref[0:DH, 0:HALF] for ref in every]),
    )


def far_own_kernel(index, mid, top, own0, own1, beyond1, beyond2, beyond3, *refs):
    k_s, v_s, q_s, acc_ref, max_ref, length_ref = refs
    sources = [(own0.at[0], own1.at[0])] + [
        (ref.at[0], ref.at[1]) for ref in (beyond1, beyond2, beyond3)
    ]
    far_pieces((index, mid, top), sources, k_s, v_s, q_s)

    def run_plain():
        steps = [(level, d) for level in range(2) for d in range(1, RATE)]

        def segment(s, carry):
            def score(item):
                level, d = item
                return dot(k_s[level, s ^ d], q_s[level, s])

            def weigh(item, block):
                return jnp.exp2(block * SCALE).astype(BF16)

            held = {}

            def gather(item, weights):
                level, d = item
                part = dot(v_s[level, s ^ d], weights)
                held[0] = part if d == 1 else held[0] + part
                if d == RATE - 1:
                    acc_ref[level, s] = held[0]
                    max_ref[level, s] = jnp.zeros((8, HALF), F32)

            in_stages(steps, score, weigh, gather)
            return carry

        lax.fori_loop(0, RATE, segment, 0, unroll=2)

    def run():
        def segment(s, carry):
            def score(level):
                return [dot(k_s[level, s ^ d], q_s[level, s]) for d in range(1, RATE)]

            scores = score(0)
            for level in range(2):
                following = score(1) if level == 0 else None
                best = column_max(scores)
                acc = None
                for d in range(1, RATE):
                    block = scores[d - 1] * SCALE - best
                    part = dot(v_s[level, s ^ d], jnp.exp2(block).astype(BF16))
                    acc = part if acc is None else acc + part
                acc_ref[level, s] = acc
                max_ref[level, s] = jnp.broadcast_to(best, (8, HALF))
                scores = following
            return carry

        lax.fori_loop(0, RATE, segment, 0)

    query_length, key_length = far_lengths(sources)
    length_ref[0] = query_length
    length_ref[1] = key_length
    plain = is_small(query_length, key_length)
    pl.when(plain)(run_plain)
    pl.when(jnp.logical_not(plain))(run)


def far_kernel(index, mid, top, *refs):
    place = (index, mid, top)
    sel2, sel3, beyond3, beyond2, beyond1, k_own, v_own, q_own, acc_in, max_in, length_in = refs[
        :11
    ]
    outs = refs[11 : 11 + RATE]
    k_s, v_s, q_s, result_s, tail_s = refs[11 + RATE :]
    same, _ = far_slots(place)
    sources = [(sel2.at[0], sel3.at[0])] + [
        (ref.at[0], ref.at[1]) for ref in (beyond1, beyond2, beyond3)
    ]
    far_pieces(place, sources, k_s, v_s, q_s)
    tail_s[...] = jnp.zeros(tail_s.shape, F32)

    tasks = [(level, chip) for level in range(2) for chip in range(2)]
    held = ((k_own, v_own, q_own), (k_s, v_s, q_s))

    def blocks(s, chip):
        return [(held[c], s ^ d) for d in range(1, RATE) for c in ((1,), (0, 1))[chip]]

    def finish(s, level, chip, acc, best):
        total = acc[DH : DH + 1, :]
        result = (acc[0:DH, :] / total).astype(BF16)
        lse = best + jnp.log2(total)
        if level == 0:
            lse = jnp.where(same, lse + 1.0, lse)
        else:
            lse = jnp.where(same, -1e30, lse)
        high = lse.astype(BF16).astype(F32)
        middle = (lse - high).astype(BF16).astype(F32)
        low = lse - high - middle
        for i in range(2):
            n = 2 * (2 * chip + i) + level
            mine = slice(i * BLK, (i + 1) * BLK)
            result_s[s, :, n * BLK : (n + 1) * BLK] = result[:, mine]
            for k, part in enumerate((high, middle, low)):
                tail_s[s, 3 * n + k : 3 * n + k + 1, :] = part[:, mine]

    def run_plain():
        def segment(s, carry):
            steps = [
                (level, chip, keys, b, n)
                for level, chip in tasks
                for n, (keys, b) in enumerate(blocks(s, chip))
            ]

            def score(item):
                level, chip, keys, b, _ = item
                return dot(keys[0][level, b], held[chip][2][level, s])

            def weigh(item, block):
                return jnp.exp2(block * SCALE).astype(BF16)

            sums = {}

            def gather(item, weights):
                level, chip, keys, b, n = item
                part = dot(keys[1][level, b], weights)
                sums[0] = sums[0] + part if n else part
                if n + 1 == len(blocks(s, chip)):
                    acc = sums[0] + acc_in[level, s] if chip == 0 else sums[0]
                    finish(s, level, chip, acc, jnp.zeros((1, HALF), F32))

            in_stages(steps, score, weigh, gather)
            return carry

        lax.fori_loop(0, RATE, segment, 0, unroll=2)

    def run():
        def segment(s, carry):
            for level, chip in tasks:
                scores = [
                    dot(keys[0][level, b], held[chip][2][level, s]) for keys, b in blocks(s, chip)
                ]
                best = column_max(scores)
                acc = jnp.zeros((DX, HALF), F32)
                if chip == 0:
                    old_max = max_in[level, s, 0:1, :]
                    best = jnp.maximum(best, old_max)
                    acc = acc_in[level, s] * jnp.exp2(old_max - best)
                for block, (keys, b) in zip(scores, blocks(s, chip)):
                    acc += dot(keys[1][level, b], jnp.exp2(block * SCALE - best).astype(BF16))
                finish(s, level, chip, acc, best)
            return carry

        lax.fori_loop(0, RATE, segment, 0)

    query_length, key_length = far_lengths(sources)
    plain = is_small(
        jnp.maximum(query_length, length_in[0]), jnp.maximum(key_length, length_in[1])
    )
    pl.when(plain)(run_plain)
    pl.when(jnp.logical_not(plain))(run)
    for s in range(RATE):
        outs[s][:, : GROUP * HALF] = result_s[s]
        outs[s][:, GROUP * HALF :] = tail_s[s].astype(BF16)


def join(acc, best, far, j):
    tail = far[:, GROUP * HALF :].astype(F32)
    lse = jnp.concatenate(
        [
            tail[3 * n : 3 * n + 1] + tail[3 * n + 1 : 3 * n + 2] + tail[3 * n + 2 : 3 * n + 3]
            for n in (2 * j, 2 * j + 1)
        ],
        axis=1,
    )
    overall = jnp.maximum(best, lse)
    near_factor, far_factor = jnp.exp2(best - overall), jnp.exp2(lse - overall)
    total = acc[DH : DH + 1] * near_factor + far_factor
    value = far[:, j * HALF : (j + 1) * HALF].astype(F32) * far_factor
    return ((acc[0:DH] * near_factor + value) / total).astype(BF16)


def combine_kernel(chip, acc_ref, max_ref, *refs):
    far, outs = refs[:-2][::-1], refs[-2:]
    for i in range(2):
        for p, results in enumerate(far):
            outs[i][p, :, 0:HALF] = join(
                acc_ref[p, 2 * i], max_ref[p, 2 * i, 0:1, :], results, 2 * chip + i
            )
            acc = acc_ref[p, 2 * i + 1]
            outs[i][p, :, HALF:] = (acc[0:DH] / acc[DH : DH + 1]).astype(BF16)


def project_kernel(sources, index, mid, top, *refs):
    place = (index, mid, top)
    parts, (w_ref, out_ref, held) = refs[:-3], refs[-3:]
    for (j, first), part in zip(sources, parts):
        for p in range(part.shape[0]):
            head = head_of(place, j, first + p)
            slots = class_of_slots(*offsets_of(place, head))
            for s in range(RATE):
                held[head_rows(head), lane_block(slots[s])] = part[
                    p, :, s * BLK : (s + 1) * BLK
                ]
    row = lax.broadcasted_iota(jnp.int32, (TOK, TOK), 0)
    col = lax.broadcasted_iota(jnp.int32, (TOK, TOK), 1)
    picker = (row == RATE * (col % BLK) + col // BLK).astype(BF16)
    attention = dot_nt(picker, held[...]).astype(BF16)
    out_ref[...] = dot(attention, w_ref[...]).astype(BF16)


def whole(shape):
    return pl.BlockSpec(shape, lambda *_: (0,) * len(shape))


def per_head(shape, skip=0):
    return pl.BlockSpec(shape, lambda h, *_: (h + skip,) + (0,) * (len(shape) - 1))


def call(
    kernel, scalars, args, grid, in_specs, outs, scratch, scores,
    limit=VMEM_LIMIT, after=(), through=(), busy=0,
):
    known = len(scalars) + len(args)
    extra = (*after, *through)
    count = len(outs)
    anywhere = pl.BlockSpec(memory_space=pl.ANY)

    def body(*refs):
        results = refs[known + len(extra) :]
        kernel(*refs[:known], *results[:count], *results[count + len(through) :])

    return pl.pallas_call(
        body if extra else kernel,
        grid_spec=pltpu.PrefetchScalarGridSpec(
            num_scalar_prefetch=len(scalars),
            grid=grid,
            in_specs=list(in_specs) + [anywhere] * len(extra),
            out_specs=[spec for spec, _ in outs] + [anywhere] * len(through),
            scratch_shapes=scratch,
        ),
        out_shape=[shape for _, shape in outs]
        + [jax.ShapeDtypeStruct(x.shape, x.dtype) for x in through],
        input_output_aliases={known + len(after) + i: count + i for i in range(len(through))},
        compiler_params=pltpu.CompilerParams(vmem_limit_bytes=limit),
        cost_estimate=pl.CostEstimate(flops=busy, bytes_accessed=0, transcendentals=0),
    )(*scalars, *args, *extra)


def handed_on(arrays):
    return call(lambda: None, (), (), (1,), [], [], [], 0, through=tuple(arrays))


def within(array, apart):
    count = lax.axis_size("seq")
    return lax.ppermute(array, "seq", [(i, i ^ apart) for i in range(count)])


def swap_segments(arrays):
    moved = {s: within(arrays[s - 1], GROUP * s) for s in (3, 2, 1)}
    return [moved[s] for s in (1, 2, 3)]


def shards_four(queries, key_states, value_states, offsets_mid, offsets_top, out_weight):
    width = queries.shape[1]
    place = (lax.axis_index("seq").astype(jnp.int32).reshape(1), offsets_mid, offsets_top)
    full = jax.ShapeDtypeStruct((HG, 3 * DH, TOK), BF16)
    piece = jax.ShapeDtypeStruct((HG, 3 * DH, HALF), BF16)
    pair = jax.ShapeDtypeStruct((2, 3 * DH, HALF), BF16)
    anywhere = pl.BlockSpec(memory_space=pl.ANY)
    shapes = [full] * 2 + [piece] * 4
    own0, own1, sel2, sel3, rest2, rest3 = call(
        pack_kernel, place, (key_states, value_states, queries), (1,),
        [anywhere] * 3,
        [(anywhere, shape) for shape in shapes],
        [pltpu.VMEM((TOK, width), BF16)] * 3
        + [pltpu.VMEM((width, TOK), BF16)] * 3
        + [pltpu.VMEM(shape.shape, BF16) for shape in shapes]
        + [pltpu.SemaphoreType.DMA((3,)), pltpu.SemaphoreType.DMA((6, 3))],
        1 << 19, VMEM_MOST,
    )
    own1 = within(own1, 1)
    sel2, sel3 = within(sel2, 2), within(sel3, 3)

    def regroup(a, b, **order):
        return call(
            regroup_kernel, (), (a, b), (1,),
            [whole(a.shape), whole(b.shape)], [(whole(pair.shape), pair)] * 3,
            [], 1 << 17, **order,
        )

    def near(held, units, tasks, old, first=0, heads=HG, step=2, **order):
        sizes = [len(members) * BLK for _, members in units]
        scores = sum(sum(sizes[low:]) * HALF for group in tasks for _, low, _ in group)
        arrays = [*held.values(), *[x for one in old for x in one]]
        shapes = [
            jax.ShapeDtypeStruct((heads, len(group), rows, HALF), F32)
            for group in tasks
            for rows in (DX, 8)
        ]
        return call(
            functools.partial(near_kernel, list(held), units, tasks, len(old), first, step),
            place, arrays, (heads // step,),
            [per_head((step,) + x.shape[1:], first // step) for x in arrays],
            [(per_head((step,) + x.shape[1:]), x) for x in shapes],
            [
                pltpu.VMEM((step, sum(sizes), DH), BF16),
                pltpu.VMEM((step, DX, sum(sizes)), BF16),
            ],
            heads * scores, **order,
        )

    def units_of(a, b):
        return [(0, [(a, 0), (b, 0)]), (1, [(a, 1), (b, 1)])], [
            (None, [(a, 2), (a, 3), (b, 2), (b, 3)])
        ]

    own_sel, own_rest = units_of(0, 1)
    other_sel, other_rest = units_of(2, 3)
    own = [(0, 0), (0, 1), (1, 0), (1, 1)]

    ours = regroup(own0, own1)
    ours = swap_segments(ours)
    held = {(0, 0): own0, (1, 0): own1}
    state_own = near(held, own_sel + own_rest, [[(q, 0, None) for q in own]], [])
    *theirs, rest2, rest3 = regroup(sel2, sel3, after=state_own[1:], through=(rest2, rest3))
    theirs = swap_segments(theirs)
    rest2, rest3 = within(rest2, 2), within(rest3, 3)

    held.update({(2, 0): sel2, (3, 0): sel3})
    out = near(
        held, own_sel + own_rest + other_sel,
        [
            [(q, 3, (0, i)) for i, q in enumerate(own)],
            [((2, 0), 0, None), ((3, 0), 0, None)],
        ],
        [state_own],
        after=ours[::-1],
    )
    state_own, state_sel = out[:2], out[2:]

    result = jax.ShapeDtypeStruct((DH, GROUP * HALF + BLK), BF16)
    piece_0 = pl.BlockSpec((1, 3 * DH, HALF), lambda *_: (0, 0, 0))
    pieces_shapes = [
        jax.ShapeDtypeStruct((2, RATE, HALF, DH), BF16),
        jax.ShapeDtypeStruct((2, RATE, DX, HALF), BF16),
        jax.ShapeDtypeStruct((2, RATE, DH, HALF), BF16),
    ]
    sums_shapes = [
        jax.ShapeDtypeStruct((2, RATE, DX, HALF), F32),
        jax.ShapeDtypeStruct((2, RATE, 8, HALF), F32),
    ]
    in_scalars = pl.BlockSpec(memory_space=pltpu.SMEM)
    far_own = call(
        far_own_kernel, place, (own0, own1, *ours), (1,),
        [piece_0] * 2 + [whole(pair.shape)] * 3,
        [(whole(x.shape), x) for x in pieces_shapes + sums_shapes]
        + [(in_scalars, jax.ShapeDtypeStruct((2,), F32))],
        [], RATE * 2 * 3 * HALF * HALF, after=(state_sel[1],),
    )
    results = call(
        far_kernel, place, (sel2, sel3, *theirs[::-1], *far_own), (1,),
        [piece_0] * 2 + [whole(pair.shape)] * 3
        + [whole(x.shape) for x in far_own[:-1]] + [in_scalars],
        [(whole(result.shape), result)] * RATE,
        [pltpu.VMEM(x.shape, BF16) for x in pieces_shapes]
        + [
            pltpu.VMEM((RATE, DH, GROUP * HALF), BF16),
            pltpu.VMEM((RATE, DH, BLK), F32),
        ],
        RATE * 2 * 3 * 3 * HALF * HALF, busy=BUSY,
    )
    back = [results[0]] + swap_segments(results[1:])

    held.update({(2, 2): rest2, (3, 2): rest3})
    units = own_sel + own_rest + other_sel + other_rest

    def combine(chip, state, far, **order):
        heads = state[0].shape[0]
        attended = jax.ShapeDtypeStruct((heads, DH, TOK), BF16)
        return call(
            functools.partial(combine_kernel, chip), (), (*state, *far[::-1]), (1,),
            [whole(x.shape) for x in state] + [whole(result.shape)] * heads,
            [(whole(attended.shape), attended)] * 2,
            [],
            1 << 18, **order,
        )

    parts = {}
    last = results[0]
    for first, heads in CHUNKS:
        state_other = near(
            held, units,
            [
                [
                    ((2, 0), 5, (0, 0)), ((2, 1), 0, None),
                    ((3, 0), 5, (0, 1)), ((3, 1), 0, None),
                ]
            ],
            [state_sel],
            first, heads, 2, after=(last,),
        )
        part2, part3 = combine(1, state_other, back[first : first + heads])
        parts[2, first], parts[3, first] = within(part2, 2), within(part3, 3)
        last = part3
    state_own = near(
        {(2, 2): rest2, (3, 2): rest3, **{q: held[q] for q in ((0, 0), (1, 0))}},
        other_rest,
        [[(q, 0, (0, i)) for i, q in enumerate(own)]],
        [state_own],
        after=(last,),
    )
    early = [parts[j, first] for first, _ in CHUNKS[:-1] for j in (2, 3)]
    part0, part1 = combine(0, state_own, back, after=early)
    parts = dict(zip(parts, handed_on(parts.values())))
    parts[0, 0], parts[1, 0] = part0, within(part1, 1)
    return call(
        functools.partial(project_kernel, list(parts)), place, (*parts.values(), out_weight), (1,),
        [whole(x.shape) for x in parts.values()] + [whole((width, width))],
        [(whole((TOK, width)), jax.ShapeDtypeStruct((TOK, width), BF16))],
        [pltpu.VMEM((width, TOK), BF16)],
        1 << 18,
    )[0]


def shards(queries, key_states, value_states, offsets_mid, offsets_top, out_weight):
    tokens, width = queries.shape
    heads = offsets_mid.shape[0]
    fits = (
        lax.axis_size("head") == 1
        and lax.axis_size("seq") == GROUP * RATE
        and tokens == TOK
        and heads == GROUP * HG
        and width == heads * DH
    )
    run = shards_four if fits else shards_general
    return run(queries, key_states, value_states, offsets_mid, offsets_top, out_weight)


def solution(mesh):
    in_specs = (
        P(("slide", "seq"), "head"),
        P(("slide", "seq"), "head"),
        P(("slide", "seq"), "head"),
        P(),
        P(),
        P("head", None),
    )
    out_specs = P(("slide", "seq", "head"), None)
    return jax.shard_map(shards, mesh=mesh, in_specs=in_specs, out_specs=out_specs, check_vma=False)
```

```python
import functools

import jax
import jax.numpy as jnp
from jax import lax
from jax.experimental import pallas as pl
from jax.experimental.pallas import tpu as pltpu
from jax.sharding import PartitionSpec as P

SEG = 2048
LOG2E = 1.4426950408889634
VMEM_LIMIT = 40 * 1024 * 1024
VMEM_MOST = 60 * 1024 * 1024
BF16 = jnp.bfloat16
F32 = jnp.float32


def partner_2(block, axis, apart):
    count = lax.axis_size(axis)
    route = []
    for low in range(count):
        high = low | 1 << apart
        if high != low and high < count:
            route += [(low, high), (high, low)]
    return lax.ppermute(block, axis, route)


def attend_head(triple_in):
    query_rows, key_rows, value_rows = triple_in
    score_scale = query_rows.shape[-1] ** (-0.5)
    scores = jnp.dot(query_rows, key_rows.T, preferred_element_type=jnp.float32) * score_scale
    row_max = jnp.max(scores, axis=1)
    shifted = jnp.exp(scores - row_max[:, None])
    row_total = jnp.sum(shifted, axis=1)
    weights = shifted.astype(jnp.bfloat16)
    numerator = jnp.dot(weights, value_rows, preferred_element_type=jnp.float32)
    return (numerator, row_total, row_max)


def attend_local(query_rows, pair_rows):
    return lax.map(
        attend_head,
        (
            query_rows.transpose(1, 0, 2),
            pair_rows[:, 0].transpose(1, 0, 2),
            pair_rows[:, 1].transpose(1, 0, 2),
        ),
    )


def pick_rows(states, offsets, rate):
    row_count, inner_count, heads_here, head_width = states.shape
    picker = (jnp.arange(rate)[:, None] == offsets[None, :]).astype(jnp.bfloat16)
    folded = states.reshape(row_count // rate, rate, inner_count, heads_here, head_width)
    return jnp.einsum("archd,rh->achd", folded, picker, preferred_element_type=jnp.float32).astype(
        jnp.bfloat16
    )


def spread_back(numerator, row_total, row_max, offsets, rate):
    heads_here, picked_count, head_width = numerator.shape
    chosen = jnp.arange(rate)[:, None] == offsets[None, :]
    full_num = jnp.where(chosen[None, :, :, None], numerator.transpose(1, 0, 2)[:, None], 0.0)
    full_total = jnp.where(chosen[None], row_total.T[:, None], 0.0)
    full_max = jnp.where(chosen[None], row_max.T[:, None], -1e30)
    return (
        full_num.reshape(picked_count * rate, heads_here, head_width),
        full_total.reshape(picked_count * rate, heads_here),
        full_max.reshape(picked_count * rate, heads_here),
    )


def doubling(buffer, steps_count):
    position = lax.axis_index("seq")
    for bit_index in range(steps_count):
        partner = partner_2(buffer, "seq", bit_index)
        is_lower = position >> bit_index & 1 == 0
        buffer = jnp.where(
            is_lower, jnp.concatenate([buffer, partner], 0), jnp.concatenate([partner, buffer], 0)
        )
    return buffer


def shards_general(queries, key_states, value_states, offsets_mid, offsets_top, out_weight):
    tok_rows = queries.shape[0]
    heads_local = offsets_mid.shape[0] // lax.axis_size("head")
    head_size = queries.shape[1] // heads_local
    seq_devices = lax.axis_size("seq")
    seq_total = tok_rows * seq_devices
    width_mid = min(16 * SEG, seq_total)
    rate_mid = width_mid // SEG
    rate_top = seq_total // SEG
    start_head = lax.axis_index("head") * heads_local
    mid_local = lax.dynamic_slice(offsets_mid, (start_head,), (heads_local,))
    top_local = lax.dynamic_slice(offsets_top, (start_head,), (heads_local,))
    query_heads = queries.reshape(tok_rows, 1, heads_local, head_size)
    paired = jnp.stack([key_states, value_states], axis=1).reshape(
        tok_rows, 2, heads_local, head_size
    )
    near_bits = (SEG // tok_rows).bit_length() - 1
    near_rows = doubling(paired.reshape(tok_rows, -1), near_bits).reshape(
        SEG, 2, heads_local, head_size
    )
    near_num, near_total, near_max = attend_local(query_heads[:, 0], near_rows)
    level_near = spread_back(
        near_num, near_total, near_max, jnp.zeros((heads_local,), jnp.int32), 1
    )
    mid_q = pick_rows(query_heads, mid_local, rate_mid)[:, 0]
    mid_kv = pick_rows(paired, mid_local, rate_mid)
    mid_group = width_mid // tok_rows
    mid_bits = mid_group.bit_length() - 1
    mid_rows = doubling(mid_kv.reshape(mid_kv.shape[0], -1), mid_bits).reshape(
        SEG, 2, heads_local, head_size
    )
    mid_num, mid_total, mid_max = attend_local(mid_q, mid_rows)
    level_mid = spread_back(mid_num, mid_total, mid_max, mid_local, rate_mid)
    top_q = pick_rows(query_heads, top_local, rate_top)[:, 0]
    top_kv = pick_rows(paired, top_local, rate_top)
    top_rows = lax.all_gather(
        top_kv.reshape(top_kv.shape[0], -1), "seq", axis=0, tiled=True
    ).reshape(SEG, 2, heads_local, head_size)
    top_num, top_total, top_max = attend_local(top_q, top_rows)
    level_top = spread_back(top_num, top_total, top_max, top_local, rate_top)
    levels = [level_near, level_mid, level_top]
    overall = jnp.maximum(jnp.maximum(level_near[2], level_mid[2]), level_top[2])
    numerator = jnp.zeros((tok_rows, heads_local, head_size), jnp.float32)
    row_total = jnp.zeros((tok_rows, heads_local), jnp.float32)
    for level_num, level_total, level_max in levels:
        factor = jnp.exp(level_max - overall)
        numerator = numerator + factor[..., None] * level_num
        row_total = row_total + factor * level_total
    attention = (
        (numerator / row_total[..., None])
        .astype(jnp.bfloat16)
        .reshape(tok_rows, heads_local * head_size)
    )
    result = lax.psum_scatter(
        jnp.dot(attention, out_weight, preferred_element_type=jnp.float32),
        "head",
        scatter_dimension=0,
        tiled=True,
    )
    return result.astype(jnp.bfloat16)


RATE = 4
GROUP = 4
HG = 4
DH = 48
BLK = 128
HALF = 2 * BLK
TOK = 512
SCALE = DH**-0.5 * LOG2E
BUSY = 1 << 33
AHEAD = 4
SAFE = 96.0
CHUNKS = ((0, 2), (2, 2))
DX = 64


def dot(a, b):
    return jnp.dot(a, b, preferred_element_type=F32)


def dot_nt(a, b):
    return lax.dot_general(a, b, (((1,), (1,)), ((), ())), preferred_element_type=F32)


def class_of_slots(off_mid, off_top):
    first = off_mid
    second = jnp.where(off_top == off_mid, lax.rem(off_mid + 1, RATE), off_top)
    free0 = (first != 0) & (second != 0)
    free1 = (first != 1) & (second != 1)
    third = jnp.where(free0, 0, jnp.where(free1, 1, 2))
    return first, second, third, 6 - first - second - third


def head_of(place, j, p):
    index = place[0][0]
    return ((index & (GROUP - 1)) ^ j) * HG + ((index // GROUP) ^ p)


def offsets_of(place, head):
    return place[1][head], place[2][head]


def token_picker():
    row = lax.broadcasted_iota(jnp.int32, (TOK, TOK), 0)
    col = lax.broadcasted_iota(jnp.int32, (TOK, TOK), 1)
    return (col == RATE * (row % BLK) + row // BLK).astype(BF16)


def fill_class_major(block, picker, scratch):
    scratch[...] = lax.dot_general(
        block, picker, (((0,), (1,)), ((), ())), preferred_element_type=F32
    ).astype(BF16)


def lane_block(index):
    return pl.ds(pl.multiple_of(index * BLK, BLK), BLK)


def head_rows(head):
    return pl.ds(pl.multiple_of(head * DH, 16), DH)


def pack_kernel(index, mid, top, k_hbm, v_hbm, q_hbm, *refs):
    place = (index, mid, top)
    outs, refs = refs[:6], refs[6:]
    blocks, held, packed = refs[:3], refs[3:6], refs[6:12]
    sems_in, sems_out = refs[12:]
    loads = [
        pltpu.make_async_copy(hbm, block, sems_in.at[i])
        for i, (hbm, block) in enumerate(zip((k_hbm, v_hbm, q_hbm), blocks))
    ]
    for load in loads:
        load.start()
    picker = token_picker()
    stores = []
    for n, (load, block, scratch) in enumerate(zip(loads, blocks, held)):
        load.wait()
        fill_class_major(block[...], picker, scratch)
        rows = slice(n * DH, (n + 1) * DH)
        for i, (j, first, count) in enumerate(
            ((0, 0, 4), (1, 0, 4), (2, 0, 2), (3, 0, 2), (2, 2, 2), (3, 2, 2))
        ):
            for p in range(HG):
                head = head_of(place, j, p)
                slots = class_of_slots(*offsets_of(place, head))
                for s in range(count):
                    packed[i][p, rows, s * BLK : (s + 1) * BLK] = scratch[
                        head_rows(head), lane_block(slots[first + s])
                    ]
            store = pltpu.make_async_copy(
                packed[i].at[:, rows], outs[i].at[:, rows], sems_out.at[i, n]
            )
            store.start()
            stores.append(store)
    for store in stores:
        store.wait()


def regroup_kernel(a_ref, b_ref, *refs):
    for s, out in enumerate(refs[-3:]):
        out[0] = a_ref[s + 1, :, 0:HALF]
        out[1] = b_ref[s + 1, :, 0:HALF]


def upright(keys_t):
    return keys_t.T


def largest(blocks):
    best = None
    for block in blocks:
        wide = block.astype(F32)
        length = jnp.sum(wide * wide, axis=0, keepdims=True)
        for low in range(0, block.shape[1], HALF):
            part = length[:, low : low + HALF]
            best = part if best is None else jnp.maximum(best, part)
    return jnp.max(best)


def is_small(query_length, key_length):
    return query_length * key_length * (SCALE * SCALE) < SAFE * SAFE


def column_max(blocks):
    best = jnp.max(blocks[0], axis=0, keepdims=True)
    for block in blocks[1:]:
        best = jnp.maximum(best, jnp.max(block, axis=0, keepdims=True))
    return best * SCALE


def in_stages(items, score, weigh, gather):
    scores = {n: score(item) for n, item in enumerate(items[:AHEAD])}
    weights = weigh(items[0], scores.pop(0))
    for n, item in enumerate(items):
        if n + AHEAD < len(items):
            scores[n + AHEAD] = score(items[n + AHEAD])
        following = weigh(items[n + 1], scores.pop(n + 1)) if n + 1 < len(items) else None
        gather(item, weights)
        weights = following


def near_kernel(inputs, units, tasks, carried, first, step, index, mid, top, *refs):
    place = (index, mid, top)
    pieces = dict(zip(inputs, refs[: len(inputs)]))
    refs = refs[len(inputs) :]
    old = [refs[2 * i : 2 * i + 2] for i in range(carried)]
    outs = refs[2 * carried : 2 * carried + 2 * len(tasks)]
    k_s, v_s = refs[-2:]
    v_s[:, DH:DX, :] = jnp.ones((step, DX - DH, v_s.shape[2]), BF16)
    lane_slot = lax.broadcasted_iota(jnp.int32, (1, HALF), 1) // BLK

    def lookup(j, slot):
        first = 0 if (j, 0) in pieces and pieces[j, 0].shape[2] > HALF else slot // 2 * 2
        return pieces[j, first], (slot - first) * BLK

    chunks = []
    row = 0
    for label, members in units:
        chunks.append((label, slice(row, row + len(members) * BLK)))
        row += len(members) * BLK
    members = [member for _, group in units for member in group]

    def prepare(h):
        for i, (j, slot) in enumerate(members):
            ref, lane = lookup(j, slot)
            rows = slice(i * BLK, (i + 1) * BLK)
            k_s[h, rows, :] = upright(ref[h, 0:DH, lane : lane + BLK])
            v_s[h, 0:DH, rows] = ref[h, DH : 2 * DH, lane : lane + BLK]

    def counted_again(h):
        off_mid, off_top = offsets_of(place, head_of(place, 0, first + pl.program_id(0) * step + h))
        same = off_mid == off_top
        return [
            jnp.where(lane_slot == 0, jnp.where(same, 1.584962500721156, 1.0), 0.0),
            jnp.where(lane_slot == 1, jnp.where(same, 0.0, 1.0), 0.0),
        ]

    def run(heads):
        again = [counted_again(h) for h in heads]
        flat = [
            (h, again_h, query, low, merge, out, i)
            for h, again_h in zip(heads, again)
            for out, group in enumerate(tasks)
            for i, (query, low, merge) in enumerate(group)
        ]

        def score(task):
            h, _, (j, half), low = task[:4]
            ref, lane = lookup(j, 2 * half)
            query = ref[h, 2 * DH :, lane : lane + HALF]
            return [dot(k_s[h, rows, :], query) for _, rows in chunks[low:]]

        scores = score(flat[0])
        for n, (h, again_h, (_, half), low, merge, out, i) in enumerate(flat):
            following = score(flat[n + 1]) if n + 1 < len(flat) else None
            best = column_max(scores)
            if merge is not None:
                acc_in, max_in = old[merge[0]]
                old_max = max_in[h, merge[1], 0:1, :]
                best = jnp.maximum(best, old_max)
            acc = None
            for (label, rows), block in zip(chunks[low:], scores):
                block = block * SCALE
                if half == 0 and label is not None:
                    block = block - (best - again_h[label])
                else:
                    block = block - best
                part = dot(v_s[h, :, rows], jnp.exp2(block).astype(BF16))
                acc = part if acc is None else acc + part
            if merge is not None:
                acc = acc + acc_in[h, merge[1]] * jnp.exp2(old_max - best)
            acc_ref, max_ref = outs[2 * out : 2 * out + 2]
            acc_ref[h, i] = acc
            max_ref[h, i] = jnp.broadcast_to(best, (8, HALF))
            scores = following

    def run_plain():
        again = [counted_again(h) for h in range(step)]
        steps = [
            (h, query, merge, out, i, c, c == low, c == len(chunks) - 1)
            for h in range(step)
            for out, group in enumerate(tasks)
            for i, (query, low, merge) in enumerate(group)
            for c in range(low, len(chunks))
        ]

        def score(item):
            h, (j, half), c = item[0], item[1], item[5]
            ref, lane = lookup(j, 2 * half)
            return dot(k_s[h, chunks[c][1], :], ref[h, 2 * DH :, lane : lane + HALF])

        def weigh(item, block):
            h, (_, half), c = item[0], item[1], item[5]
            label = chunks[c][0]
            block = block * SCALE
            if half == 0 and label is not None:
                block = block + again[h][label]
            return jnp.exp2(block).astype(BF16)

        held = {}

        def gather(item, weights):
            h, _, merge, out, i, c, begins, ends = item
            part = dot(v_s[h, :, chunks[c][1]], weights)
            acc = part if begins else held[0] + part
            if ends:
                if merge is not None:
                    acc = acc + old[merge[0]][0][h, merge[1]]
                acc_ref, max_ref = outs[2 * out : 2 * out + 2]
                acc_ref[h, i] = acc
                max_ref[h, i] = jnp.zeros((8, HALF), F32)
            held[0] = acc

        in_stages(steps, score, weigh, gather)

    for h in range(step):
        prepare(h)
    plain = is_small(
        largest([ref[h, 2 * DH :, :] for ref in pieces.values() for h in range(step)]),
        largest([ref[h, 0:DH, :] for ref in pieces.values() for h in range(step)]),
    )
    for _, max_in in old:
        plain = plain & (jnp.max(jnp.abs(max_in[...])) == 0.0)

    @pl.when(plain)
    def _():
        run_plain()

    @pl.when(jnp.logical_not(plain))
    def _():
        @pl.loop(0, step)
        def _(h):
            run([h])


def far_slots(place):
    off_mid, off_top = offsets_of(place, head_of(place, 0, 0))
    same = off_mid == off_top
    return same, (0, jnp.where(same, 0, 1))


def far_pieces(place, sources, k_s, v_s, q_s):
    _, slots = far_slots(place)
    for s, pair in enumerate(sources):
        for i, ref in enumerate(pair):
            here = slice(i * BLK, (i + 1) * BLK)
            for level, slot in enumerate(slots):
                k_s[level, s, here, :] = upright(ref[0:DH, lane_block(slot)])
                v_s[level, s, 0:DH, here] = ref[DH : 2 * DH, lane_block(slot)]
                q_s[level, s, :, here] = ref[2 * DH : 3 * DH, lane_block(slot)]
    v_s[:, :, DH:DX, :] = jnp.ones((2, RATE, DX - DH, HALF), BF16)


def far_lengths(sources):
    every = [ref for pair in sources for ref in pair]
    return (
        largest([ref[2 * DH : 3 * DH, 0:HALF] for ref in every]),
        largest([ref[0:DH, 0:HALF] for ref in every]),
    )


def far_own_kernel(index, mid, top, own0, own1, beyond1, beyond2, beyond3, *refs):
    k_s, v_s, q_s, acc_ref, max_ref, length_ref = refs
    sources = [(own0.at[0], own1.at[0])] + [
        (ref.at[0], ref.at[1]) for ref in (beyond1, beyond2, beyond3)
    ]
    far_pieces((index, mid, top), sources, k_s, v_s, q_s)

    def run_plain():
        steps = [(level, d) for level in range(2) for d in range(1, RATE)]

        def segment(s, carry):
            def score(item):
                level, d = item
                return dot(k_s[level, s ^ d], q_s[level, s])

            def weigh(item, block):
                return jnp.exp2(block * SCALE).astype(BF16)

            held = {}

            def gather(item, weights):
                level, d = item
                part = dot(v_s[level, s ^ d], weights)
                held[0] = part if d == 1 else held[0] + part
                if d == RATE - 1:
                    acc_ref[level, s] = held[0]
                    max_ref[level, s] = jnp.zeros((8, HALF), F32)

            in_stages(steps, score, weigh, gather)
            return carry

        lax.fori_loop(0, RATE, segment, 0, unroll=2)

    def run():
        def segment(s, carry):
            def score(level):
                return [dot(k_s[level, s ^ d], q_s[level, s]) for d in range(1, RATE)]

            scores = score(0)
            for level in range(2):
                following = score(1) if level == 0 else None
                best = column_max(scores)
                acc = None
                for d in range(1, RATE):
                    block = scores[d - 1] * SCALE - best
                    part = dot(v_s[level, s ^ d], jnp.exp2(block).astype(BF16))
                    acc = part if acc is None else acc + part
                acc_ref[level, s] = acc
                max_ref[level, s] = jnp.broadcast_to(best, (8, HALF))
                scores = following
            return carry

        lax.fori_loop(0, RATE, segment, 0)

    query_length, key_length = far_lengths(sources)
    length_ref[0] = query_length
    length_ref[1] = key_length
    plain = is_small(query_length, key_length)
    pl.when(plain)(run_plain)
    pl.when(jnp.logical_not(plain))(run)


def far_kernel(index, mid, top, *refs):
    place = (index, mid, top)
    sel2, sel3, beyond3, beyond2, beyond1, k_own, v_own, q_own, acc_in, max_in, length_in = refs[
        :11
    ]
    outs = refs[11 : 11 + RATE]
    k_s, v_s, q_s, result_s, tail_s = refs[11 + RATE :]
    same, _ = far_slots(place)
    sources = [(sel2.at[0], sel3.at[0])] + [
        (ref.at[0], ref.at[1]) for ref in (beyond1, beyond2, beyond3)
    ]
    far_pieces(place, sources, k_s, v_s, q_s)
    tail_s[...] = jnp.zeros(tail_s.shape, F32)

    tasks = [(level, chip) for level in range(2) for chip in range(2)]
    held = ((k_own, v_own, q_own), (k_s, v_s, q_s))

    def blocks(s, chip):
        return [(held[c], s ^ d) for d in range(1, RATE) for c in ((1,), (0, 1))[chip]]

    def finish(s, level, chip, acc, best):
        total = acc[DH : DH + 1, :]
        result = (acc[0:DH, :] / total).astype(BF16)
        lse = best + jnp.log2(total)
        if level == 0:
            lse = jnp.where(same, lse + 1.0, lse)
        else:
            lse = jnp.where(same, -1e30, lse)
        high = lse.astype(BF16).astype(F32)
        middle = (lse - high).astype(BF16).astype(F32)
        low = lse - high - middle
        for i in range(2):
            n = 2 * (2 * chip + i) + level
            mine = slice(i * BLK, (i + 1) * BLK)
            result_s[s, :, n * BLK : (n + 1) * BLK] = result[:, mine]
            for k, part in enumerate((high, middle, low)):
                tail_s[s, 3 * n + k : 3 * n + k + 1, :] = part[:, mine]

    def run_plain():
        def segment(s, carry):
            steps = [
                (level, chip, keys, b, n)
                for level, chip in tasks
                for n, (keys, b) in enumerate(blocks(s, chip))
            ]

            def score(item):
                level, chip, keys, b, _ = item
                return dot(keys[0][level, b], held[chip][2][level, s])

            def weigh(item, block):
                return jnp.exp2(block * SCALE).astype(BF16)

            sums = {}

            def gather(item, weights):
                level, chip, keys, b, n = item
                part = dot(keys[1][level, b], weights)
                sums[0] = sums[0] + part if n else part
                if n + 1 == len(blocks(s, chip)):
                    acc = sums[0] + acc_in[level, s] if chip == 0 else sums[0]
                    finish(s, level, chip, acc, jnp.zeros((1, HALF), F32))

            in_stages(steps, score, weigh, gather)
            return carry

        lax.fori_loop(0, RATE, segment, 0, unroll=2)

    def run():
        def segment(s, carry):
            for level, chip in tasks:
                scores = [
                    dot(keys[0][level, b], held[chip][2][level, s]) for keys, b in blocks(s, chip)
                ]
                best = column_max(scores)
                acc = jnp.zeros((DX, HALF), F32)
                if chip == 0:
                    old_max = max_in[level, s, 0:1, :]
                    best = jnp.maximum(best, old_max)
                    acc = acc_in[level, s] * jnp.exp2(old_max - best)
                for block, (keys, b) in zip(scores, blocks(s, chip)):
                    acc += dot(keys[1][level, b], jnp.exp2(block * SCALE - best).astype(BF16))
                finish(s, level, chip, acc, best)
            return carry

        lax.fori_loop(0, RATE, segment, 0)

    query_length, key_length = far_lengths(sources)
    plain = is_small(
        jnp.maximum(query_length, length_in[0]), jnp.maximum(key_length, length_in[1])
    )
    pl.when(plain)(run_plain)
    pl.when(jnp.logical_not(plain))(run)
    for s in range(RATE):
        outs[s][:, : GROUP * HALF] = result_s[s]
        outs[s][:, GROUP * HALF :] = tail_s[s].astype(BF16)


def join(acc, best, far, j):
    tail = far[:, GROUP * HALF :].astype(F32)
    lse = jnp.concatenate(
        [
            tail[3 * n : 3 * n + 1] + tail[3 * n + 1 : 3 * n + 2] + tail[3 * n + 2 : 3 * n + 3]
            for n in (2 * j, 2 * j + 1)
        ],
        axis=1,
    )
    overall = jnp.maximum(best, lse)
    near_factor, far_factor = jnp.exp2(best - overall), jnp.exp2(lse - overall)
    total = acc[DH : DH + 1] * near_factor + far_factor
    value = far[:, j * HALF : (j + 1) * HALF].astype(F32) * far_factor
    return ((acc[0:DH] * near_factor + value) / total).astype(BF16)


def combine_kernel(chip, acc_ref, max_ref, *refs):
    far, outs = refs[:-2][::-1], refs[-2:]
    for i in range(2):
        for p, results in enumerate(far):
            outs[i][p, :, 0:HALF] = join(
                acc_ref[p, 2 * i], max_ref[p, 2 * i, 0:1, :], results, 2 * chip + i
            )
            acc = acc_ref[p, 2 * i + 1]
            outs[i][p, :, HALF:] = (acc[0:DH] / acc[DH : DH + 1]).astype(BF16)


def project_kernel(sources, index, mid, top, *refs):
    place = (index, mid, top)
    parts, (w_ref, out_ref, held) = refs[:-3], refs[-3:]
    for (j, first), part in zip(sources, parts):
        for p in range(part.shape[0]):
            head = head_of(place, j, first + p)
            slots = class_of_slots(*offsets_of(place, head))
            for s in range(RATE):
                held[head_rows(head), lane_block(slots[s])] = part[
                    p, :, s * BLK : (s + 1) * BLK
                ]
    row = lax.broadcasted_iota(jnp.int32, (TOK, TOK), 0)
    col = lax.broadcasted_iota(jnp.int32, (TOK, TOK), 1)
    picker = (row == RATE * (col % BLK) + col // BLK).astype(BF16)
    attention = dot_nt(picker, held[...]).astype(BF16)
    out_ref[...] = dot(attention, w_ref[...]).astype(BF16)


def whole(shape):
    return pl.BlockSpec(shape, lambda *_: (0,) * len(shape))


def per_head(shape, skip=0):
    return pl.BlockSpec(shape, lambda h, *_: (h + skip,) + (0,) * (len(shape) - 1))


def call(
    kernel, scalars, args, grid, in_specs, outs, scratch, scores,
    limit=VMEM_LIMIT, after=(), through=(), busy=0,
):
    known = len(scalars) + len(args)
    extra = (*after, *through)
    count = len(outs)
    anywhere = pl.BlockSpec(memory_space=pl.ANY)

    def body(*refs):
        results = refs[known + len(extra) :]
        kernel(*refs[:known], *results[:count], *results[count + len(through) :])

    return pl.pallas_call(
        body if extra else kernel,
        grid_spec=pltpu.PrefetchScalarGridSpec(
            num_scalar_prefetch=len(scalars),
            grid=grid,
            in_specs=list(in_specs) + [anywhere] * len(extra),
            out_specs=[spec for spec, _ in outs] + [anywhere] * len(through),
            scratch_shapes=scratch,
        ),
        out_shape=[shape for _, shape in outs]
        + [jax.ShapeDtypeStruct(x.shape, x.dtype) for x in through],
        input_output_aliases={known + len(after) + i: count + i for i in range(len(through))},
        compiler_params=pltpu.CompilerParams(vmem_limit_bytes=limit),
        cost_estimate=pl.CostEstimate(flops=busy, bytes_accessed=0, transcendentals=0),
    )(*scalars, *args, *extra)


def handed_on(arrays, **order):
    return call(lambda: None, (), (), (1,), [], [], [], 0, through=tuple(arrays), **order)


def within(array, apart):
    count = lax.axis_size("seq")
    return lax.ppermute(array, "seq", [(i, i ^ apart) for i in range(count)])


def swap_segments(arrays):
    moved = {s: within(arrays[s - 1], GROUP * s) for s in (3, 2, 1)}
    return [moved[s] for s in (1, 2, 3)]


def shards_four(queries, key_states, value_states, offsets_mid, offsets_top, out_weight):
    width = queries.shape[1]
    place = (lax.axis_index("seq").astype(jnp.int32).reshape(1), offsets_mid, offsets_top)
    full = jax.ShapeDtypeStruct((HG, 3 * DH, TOK), BF16)
    piece = jax.ShapeDtypeStruct((HG, 3 * DH, HALF), BF16)
    pair = jax.ShapeDtypeStruct((2, 3 * DH, HALF), BF16)
    anywhere = pl.BlockSpec(memory_space=pl.ANY)
    shapes = [full] * 2 + [piece] * 4
    own0, own1, sel2, sel3, rest2, rest3 = call(
        pack_kernel, place, (key_states, value_states, queries), (1,),
        [anywhere] * 3,
        [(anywhere, shape) for shape in shapes],
        [pltpu.VMEM((TOK, width), BF16)] * 3
        + [pltpu.VMEM((width, TOK), BF16)] * 3
        + [pltpu.VMEM(shape.shape, BF16) for shape in shapes]
        + [pltpu.SemaphoreType.DMA((3,)), pltpu.SemaphoreType.DMA((6, 3))],
        1 << 19, VMEM_MOST,
    )
    own1 = within(own1, 1)
    sel2, sel3 = within(sel2, 2), within(sel3, 3)

    def regroup(a, b, **order):
        return call(
            regroup_kernel, (), (a, b), (1,),
            [whole(a.shape), whole(b.shape)], [(whole(pair.shape), pair)] * 3,
            [], 1 << 17, **order,
        )

    def near(held, units, tasks, old, first=0, heads=HG, step=2, **order):
        sizes = [len(members) * BLK for _, members in units]
        scores = sum(sum(sizes[low:]) * HALF for group in tasks for _, low, _ in group)
        arrays = [*held.values(), *[x for one in old for x in one]]
        shapes = [
            jax.ShapeDtypeStruct((heads, len(group), rows, HALF), F32)
            for group in tasks
            for rows in (DX, 8)
        ]
        return call(
            functools.partial(near_kernel, list(held), units, tasks, len(old), first, step),
            place, arrays, (heads // step,),
            [per_head((step,) + x.shape[1:], first // step) for x in arrays],
            [(per_head((step,) + x.shape[1:]), x) for x in shapes],
            [
                pltpu.VMEM((step, sum(sizes), DH), BF16),
                pltpu.VMEM((step, DX, sum(sizes)), BF16),
            ],
            heads * scores, **order,
        )

    def units_of(a, b):
        return [(0, [(a, 0), (b, 0)]), (1, [(a, 1), (b, 1)])], [
            (None, [(a, 2), (a, 3), (b, 2), (b, 3)])
        ]

    own_sel, own_rest = units_of(0, 1)
    other_sel, other_rest = units_of(2, 3)
    own = [(0, 0), (0, 1), (1, 0), (1, 1)]

    ours = regroup(own0, own1)
    ours = swap_segments(ours)
    held = {(0, 0): own0, (1, 0): own1}
    state_own = near(held, own_sel + own_rest, [[(q, 0, None) for q in own]], [])
    *theirs, rest2, rest3 = regroup(sel2, sel3, after=state_own[1:], through=(rest2, rest3))
    theirs = swap_segments(theirs)
    rest2, rest3 = within(rest2, 2), within(rest3, 3)

    held.update({(2, 0): sel2, (3, 0): sel3})
    out = near(
        held, own_sel + own_rest + other_sel,
        [
            [(q, 3, (0, i)) for i, q in enumerate(own)],
            [((2, 0), 0, None), ((3, 0), 0, None)],
        ],
        [state_own],
        after=ours[::-1],
    )
    state_own, state_sel = out[:2], out[2:]

    result = jax.ShapeDtypeStruct((DH, GROUP * HALF + BLK), BF16)
    piece_0 = pl.BlockSpec((1, 3 * DH, HALF), lambda *_: (0, 0, 0))
    pieces_shapes = [
        jax.ShapeDtypeStruct((2, RATE, HALF, DH), BF16),
        jax.ShapeDtypeStruct((2, RATE, DX, HALF), BF16),
        jax.ShapeDtypeStruct((2, RATE, DH, HALF), BF16),
    ]
    sums_shapes = [
        jax.ShapeDtypeStruct((2, RATE, DX, HALF), F32),
        jax.ShapeDtypeStruct((2, RATE, 8, HALF), F32),
    ]
    in_scalars = pl.BlockSpec(memory_space=pltpu.SMEM)
    far_own = call(
        far_own_kernel, place, (own0, own1, *ours), (1,),
        [piece_0] * 2 + [whole(pair.shape)] * 3,
        [(whole(x.shape), x) for x in pieces_shapes + sums_shapes]
        + [(in_scalars, jax.ShapeDtypeStruct((2,), F32))],
        [], RATE * 2 * 3 * HALF * HALF, after=(state_sel[1],),
    )
    results = call(
        far_kernel, place, (sel2, sel3, *theirs[::-1], *far_own), (1,),
        [piece_0] * 2 + [whole(pair.shape)] * 3
        + [whole(x.shape) for x in far_own[:-1]] + [in_scalars],
        [(whole(result.shape), result)] * RATE,
        [pltpu.VMEM(x.shape, BF16) for x in pieces_shapes]
        + [
            pltpu.VMEM((RATE, DH, GROUP * HALF), BF16),
            pltpu.VMEM((RATE, DH, BLK), F32),
        ],
        RATE * 2 * 3 * 3 * HALF * HALF, busy=BUSY,
    )
    back = [results[0]] + swap_segments(results[1:])

    held.update({(2, 2): rest2, (3, 2): rest3})
    units = own_sel + own_rest + other_sel + other_rest

    def combine(chip, state, far, **order):
        heads = state[0].shape[0]
        attended = jax.ShapeDtypeStruct((heads, DH, TOK), BF16)
        return call(
            functools.partial(combine_kernel, chip), (), (*state, *far[::-1]), (1,),
            [whole(x.shape) for x in state] + [whole(result.shape)] * heads,
            [(whole(attended.shape), attended)] * 2,
            [],
            1 << 18, **order,
        )

    parts, last = {}, results[0]
    for first, heads in CHUNKS:
        state_other = near(
            held, units,
            [
                [
                    ((2, 0), 5, (0, 0)), ((2, 1), 0, None),
                    ((3, 0), 5, (0, 1)), ((3, 1), 0, None),
                ]
            ],
            [state_sel],
            first, heads, 2, after=(last,),
        )
        if first:
            back[1:] = handed_on(back[1:], after=state_other[1:])
        part2, part3 = combine(
            1, state_other, back[first : first + heads], after=tuple(parts.values())
        )
        parts[2, first], parts[3, first] = within(part2, 2), within(part3, 3)
        last = part3
    state_own = near(
        {(2, 2): rest2, (3, 2): rest3, **{q: held[q] for q in ((0, 0), (1, 0))}},
        other_rest,
        [[(q, 0, (0, i)) for i, q in enumerate(own)]],
        [state_own],
        after=(last,),
    )
    part0, part1 = combine(0, state_own, back)
    parts = dict(zip(parts, handed_on(parts.values(), busy=BUSY)))
    parts[0, 0], parts[1, 0] = part0, within(part1, 1)
    return call(
        functools.partial(project_kernel, list(parts)), place, (*parts.values(), out_weight), (1,),
        [whole(x.shape) for x in parts.values()] + [whole((width, width))],
        [(whole((TOK, width)), jax.ShapeDtypeStruct((TOK, width), BF16))],
        [pltpu.VMEM((width, TOK), BF16)],
        1 << 18,
    )[0]


def shards(queries, key_states, value_states, offsets_mid, offsets_top, out_weight):
    tokens, width = queries.shape
    heads = offsets_mid.shape[0]
    fits = (
        lax.axis_size("head") == 1
        and lax.axis_size("seq") == GROUP * RATE
        and tokens == TOK
        and heads == GROUP * HG
        and width == heads * DH
    )
    run = shards_four if fits else shards_general
    return run(queries, key_states, value_states, offsets_mid, offsets_top, out_weight)


def solution(mesh):
    in_specs = (
        P(("slide", "seq"), "head"),
        P(("slide", "seq"), "head"),
        P(("slide", "seq"), "head"),
        P(),
        P(),
        P("head", None),
    )
    out_specs = P(("slide", "seq", "head"), None)
    return jax.shard_map(shards, mesh=mesh, in_specs=in_specs, out_specs=out_specs, check_vma=False)
```

```python
import functools

import jax
import jax.numpy as jnp
from jax import lax
from jax.experimental import pallas as pl
from jax.experimental.pallas import tpu as pltpu
from jax.sharding import PartitionSpec as P

SEG = 2048
LOG2E = 1.4426950408889634
VMEM_LIMIT = 40 * 1024 * 1024
VMEM_MOST = 60 * 1024 * 1024
BF16 = jnp.bfloat16
F32 = jnp.float32


def partner_2(block, axis, apart):
    count = lax.axis_size(axis)
    route = []
    for low in range(count):
        high = low | 1 << apart
        if high != low and high < count:
            route += [(low, high), (high, low)]
    return lax.ppermute(block, axis, route)


def attend_head(triple_in):
    query_rows, key_rows, value_rows = triple_in
    score_scale = query_rows.shape[-1] ** (-0.5)
    scores = jnp.dot(query_rows, key_rows.T, preferred_element_type=jnp.float32) * score_scale
    row_max = jnp.max(scores, axis=1)
    shifted = jnp.exp(scores - row_max[:, None])
    row_total = jnp.sum(shifted, axis=1)
    weights = shifted.astype(jnp.bfloat16)
    numerator = jnp.dot(weights, value_rows, preferred_element_type=jnp.float32)
    return (numerator, row_total, row_max)


def attend_local(query_rows, pair_rows):
    return lax.map(
        attend_head,
        (
            query_rows.transpose(1, 0, 2),
            pair_rows[:, 0].transpose(1, 0, 2),
            pair_rows[:, 1].transpose(1, 0, 2),
        ),
    )


def pick_rows(states, offsets, rate):
    row_count, inner_count, heads_here, head_width = states.shape
    picker = (jnp.arange(rate)[:, None] == offsets[None, :]).astype(jnp.bfloat16)
    folded = states.reshape(row_count // rate, rate, inner_count, heads_here, head_width)
    return jnp.einsum("archd,rh->achd", folded, picker, preferred_element_type=jnp.float32).astype(
        jnp.bfloat16
    )


def spread_back(numerator, row_total, row_max, offsets, rate):
    heads_here, picked_count, head_width = numerator.shape
    chosen = jnp.arange(rate)[:, None] == offsets[None, :]
    full_num = jnp.where(chosen[None, :, :, None], numerator.transpose(1, 0, 2)[:, None], 0.0)
    full_total = jnp.where(chosen[None], row_total.T[:, None], 0.0)
    full_max = jnp.where(chosen[None], row_max.T[:, None], -1e30)
    return (
        full_num.reshape(picked_count * rate, heads_here, head_width),
        full_total.reshape(picked_count * rate, heads_here),
        full_max.reshape(picked_count * rate, heads_here),
    )


def doubling(buffer, steps_count):
    position = lax.axis_index("seq")
    for bit_index in range(steps_count):
        partner = partner_2(buffer, "seq", bit_index)
        is_lower = position >> bit_index & 1 == 0
        buffer = jnp.where(
            is_lower, jnp.concatenate([buffer, partner], 0), jnp.concatenate([partner, buffer], 0)
        )
    return buffer


def shards_general(queries, key_states, value_states, offsets_mid, offsets_top, out_weight):
    tok_rows = queries.shape[0]
    heads_local = offsets_mid.shape[0] // lax.axis_size("head")
    head_size = queries.shape[1] // heads_local
    seq_devices = lax.axis_size("seq")
    seq_total = tok_rows * seq_devices
    width_mid = min(16 * SEG, seq_total)
    rate_mid = width_mid // SEG
    rate_top = seq_total // SEG
    start_head = lax.axis_index("head") * heads_local
    mid_local = lax.dynamic_slice(offsets_mid, (start_head,), (heads_local,))
    top_local = lax.dynamic_slice(offsets_top, (start_head,), (heads_local,))
    query_heads = queries.reshape(tok_rows, 1, heads_local, head_size)
    paired = jnp.stack([key_states, value_states], axis=1).reshape(
        tok_rows, 2, heads_local, head_size
    )
    near_bits = (SEG // tok_rows).bit_length() - 1
    near_rows = doubling(paired.reshape(tok_rows, -1), near_bits).reshape(
        SEG, 2, heads_local, head_size
    )
    near_num, near_total, near_max = attend_local(query_heads[:, 0], near_rows)
    level_near = spread_back(
        near_num, near_total, near_max, jnp.zeros((heads_local,), jnp.int32), 1
    )
    mid_q = pick_rows(query_heads, mid_local, rate_mid)[:, 0]
    mid_kv = pick_rows(paired, mid_local, rate_mid)
    mid_group = width_mid // tok_rows
    mid_bits = mid_group.bit_length() - 1
    mid_rows = doubling(mid_kv.reshape(mid_kv.shape[0], -1), mid_bits).reshape(
        SEG, 2, heads_local, head_size
    )
    mid_num, mid_total, mid_max = attend_local(mid_q, mid_rows)
    level_mid = spread_back(mid_num, mid_total, mid_max, mid_local, rate_mid)
    top_q = pick_rows(query_heads, top_local, rate_top)[:, 0]
    top_kv = pick_rows(paired, top_local, rate_top)
    top_rows = lax.all_gather(
        top_kv.reshape(top_kv.shape[0], -1), "seq", axis=0, tiled=True
    ).reshape(SEG, 2, heads_local, head_size)
    top_num, top_total, top_max = attend_local(top_q, top_rows)
    level_top = spread_back(top_num, top_total, top_max, top_local, rate_top)
    levels = [level_near, level_mid, level_top]
    overall = jnp.maximum(jnp.maximum(level_near[2], level_mid[2]), level_top[2])
    numerator = jnp.zeros((tok_rows, heads_local, head_size), jnp.float32)
    row_total = jnp.zeros((tok_rows, heads_local), jnp.float32)
    for level_num, level_total, level_max in levels:
        factor = jnp.exp(level_max - overall)
        numerator = numerator + factor[..., None] * level_num
        row_total = row_total + factor * level_total
    attention = (
        (numerator / row_total[..., None])
        .astype(jnp.bfloat16)
        .reshape(tok_rows, heads_local * head_size)
    )
    result = lax.psum_scatter(
        jnp.dot(attention, out_weight, preferred_element_type=jnp.float32),
        "head",
        scatter_dimension=0,
        tiled=True,
    )
    return result.astype(jnp.bfloat16)


RATE = 4
GROUP = 4
HG = 4
DH = 48
BLK = 128
HALF = 2 * BLK
TOK = 512
SCALE = DH**-0.5 * LOG2E
BUSY = 1 << 33
AHEAD = 4
SAFE = 96.0
CHUNKS = ((0, 2), (2, 2))
DX = 64


def dot(a, b):
    return jnp.dot(a, b, preferred_element_type=F32)


def dot_nt(a, b):
    return lax.dot_general(a, b, (((1,), (1,)), ((), ())), preferred_element_type=F32)


def class_of_slots(off_mid, off_top):
    first = off_mid
    second = jnp.where(off_top == off_mid, lax.rem(off_mid + 1, RATE), off_top)
    free0 = (first != 0) & (second != 0)
    free1 = (first != 1) & (second != 1)
    third = jnp.where(free0, 0, jnp.where(free1, 1, 2))
    return first, second, third, 6 - first - second - third


def head_of(place, j, p):
    index = place[0][0]
    return ((index & (GROUP - 1)) ^ j) * HG + ((index // GROUP) ^ p)


def offsets_of(place, head):
    return place[1][head], place[2][head]


def token_picker():
    row = lax.broadcasted_iota(jnp.int32, (TOK, TOK), 0)
    col = lax.broadcasted_iota(jnp.int32, (TOK, TOK), 1)
    return (col == RATE * (row % BLK) + row // BLK).astype(BF16)


def fill_class_major(block, picker, scratch):
    scratch[...] = lax.dot_general(
        block, picker, (((0,), (1,)), ((), ())), preferred_element_type=F32
    ).astype(BF16)


def lane_block(index):
    return pl.ds(pl.multiple_of(index * BLK, BLK), BLK)


def head_rows(head):
    return pl.ds(pl.multiple_of(head * DH, 16), DH)


def pack_kernel(index, mid, top, k_hbm, v_hbm, q_hbm, *refs):
    place = (index, mid, top)
    outs, refs = refs[:6], refs[6:]
    blocks, held, packed = refs[:3], refs[3:6], refs[6:12]
    sems_in, sems_out = refs[12:]
    loads = [
        pltpu.make_async_copy(hbm, block, sems_in.at[i])
        for i, (hbm, block) in enumerate(zip((k_hbm, v_hbm, q_hbm), blocks))
    ]
    for load in loads:
        load.start()
    picker = token_picker()
    stores = []
    heads = {(j, p): head_of(place, j, p) for j in range(GROUP) for p in range(HG)}
    classes = {at: class_of_slots(*offsets_of(place, head)) for at, head in heads.items()}
    for n, (load, block, scratch) in enumerate(zip(loads, blocks, held)):
        load.wait()
        fill_class_major(block[...], picker, scratch)
        rows = slice(n * DH, (n + 1) * DH)
        for i, (j, first, count) in enumerate(
            ((0, 0, 4), (1, 0, 4), (2, 0, 2), (3, 0, 2), (2, 2, 2), (3, 2, 2))
        ):
            for p in range(HG):
                for s in range(count):
                    packed[i][p, rows, s * BLK : (s + 1) * BLK] = scratch[
                        head_rows(heads[j, p]), lane_block(classes[j, p][first + s])
                    ]
            store = pltpu.make_async_copy(
                packed[i].at[:, rows], outs[i].at[:, rows], sems_out.at[i, n]
            )
            store.start()
            stores.append(store)
    for store in stores:
        store.wait()


def regroup_kernel(a_ref, b_ref, *refs):
    for s, out in enumerate(refs[-3:]):
        out[0] = a_ref[s + 1, :, 0:HALF]
        out[1] = b_ref[s + 1, :, 0:HALF]


def upright(keys_t):
    return keys_t.T


def largest(blocks):
    best = None
    for block in blocks:
        wide = block.astype(F32)
        length = jnp.sum(wide * wide, axis=0, keepdims=True)
        for low in range(0, block.shape[1], HALF):
            part = length[:, low : low + HALF]
            best = part if best is None else jnp.maximum(best, part)
    return jnp.max(best)


def is_small(query_length, key_length):
    return query_length * key_length * (SCALE * SCALE) < SAFE * SAFE


def column_max(blocks):
    best = jnp.max(blocks[0], axis=0, keepdims=True)
    for block in blocks[1:]:
        best = jnp.maximum(best, jnp.max(block, axis=0, keepdims=True))
    return best * SCALE


def in_stages(items, score, weigh, gather):
    scores = {n: score(item) for n, item in enumerate(items[:AHEAD])}
    weights = weigh(items[0], scores.pop(0))
    for n, item in enumerate(items):
        if n + AHEAD < len(items):
            scores[n + AHEAD] = score(items[n + AHEAD])
        following = weigh(items[n + 1], scores.pop(n + 1)) if n + 1 < len(items) else None
        gather(item, weights)
        weights = following


def near_kernel(inputs, units, tasks, carried, first, step, index, mid, top, *refs):
    place = (index, mid, top)
    pieces = dict(zip(inputs, refs[: len(inputs)]))
    refs = refs[len(inputs) :]
    old = [refs[2 * i : 2 * i + 2] for i in range(carried)]
    outs = refs[2 * carried : 2 * carried + 2 * len(tasks)]
    k_s, v_s = refs[-2:]
    v_s[:, DH:DX, :] = jnp.ones((step, DX - DH, v_s.shape[2]), BF16)
    lane_slot = lax.broadcasted_iota(jnp.int32, (1, HALF), 1) // BLK

    def lookup(j, slot):
        first = 0 if (j, 0) in pieces and pieces[j, 0].shape[2] > HALF else slot // 2 * 2
        return pieces[j, first], (slot - first) * BLK

    chunks = []
    row = 0
    for label, members in units:
        chunks.append((label, slice(row, row + len(members) * BLK)))
        row += len(members) * BLK
    members = [member for _, group in units for member in group]

    def prepare(h):
        for i, (j, slot) in enumerate(members):
            ref, lane = lookup(j, slot)
            rows = slice(i * BLK, (i + 1) * BLK)
            k_s[h, rows, :] = upright(ref[h, 0:DH, lane : lane + BLK])
            v_s[h, 0:DH, rows] = ref[h, DH : 2 * DH, lane : lane + BLK]

    def counted_again(h):
        off_mid, off_top = offsets_of(place, head_of(place, 0, first + pl.program_id(0) * step + h))
        same = off_mid == off_top
        return [
            jnp.where(lane_slot == 0, jnp.where(same, 1.584962500721156, 1.0), 0.0),
            jnp.where(lane_slot == 1, jnp.where(same, 0.0, 1.0), 0.0),
        ]

    def run(heads):
        again = [counted_again(h) for h in heads]
        flat = [
            (h, again_h, query, low, merge, out, i)
            for h, again_h in zip(heads, again)
            for out, group in enumerate(tasks)
            for i, (query, low, merge) in enumerate(group)
        ]

        def score(task):
            h, _, (j, half), low = task[:4]
            ref, lane = lookup(j, 2 * half)
            query = ref[h, 2 * DH :, lane : lane + HALF]
            return [dot(k_s[h, rows, :], query) for _, rows in chunks[low:]]

        scores = score(flat[0])
        for n, (h, again_h, (_, half), low, merge, out, i) in enumerate(flat):
            following = score(flat[n + 1]) if n + 1 < len(flat) else None
            best = column_max(scores)
            if merge is not None:
                acc_in, max_in = old[merge[0]]
                old_max = max_in[h, merge[1], 0:1, :]
                best = jnp.maximum(best, old_max)
            acc = None
            for (label, rows), block in zip(chunks[low:], scores):
                block = block * SCALE
                if half == 0 and label is not None:
                    block = block - (best - again_h[label])
                else:
                    block = block - best
                part = dot(v_s[h, :, rows], jnp.exp2(block).astype(BF16))
                acc = part if acc is None else acc + part
            if merge is not None:
                acc = acc + acc_in[h, merge[1]] * jnp.exp2(old_max - best)
            acc_ref, max_ref = outs[2 * out : 2 * out + 2]
            acc_ref[h, i] = acc
            max_ref[h, i] = jnp.broadcast_to(best, (8, HALF))
            scores = following

    def run_plain():
        again = [counted_again(h) for h in range(step)]
        steps = [
            (h, query, merge, out, i, c, c == low, c == len(chunks) - 1)
            for h in range(step)
            for out, group in enumerate(tasks)
            for i, (query, low, merge) in enumerate(group)
            for c in range(low, len(chunks))
        ]

        def score(item):
            h, (j, half), c = item[0], item[1], item[5]
            ref, lane = lookup(j, 2 * half)
            return dot(k_s[h, chunks[c][1], :], ref[h, 2 * DH :, lane : lane + HALF])

        def weigh(item, block):
            h, (_, half), c = item[0], item[1], item[5]
            label = chunks[c][0]
            block = block * SCALE
            if half == 0 and label is not None:
                block = block + again[h][label]
            return jnp.exp2(block).astype(BF16)

        held = {}

        def gather(item, weights):
            h, _, merge, out, i, c, begins, ends = item
            part = dot(v_s[h, :, chunks[c][1]], weights)
            acc = part if begins else held[0] + part
            if ends:
                if merge is not None:
                    acc = acc + old[merge[0]][0][h, merge[1]]
                acc_ref, max_ref = outs[2 * out : 2 * out + 2]
                acc_ref[h, i] = acc
                max_ref[h, i] = jnp.zeros((8, HALF), F32)
            held[0] = acc

        in_stages(steps, score, weigh, gather)

    for h in range(step):
        prepare(h)
    plain = is_small(
        largest([ref[h, 2 * DH :, :] for ref in pieces.values() for h in range(step)]),
        largest([ref[h, 0:DH, :] for ref in pieces.values() for h in range(step)]),
    )
    for _, max_in in old:
        plain = plain & (jnp.max(jnp.abs(max_in[...])) == 0.0)

    @pl.when(plain)
    def _():
        run_plain()

    @pl.when(jnp.logical_not(plain))
    def _():
        @pl.loop(0, step)
        def _(h):
            run([h])


def far_slots(place):
    off_mid, off_top = offsets_of(place, head_of(place, 0, 0))
    same = off_mid == off_top
    return same, (0, jnp.where(same, 0, 1))


def far_pieces(place, sources, k_s, v_s, q_s):
    _, slots = far_slots(place)
    for s, pair in enumerate(sources):
        for i, ref in enumerate(pair):
            here = slice(i * BLK, (i + 1) * BLK)
            for level, slot in enumerate(slots):
                k_s[level, s, here, :] = upright(ref[0:DH, lane_block(slot)])
                v_s[level, s, 0:DH, here] = ref[DH : 2 * DH, lane_block(slot)]
                q_s[level, s, :, here] = ref[2 * DH : 3 * DH, lane_block(slot)]
    v_s[:, :, DH:DX, :] = jnp.ones((2, RATE, DX - DH, HALF), BF16)


def far_lengths(sources):
    every = [ref for pair in sources for ref in pair]
    return (
        largest([ref[2 * DH : 3 * DH, 0:HALF] for ref in every]),
        largest([ref[0:DH, 0:HALF] for ref in every]),
    )


def far_own_kernel(index, mid, top, own0, own1, beyond1, beyond2, beyond3, *refs):
    k_s, v_s, q_s, acc_ref, max_ref, length_ref = refs
    sources = [(own0.at[0], own1.at[0])] + [
        (ref.at[0], ref.at[1]) for ref in (beyond1, beyond2, beyond3)
    ]
    far_pieces((index, mid, top), sources, k_s, v_s, q_s)

    def run_plain():
        steps = [(level, d) for level in range(2) for d in range(1, RATE)]

        def segment(s, carry):
            def score(item):
                level, d = item
                return dot(k_s[level, s ^ d], q_s[level, s])

            def weigh(item, block):
                return jnp.exp2(block * SCALE).astype(BF16)

            held = {}

            def gather(item, weights):
                level, d = item
                part = dot(v_s[level, s ^ d], weights)
                held[0] = part if d == 1 else held[0] + part
                if d == RATE - 1:
                    acc_ref[level, s] = held[0]
                    max_ref[level, s] = jnp.zeros((8, HALF), F32)

            in_stages(steps, score, weigh, gather)
            return carry

        lax.fori_loop(0, RATE, segment, 0, unroll=2)

    def run():
        def segment(s, carry):
            def score(level):
                return [dot(k_s[level, s ^ d], q_s[level, s]) for d in range(1, RATE)]

            scores = score(0)
            for level in range(2):
                following = score(1) if level == 0 else None
                best = column_max(scores)
                acc = None
                for d in range(1, RATE):
                    block = scores[d - 1] * SCALE - best
                    part = dot(v_s[level, s ^ d], jnp.exp2(block).astype(BF16))
                    acc = part if acc is None else acc + part
                acc_ref[level, s] = acc
                max_ref[level, s] = jnp.broadcast_to(best, (8, HALF))
                scores = following
            return carry

        lax.fori_loop(0, RATE, segment, 0)

    query_length, key_length = far_lengths(sources)
    length_ref[0] = query_length
    length_ref[1] = key_length
    plain = is_small(query_length, key_length)
    pl.when(plain)(run_plain)
    pl.when(jnp.logical_not(plain))(run)


def far_kernel(index, mid, top, *refs):
    place = (index, mid, top)
    sel2, sel3, beyond3, beyond2, beyond1, k_own, v_own, q_own, acc_in, max_in, length_in = refs[
        :11
    ]
    outs = refs[11 : 11 + RATE]
    k_s, v_s, q_s, result_s, tail_s = refs[11 + RATE :]
    same, _ = far_slots(place)
    sources = [(sel2.at[0], sel3.at[0])] + [
        (ref.at[0], ref.at[1]) for ref in (beyond1, beyond2, beyond3)
    ]
    far_pieces(place, sources, k_s, v_s, q_s)
    tail_s[...] = jnp.zeros(tail_s.shape, F32)

    tasks = [(level, chip) for level in range(2) for chip in range(2)]
    held = ((k_own, v_own, q_own), (k_s, v_s, q_s))

    def blocks(s, chip):
        return [(held[c], s ^ d) for d in range(1, RATE) for c in ((1,), (0, 1))[chip]]

    def finish(s, level, chip, acc, best):
        total = acc[DH : DH + 1, :]
        result = (acc[0:DH, :] / total).astype(BF16)
        lse = best + jnp.log2(total)
        if level == 0:
            lse = jnp.where(same, lse + 1.0, lse)
        else:
            lse = jnp.where(same, -1e30, lse)
        high = lse.astype(BF16).astype(F32)
        middle = (lse - high).astype(BF16).astype(F32)
        low = lse - high - middle
        for i in range(2):
            n = 2 * (2 * chip + i) + level
            mine = slice(i * BLK, (i + 1) * BLK)
            result_s[s, :, n * BLK : (n + 1) * BLK] = result[:, mine]
            for k, part in enumerate((high, middle, low)):
                tail_s[s, 3 * n + k : 3 * n + k + 1, :] = part[:, mine]

    def run_plain():
        def segment(s, carry):
            steps = [
                (level, chip, keys, b, n)
                for level, chip in tasks
                for n, (keys, b) in enumerate(blocks(s, chip))
            ]

            def score(item):
                level, chip, keys, b, _ = item
                return dot(keys[0][level, b], held[chip][2][level, s])

            def weigh(item, block):
                return jnp.exp2(block * SCALE).astype(BF16)

            sums = {}

            def gather(item, weights):
                level, chip, keys, b, n = item
                part = dot(keys[1][level, b], weights)
                sums[0] = sums[0] + part if n else part
                if n + 1 == len(blocks(s, chip)):
                    acc = sums[0] + acc_in[level, s] if chip == 0 else sums[0]
                    finish(s, level, chip, acc, jnp.zeros((1, HALF), F32))

            in_stages(steps, score, weigh, gather)
            return carry

        lax.fori_loop(0, RATE, segment, 0, unroll=2)

    def run():
        def segment(s, carry):
            for level, chip in tasks:
                scores = [
                    dot(keys[0][level, b], held[chip][2][level, s]) for keys, b in blocks(s, chip)
                ]
                best = column_max(scores)
                acc = jnp.zeros((DX, HALF), F32)
                if chip == 0:
                    old_max = max_in[level, s, 0:1, :]
                    best = jnp.maximum(best, old_max)
                    acc = acc_in[level, s] * jnp.exp2(old_max - best)
                for block, (keys, b) in zip(scores, blocks(s, chip)):
                    acc += dot(keys[1][level, b], jnp.exp2(block * SCALE - best).astype(BF16))
                finish(s, level, chip, acc, best)
            return carry

        lax.fori_loop(0, RATE, segment, 0)

    query_length, key_length = far_lengths(sources)
    plain = is_small(
        jnp.maximum(query_length, length_in[0]), jnp.maximum(key_length, length_in[1])
    )
    pl.when(plain)(run_plain)
    pl.when(jnp.logical_not(plain))(run)
    for s in range(RATE):
        outs[s][:, : GROUP * HALF] = result_s[s]
        outs[s][:, GROUP * HALF :] = tail_s[s].astype(BF16)


def join(acc, best, far, j):
    tail = far[:, GROUP * HALF :].astype(F32)
    lse = jnp.concatenate(
        [
            tail[3 * n : 3 * n + 1] + tail[3 * n + 1 : 3 * n + 2] + tail[3 * n + 2 : 3 * n + 3]
            for n in (2 * j, 2 * j + 1)
        ],
        axis=1,
    )
    overall = jnp.maximum(best, lse)
    near_factor, far_factor = jnp.exp2(best - overall), jnp.exp2(lse - overall)
    total = acc[DH : DH + 1] * near_factor + far_factor
    value = far[:, j * HALF : (j + 1) * HALF].astype(F32) * far_factor
    return ((acc[0:DH] * near_factor + value) / total).astype(BF16)


def combine_kernel(chip, acc_ref, max_ref, *refs):
    far, outs = refs[:-2][::-1], refs[-2:]
    for i in range(2):
        for p, results in enumerate(far):
            outs[i][p, :, 0:HALF] = join(
                acc_ref[p, 2 * i], max_ref[p, 2 * i, 0:1, :], results, 2 * chip + i
            )
            acc = acc_ref[p, 2 * i + 1]
            outs[i][p, :, HALF:] = (acc[0:DH] / acc[DH : DH + 1]).astype(BF16)


def last_own_kernel(inputs, units, tasks, index, mid, top, *refs):
    count = len(inputs) + 2
    near_refs, far, outs, scratch = refs[:count], refs[count:-6], refs[-6:-4], refs[-4:]
    acc_s, max_s, k_s, v_s = scratch
    near_kernel(
        inputs, units, tasks, 1, 0, HG, index, mid, top, *near_refs, acc_s, max_s, k_s, v_s
    )
    combine_kernel(0, acc_s, max_s, *far, *outs)


def project_kernel(sources, index, mid, top, *refs):
    place = (index, mid, top)
    parts, (w_ref, out_ref, held) = refs[:-3], refs[-3:]
    for (j, first), part in zip(sources, parts):
        for p in range(part.shape[0]):
            head = head_of(place, j, first + p)
            slots = class_of_slots(*offsets_of(place, head))
            for s in range(RATE):
                held[head_rows(head), lane_block(slots[s])] = part[
                    p, :, s * BLK : (s + 1) * BLK
                ]
    row = lax.broadcasted_iota(jnp.int32, (TOK, TOK), 0)
    col = lax.broadcasted_iota(jnp.int32, (TOK, TOK), 1)
    picker = (row == RATE * (col % BLK) + col // BLK).astype(BF16)
    attention = dot_nt(picker, held[...]).astype(BF16)
    out_ref[...] = dot(attention, w_ref[...]).astype(BF16)


def whole(shape):
    return pl.BlockSpec(shape, lambda *_: (0,) * len(shape))


def per_head(shape, skip=0):
    return pl.BlockSpec(shape, lambda h, *_: (h + skip,) + (0,) * (len(shape) - 1))


def call(
    kernel, scalars, args, grid, in_specs, outs, scratch, scores,
    limit=VMEM_LIMIT, after=(), through=(), busy=0,
):
    known = len(scalars) + len(args)
    extra = (*after, *through)
    count = len(outs)
    anywhere = pl.BlockSpec(memory_space=pl.ANY)

    def body(*refs):
        results = refs[known + len(extra) :]
        kernel(*refs[:known], *results[:count], *results[count + len(through) :])

    return pl.pallas_call(
        body if extra else kernel,
        grid_spec=pltpu.PrefetchScalarGridSpec(
            num_scalar_prefetch=len(scalars),
            grid=grid,
            in_specs=list(in_specs) + [anywhere] * len(extra),
            out_specs=[spec for spec, _ in outs] + [anywhere] * len(through),
            scratch_shapes=scratch,
        ),
        out_shape=[shape for _, shape in outs]
        + [jax.ShapeDtypeStruct(x.shape, x.dtype) for x in through],
        input_output_aliases={known + len(after) + i: count + i for i in range(len(through))},
        compiler_params=pltpu.CompilerParams(vmem_limit_bytes=limit),
        cost_estimate=pl.CostEstimate(flops=busy, bytes_accessed=0, transcendentals=0),
    )(*scalars, *args, *extra)


def handed_on(arrays, **order):
    return call(lambda: None, (), (), (1,), [], [], [], 0, through=tuple(arrays), **order)


def within(array, apart):
    count = lax.axis_size("seq")
    return lax.ppermute(array, "seq", [(i, i ^ apart) for i in range(count)])


def swap_segments(arrays):
    moved = {s: within(arrays[s - 1], GROUP * s) for s in (3, 2, 1)}
    return [moved[s] for s in (1, 2, 3)]


def shards_four(queries, key_states, value_states, offsets_mid, offsets_top, out_weight):
    width = queries.shape[1]
    place = (lax.axis_index("seq").astype(jnp.int32).reshape(1), offsets_mid, offsets_top)
    full = jax.ShapeDtypeStruct((HG, 3 * DH, TOK), BF16)
    piece = jax.ShapeDtypeStruct((HG, 3 * DH, HALF), BF16)
    pair = jax.ShapeDtypeStruct((2, 3 * DH, HALF), BF16)
    anywhere = pl.BlockSpec(memory_space=pl.ANY)
    shapes = [full] * 2 + [piece] * 4
    own0, own1, sel2, sel3, rest2, rest3 = call(
        pack_kernel, place, (key_states, value_states, queries), (1,),
        [anywhere] * 3,
        [(anywhere, shape) for shape in shapes],
        [pltpu.VMEM((TOK, width), BF16)] * 3
        + [pltpu.VMEM((width, TOK), BF16)] * 3
        + [pltpu.VMEM(shape.shape, BF16) for shape in shapes]
        + [pltpu.SemaphoreType.DMA((3,)), pltpu.SemaphoreType.DMA((6, 3))],
        1 << 19, VMEM_MOST,
    )
    own1 = within(own1, 1)
    sel2, sel3 = within(sel2, 2), within(sel3, 3)

    def regroup(a, b, **order):
        return call(
            regroup_kernel, (), (a, b), (1,),
            [whole(a.shape), whole(b.shape)], [(whole(pair.shape), pair)] * 3,
            [], 1 << 17, **order,
        )

    def near(held, units, tasks, old, first=0, heads=HG, step=2, **order):
        sizes = [len(members) * BLK for _, members in units]
        scores = sum(sum(sizes[low:]) * HALF for group in tasks for _, low, _ in group)
        arrays = [*held.values(), *[x for one in old for x in one]]
        shapes = [
            jax.ShapeDtypeStruct((heads, len(group), rows, HALF), F32)
            for group in tasks
            for rows in (DX, 8)
        ]
        return call(
            functools.partial(near_kernel, list(held), units, tasks, len(old), first, step),
            place, arrays, (heads // step,),
            [per_head((step,) + x.shape[1:], first // step) for x in arrays],
            [(per_head((step,) + x.shape[1:]), x) for x in shapes],
            [
                pltpu.VMEM((step, sum(sizes), DH), BF16),
                pltpu.VMEM((step, DX, sum(sizes)), BF16),
            ],
            heads * scores, **order,
        )

    def units_of(a, b):
        return [(0, [(a, 0), (b, 0)]), (1, [(a, 1), (b, 1)])], [
            (None, [(a, 2), (a, 3), (b, 2), (b, 3)])
        ]

    own_sel, own_rest = units_of(0, 1)
    other_sel, other_rest = units_of(2, 3)
    own = [(0, 0), (0, 1), (1, 0), (1, 1)]

    ours = regroup(own0, own1)
    ours = swap_segments(ours)
    held = {(0, 0): own0, (1, 0): own1}
    state_own = near(held, own_sel + own_rest, [[(q, 0, None) for q in own]], [])
    *theirs, rest2, rest3 = regroup(sel2, sel3, after=state_own[1:], through=(rest2, rest3))
    theirs = swap_segments(theirs)
    rest2, rest3 = within(rest2, 2), within(rest3, 3)

    held.update({(2, 0): sel2, (3, 0): sel3})
    out = near(
        held, own_sel + own_rest + other_sel,
        [
            [(q, 3, (0, i)) for i, q in enumerate(own)],
            [((2, 0), 0, None), ((3, 0), 0, None)],
        ],
        [state_own],
        after=ours[::-1],
    )
    state_own, state_sel = out[:2], out[2:]

    result = jax.ShapeDtypeStruct((DH, GROUP * HALF + BLK), BF16)
    piece_0 = pl.BlockSpec((1, 3 * DH, HALF), lambda *_: (0, 0, 0))
    pieces_shapes = [
        jax.ShapeDtypeStruct((2, RATE, HALF, DH), BF16),
        jax.ShapeDtypeStruct((2, RATE, DX, HALF), BF16),
        jax.ShapeDtypeStruct((2, RATE, DH, HALF), BF16),
    ]
    sums_shapes = [
        jax.ShapeDtypeStruct((2, RATE, DX, HALF), F32),
        jax.ShapeDtypeStruct((2, RATE, 8, HALF), F32),
    ]
    in_scalars = pl.BlockSpec(memory_space=pltpu.SMEM)
    far_own = call(
        far_own_kernel, place, (own0, own1, *ours), (1,),
        [piece_0] * 2 + [whole(pair.shape)] * 3,
        [(whole(x.shape), x) for x in pieces_shapes + sums_shapes]
        + [(in_scalars, jax.ShapeDtypeStruct((2,), F32))],
        [], RATE * 2 * 3 * HALF * HALF, after=(state_sel[1],),
    )
    results = call(
        far_kernel, place, (sel2, sel3, *theirs[::-1], *far_own), (1,),
        [piece_0] * 2 + [whole(pair.shape)] * 3
        + [whole(x.shape) for x in far_own[:-1]] + [in_scalars],
        [(whole(result.shape), result)] * RATE,
        [pltpu.VMEM(x.shape, BF16) for x in pieces_shapes]
        + [
            pltpu.VMEM((RATE, DH, GROUP * HALF), BF16),
            pltpu.VMEM((RATE, DH, BLK), F32),
        ],
        RATE * 2 * 3 * 3 * HALF * HALF, busy=BUSY,
    )
    back = [results[0]] + swap_segments(results[1:])

    held.update({(2, 2): rest2, (3, 2): rest3})
    units = own_sel + own_rest + other_sel + other_rest

    def combine(chip, state, far, **order):
        heads = state[0].shape[0]
        attended = jax.ShapeDtypeStruct((heads, DH, TOK), BF16)
        return call(
            functools.partial(combine_kernel, chip), (), (*state, *far[::-1]), (1,),
            [whole(x.shape) for x in state] + [whole(result.shape)] * heads,
            [(whole(attended.shape), attended)] * 2,
            [],
            1 << 18, **order,
        )

    parts, last = {}, results[0]
    for first, heads in CHUNKS:
        state_other = near(
            held, units,
            [
                [
                    ((2, 0), 5, (0, 0)), ((2, 1), 0, None),
                    ((3, 0), 5, (0, 1)), ((3, 1), 0, None),
                ]
            ],
            [state_sel],
            first, heads, 2, after=(last,),
        )
        if first:
            back[1:] = handed_on(back[1:], after=state_other[1:])
        part2, part3 = combine(
            1, state_other, back[first : first + heads], after=tuple(parts.values())
        )
        parts[2, first], parts[3, first] = within(part2, 2), within(part3, 3)
        last = part3
    pieces = {(2, 2): rest2, (3, 2): rest3, **{q: held[q] for q in ((0, 0), (1, 0))}}
    arrays = [*pieces.values(), *state_own, *back[::-1]]
    attended = jax.ShapeDtypeStruct((HG, DH, TOK), BF16)
    part0, part1 = call(
        functools.partial(
            last_own_kernel, list(pieces), other_rest, [[(q, 0, (0, i)) for i, q in enumerate(own)]]
        ),
        place, arrays, (1,),
        [whole(x.shape) for x in arrays],
        [(whole(attended.shape), attended)] * 2,
        [pltpu.VMEM(x.shape, F32) for x in state_own]
        + [pltpu.VMEM((HG, TOK, DH), BF16), pltpu.VMEM((HG, DX, TOK), BF16)],
        HG * TOK * GROUP * HALF, after=(last,),
    )
    parts = dict(zip(parts, handed_on(parts.values(), busy=BUSY)))
    parts[0, 0], parts[1, 0] = part0, within(part1, 1)
    return call(
        functools.partial(project_kernel, list(parts)), place, (*parts.values(), out_weight), (1,),
        [whole(x.shape) for x in parts.values()] + [whole((width, width))],
        [(whole((TOK, width)), jax.ShapeDtypeStruct((TOK, width), BF16))],
        [pltpu.VMEM((width, TOK), BF16)],
        1 << 18,
    )[0]


def shards(queries, key_states, value_states, offsets_mid, offsets_top, out_weight):
    tokens, width = queries.shape
    heads = offsets_mid.shape[0]
    fits = (
        lax.axis_size("head") == 1
        and lax.axis_size("seq") == GROUP * RATE
        and tokens == TOK
        and heads == GROUP * HG
        and width == heads * DH
    )
    run = shards_four if fits else shards_general
    return run(queries, key_states, value_states, offsets_mid, offsets_top, out_weight)


def solution(mesh):
    in_specs = (
        P(("slide", "seq"), "head"),
        P(("slide", "seq"), "head"),
        P(("slide", "seq"), "head"),
        P(),
        P(),
        P("head", None),
    )
    out_specs = P(("slide", "seq", "head"), None)
    return jax.shard_map(shards, mesh=mesh, in_specs=in_specs, out_specs=out_specs, check_vma=False)
```

```python
import functools

import jax
import jax.numpy as jnp
from jax import lax
from jax.experimental import pallas as pl
from jax.experimental.pallas import tpu as pltpu
from jax.sharding import PartitionSpec as P

SEG = 2048
LOG2E = 1.4426950408889634
VMEM_LIMIT = 40 * 1024 * 1024
VMEM_MOST = 60 * 1024 * 1024
BF16 = jnp.bfloat16
F32 = jnp.float32


def partner_2(block, axis, apart):
    count = lax.axis_size(axis)
    route = []
    for low in range(count):
        high = low | 1 << apart
        if high != low and high < count:
            route += [(low, high), (high, low)]
    return lax.ppermute(block, axis, route)


def attend_head(triple_in):
    query_rows, key_rows, value_rows = triple_in
    score_scale = query_rows.shape[-1] ** (-0.5)
    scores = jnp.dot(query_rows, key_rows.T, preferred_element_type=jnp.float32) * score_scale
    row_max = jnp.max(scores, axis=1)
    shifted = jnp.exp(scores - row_max[:, None])
    row_total = jnp.sum(shifted, axis=1)
    weights = shifted.astype(jnp.bfloat16)
    numerator = jnp.dot(weights, value_rows, preferred_element_type=jnp.float32)
    return (numerator, row_total, row_max)


def attend_local(query_rows, pair_rows):
    return lax.map(
        attend_head,
        (
            query_rows.transpose(1, 0, 2),
            pair_rows[:, 0].transpose(1, 0, 2),
            pair_rows[:, 1].transpose(1, 0, 2),
        ),
    )


def pick_rows(states, offsets, rate):
    row_count, inner_count, heads_here, head_width = states.shape
    picker = (jnp.arange(rate)[:, None] == offsets[None, :]).astype(jnp.bfloat16)
    folded = states.reshape(row_count // rate, rate, inner_count, heads_here, head_width)
    return jnp.einsum("archd,rh->achd", folded, picker, preferred_element_type=jnp.float32).astype(
        jnp.bfloat16
    )


def spread_back(numerator, row_total, row_max, offsets, rate):
    heads_here, picked_count, head_width = numerator.shape
    chosen = jnp.arange(rate)[:, None] == offsets[None, :]
    full_num = jnp.where(chosen[None, :, :, None], numerator.transpose(1, 0, 2)[:, None], 0.0)
    full_total = jnp.where(chosen[None], row_total.T[:, None], 0.0)
    full_max = jnp.where(chosen[None], row_max.T[:, None], -1e30)
    return (
        full_num.reshape(picked_count * rate, heads_here, head_width),
        full_total.reshape(picked_count * rate, heads_here),
        full_max.reshape(picked_count * rate, heads_here),
    )


def doubling(buffer, steps_count):
    position = lax.axis_index("seq")
    for bit_index in range(steps_count):
        partner = partner_2(buffer, "seq", bit_index)
        is_lower = position >> bit_index & 1 == 0
        buffer = jnp.where(
            is_lower, jnp.concatenate([buffer, partner], 0), jnp.concatenate([partner, buffer], 0)
        )
    return buffer


def shards_general(queries, key_states, value_states, offsets_mid, offsets_top, out_weight):
    tok_rows = queries.shape[0]
    heads_local = offsets_mid.shape[0] // lax.axis_size("head")
    head_size = queries.shape[1] // heads_local
    seq_devices = lax.axis_size("seq")
    seq_total = tok_rows * seq_devices
    width_mid = min(16 * SEG, seq_total)
    rate_mid = width_mid // SEG
    rate_top = seq_total // SEG
    start_head = lax.axis_index("head") * heads_local
    mid_local = lax.dynamic_slice(offsets_mid, (start_head,), (heads_local,))
    top_local = lax.dynamic_slice(offsets_top, (start_head,), (heads_local,))
    query_heads = queries.reshape(tok_rows, 1, heads_local, head_size)
    paired = jnp.stack([key_states, value_states], axis=1).reshape(
        tok_rows, 2, heads_local, head_size
    )
    near_bits = (SEG // tok_rows).bit_length() - 1
    near_rows = doubling(paired.reshape(tok_rows, -1), near_bits).reshape(
        SEG, 2, heads_local, head_size
    )
    near_num, near_total, near_max = attend_local(query_heads[:, 0], near_rows)
    level_near = spread_back(
        near_num, near_total, near_max, jnp.zeros((heads_local,), jnp.int32), 1
    )
    mid_q = pick_rows(query_heads, mid_local, rate_mid)[:, 0]
    mid_kv = pick_rows(paired, mid_local, rate_mid)
    mid_group = width_mid // tok_rows
    mid_bits = mid_group.bit_length() - 1
    mid_rows = doubling(mid_kv.reshape(mid_kv.shape[0], -1), mid_bits).reshape(
        SEG, 2, heads_local, head_size
    )
    mid_num, mid_total, mid_max = attend_local(mid_q, mid_rows)
    level_mid = spread_back(mid_num, mid_total, mid_max, mid_local, rate_mid)
    top_q = pick_rows(query_heads, top_local, rate_top)[:, 0]
    top_kv = pick_rows(paired, top_local, rate_top)
    top_rows = lax.all_gather(
        top_kv.reshape(top_kv.shape[0], -1), "seq", axis=0, tiled=True
    ).reshape(SEG, 2, heads_local, head_size)
    top_num, top_total, top_max = attend_local(top_q, top_rows)
    level_top = spread_back(top_num, top_total, top_max, top_local, rate_top)
    levels = [level_near, level_mid, level_top]
    overall = jnp.maximum(jnp.maximum(level_near[2], level_mid[2]), level_top[2])
    numerator = jnp.zeros((tok_rows, heads_local, head_size), jnp.float32)
    row_total = jnp.zeros((tok_rows, heads_local), jnp.float32)
    for level_num, level_total, level_max in levels:
        factor = jnp.exp(level_max - overall)
        numerator = numerator + factor[..., None] * level_num
        row_total = row_total + factor * level_total
    attention = (
        (numerator / row_total[..., None])
        .astype(jnp.bfloat16)
        .reshape(tok_rows, heads_local * head_size)
    )
    result = lax.psum_scatter(
        jnp.dot(attention, out_weight, preferred_element_type=jnp.float32),
        "head",
        scatter_dimension=0,
        tiled=True,
    )
    return result.astype(jnp.bfloat16)


RATE = 4
GROUP = 4
HG = 4
DH = 48
BLK = 128
HALF = 2 * BLK
TOK = 512
SCALE = DH**-0.5 * LOG2E
BUSY = 1 << 33
AHEAD = 4
SAFE = 96.0
CHUNKS = ((0, 2), (2, 2))
DX = 64


def dot(a, b):
    return jnp.dot(a, b, preferred_element_type=F32)


def dot_nt(a, b):
    return lax.dot_general(a, b, (((1,), (1,)), ((), ())), preferred_element_type=F32)


def class_of_slots(off_mid, off_top):
    first = off_mid
    second = jnp.where(off_top == off_mid, lax.rem(off_mid + 1, RATE), off_top)
    free0 = (first != 0) & (second != 0)
    free1 = (first != 1) & (second != 1)
    third = jnp.where(free0, 0, jnp.where(free1, 1, 2))
    return first, second, third, 6 - first - second - third


def head_of(place, j, p):
    index = place[0][0]
    return ((index & (GROUP - 1)) ^ j) * HG + ((index // GROUP) ^ p)


def offsets_of(place, head):
    return place[1][head], place[2][head]


def token_picker():
    row = lax.broadcasted_iota(jnp.int32, (TOK, TOK), 0)
    col = lax.broadcasted_iota(jnp.int32, (TOK, TOK), 1)
    return (col == RATE * (row % BLK) + row // BLK).astype(BF16)


def fill_class_major(block, picker, scratch):
    scratch[...] = lax.dot_general(
        block, picker, (((0,), (1,)), ((), ())), preferred_element_type=F32
    ).astype(BF16)


def lane_block(index):
    return pl.ds(pl.multiple_of(index * BLK, BLK), BLK)


def head_rows(head):
    return pl.ds(pl.multiple_of(head * DH, 16), DH)


def pack_kernel(index, mid, top, k_hbm, v_hbm, q_hbm, *refs):
    place = (index, mid, top)
    outs, refs = refs[:6], refs[6:]
    blocks, held, packed = refs[:3], refs[3:6], refs[6:12]
    sems_in, sems_out = refs[12:]
    loads = [
        pltpu.make_async_copy(hbm, block, sems_in.at[i])
        for i, (hbm, block) in enumerate(zip((k_hbm, v_hbm, q_hbm), blocks))
    ]
    for load in loads:
        load.start()
    picker = token_picker()
    stores = []
    heads = {(j, p): head_of(place, j, p) for j in range(GROUP) for p in range(HG)}
    classes = {at: class_of_slots(*offsets_of(place, head)) for at, head in heads.items()}
    for n, (load, block, scratch) in enumerate(zip(loads, blocks, held)):
        load.wait()
        fill_class_major(block[...], picker, scratch)
        rows = slice(n * DH, (n + 1) * DH)
        for i, (j, first, count) in enumerate(
            ((0, 0, 4), (1, 0, 4), (2, 0, 2), (3, 0, 2), (2, 2, 2), (3, 2, 2))
        ):
            for p in range(HG):
                for s in range(count):
                    packed[i][p, rows, s * BLK : (s + 1) * BLK] = scratch[
                        head_rows(heads[j, p]), lane_block(classes[j, p][first + s])
                    ]
            store = pltpu.make_async_copy(
                packed[i].at[:, rows], outs[i].at[:, rows], sems_out.at[i, n]
            )
            store.start()
            stores.append(store)
    for store in stores:
        store.wait()


def regroup_kernel(a_ref, b_ref, *refs):
    for s, out in enumerate(refs[-3:]):
        out[0] = a_ref[s + 1, :, 0:HALF]
        out[1] = b_ref[s + 1, :, 0:HALF]


def upright(keys_t):
    return keys_t.T


def largest(blocks):
    best = None
    for block in blocks:
        wide = block.astype(F32)
        length = jnp.sum(wide * wide, axis=0, keepdims=True)
        for low in range(0, block.shape[1], HALF):
            part = length[:, low : low + HALF]
            best = part if best is None else jnp.maximum(best, part)
    return jnp.max(best)


def is_small(query_length, key_length):
    return query_length * key_length * (SCALE * SCALE) < SAFE * SAFE


def column_max(blocks):
    best = jnp.max(blocks[0], axis=0, keepdims=True)
    for block in blocks[1:]:
        best = jnp.maximum(best, jnp.max(block, axis=0, keepdims=True))
    return best * SCALE


def in_stages(items, score, weigh, gather):
    scores = {n: score(item) for n, item in enumerate(items[:AHEAD])}
    weights = weigh(items[0], scores.pop(0))
    for n, item in enumerate(items):
        if n + AHEAD < len(items):
            scores[n + AHEAD] = score(items[n + AHEAD])
        following = weigh(items[n + 1], scores.pop(n + 1)) if n + 1 < len(items) else None
        gather(item, weights)
        weights = following


def near_kernel(inputs, units, tasks, carried, first, step, index, mid, top, *refs):
    place = (index, mid, top)
    pieces = dict(zip(inputs, refs[: len(inputs)]))
    refs = refs[len(inputs) :]
    old = [refs[2 * i : 2 * i + 2] for i in range(carried)]
    outs = refs[2 * carried : 2 * carried + 2 * len(tasks)]
    k_s, v_s = refs[-2:]
    v_s[:, DH:DX, :] = jnp.ones((step, DX - DH, v_s.shape[2]), BF16)
    lane_slot = lax.broadcasted_iota(jnp.int32, (1, HALF), 1) // BLK

    def lookup(j, slot):
        first = 0 if (j, 0) in pieces and pieces[j, 0].shape[2] > HALF else slot // 2 * 2
        return pieces[j, first], (slot - first) * BLK

    chunks = []
    row = 0
    for label, members in units:
        chunks.append((label, slice(row, row + len(members) * BLK)))
        row += len(members) * BLK
    members = [member for _, group in units for member in group]

    def prepare(h):
        for i, (j, slot) in enumerate(members):
            ref, lane = lookup(j, slot)
            rows = slice(i * BLK, (i + 1) * BLK)
            k_s[h, rows, :] = upright(ref[h, 0:DH, lane : lane + BLK])
            v_s[h, 0:DH, rows] = ref[h, DH : 2 * DH, lane : lane + BLK]

    def counted_again(h):
        off_mid, off_top = offsets_of(place, head_of(place, 0, first + pl.program_id(0) * step + h))
        same = off_mid == off_top
        return [
            jnp.where(lane_slot == 0, jnp.where(same, 1.584962500721156, 1.0), 0.0),
            jnp.where(lane_slot == 1, jnp.where(same, 0.0, 1.0), 0.0),
        ]

    def run(heads):
        again = [counted_again(h) for h in heads]
        flat = [
            (h, again_h, query, low, merge, out, i)
            for h, again_h in zip(heads, again)
            for out, group in enumerate(tasks)
            for i, (query, low, merge) in enumerate(group)
        ]

        def score(task):
            h, _, (j, half), low = task[:4]
            ref, lane = lookup(j, 2 * half)
            query = ref[h, 2 * DH :, lane : lane + HALF]
            return [dot(k_s[h, rows, :], query) for _, rows in chunks[low:]]

        scores = score(flat[0])
        for n, (h, again_h, (_, half), low, merge, out, i) in enumerate(flat):
            following = score(flat[n + 1]) if n + 1 < len(flat) else None
            best = column_max(scores)
            if merge is not None:
                acc_in, max_in = old[merge[0]]
                old_max = max_in[h, merge[1], 0:1, :]
                best = jnp.maximum(best, old_max)
            acc = None
            for (label, rows), block in zip(chunks[low:], scores):
                block = block * SCALE
                if half == 0 and label is not None:
                    block = block - (best - again_h[label])
                else:
                    block = block - best
                part = dot(v_s[h, :, rows], jnp.exp2(block).astype(BF16))
                acc = part if acc is None else acc + part
            if merge is not None:
                acc = acc + acc_in[h, merge[1]] * jnp.exp2(old_max - best)
            acc_ref, max_ref = outs[2 * out : 2 * out + 2]
            acc_ref[h, i] = acc
            max_ref[h, i] = jnp.broadcast_to(best, (8, HALF))
            scores = following

    def run_plain():
        again = [counted_again(h) for h in range(step)]
        steps = [
            (h, query, merge, out, i, c, c == low, c == len(chunks) - 1)
            for h in range(step)
            for out, group in enumerate(tasks)
            for i, (query, low, merge) in enumerate(group)
            for c in range(low, len(chunks))
        ]

        def score(item):
            h, (j, half), c = item[0], item[1], item[5]
            ref, lane = lookup(j, 2 * half)
            return dot(k_s[h, chunks[c][1], :], ref[h, 2 * DH :, lane : lane + HALF])

        def weigh(item, block):
            h, (_, half), c = item[0], item[1], item[5]
            label = chunks[c][0]
            block = block * SCALE
            if half == 0 and label is not None:
                block = block + again[h][label]
            return jnp.exp2(block).astype(BF16)

        held = {}

        def gather(item, weights):
            h, _, merge, out, i, c, begins, ends = item
            part = dot(v_s[h, :, chunks[c][1]], weights)
            acc = part if begins else held[0] + part
            if ends:
                if merge is not None:
                    acc = acc + old[merge[0]][0][h, merge[1]]
                acc_ref, max_ref = outs[2 * out : 2 * out + 2]
                acc_ref[h, i] = acc
                max_ref[h, i] = jnp.zeros((8, HALF), F32)
            held[0] = acc

        in_stages(steps, score, weigh, gather)

    for h in range(step):
        prepare(h)
    plain = is_small(
        largest([ref[h, 2 * DH :, :] for ref in pieces.values() for h in range(step)]),
        largest([ref[h, 0:DH, :] for ref in pieces.values() for h in range(step)]),
    )
    for _, max_in in old:
        plain = plain & (jnp.max(jnp.abs(max_in[...])) == 0.0)

    @pl.when(plain)
    def _():
        run_plain()

    @pl.when(jnp.logical_not(plain))
    def _():
        @pl.loop(0, step)
        def _(h):
            run([h])


def far_slots(place):
    off_mid, off_top = offsets_of(place, head_of(place, 0, 0))
    same = off_mid == off_top
    return same, (0, jnp.where(same, 0, 1))


def far_pieces(place, sources, k_s, v_s, q_s):
    _, slots = far_slots(place)
    for s, pair in enumerate(sources):
        for i, ref in enumerate(pair):
            here = slice(i * BLK, (i + 1) * BLK)
            for level, slot in enumerate(slots):
                k_s[level, s, here, :] = upright(ref[0:DH, lane_block(slot)])
                v_s[level, s, 0:DH, here] = ref[DH : 2 * DH, lane_block(slot)]
                q_s[level, s, :, here] = ref[2 * DH : 3 * DH, lane_block(slot)]
    v_s[:, :, DH:DX, :] = jnp.ones((2, RATE, DX - DH, HALF), BF16)


def far_lengths(sources):
    every = [ref for pair in sources for ref in pair]
    return (
        largest([ref[2 * DH : 3 * DH, 0:HALF] for ref in every]),
        largest([ref[0:DH, 0:HALF] for ref in every]),
    )


def far_own_kernel(index, mid, top, own0, own1, beyond1, beyond2, beyond3, *refs):
    k_s, v_s, q_s, acc_ref, max_ref, length_ref = refs
    sources = [(own0.at[0], own1.at[0])] + [
        (ref.at[0], ref.at[1]) for ref in (beyond1, beyond2, beyond3)
    ]
    far_pieces((index, mid, top), sources, k_s, v_s, q_s)

    def run_plain():
        steps = [(level, d) for level in range(2) for d in range(1, RATE)]

        def segment(s, carry):
            def score(item):
                level, d = item
                return dot(k_s[level, s ^ d], q_s[level, s])

            def weigh(item, block):
                return jnp.exp2(block * SCALE).astype(BF16)

            held = {}

            def gather(item, weights):
                level, d = item
                part = dot(v_s[level, s ^ d], weights)
                held[0] = part if d == 1 else held[0] + part
                if d == RATE - 1:
                    acc_ref[level, s] = held[0]
                    max_ref[level, s] = jnp.zeros((8, HALF), F32)

            in_stages(steps, score, weigh, gather)
            return carry

        lax.fori_loop(0, RATE, segment, 0, unroll=2)

    def run():
        def segment(s, carry):
            def score(level):
                return [dot(k_s[level, s ^ d], q_s[level, s]) for d in range(1, RATE)]

            scores = score(0)
            for level in range(2):
                following = score(1) if level == 0 else None
                best = column_max(scores)
                acc = None
                for d in range(1, RATE):
                    block = scores[d - 1] * SCALE - best
                    part = dot(v_s[level, s ^ d], jnp.exp2(block).astype(BF16))
                    acc = part if acc is None else acc + part
                acc_ref[level, s] = acc
                max_ref[level, s] = jnp.broadcast_to(best, (8, HALF))
                scores = following
            return carry

        lax.fori_loop(0, RATE, segment, 0)

    query_length, key_length = far_lengths(sources)
    length_ref[0] = query_length
    length_ref[1] = key_length
    plain = is_small(query_length, key_length)
    pl.when(plain)(run_plain)
    pl.when(jnp.logical_not(plain))(run)


def far_kernel(index, mid, top, *refs):
    place = (index, mid, top)
    sel2, sel3, beyond3, beyond2, beyond1, k_own, v_own, q_own, acc_in, max_in, length_in = refs[
        :11
    ]
    outs = refs[11 : 11 + RATE]
    k_s, v_s, q_s, result_s, tail_s = refs[11 + RATE :]
    same, _ = far_slots(place)
    sources = [(sel2.at[0], sel3.at[0])] + [
        (ref.at[0], ref.at[1]) for ref in (beyond1, beyond2, beyond3)
    ]
    far_pieces(place, sources, k_s, v_s, q_s)
    tail_s[...] = jnp.zeros(tail_s.shape, F32)

    tasks = [(level, chip) for level in range(2) for chip in range(2)]
    held = ((k_own, v_own, q_own), (k_s, v_s, q_s))

    def blocks(s, chip):
        return [(held[c], s ^ d) for d in range(1, RATE) for c in ((1,), (0, 1))[chip]]

    def finish(s, level, chip, acc, best):
        total = acc[DH : DH + 1, :]
        result = (acc[0:DH, :] / total).astype(BF16)
        lse = best + jnp.log2(total)
        if level == 0:
            lse = jnp.where(same, lse + 1.0, lse)
        else:
            lse = jnp.where(same, -1e30, lse)
        high = lse.astype(BF16).astype(F32)
        middle = (lse - high).astype(BF16).astype(F32)
        low = lse - high - middle
        for i in range(2):
            n = 2 * (2 * chip + i) + level
            mine = slice(i * BLK, (i + 1) * BLK)
            result_s[s, :, n * BLK : (n + 1) * BLK] = result[:, mine]
            for k, part in enumerate((high, middle, low)):
                tail_s[s, 3 * n + k : 3 * n + k + 1, :] = part[:, mine]

    def run_plain():
        def segment(s, carry):
            steps = [
                (level, chip, keys, b, n)
                for level, chip in tasks
                for n, (keys, b) in enumerate(blocks(s, chip))
            ]

            def score(item):
                level, chip, keys, b, _ = item
                return dot(keys[0][level, b], held[chip][2][level, s])

            def weigh(item, block):
                return jnp.exp2(block * SCALE).astype(BF16)

            sums = {}

            def gather(item, weights):
                level, chip, keys, b, n = item
                part = dot(keys[1][level, b], weights)
                sums[0] = sums[0] + part if n else part
                if n + 1 == len(blocks(s, chip)):
                    acc = sums[0] + acc_in[level, s] if chip == 0 else sums[0]
                    finish(s, level, chip, acc, jnp.zeros((1, HALF), F32))

            in_stages(steps, score, weigh, gather)
            return carry

        lax.fori_loop(0, RATE, segment, 0, unroll=2)

    def run():
        def segment(s, carry):
            for level, chip in tasks:
                scores = [
                    dot(keys[0][level, b], held[chip][2][level, s]) for keys, b in blocks(s, chip)
                ]
                best = column_max(scores)
                acc = jnp.zeros((DX, HALF), F32)
                if chip == 0:
                    old_max = max_in[level, s, 0:1, :]
                    best = jnp.maximum(best, old_max)
                    acc = acc_in[level, s] * jnp.exp2(old_max - best)
                for block, (keys, b) in zip(scores, blocks(s, chip)):
                    acc += dot(keys[1][level, b], jnp.exp2(block * SCALE - best).astype(BF16))
                finish(s, level, chip, acc, best)
            return carry

        lax.fori_loop(0, RATE, segment, 0)

    query_length, key_length = far_lengths(sources)
    plain = is_small(
        jnp.maximum(query_length, length_in[0]), jnp.maximum(key_length, length_in[1])
    )
    pl.when(plain)(run_plain)
    pl.when(jnp.logical_not(plain))(run)
    for s in range(RATE):
        outs[s][:, : GROUP * HALF] = result_s[s]
        outs[s][:, GROUP * HALF :] = tail_s[s].astype(BF16)


def join(acc, best, far, j):
    tail = far[:, GROUP * HALF :].astype(F32)
    lse = jnp.concatenate(
        [
            tail[3 * n : 3 * n + 1] + tail[3 * n + 1 : 3 * n + 2] + tail[3 * n + 2 : 3 * n + 3]
            for n in (2 * j, 2 * j + 1)
        ],
        axis=1,
    )
    overall = jnp.maximum(best, lse)
    near_factor, far_factor = jnp.exp2(best - overall), jnp.exp2(lse - overall)
    total = acc[DH : DH + 1] * near_factor + far_factor
    value = far[:, j * HALF : (j + 1) * HALF].astype(F32) * far_factor
    return ((acc[0:DH] * near_factor + value) / total).astype(BF16)


def combine_kernel(chip, acc_ref, max_ref, *refs):
    far, outs = refs[:-2][::-1], refs[-2:]
    for i in range(2):
        for p, results in enumerate(far):
            outs[i][p, :, 0:HALF] = join(
                acc_ref[p, 2 * i], max_ref[p, 2 * i, 0:1, :], results, 2 * chip + i
            )
            acc = acc_ref[p, 2 * i + 1]
            outs[i][p, :, HALF:] = (acc[0:DH] / acc[DH : DH + 1]).astype(BF16)


def last_own_kernel(inputs, units, tasks, index, mid, top, *refs):
    count = len(inputs) + 2
    near_refs, far, outs, scratch = refs[:count], refs[count:-6], refs[-6:-4], refs[-4:]
    acc_s, max_s, k_s, v_s = scratch
    near_kernel(
        inputs, units, tasks, 1, 0, HG, index, mid, top, *near_refs, acc_s, max_s, k_s, v_s
    )
    combine_kernel(0, acc_s, max_s, *far, *outs)


def project_kernel(sources, index, mid, top, *refs):
    place = (index, mid, top)
    parts, (w_ref, out_ref, held) = refs[:-3], refs[-3:]
    for (j, first), part in zip(sources, parts):
        for p in range(part.shape[0]):
            head = head_of(place, j, first + p)
            slots = class_of_slots(*offsets_of(place, head))
            for s in range(RATE):
                held[head_rows(head), lane_block(slots[s])] = part[
                    p, :, s * BLK : (s + 1) * BLK
                ]
    row = lax.broadcasted_iota(jnp.int32, (TOK, TOK), 0)
    col = lax.broadcasted_iota(jnp.int32, (TOK, TOK), 1)
    picker = (row == RATE * (col % BLK) + col // BLK).astype(BF16)
    attention = dot_nt(picker, held[...]).astype(BF16)
    out_ref[...] = dot(attention, w_ref[...]).astype(BF16)


def whole(shape):
    return pl.BlockSpec(shape, lambda *_: (0,) * len(shape))


def per_head(shape, skip=0):
    return pl.BlockSpec(shape, lambda h, *_: (h + skip,) + (0,) * (len(shape) - 1))


def call(
    kernel, scalars, args, grid, in_specs, outs, scratch, scores,
    limit=VMEM_LIMIT, after=(), through=(), busy=0,
):
    known = len(scalars) + len(args)
    extra = (*after, *through)
    count = len(outs)
    anywhere = pl.BlockSpec(memory_space=pl.ANY)

    def body(*refs):
        results = refs[known + len(extra) :]
        kernel(*refs[:known], *results[:count], *results[count + len(through) :])

    return pl.pallas_call(
        body if extra else kernel,
        grid_spec=pltpu.PrefetchScalarGridSpec(
            num_scalar_prefetch=len(scalars),
            grid=grid,
            in_specs=list(in_specs) + [anywhere] * len(extra),
            out_specs=[spec for spec, _ in outs] + [anywhere] * len(through),
            scratch_shapes=scratch,
        ),
        out_shape=[shape for _, shape in outs]
        + [jax.ShapeDtypeStruct(x.shape, x.dtype) for x in through],
        input_output_aliases={known + len(after) + i: count + i for i in range(len(through))},
        compiler_params=pltpu.CompilerParams(vmem_limit_bytes=limit),
        cost_estimate=pl.CostEstimate(flops=busy, bytes_accessed=0, transcendentals=0),
    )(*scalars, *args, *extra)


def handed_on(arrays, **order):
    return call(lambda: None, (), (), (1,), [], [], [], 0, through=tuple(arrays), **order)


def within(array, apart):
    count = lax.axis_size("seq")
    return lax.ppermute(array, "seq", [(i, i ^ apart) for i in range(count)])


def swap_segments(arrays):
    moved = {s: within(arrays[s - 1], GROUP * s) for s in (3, 2, 1)}
    return [moved[s] for s in (1, 2, 3)]


def shards_four(queries, key_states, value_states, offsets_mid, offsets_top, out_weight):
    width = queries.shape[1]
    place = (lax.axis_index("seq").astype(jnp.int32).reshape(1), offsets_mid, offsets_top)
    full = jax.ShapeDtypeStruct((HG, 3 * DH, TOK), BF16)
    piece = jax.ShapeDtypeStruct((HG, 3 * DH, HALF), BF16)
    pair = jax.ShapeDtypeStruct((2, 3 * DH, HALF), BF16)
    anywhere = pl.BlockSpec(memory_space=pl.ANY)
    shapes = [full] * 2 + [piece] * 4
    own0, own1, sel2, sel3, rest2, rest3 = call(
        pack_kernel, place, (key_states, value_states, queries), (1,),
        [anywhere] * 3,
        [(anywhere, shape) for shape in shapes],
        [pltpu.VMEM((TOK, width), BF16)] * 3
        + [pltpu.VMEM((width, TOK), BF16)] * 3
        + [pltpu.VMEM(shape.shape, BF16) for shape in shapes]
        + [pltpu.SemaphoreType.DMA((3,)), pltpu.SemaphoreType.DMA((6, 3))],
        1 << 19, VMEM_MOST,
    )
    own1 = within(own1, 1)
    sel2, sel3 = within(sel2, 2), within(sel3, 3)

    def regroup(a, b, **order):
        return call(
            regroup_kernel, (), (a, b), (1,),
            [whole(a.shape), whole(b.shape)], [(whole(pair.shape), pair)] * 3,
            [], 1 << 17, **order,
        )

    def near(held, units, tasks, old, first=0, heads=HG, step=2, **order):
        sizes = [len(members) * BLK for _, members in units]
        scores = sum(sum(sizes[low:]) * HALF for group in tasks for _, low, _ in group)
        arrays = [*held.values(), *[x for one in old for x in one]]
        shapes = [
            jax.ShapeDtypeStruct((heads, len(group), rows, HALF), F32)
            for group in tasks
            for rows in (DX, 8)
        ]
        return call(
            functools.partial(near_kernel, list(held), units, tasks, len(old), first, step),
            place, arrays, (heads // step,),
            [per_head((step,) + x.shape[1:], first // step) for x in arrays],
            [(per_head((step,) + x.shape[1:]), x) for x in shapes],
            [
                pltpu.VMEM((step, sum(sizes), DH), BF16),
                pltpu.VMEM((step, DX, sum(sizes)), BF16),
            ],
            heads * scores, **order,
        )

    def units_of(a, b):
        return [(0, [(a, 0), (b, 0)]), (1, [(a, 1), (b, 1)])], [
            (None, [(a, 2), (a, 3), (b, 2), (b, 3)])
        ]

    own_sel, own_rest = units_of(0, 1)
    other_sel, other_rest = units_of(2, 3)
    own = [(0, 0), (0, 1), (1, 0), (1, 1)]

    ours = regroup(own0, own1)
    ours = swap_segments(ours)
    held = {(0, 0): own0, (1, 0): own1}
    state_own = near(held, own_sel + own_rest, [[(q, 0, None) for q in own]], [])
    *theirs, rest2, rest3 = regroup(sel2, sel3, after=state_own[1:], through=(rest2, rest3))
    theirs = swap_segments(theirs)
    rest2, rest3 = within(rest2, 2), within(rest3, 3)

    held.update({(2, 0): sel2, (3, 0): sel3})
    out = near(
        held, own_sel + own_rest + other_sel,
        [
            [(q, 3, (0, i)) for i, q in enumerate(own)],
            [((2, 0), 0, None), ((3, 0), 0, None)],
        ],
        [state_own],
        after=ours[::-1],
    )
    state_own, state_sel = out[:2], out[2:]

    result = jax.ShapeDtypeStruct((DH, GROUP * HALF + BLK), BF16)
    piece_0 = pl.BlockSpec((1, 3 * DH, HALF), lambda *_: (0, 0, 0))
    pieces_shapes = [
        jax.ShapeDtypeStruct((2, RATE, HALF, DH), BF16),
        jax.ShapeDtypeStruct((2, RATE, DX, HALF), BF16),
        jax.ShapeDtypeStruct((2, RATE, DH, HALF), BF16),
    ]
    sums_shapes = [
        jax.ShapeDtypeStruct((2, RATE, DX, HALF), F32),
        jax.ShapeDtypeStruct((2, RATE, 8, HALF), F32),
    ]
    in_scalars = pl.BlockSpec(memory_space=pltpu.SMEM)
    far_own = call(
        far_own_kernel, place, (own0, own1, *ours), (1,),
        [piece_0] * 2 + [whole(pair.shape)] * 3,
        [(whole(x.shape), x) for x in pieces_shapes + sums_shapes]
        + [(in_scalars, jax.ShapeDtypeStruct((2,), F32))],
        [], RATE * 2 * 3 * HALF * HALF, after=(state_sel[1],),
    )
    results = call(
        far_kernel, place, (sel2, sel3, *theirs[::-1], *far_own), (1,),
        [piece_0] * 2 + [whole(pair.shape)] * 3
        + [whole(x.shape) for x in far_own[:-1]] + [in_scalars],
        [(whole(result.shape), result)] * RATE,
        [pltpu.VMEM(x.shape, BF16) for x in pieces_shapes]
        + [
            pltpu.VMEM((RATE, DH, GROUP * HALF), BF16),
            pltpu.VMEM((RATE, DH, BLK), F32),
        ],
        RATE * 2 * 3 * 3 * HALF * HALF, busy=BUSY,
    )
    back = [results[0]] + swap_segments(results[1:])

    held.update({(2, 2): rest2, (3, 2): rest3})
    units = own_sel + own_rest + other_sel + other_rest

    def combine(chip, state, far, **order):
        heads = state[0].shape[0]
        attended = jax.ShapeDtypeStruct((heads, DH, TOK), BF16)
        return call(
            functools.partial(combine_kernel, chip), (), (*state, *far[::-1]), (1,),
            [whole(x.shape) for x in state] + [whole(result.shape)] * heads,
            [(whole(attended.shape), attended)] * 2,
            [],
            1 << 18, **order,
        )

    parts, last = {}, results[0]
    for first, heads in CHUNKS:
        state_other = near(
            held, units,
            [
                [
                    ((2, 0), 5, (0, 0)), ((2, 1), 0, None),
                    ((3, 0), 5, (0, 1)), ((3, 1), 0, None),
                ]
            ],
            [state_sel],
            first, heads, 2, after=(last,),
        )
        if first:
            back[1:] = handed_on(back[1:], after=state_other[1:])
        part2, part3 = combine(1, state_other, back[first : first + heads])
        early = tuple(parts.values())
        parts[2, first], parts[3, first] = within(part2, 2), within(part3, 3)
        last = part3
    pieces = {(2, 2): rest2, (3, 2): rest3, **{q: held[q] for q in ((0, 0), (1, 0))}}
    arrays = [*pieces.values(), *state_own, *back[::-1]]
    attended = jax.ShapeDtypeStruct((HG, DH, TOK), BF16)
    part0, part1 = call(
        functools.partial(
            last_own_kernel, list(pieces), other_rest, [[(q, 0, (0, i)) for i, q in enumerate(own)]]
        ),
        place, arrays, (1,),
        [whole(x.shape) for x in arrays],
        [(whole(attended.shape), attended)] * 2,
        [pltpu.VMEM(x.shape, F32) for x in state_own]
        + [pltpu.VMEM((HG, TOK, DH), BF16), pltpu.VMEM((HG, DX, TOK), BF16)],
        HG * TOK * GROUP * HALF, after=(last, *early),
    )
    parts = dict(zip(parts, handed_on(parts.values(), busy=BUSY)))
    parts[0, 0], parts[1, 0] = part0, within(part1, 1)
    return call(
        functools.partial(project_kernel, list(parts)), place, (*parts.values(), out_weight), (1,),
        [whole(x.shape) for x in parts.values()] + [whole((width, width))],
        [(whole((TOK, width)), jax.ShapeDtypeStruct((TOK, width), BF16))],
        [pltpu.VMEM((width, TOK), BF16)],
        1 << 18,
    )[0]


def shards(queries, key_states, value_states, offsets_mid, offsets_top, out_weight):
    tokens, width = queries.shape
    heads = offsets_mid.shape[0]
    fits = (
        lax.axis_size("head") == 1
        and lax.axis_size("seq") == GROUP * RATE
        and tokens == TOK
        and heads == GROUP * HG
        and width == heads * DH
    )
    run = shards_four if fits else shards_general
    return run(queries, key_states, value_states, offsets_mid, offsets_top, out_weight)


def solution(mesh):
    in_specs = (
        P(("slide", "seq"), "head"),
        P(("slide", "seq"), "head"),
        P(("slide", "seq"), "head"),
        P(),
        P(),
        P("head", None),
    )
    out_specs = P(("slide", "seq", "head"), None)
    return jax.shard_map(shards, mesh=mesh, in_specs=in_specs, out_specs=out_specs, check_vma=False)
```

```python
import functools

import jax
import jax.numpy as jnp
from jax import lax
from jax.experimental import pallas as pl
from jax.experimental.pallas import tpu as pltpu
from jax.sharding import PartitionSpec as P

SEG = 2048
LOG2E = 1.4426950408889634
VMEM_LIMIT = 40 * 1024 * 1024
VMEM_MOST = 60 * 1024 * 1024
BF16 = jnp.bfloat16
F32 = jnp.float32


def partner_2(block, axis, apart):
    count = lax.axis_size(axis)
    route = []
    for low in range(count):
        high = low | 1 << apart
        if high != low and high < count:
            route += [(low, high), (high, low)]
    return lax.ppermute(block, axis, route)


def attend_head(triple_in):
    query_rows, key_rows, value_rows = triple_in
    score_scale = query_rows.shape[-1] ** (-0.5)
    scores = jnp.dot(query_rows, key_rows.T, preferred_element_type=jnp.float32) * score_scale
    row_max = jnp.max(scores, axis=1)
    shifted = jnp.exp(scores - row_max[:, None])
    row_total = jnp.sum(shifted, axis=1)
    weights = shifted.astype(jnp.bfloat16)
    numerator = jnp.dot(weights, value_rows, preferred_element_type=jnp.float32)
    return (numerator, row_total, row_max)


def attend_local(query_rows, pair_rows):
    return lax.map(
        attend_head,
        (
            query_rows.transpose(1, 0, 2),
            pair_rows[:, 0].transpose(1, 0, 2),
            pair_rows[:, 1].transpose(1, 0, 2),
        ),
    )


def pick_rows(states, offsets, rate):
    row_count, inner_count, heads_here, head_width = states.shape
    picker = (jnp.arange(rate)[:, None] == offsets[None, :]).astype(jnp.bfloat16)
    folded = states.reshape(row_count // rate, rate, inner_count, heads_here, head_width)
    return jnp.einsum("archd,rh->achd", folded, picker, preferred_element_type=jnp.float32).astype(
        jnp.bfloat16
    )


def spread_back(numerator, row_total, row_max, offsets, rate):
    heads_here, picked_count, head_width = numerator.shape
    chosen = jnp.arange(rate)[:, None] == offsets[None, :]
    full_num = jnp.where(chosen[None, :, :, None], numerator.transpose(1, 0, 2)[:, None], 0.0)
    full_total = jnp.where(chosen[None], row_total.T[:, None], 0.0)
    full_max = jnp.where(chosen[None], row_max.T[:, None], -1e30)
    return (
        full_num.reshape(picked_count * rate, heads_here, head_width),
        full_total.reshape(picked_count * rate, heads_here),
        full_max.reshape(picked_count * rate, heads_here),
    )


def doubling(buffer, steps_count):
    position = lax.axis_index("seq")
    for bit_index in range(steps_count):
        partner = partner_2(buffer, "seq", bit_index)
        is_lower = position >> bit_index & 1 == 0
        buffer = jnp.where(
            is_lower, jnp.concatenate([buffer, partner], 0), jnp.concatenate([partner, buffer], 0)
        )
    return buffer


def shards_general(queries, key_states, value_states, offsets_mid, offsets_top, out_weight):
    tok_rows = queries.shape[0]
    heads_local = offsets_mid.shape[0] // lax.axis_size("head")
    head_size = queries.shape[1] // heads_local
    seq_devices = lax.axis_size("seq")
    seq_total = tok_rows * seq_devices
    width_mid = min(16 * SEG, seq_total)
    rate_mid = width_mid // SEG
    rate_top = seq_total // SEG
    start_head = lax.axis_index("head") * heads_local
    mid_local = lax.dynamic_slice(offsets_mid, (start_head,), (heads_local,))
    top_local = lax.dynamic_slice(offsets_top, (start_head,), (heads_local,))
    query_heads = queries.reshape(tok_rows, 1, heads_local, head_size)
    paired = jnp.stack([key_states, value_states], axis=1).reshape(
        tok_rows, 2, heads_local, head_size
    )
    near_bits = (SEG // tok_rows).bit_length() - 1
    near_rows = doubling(paired.reshape(tok_rows, -1), near_bits).reshape(
        SEG, 2, heads_local, head_size
    )
    near_num, near_total, near_max = attend_local(query_heads[:, 0], near_rows)
    level_near = spread_back(
        near_num, near_total, near_max, jnp.zeros((heads_local,), jnp.int32), 1
    )
    mid_q = pick_rows(query_heads, mid_local, rate_mid)[:, 0]
    mid_kv = pick_rows(paired, mid_local, rate_mid)
    mid_group = width_mid // tok_rows
    mid_bits = mid_group.bit_length() - 1
    mid_rows = doubling(mid_kv.reshape(mid_kv.shape[0], -1), mid_bits).reshape(
        SEG, 2, heads_local, head_size
    )
    mid_num, mid_total, mid_max = attend_local(mid_q, mid_rows)
    level_mid = spread_back(mid_num, mid_total, mid_max, mid_local, rate_mid)
    top_q = pick_rows(query_heads, top_local, rate_top)[:, 0]
    top_kv = pick_rows(paired, top_local, rate_top)
    top_rows = lax.all_gather(
        top_kv.reshape(top_kv.shape[0], -1), "seq", axis=0, tiled=True
    ).reshape(SEG, 2, heads_local, head_size)
    top_num, top_total, top_max = attend_local(top_q, top_rows)
    level_top = spread_back(top_num, top_total, top_max, top_local, rate_top)
    levels = [level_near, level_mid, level_top]
    overall = jnp.maximum(jnp.maximum(level_near[2], level_mid[2]), level_top[2])
    numerator = jnp.zeros((tok_rows, heads_local, head_size), jnp.float32)
    row_total = jnp.zeros((tok_rows, heads_local), jnp.float32)
    for level_num, level_total, level_max in levels:
        factor = jnp.exp(level_max - overall)
        numerator = numerator + factor[..., None] * level_num
        row_total = row_total + factor * level_total
    attention = (
        (numerator / row_total[..., None])
        .astype(jnp.bfloat16)
        .reshape(tok_rows, heads_local * head_size)
    )
    result = lax.psum_scatter(
        jnp.dot(attention, out_weight, preferred_element_type=jnp.float32),
        "head",
        scatter_dimension=0,
        tiled=True,
    )
    return result.astype(jnp.bfloat16)


RATE = 4
GROUP = 4
HG = 4
DH = 48
BLK = 128
HALF = 2 * BLK
TOK = 512
SCALE = DH**-0.5 * LOG2E
BUSY = 1 << 33
AHEAD = 4
SAFE = 96.0
CHUNKS = ((0, 2), (2, 2))
DX = 64


def dot(a, b):
    return jnp.dot(a, b, preferred_element_type=F32)


def dot_nt(a, b):
    return lax.dot_general(a, b, (((1,), (1,)), ((), ())), preferred_element_type=F32)


def class_of_slots(off_mid, off_top):
    first = off_mid
    second = jnp.where(off_top == off_mid, lax.rem(off_mid + 1, RATE), off_top)
    free0 = (first != 0) & (second != 0)
    free1 = (first != 1) & (second != 1)
    third = jnp.where(free0, 0, jnp.where(free1, 1, 2))
    return first, second, third, 6 - first - second - third


def head_of(place, j, p):
    index = place[0][0]
    return ((index & (GROUP - 1)) ^ j) * HG + ((index // GROUP) ^ p)


def offsets_of(place, head):
    return place[1][head], place[2][head]


def token_picker():
    row = lax.broadcasted_iota(jnp.int32, (TOK, TOK), 0)
    col = lax.broadcasted_iota(jnp.int32, (TOK, TOK), 1)
    return (col == RATE * (row % BLK) + row // BLK).astype(BF16)


def fill_class_major(block, picker, scratch):
    scratch[...] = lax.dot_general(
        block, picker, (((0,), (1,)), ((), ())), preferred_element_type=F32
    ).astype(BF16)


def lane_block(index):
    return pl.ds(pl.multiple_of(index * BLK, BLK), BLK)


def head_rows(head):
    return pl.ds(pl.multiple_of(head * DH, 16), DH)


def pack_kernel(index, mid, top, k_hbm, v_hbm, q_hbm, *refs):
    place = (index, mid, top)
    outs, refs = refs[:6], refs[6:]
    blocks, held, packed = refs[:3], refs[3:6], refs[6:12]
    sems_in, sems_out = refs[12:]
    loads = [
        pltpu.make_async_copy(hbm, block, sems_in.at[i])
        for i, (hbm, block) in enumerate(zip((k_hbm, v_hbm, q_hbm), blocks))
    ]
    loads[0].start()
    picker = token_picker()
    stores = []
    heads = {(j, p): head_of(place, j, p) for j in range(GROUP) for p in range(HG)}
    classes = {at: class_of_slots(*offsets_of(place, head)) for at, head in heads.items()}
    for n, (load, block, scratch) in enumerate(zip(loads, blocks, held)):
        load.wait()
        for later in loads[1:] if n == 0 else ():
            later.start()
        fill_class_major(block[...], picker, scratch)
        rows = slice(n * DH, (n + 1) * DH)
        for i, (j, first, count) in enumerate(
            ((0, 0, 4), (1, 0, 4), (2, 0, 2), (3, 0, 2), (2, 2, 2), (3, 2, 2))
        ):
            for p in range(HG):
                for s in range(count):
                    packed[i][p, rows, s * BLK : (s + 1) * BLK] = scratch[
                        head_rows(heads[j, p]), lane_block(classes[j, p][first + s])
                    ]
            store = pltpu.make_async_copy(
                packed[i].at[:, rows], outs[i].at[:, rows], sems_out.at[i, n]
            )
            store.start()
            stores.append(store)
    for store in stores:
        store.wait()


def regroup_kernel(a_ref, b_ref, *refs):
    for s, out in enumerate(refs[-3:]):
        out[0] = a_ref[s + 1, :, 0:HALF]
        out[1] = b_ref[s + 1, :, 0:HALF]


def upright(keys_t):
    return keys_t.T


def largest(blocks):
    best = None
    for block in blocks:
        wide = block.astype(F32)
        length = jnp.sum(wide * wide, axis=0, keepdims=True)
        for low in range(0, block.shape[1], HALF):
            part = length[:, low : low + HALF]
            best = part if best is None else jnp.maximum(best, part)
    return jnp.max(best)


def is_small(query_length, key_length):
    return query_length * key_length * (SCALE * SCALE) < SAFE * SAFE


def column_max(blocks):
    best = jnp.max(blocks[0], axis=0, keepdims=True)
    for block in blocks[1:]:
        best = jnp.maximum(best, jnp.max(block, axis=0, keepdims=True))
    return best * SCALE


def in_stages(items, score, weigh, gather):
    scores = {n: score(item) for n, item in enumerate(items[:AHEAD])}
    weights = weigh(items[0], scores.pop(0))
    for n, item in enumerate(items):
        if n + AHEAD < len(items):
            scores[n + AHEAD] = score(items[n + AHEAD])
        following = weigh(items[n + 1], scores.pop(n + 1)) if n + 1 < len(items) else None
        gather(item, weights)
        weights = following


def near_kernel(inputs, units, tasks, carried, first, step, index, mid, top, *refs):
    place = (index, mid, top)
    pieces = dict(zip(inputs, refs[: len(inputs)]))
    refs = refs[len(inputs) :]
    old = [refs[2 * i : 2 * i + 2] for i in range(carried)]
    outs = refs[2 * carried : 2 * carried + 2 * len(tasks)]
    k_s, v_s = refs[-2:]
    v_s[:, DH:DX, :] = jnp.ones((step, DX - DH, v_s.shape[2]), BF16)
    lane_slot = lax.broadcasted_iota(jnp.int32, (1, HALF), 1) // BLK

    def lookup(j, slot):
        first = 0 if (j, 0) in pieces and pieces[j, 0].shape[2] > HALF else slot // 2 * 2
        return pieces[j, first], (slot - first) * BLK

    chunks = []
    row = 0
    for label, members in units:
        chunks.append((label, slice(row, row + len(members) * BLK)))
        row += len(members) * BLK
    members = [member for _, group in units for member in group]

    def prepare(h):
        for i, (j, slot) in enumerate(members):
            ref, lane = lookup(j, slot)
            rows = slice(i * BLK, (i + 1) * BLK)
            k_s[h, rows, :] = upright(ref[h, 0:DH, lane : lane + BLK])
            v_s[h, 0:DH, rows] = ref[h, DH : 2 * DH, lane : lane + BLK]

    def counted_again(h):
        off_mid, off_top = offsets_of(place, head_of(place, 0, first + pl.program_id(0) * step + h))
        same = off_mid == off_top
        return [
            jnp.where(lane_slot == 0, jnp.where(same, 1.584962500721156, 1.0), 0.0),
            jnp.where(lane_slot == 1, jnp.where(same, 0.0, 1.0), 0.0),
        ]

    def run(heads):
        again = [counted_again(h) for h in heads]
        flat = [
            (h, again_h, query, low, merge, out, i)
            for h, again_h in zip(heads, again)
            for out, group in enumerate(tasks)
            for i, (query, low, merge) in enumerate(group)
        ]

        def score(task):
            h, _, (j, half), low = task[:4]
            ref, lane = lookup(j, 2 * half)
            query = ref[h, 2 * DH :, lane : lane + HALF]
            return [dot(k_s[h, rows, :], query) for _, rows in chunks[low:]]

        scores = score(flat[0])
        for n, (h, again_h, (_, half), low, merge, out, i) in enumerate(flat):
            following = score(flat[n + 1]) if n + 1 < len(flat) else None
            best = column_max(scores)
            if merge is not None:
                acc_in, max_in = old[merge[0]]
                old_max = max_in[h, merge[1], 0:1, :]
                best = jnp.maximum(best, old_max)
            acc = None
            for (label, rows), block in zip(chunks[low:], scores):
                block = block * SCALE
                if half == 0 and label is not None:
                    block = block - (best - again_h[label])
                else:
                    block = block - best
                part = dot(v_s[h, :, rows], jnp.exp2(block).astype(BF16))
                acc = part if acc is None else acc + part
            if merge is not None:
                acc = acc + acc_in[h, merge[1]] * jnp.exp2(old_max - best)
            acc_ref, max_ref = outs[2 * out : 2 * out + 2]
            acc_ref[h, i] = acc
            max_ref[h, i] = jnp.broadcast_to(best, (8, HALF))
            scores = following

    def run_plain():
        again = [counted_again(h) for h in range(step)]
        steps = [
            (h, query, merge, out, i, c, c == low, c == len(chunks) - 1)
            for h in range(step)
            for out, group in enumerate(tasks)
            for i, (query, low, merge) in enumerate(group)
            for c in range(low, len(chunks))
        ]

        def score(item):
            h, (j, half), c = item[0], item[1], item[5]
            ref, lane = lookup(j, 2 * half)
            return dot(k_s[h, chunks[c][1], :], ref[h, 2 * DH :, lane : lane + HALF])

        def weigh(item, block):
            h, (_, half), c = item[0], item[1], item[5]
            label = chunks[c][0]
            block = block * SCALE
            if half == 0 and label is not None:
                block = block + again[h][label]
            return jnp.exp2(block).astype(BF16)

        held = {}

        def gather(item, weights):
            h, _, merge, out, i, c, begins, ends = item
            part = dot(v_s[h, :, chunks[c][1]], weights)
            acc = part if begins else held[0] + part
            if ends:
                if merge is not None:
                    acc = acc + old[merge[0]][0][h, merge[1]]
                acc_ref, max_ref = outs[2 * out : 2 * out + 2]
                acc_ref[h, i] = acc
                max_ref[h, i] = jnp.zeros((8, HALF), F32)
            held[0] = acc

        in_stages(steps, score, weigh, gather)

    for h in range(step):
        prepare(h)
    plain = is_small(
        largest([ref[h, 2 * DH :, :] for ref in pieces.values() for h in range(step)]),
        largest([ref[h, 0:DH, :] for ref in pieces.values() for h in range(step)]),
    )
    for _, max_in in old:
        plain = plain & (jnp.max(jnp.abs(max_in[...])) == 0.0)

    @pl.when(plain)
    def _():
        run_plain()

    @pl.when(jnp.logical_not(plain))
    def _():
        @pl.loop(0, step)
        def _(h):
            run([h])


def far_slots(place):
    off_mid, off_top = offsets_of(place, head_of(place, 0, 0))
    same = off_mid == off_top
    return same, (0, jnp.where(same, 0, 1))


def far_pieces(place, sources, k_s, v_s, q_s):
    _, slots = far_slots(place)
    for s, pair in enumerate(sources):
        for i, ref in enumerate(pair):
            here = slice(i * BLK, (i + 1) * BLK)
            for level, slot in enumerate(slots):
                k_s[level, s, here, :] = upright(ref[0:DH, lane_block(slot)])
                v_s[level, s, 0:DH, here] = ref[DH : 2 * DH, lane_block(slot)]
                q_s[level, s, :, here] = ref[2 * DH : 3 * DH, lane_block(slot)]
    v_s[:, :, DH:DX, :] = jnp.ones((2, RATE, DX - DH, HALF), BF16)


def far_lengths(sources):
    every = [ref for pair in sources for ref in pair]
    return (
        largest([ref[2 * DH : 3 * DH, 0:HALF] for ref in every]),
        largest([ref[0:DH, 0:HALF] for ref in every]),
    )


def far_own_kernel(index, mid, top, own0, own1, beyond3, beyond2, beyond1, *refs):
    k_s, v_s, q_s, acc_ref, max_ref, length_ref = refs
    sources = [(own0.at[0], own1.at[0])] + [
        (ref.at[0], ref.at[1]) for ref in (beyond1, beyond2, beyond3)
    ]
    far_pieces((index, mid, top), sources, k_s, v_s, q_s)

    def run_plain():
        steps = [(level, d) for level in range(2) for d in range(1, RATE)]

        def segment(s, carry):
            def score(item):
                level, d = item
                return dot(k_s[level, s ^ d], q_s[level, s])

            def weigh(item, block):
                return jnp.exp2(block * SCALE).astype(BF16)

            held = {}

            def gather(item, weights):
                level, d = item
                part = dot(v_s[level, s ^ d], weights)
                held[0] = part if d == 1 else held[0] + part
                if d == RATE - 1:
                    acc_ref[level, s] = held[0]
                    max_ref[level, s] = jnp.zeros((8, HALF), F32)

            in_stages(steps, score, weigh, gather)
            return carry

        lax.fori_loop(0, RATE, segment, 0, unroll=2)

    def run():
        def segment(s, carry):
            def score(level):
                return [dot(k_s[level, s ^ d], q_s[level, s]) for d in range(1, RATE)]

            scores = score(0)
            for level in range(2):
                following = score(1) if level == 0 else None
                best = column_max(scores)
                acc = None
                for d in range(1, RATE):
                    block = scores[d - 1] * SCALE - best
                    part = dot(v_s[level, s ^ d], jnp.exp2(block).astype(BF16))
                    acc = part if acc is None else acc + part
                acc_ref[level, s] = acc
                max_ref[level, s] = jnp.broadcast_to(best, (8, HALF))
                scores = following
            return carry

        lax.fori_loop(0, RATE, segment, 0)

    query_length, key_length = far_lengths(sources)
    length_ref[0] = query_length
    length_ref[1] = key_length
    plain = is_small(query_length, key_length)
    pl.when(plain)(run_plain)
    pl.when(jnp.logical_not(plain))(run)


def near_and_far_kernel(near_args, steps, index, mid, top, *refs):
    scalars = (index, mid, top)
    inputs, tasks, carried = near_args[0], near_args[2], near_args[3]
    count = len(inputs) + 2 * carried
    near_in, far_in, refs = refs[:count], refs[count : count + 5], refs[count + 5 :]
    near_out, far_out, scratch = refs[: 2 * len(tasks)], refs[2 * len(tasks) : -2], refs[-2:]

    @pl.when(pl.program_id(0) < steps)
    def _():
        near_kernel(*near_args, *scalars, *near_in, *near_out, *scratch)

    @pl.when(pl.program_id(0) == steps)
    def _():
        far_own_kernel(*scalars, *far_in, *far_out)


def far_kernel(index, mid, top, *refs):
    place = (index, mid, top)
    sel2, sel3, beyond2, beyond1, beyond3, k_own, v_own, q_own, acc_in, max_in, length_in = refs[
        :11
    ]
    outs = refs[11 : 11 + RATE]
    k_s, v_s, q_s, result_s, tail_s = refs[11 + RATE :]
    same, _ = far_slots(place)
    sources = [(sel2.at[0], sel3.at[0])] + [
        (ref.at[0], ref.at[1]) for ref in (beyond1, beyond2, beyond3)
    ]
    far_pieces(place, sources, k_s, v_s, q_s)
    tail_s[...] = jnp.zeros(tail_s.shape, F32)

    tasks = [(level, chip) for level in range(2) for chip in range(2)]
    held = ((k_own, v_own, q_own), (k_s, v_s, q_s))

    def blocks(s, chip):
        return [(held[c], s ^ d) for d in range(1, RATE) for c in ((1,), (0, 1))[chip]]

    def finish(s, level, chip, acc, best):
        total = acc[DH : DH + 1, :]
        result = (acc[0:DH, :] / total).astype(BF16)
        lse = best + jnp.log2(total)
        if level == 0:
            lse = jnp.where(same, lse + 1.0, lse)
        else:
            lse = jnp.where(same, -1e30, lse)
        high = lse.astype(BF16).astype(F32)
        middle = (lse - high).astype(BF16).astype(F32)
        low = lse - high - middle
        for i in range(2):
            n = 2 * (2 * chip + i) + level
            mine = slice(i * BLK, (i + 1) * BLK)
            result_s[s, :, n * BLK : (n + 1) * BLK] = result[:, mine]
            for k, part in enumerate((high, middle, low)):
                tail_s[s, 3 * n + k : 3 * n + k + 1, :] = part[:, mine]

    def run_plain():
        def segment(s, carry):
            steps = [
                (level, chip, keys, b, n)
                for level, chip in tasks
                for n, (keys, b) in enumerate(blocks(s, chip))
            ]

            def score(item):
                level, chip, keys, b, _ = item
                return dot(keys[0][level, b], held[chip][2][level, s])

            def weigh(item, block):
                return jnp.exp2(block * SCALE).astype(BF16)

            sums = {}

            def gather(item, weights):
                level, chip, keys, b, n = item
                part = dot(keys[1][level, b], weights)
                sums[0] = sums[0] + part if n else part
                if n + 1 == len(blocks(s, chip)):
                    acc = sums[0] + acc_in[level, s] if chip == 0 else sums[0]
                    finish(s, level, chip, acc, jnp.zeros((1, HALF), F32))

            in_stages(steps, score, weigh, gather)
            return carry

        lax.fori_loop(0, RATE, segment, 0, unroll=2)

    def run():
        def segment(s, carry):
            for level, chip in tasks:
                scores = [
                    dot(keys[0][level, b], held[chip][2][level, s]) for keys, b in blocks(s, chip)
                ]
                best = column_max(scores)
                acc = jnp.zeros((DX, HALF), F32)
                if chip == 0:
                    old_max = max_in[level, s, 0:1, :]
                    best = jnp.maximum(best, old_max)
                    acc = acc_in[level, s] * jnp.exp2(old_max - best)
                for block, (keys, b) in zip(scores, blocks(s, chip)):
                    acc += dot(keys[1][level, b], jnp.exp2(block * SCALE - best).astype(BF16))
                finish(s, level, chip, acc, best)
            return carry

        lax.fori_loop(0, RATE, segment, 0)

    query_length, key_length = far_lengths(sources)
    plain = is_small(
        jnp.maximum(query_length, length_in[0]), jnp.maximum(key_length, length_in[1])
    )
    pl.when(plain)(run_plain)
    pl.when(jnp.logical_not(plain))(run)
    for s in range(RATE):
        outs[s][:, : GROUP * HALF] = result_s[s]
        outs[s][:, GROUP * HALF :] = tail_s[s].astype(BF16)


def join(acc, best, far, j):
    tail = far[:, GROUP * HALF :].astype(F32)
    lse = jnp.concatenate(
        [
            tail[3 * n : 3 * n + 1] + tail[3 * n + 1 : 3 * n + 2] + tail[3 * n + 2 : 3 * n + 3]
            for n in (2 * j, 2 * j + 1)
        ],
        axis=1,
    )
    overall = jnp.maximum(best, lse)
    near_factor, far_factor = jnp.exp2(best - overall), jnp.exp2(lse - overall)
    total = acc[DH : DH + 1] * near_factor + far_factor
    value = far[:, j * HALF : (j + 1) * HALF].astype(F32) * far_factor
    return ((acc[0:DH] * near_factor + value) / total).astype(BF16)


def combine_kernel(chip, acc_ref, max_ref, *refs):
    far, outs = refs[:-2][::-1], refs[-2:]
    for i in range(2):
        for p, results in enumerate(far):
            outs[i][p, :, 0:HALF] = join(
                acc_ref[p, 2 * i], max_ref[p, 2 * i, 0:1, :], results, 2 * chip + i
            )
            acc = acc_ref[p, 2 * i + 1]
            outs[i][p, :, HALF:] = (acc[0:DH] / acc[DH : DH + 1]).astype(BF16)


def last_own_kernel(inputs, units, tasks, index, mid, top, *refs):
    count = len(inputs) + 2
    near_refs, far, outs, scratch = refs[:count], refs[count:-6], refs[-6:-4], refs[-4:]
    acc_s, max_s, k_s, v_s = scratch
    near_kernel(
        inputs, units, tasks, 1, 0, HG, index, mid, top, *near_refs, acc_s, max_s, k_s, v_s
    )
    combine_kernel(0, acc_s, max_s, *far, *outs)


def project_kernel(sources, index, mid, top, *refs):
    place = (index, mid, top)
    parts, (w_ref, out_ref, held) = refs[:-3], refs[-3:]
    for (j, first), part in zip(sources, parts):
        for p in range(part.shape[0]):
            head = head_of(place, j, first + p)
            slots = class_of_slots(*offsets_of(place, head))
            for s in range(RATE):
                held[head_rows(head), lane_block(slots[s])] = part[
                    p, :, s * BLK : (s + 1) * BLK
                ]
    row = lax.broadcasted_iota(jnp.int32, (TOK, TOK), 0)
    col = lax.broadcasted_iota(jnp.int32, (TOK, TOK), 1)
    picker = (row == RATE * (col % BLK) + col // BLK).astype(BF16)
    attention = dot_nt(picker, held[...]).astype(BF16)
    out_ref[...] = dot(attention, w_ref[...]).astype(BF16)


def whole(shape):
    return pl.BlockSpec(shape, lambda *_: (0,) * len(shape))


def per_head(shape, skip=0, last=None):
    def index(h, *_):
        at = h + skip if last is None else jnp.minimum(h, last)
        return (at,) + (0,) * (len(shape) - 1)

    return pl.BlockSpec(shape, index)


def call(
    kernel, scalars, args, grid, in_specs, outs, scratch, scores,
    limit=VMEM_LIMIT, after=(), through=(), busy=0,
):
    known = len(scalars) + len(args)
    extra = (*after, *through)
    count = len(outs)
    anywhere = pl.BlockSpec(memory_space=pl.ANY)

    def body(*refs):
        results = refs[known + len(extra) :]
        kernel(*refs[:known], *results[:count], *results[count + len(through) :])

    return pl.pallas_call(
        body if extra else kernel,
        grid_spec=pltpu.PrefetchScalarGridSpec(
            num_scalar_prefetch=len(scalars),
            grid=grid,
            in_specs=list(in_specs) + [anywhere] * len(extra),
            out_specs=[spec for spec, _ in outs] + [anywhere] * len(through),
            scratch_shapes=scratch,
        ),
        out_shape=[shape for _, shape in outs]
        + [jax.ShapeDtypeStruct(x.shape, x.dtype) for x in through],
        input_output_aliases={known + len(after) + i: count + i for i in range(len(through))},
        compiler_params=pltpu.CompilerParams(vmem_limit_bytes=limit),
        cost_estimate=pl.CostEstimate(flops=busy, bytes_accessed=0, transcendentals=0),
    )(*scalars, *args, *extra)


def handed_on(arrays, **order):
    return call(lambda: None, (), (), (1,), [], [], [], 0, through=tuple(arrays), **order)


def within(array, apart):
    count = lax.axis_size("seq")
    return lax.ppermute(array, "seq", [(i, i ^ apart) for i in range(count)])


def swap_segments(arrays):
    moved = {s: within(arrays[s - 1], GROUP * s) for s in (3, 2, 1)}
    return [moved[s] for s in (1, 2, 3)]


def shards_four(queries, key_states, value_states, offsets_mid, offsets_top, out_weight):
    width = queries.shape[1]
    place = (lax.axis_index("seq").astype(jnp.int32).reshape(1), offsets_mid, offsets_top)
    full = jax.ShapeDtypeStruct((HG, 3 * DH, TOK), BF16)
    piece = jax.ShapeDtypeStruct((HG, 3 * DH, HALF), BF16)
    pair = jax.ShapeDtypeStruct((2, 3 * DH, HALF), BF16)
    anywhere = pl.BlockSpec(memory_space=pl.ANY)
    shapes = [full] * 2 + [piece] * 4
    own0, own1, sel2, sel3, rest2, rest3 = call(
        pack_kernel, place, (key_states, value_states, queries), (1,),
        [anywhere] * 3,
        [(anywhere, shape) for shape in shapes],
        [pltpu.VMEM((TOK, width), BF16)] * 3
        + [pltpu.VMEM((width, TOK), BF16)] * 3
        + [pltpu.VMEM(shape.shape, BF16) for shape in shapes]
        + [pltpu.SemaphoreType.DMA((3,)), pltpu.SemaphoreType.DMA((6, 3))],
        1 << 19, VMEM_MOST,
    )
    own1 = within(own1, 1)
    sel2, sel3 = within(sel2, 2), within(sel3, 3)

    def regroup(a, b, **order):
        return call(
            regroup_kernel, (), (a, b), (1,),
            [whole(a.shape), whole(b.shape)], [(whole(pair.shape), pair)] * 3,
            [], 1 << 17, **order,
        )

    def near(held, units, tasks, old, first=0, heads=HG, step=2, **order):
        sizes = [len(members) * BLK for _, members in units]
        scores = sum(sum(sizes[low:]) * HALF for group in tasks for _, low, _ in group)
        arrays = [*held.values(), *[x for one in old for x in one]]
        shapes = [
            jax.ShapeDtypeStruct((heads, len(group), rows, HALF), F32)
            for group in tasks
            for rows in (DX, 8)
        ]
        return call(
            functools.partial(near_kernel, list(held), units, tasks, len(old), first, step),
            place, arrays, (heads // step,),
            [per_head((step,) + x.shape[1:], first // step) for x in arrays],
            [(per_head((step,) + x.shape[1:]), x) for x in shapes],
            [
                pltpu.VMEM((step, sum(sizes), DH), BF16),
                pltpu.VMEM((step, DX, sum(sizes)), BF16),
            ],
            heads * scores, **order,
        )

    def units_of(a, b):
        return [(0, [(a, 0), (b, 0)]), (1, [(a, 1), (b, 1)])], [
            (None, [(a, 2), (a, 3), (b, 2), (b, 3)])
        ]

    own_sel, own_rest = units_of(0, 1)
    other_sel, other_rest = units_of(2, 3)
    own = [(0, 0), (0, 1), (1, 0), (1, 1)]

    ours = regroup(own0, own1)
    ours = swap_segments(ours)
    held = {(0, 0): own0, (1, 0): own1}
    state_own = near(held, own_sel + own_rest, [[(q, 0, None) for q in own]], [])
    *theirs, rest2, rest3 = regroup(sel2, sel3, after=state_own[1:], through=(rest2, rest3))
    theirs = swap_segments(theirs)
    rest2, rest3 = within(rest2, 2), within(rest3, 3)

    held.update({(2, 0): sel2, (3, 0): sel3})
    units = own_sel + own_rest + other_sel
    tasks = [
        [(q, 3, (0, i)) for i, q in enumerate(own)],
        [((2, 0), 0, None), ((3, 0), 0, None)],
    ]
    arrays = [*held.values(), *state_own]
    near_shapes = [
        jax.ShapeDtypeStruct((HG, len(group), rows, HALF), F32)
        for group in tasks
        for rows in (DX, 8)
    ]
    far_shapes = [
        jax.ShapeDtypeStruct((2, RATE, HALF, DH), BF16),
        jax.ShapeDtypeStruct((2, RATE, DX, HALF), BF16),
        jax.ShapeDtypeStruct((2, RATE, DH, HALF), BF16),
        jax.ShapeDtypeStruct((2, RATE, DX, HALF), F32),
        jax.ShapeDtypeStruct((2, RATE, 8, HALF), F32),
    ]
    piece_0 = pl.BlockSpec((1, 3 * DH, HALF), lambda *_: (0, 0, 0))
    in_scalars = pl.BlockSpec(memory_space=pltpu.SMEM)
    step, steps = 2, HG // 2
    keys = sum(len(members) for _, members in units) * BLK
    out = call(
        functools.partial(
            near_and_far_kernel, (list(held), units, tasks, 1, 0, step), steps
        ),
        place, (*arrays, own0, own1, *ours[::-1]), (steps + 1,),
        [per_head((step,) + x.shape[1:], last=steps - 1) for x in arrays]
        + [piece_0] * 2 + [whole(pair.shape)] * 3,
        [(per_head((step,) + x.shape[1:], last=steps - 1), x) for x in near_shapes]
        + [(whole(x.shape), x) for x in far_shapes]
        + [(in_scalars, jax.ShapeDtypeStruct((2,), F32))],
        [pltpu.VMEM((step, keys, DH), BF16), pltpu.VMEM((step, DX, keys), BF16)],
        1 << 18,
    )
    state_own, state_sel, far_own = out[:2], out[2:4], out[4:]

    result = jax.ShapeDtypeStruct((DH, GROUP * HALF + BLK), BF16)
    results = call(
        far_kernel, place, (sel2, sel3, theirs[1], theirs[0], theirs[2], *far_own), (1,),
        [piece_0] * 2 + [whole(pair.shape)] * 3
        + [whole(x.shape) for x in far_own[:-1]] + [in_scalars],
        [(whole(result.shape), result)] * RATE,
        [pltpu.VMEM(x.shape, BF16) for x in far_shapes[:3]]
        + [
            pltpu.VMEM((RATE, DH, GROUP * HALF), BF16),
            pltpu.VMEM((RATE, DH, BLK), F32),
        ],
        RATE * 2 * 3 * 3 * HALF * HALF, busy=BUSY,
    )
    back = [results[0]] + swap_segments(results[1:])

    held.update({(2, 2): rest2, (3, 2): rest3})
    units = own_sel + own_rest + other_sel + other_rest

    def combine(chip, state, far, **order):
        heads = state[0].shape[0]
        attended = jax.ShapeDtypeStruct((heads, DH, TOK), BF16)
        return call(
            functools.partial(combine_kernel, chip), (), (*state, *far[::-1]), (1,),
            [whole(x.shape) for x in state] + [whole(result.shape)] * heads,
            [(whole(attended.shape), attended)] * 2,
            [],
            1 << 18, **order,
        )

    parts, last = {}, results[0]
    for first, heads in CHUNKS:
        state_other = near(
            held, units,
            [
                [
                    ((2, 0), 5, (0, 0)), ((2, 1), 0, None),
                    ((3, 0), 5, (0, 1)), ((3, 1), 0, None),
                ]
            ],
            [state_sel],
            first, heads, 2, after=(last,),
        )
        if first:
            back[1:] = handed_on(back[1:], after=state_other[1:])
        part2, part3 = combine(1, state_other, back[first : first + heads])
        early = tuple(parts.values())
        parts[2, first], parts[3, first] = within(part2, 2), within(part3, 3)
        last = part3
    pieces = {(2, 2): rest2, (3, 2): rest3, **{q: held[q] for q in ((0, 0), (1, 0))}}
    arrays = [*pieces.values(), *state_own, *back[::-1]]
    attended = jax.ShapeDtypeStruct((HG, DH, TOK), BF16)
    part0, part1 = call(
        functools.partial(
            last_own_kernel, list(pieces), other_rest, [[(q, 0, (0, i)) for i, q in enumerate(own)]]
        ),
        place, arrays, (1,),
        [whole(x.shape) for x in arrays],
        [(whole(attended.shape), attended)] * 2,
        [pltpu.VMEM(x.shape, F32) for x in state_own]
        + [pltpu.VMEM((HG, TOK, DH), BF16), pltpu.VMEM((HG, DX, TOK), BF16)],
        HG * TOK * GROUP * HALF, after=(last, *early),
    )
    parts = dict(zip(parts, handed_on(parts.values(), busy=BUSY)))
    parts[0, 0], parts[1, 0] = part0, within(part1, 1)
    return call(
        functools.partial(project_kernel, list(parts)), place, (*parts.values(), out_weight), (1,),
        [whole(x.shape) for x in parts.values()] + [whole((width, width))],
        [(whole((TOK, width)), jax.ShapeDtypeStruct((TOK, width), BF16))],
        [pltpu.VMEM((width, TOK), BF16)],
        1 << 18,
    )[0]


def shards(queries, key_states, value_states, offsets_mid, offsets_top, out_weight):
    tokens, width = queries.shape
    heads = offsets_mid.shape[0]
    fits = (
        lax.axis_size("head") == 1
        and lax.axis_size("seq") == GROUP * RATE
        and tokens == TOK
        and heads == GROUP * HG
        and width == heads * DH
    )
    run = shards_four if fits else shards_general
    return run(queries, key_states, value_states, offsets_mid, offsets_top, out_weight)


def solution(mesh):
    in_specs = (
        P(("slide", "seq"), "head"),
        P(("slide", "seq"), "head"),
        P(("slide", "seq"), "head"),
        P(),
        P(),
        P("head", None),
    )
    out_specs = P(("slide", "seq", "head"), None)
    return jax.shard_map(shards, mesh=mesh, in_specs=in_specs, out_specs=out_specs, check_vma=False)
```

```python
import functools

import jax
import jax.numpy as jnp
from jax import lax
from jax.experimental import pallas as pl
from jax.experimental.pallas import tpu as pltpu
from jax.sharding import PartitionSpec as P

SEG = 2048
LOG2E = 1.4426950408889634
VMEM_LIMIT = 40 * 1024 * 1024
VMEM_MOST = 60 * 1024 * 1024
BF16 = jnp.bfloat16
F32 = jnp.float32


def partner_2(block, axis, apart):
    count = lax.axis_size(axis)
    route = []
    for low in range(count):
        high = low | 1 << apart
        if high != low and high < count:
            route += [(low, high), (high, low)]
    return lax.ppermute(block, axis, route)


def attend_head(triple_in):
    query_rows, key_rows, value_rows = triple_in
    score_scale = query_rows.shape[-1] ** (-0.5)
    scores = jnp.dot(query_rows, key_rows.T, preferred_element_type=jnp.float32) * score_scale
    row_max = jnp.max(scores, axis=1)
    shifted = jnp.exp(scores - row_max[:, None])
    row_total = jnp.sum(shifted, axis=1)
    weights = shifted.astype(jnp.bfloat16)
    numerator = jnp.dot(weights, value_rows, preferred_element_type=jnp.float32)
    return (numerator, row_total, row_max)


def attend_local(query_rows, pair_rows):
    return lax.map(
        attend_head,
        (
            query_rows.transpose(1, 0, 2),
            pair_rows[:, 0].transpose(1, 0, 2),
            pair_rows[:, 1].transpose(1, 0, 2),
        ),
    )


def pick_rows(states, offsets, rate):
    row_count, inner_count, heads_here, head_width = states.shape
    picker = (jnp.arange(rate)[:, None] == offsets[None, :]).astype(jnp.bfloat16)
    folded = states.reshape(row_count // rate, rate, inner_count, heads_here, head_width)
    return jnp.einsum("archd,rh->achd", folded, picker, preferred_element_type=jnp.float32).astype(
        jnp.bfloat16
    )


def spread_back(numerator, row_total, row_max, offsets, rate):
    heads_here, picked_count, head_width = numerator.shape
    chosen = jnp.arange(rate)[:, None] == offsets[None, :]
    full_num = jnp.where(chosen[None, :, :, None], numerator.transpose(1, 0, 2)[:, None], 0.0)
    full_total = jnp.where(chosen[None], row_total.T[:, None], 0.0)
    full_max = jnp.where(chosen[None], row_max.T[:, None], -1e30)
    return (
        full_num.reshape(picked_count * rate, heads_here, head_width),
        full_total.reshape(picked_count * rate, heads_here),
        full_max.reshape(picked_count * rate, heads_here),
    )


def doubling(buffer, steps_count):
    position = lax.axis_index("seq")
    for bit_index in range(steps_count):
        partner = partner_2(buffer, "seq", bit_index)
        is_lower = position >> bit_index & 1 == 0
        buffer = jnp.where(
            is_lower, jnp.concatenate([buffer, partner], 0), jnp.concatenate([partner, buffer], 0)
        )
    return buffer


def shards_general(queries, key_states, value_states, offsets_mid, offsets_top, out_weight):
    tok_rows = queries.shape[0]
    heads_local = offsets_mid.shape[0] // lax.axis_size("head")
    head_size = queries.shape[1] // heads_local
    seq_devices = lax.axis_size("seq")
    seq_total = tok_rows * seq_devices
    width_mid = min(16 * SEG, seq_total)
    rate_mid = width_mid // SEG
    rate_top = seq_total // SEG
    start_head = lax.axis_index("head") * heads_local
    mid_local = lax.dynamic_slice(offsets_mid, (start_head,), (heads_local,))
    top_local = lax.dynamic_slice(offsets_top, (start_head,), (heads_local,))
    query_heads = queries.reshape(tok_rows, 1, heads_local, head_size)
    paired = jnp.stack([key_states, value_states], axis=1).reshape(
        tok_rows, 2, heads_local, head_size
    )
    near_bits = (SEG // tok_rows).bit_length() - 1
    near_rows = doubling(paired.reshape(tok_rows, -1), near_bits).reshape(
        SEG, 2, heads_local, head_size
    )
    near_num, near_total, near_max = attend_local(query_heads[:, 0], near_rows)
    level_near = spread_back(
        near_num, near_total, near_max, jnp.zeros((heads_local,), jnp.int32), 1
    )
    mid_q = pick_rows(query_heads, mid_local, rate_mid)[:, 0]
    mid_kv = pick_rows(paired, mid_local, rate_mid)
    mid_group = width_mid // tok_rows
    mid_bits = mid_group.bit_length() - 1
    mid_rows = doubling(mid_kv.reshape(mid_kv.shape[0], -1), mid_bits).reshape(
        SEG, 2, heads_local, head_size
    )
    mid_num, mid_total, mid_max = attend_local(mid_q, mid_rows)
    level_mid = spread_back(mid_num, mid_total, mid_max, mid_local, rate_mid)
    top_q = pick_rows(query_heads, top_local, rate_top)[:, 0]
    top_kv = pick_rows(paired, top_local, rate_top)
    top_rows = lax.all_gather(
        top_kv.reshape(top_kv.shape[0], -1), "seq", axis=0, tiled=True
    ).reshape(SEG, 2, heads_local, head_size)
    top_num, top_total, top_max = attend_local(top_q, top_rows)
    level_top = spread_back(top_num, top_total, top_max, top_local, rate_top)
    levels = [level_near, level_mid, level_top]
    overall = jnp.maximum(jnp.maximum(level_near[2], level_mid[2]), level_top[2])
    numerator = jnp.zeros((tok_rows, heads_local, head_size), jnp.float32)
    row_total = jnp.zeros((tok_rows, heads_local), jnp.float32)
    for level_num, level_total, level_max in levels:
        factor = jnp.exp(level_max - overall)
        numerator = numerator + factor[..., None] * level_num
        row_total = row_total + factor * level_total
    attention = (
        (numerator / row_total[..., None])
        .astype(jnp.bfloat16)
        .reshape(tok_rows, heads_local * head_size)
    )
    result = lax.psum_scatter(
        jnp.dot(attention, out_weight, preferred_element_type=jnp.float32),
        "head",
        scatter_dimension=0,
        tiled=True,
    )
    return result.astype(jnp.bfloat16)


RATE = 4
GROUP = 4
HG = 4
DH = 48
BLK = 128
HALF = 2 * BLK
TOK = 512
SCALE = DH**-0.5 * LOG2E
BUSY = 1 << 33
AHEAD = 4
SAFE = 96.0
CHUNKS = ((0, 2), (2, 2))
DX = 64


def dot(a, b):
    return jnp.dot(a, b, preferred_element_type=F32)


def dot_nt(a, b):
    return lax.dot_general(a, b, (((1,), (1,)), ((), ())), preferred_element_type=F32)


def class_of_slots(off_mid, off_top):
    first = off_mid
    second = jnp.where(off_top == off_mid, lax.rem(off_mid + 1, RATE), off_top)
    free0 = (first != 0) & (second != 0)
    free1 = (first != 1) & (second != 1)
    third = jnp.where(free0, 0, jnp.where(free1, 1, 2))
    return first, second, third, 6 - first - second - third


def head_of(place, j, p):
    index = place[0][0]
    return ((index & (GROUP - 1)) ^ j) * HG + ((index // GROUP) ^ p)


def offsets_of(place, head):
    return place[1][head], place[2][head]


def token_picker():
    row = lax.broadcasted_iota(jnp.int32, (TOK, TOK), 0)
    col = lax.broadcasted_iota(jnp.int32, (TOK, TOK), 1)
    return (col == RATE * (row % BLK) + row // BLK).astype(BF16)


def fill_class_major(block, picker, scratch):
    scratch[...] = lax.dot_general(
        block, picker, (((0,), (1,)), ((), ())), preferred_element_type=F32
    ).astype(BF16)


def lane_block(index):
    return pl.ds(pl.multiple_of(index * BLK, BLK), BLK)


def head_rows(head):
    return pl.ds(pl.multiple_of(head * DH, 16), DH)


def pack_kernel(index, mid, top, k_hbm, v_hbm, q_hbm, *refs):
    place = (index, mid, top)
    outs, refs = refs[:6], refs[6:]
    blocks, held, packed = refs[:3], refs[3:6], refs[6:12]
    sems_in, sems_out = refs[12:]
    loads = [
        [
            pltpu.make_async_copy(hbm.at[rows], block.at[rows], sems_in.at[i, n])
            for n, rows in enumerate((slice(0, HALF), slice(HALF, TOK)))
        ]
        for i, (hbm, block) in enumerate(zip((k_hbm, v_hbm, q_hbm), blocks))
    ]
    for pair in loads:
        for load in pair:
            load.start()
    picker = token_picker()
    stores = []
    heads = {(j, p): head_of(place, j, p) for j in range(GROUP) for p in range(HG)}
    classes = {at: class_of_slots(*offsets_of(place, head)) for at, head in heads.items()}
    for n, (load, block, scratch) in enumerate(zip(loads, blocks, held)):
        for half in load:
            half.wait()
        fill_class_major(block[...], picker, scratch)
        rows = slice(n * DH, (n + 1) * DH)
        for i, (j, first, count) in enumerate(
            ((0, 0, 4), (1, 0, 4), (2, 0, 2), (3, 0, 2), (2, 2, 2), (3, 2, 2))
        ):
            for p in range(HG):
                for s in range(count):
                    packed[i][p, rows, s * BLK : (s + 1) * BLK] = scratch[
                        head_rows(heads[j, p]), lane_block(classes[j, p][first + s])
                    ]
            store = pltpu.make_async_copy(
                packed[i].at[:, rows], outs[i].at[:, rows], sems_out.at[i, n]
            )
            store.start()
            stores.append(store)
    for store in stores:
        store.wait()


def regroup_kernel(a_ref, b_ref, *refs):
    for s, out in enumerate(refs[-3:]):
        out[0] = a_ref[s + 1, :, 0:HALF]
        out[1] = b_ref[s + 1, :, 0:HALF]


def upright(keys_t):
    return keys_t.T


def largest(blocks):
    best = None
    for block in blocks:
        wide = block.astype(F32)
        length = jnp.sum(wide * wide, axis=0, keepdims=True)
        for low in range(0, block.shape[1], HALF):
            part = length[:, low : low + HALF]
            best = part if best is None else jnp.maximum(best, part)
    return jnp.max(best)


def is_small(query_length, key_length):
    return query_length * key_length * (SCALE * SCALE) < SAFE * SAFE


def column_max(blocks):
    best = jnp.max(blocks[0], axis=0, keepdims=True)
    for block in blocks[1:]:
        best = jnp.maximum(best, jnp.max(block, axis=0, keepdims=True))
    return best * SCALE


def in_stages(items, score, weigh, gather):
    scores = {n: score(item) for n, item in enumerate(items[:AHEAD])}
    weights = weigh(items[0], scores.pop(0))
    for n, item in enumerate(items):
        if n + AHEAD < len(items):
            scores[n + AHEAD] = score(items[n + AHEAD])
        following = weigh(items[n + 1], scores.pop(n + 1)) if n + 1 < len(items) else None
        gather(item, weights)
        weights = following


def near_kernel(inputs, units, tasks, carried, first, step, index, mid, top, *refs):
    place = (index, mid, top)
    pieces = dict(zip(inputs, refs[: len(inputs)]))
    refs = refs[len(inputs) :]
    old = [refs[2 * i : 2 * i + 2] for i in range(carried)]
    outs = refs[2 * carried : 2 * carried + 2 * len(tasks)]
    k_s, v_s = refs[-2:]
    v_s[:, DH:DX, :] = jnp.ones((step, DX - DH, v_s.shape[2]), BF16)
    lane_slot = lax.broadcasted_iota(jnp.int32, (1, HALF), 1) // BLK

    def lookup(j, slot):
        first = 0 if (j, 0) in pieces and pieces[j, 0].shape[2] > HALF else slot // 2 * 2
        return pieces[j, first], (slot - first) * BLK

    chunks = []
    row = 0
    for label, members in units:
        chunks.append((label, slice(row, row + len(members) * BLK)))
        row += len(members) * BLK
    members = [member for _, group in units for member in group]

    def prepare(h):
        for i, (j, slot) in enumerate(members):
            ref, lane = lookup(j, slot)
            rows = slice(i * BLK, (i + 1) * BLK)
            k_s[h, rows, :] = upright(ref[h, 0:DH, lane : lane + BLK])
            v_s[h, 0:DH, rows] = ref[h, DH : 2 * DH, lane : lane + BLK]

    def counted_again(h):
        off_mid, off_top = offsets_of(place, head_of(place, 0, first + pl.program_id(0) * step + h))
        same = off_mid == off_top
        return [
            jnp.where(lane_slot == 0, jnp.where(same, 1.584962500721156, 1.0), 0.0),
            jnp.where(lane_slot == 1, jnp.where(same, 0.0, 1.0), 0.0),
        ]

    def run(heads):
        again = [counted_again(h) for h in heads]
        flat = [
            (h, again_h, query, low, merge, out, i)
            for h, again_h in zip(heads, again)
            for out, group in enumerate(tasks)
            for i, (query, low, merge) in enumerate(group)
        ]

        def score(task):
            h, _, (j, half), low = task[:4]
            ref, lane = lookup(j, 2 * half)
            query = ref[h, 2 * DH :, lane : lane + HALF]
            return [dot(k_s[h, rows, :], query) for _, rows in chunks[low:]]

        scores = score(flat[0])
        for n, (h, again_h, (_, half), low, merge, out, i) in enumerate(flat):
            following = score(flat[n + 1]) if n + 1 < len(flat) else None
            best = column_max(scores)
            if merge is not None:
                acc_in, max_in = old[merge[0]]
                old_max = max_in[h, merge[1], 0:1, :]
                best = jnp.maximum(best, old_max)
            acc = None
            for (label, rows), block in zip(chunks[low:], scores):
                block = block * SCALE
                if half == 0 and label is not None:
                    block = block - (best - again_h[label])
                else:
                    block = block - best
                part = dot(v_s[h, :, rows], jnp.exp2(block).astype(BF16))
                acc = part if acc is None else acc + part
            if merge is not None:
                acc = acc + acc_in[h, merge[1]] * jnp.exp2(old_max - best)
            acc_ref, max_ref = outs[2 * out : 2 * out + 2]
            acc_ref[h, i] = acc
            max_ref[h, i] = jnp.broadcast_to(best, (8, HALF))
            scores = following

    def run_plain():
        again = [counted_again(h) for h in range(step)]
        steps = [
            (h, query, merge, out, i, c, c == low, c == len(chunks) - 1)
            for h in range(step)
            for out, group in enumerate(tasks)
            for i, (query, low, merge) in enumerate(group)
            for c in range(low, len(chunks))
        ]

        def score(item):
            h, (j, half), c = item[0], item[1], item[5]
            ref, lane = lookup(j, 2 * half)
            return dot(k_s[h, chunks[c][1], :], ref[h, 2 * DH :, lane : lane + HALF])

        def weigh(item, block):
            h, (_, half), c = item[0], item[1], item[5]
            label = chunks[c][0]
            block = block * SCALE
            if half == 0 and label is not None:
                block = block + again[h][label]
            return jnp.exp2(block).astype(BF16)

        held = {}

        def gather(item, weights):
            h, _, merge, out, i, c, begins, ends = item
            part = dot(v_s[h, :, chunks[c][1]], weights)
            acc = part if begins else held[0] + part
            if ends:
                if merge is not None:
                    acc = acc + old[merge[0]][0][h, merge[1]]
                acc_ref, max_ref = outs[2 * out : 2 * out + 2]
                acc_ref[h, i] = acc
                max_ref[h, i] = jnp.zeros((8, HALF), F32)
            held[0] = acc

        in_stages(steps, score, weigh, gather)

    for h in range(step):
        prepare(h)
    plain = is_small(
        largest([ref[h, 2 * DH :, :] for ref in pieces.values() for h in range(step)]),
        largest([ref[h, 0:DH, :] for ref in pieces.values() for h in range(step)]),
    )
    for _, max_in in old:
        plain = plain & (jnp.max(jnp.abs(max_in[...])) == 0.0)

    @pl.when(plain)
    def _():
        run_plain()

    @pl.when(jnp.logical_not(plain))
    def _():
        @pl.loop(0, step)
        def _(h):
            run([h])


def far_slots(place):
    off_mid, off_top = offsets_of(place, head_of(place, 0, 0))
    same = off_mid == off_top
    return same, (0, jnp.where(same, 0, 1))


def far_pieces(place, sources, k_s, v_s, q_s):
    _, slots = far_slots(place)
    for s, pair in enumerate(sources):
        for i, ref in enumerate(pair):
            here = slice(i * BLK, (i + 1) * BLK)
            for level, slot in enumerate(slots):
                k_s[level, s, here, :] = upright(ref[0:DH, lane_block(slot)])
                v_s[level, s, 0:DH, here] = ref[DH : 2 * DH, lane_block(slot)]
                q_s[level, s, :, here] = ref[2 * DH : 3 * DH, lane_block(slot)]
    v_s[:, :, DH:DX, :] = jnp.ones((2, RATE, DX - DH, HALF), BF16)


def far_lengths(sources):
    every = [ref for pair in sources for ref in pair]
    return (
        largest([ref[2 * DH : 3 * DH, 0:HALF] for ref in every]),
        largest([ref[0:DH, 0:HALF] for ref in every]),
    )


def far_own_kernel(index, mid, top, own0, own1, beyond3, beyond2, beyond1, *refs):
    k_s, v_s, q_s, acc_ref, max_ref, length_ref = refs
    sources = [(own0.at[0], own1.at[0])] + [
        (ref.at[0], ref.at[1]) for ref in (beyond1, beyond2, beyond3)
    ]
    far_pieces((index, mid, top), sources, k_s, v_s, q_s)

    def run_plain():
        steps = [(level, d) for level in range(2) for d in range(1, RATE)]

        def segment(s, carry):
            def score(item):
                level, d = item
                return dot(k_s[level, s ^ d], q_s[level, s])

            def weigh(item, block):
                return jnp.exp2(block * SCALE).astype(BF16)

            held = {}

            def gather(item, weights):
                level, d = item
                part = dot(v_s[level, s ^ d], weights)
                held[0] = part if d == 1 else held[0] + part
                if d == RATE - 1:
                    acc_ref[level, s] = held[0]
                    max_ref[level, s] = jnp.zeros((8, HALF), F32)

            in_stages(steps, score, weigh, gather)
            return carry

        lax.fori_loop(0, RATE, segment, 0, unroll=2)

    def run():
        def segment(s, carry):
            def score(level):
                return [dot(k_s[level, s ^ d], q_s[level, s]) for d in range(1, RATE)]

            scores = score(0)
            for level in range(2):
                following = score(1) if level == 0 else None
                best = column_max(scores)
                acc = None
                for d in range(1, RATE):
                    block = scores[d - 1] * SCALE - best
                    part = dot(v_s[level, s ^ d], jnp.exp2(block).astype(BF16))
                    acc = part if acc is None else acc + part
                acc_ref[level, s] = acc
                max_ref[level, s] = jnp.broadcast_to(best, (8, HALF))
                scores = following
            return carry

        lax.fori_loop(0, RATE, segment, 0)

    query_length, key_length = far_lengths(sources)
    length_ref[0] = query_length
    length_ref[1] = key_length
    plain = is_small(query_length, key_length)
    pl.when(plain)(run_plain)
    pl.when(jnp.logical_not(plain))(run)


def near_and_far_kernel(near_args, steps, index, mid, top, *refs):
    scalars = (index, mid, top)
    inputs, tasks, carried = near_args[0], near_args[2], near_args[3]
    count = len(inputs) + 2 * carried
    near_in, far_in, refs = refs[:count], refs[count : count + 5], refs[count + 5 :]
    near_out, far_out, scratch = refs[: 2 * len(tasks)], refs[2 * len(tasks) : -2], refs[-2:]

    @pl.when(pl.program_id(0) < steps)
    def _():
        near_kernel(*near_args, *scalars, *near_in, *near_out, *scratch)

    @pl.when(pl.program_id(0) == steps)
    def _():
        far_own_kernel(*scalars, *far_in, *far_out)


def far_kernel(index, mid, top, *refs):
    place = (index, mid, top)
    sel2, sel3, beyond2, beyond1, beyond3, k_own, v_own, q_own, acc_in, max_in, length_in = refs[
        :11
    ]
    outs = refs[11 : 11 + RATE]
    k_s, v_s, q_s, result_s, tail_s = refs[11 + RATE :]
    same, _ = far_slots(place)
    sources = [(sel2.at[0], sel3.at[0])] + [
        (ref.at[0], ref.at[1]) for ref in (beyond1, beyond2, beyond3)
    ]
    far_pieces(place, sources, k_s, v_s, q_s)
    tail_s[...] = jnp.zeros(tail_s.shape, F32)

    tasks = [(level, chip) for level in range(2) for chip in range(2)]
    held = ((k_own, v_own, q_own), (k_s, v_s, q_s))

    def blocks(s, chip):
        return [(held[c], s ^ d) for d in range(1, RATE) for c in ((1,), (0, 1))[chip]]

    def finish(s, level, chip, acc, best):
        total = acc[DH : DH + 1, :]
        result = (acc[0:DH, :] / total).astype(BF16)
        lse = best + jnp.log2(total)
        if level == 0:
            lse = jnp.where(same, lse + 1.0, lse)
        else:
            lse = jnp.where(same, -1e30, lse)
        high = lse.astype(BF16).astype(F32)
        middle = (lse - high).astype(BF16).astype(F32)
        low = lse - high - middle
        for i in range(2):
            n = 2 * (2 * chip + i) + level
            mine = slice(i * BLK, (i + 1) * BLK)
            result_s[s, :, n * BLK : (n + 1) * BLK] = result[:, mine]
            for k, part in enumerate((high, middle, low)):
                tail_s[s, 3 * n + k : 3 * n + k + 1, :] = part[:, mine]

    def run_plain():
        def segment(s, carry):
            steps = [
                (level, chip, keys, b, n)
                for level, chip in tasks
                for n, (keys, b) in enumerate(blocks(s, chip))
            ]

            def score(item):
                level, chip, keys, b, _ = item
                return dot(keys[0][level, b], held[chip][2][level, s])

            def weigh(item, block):
                return jnp.exp2(block * SCALE).astype(BF16)

            sums = {}

            def gather(item, weights):
                level, chip, keys, b, n = item
                part = dot(keys[1][level, b], weights)
                sums[0] = sums[0] + part if n else part
                if n + 1 == len(blocks(s, chip)):
                    acc = sums[0] + acc_in[level, s] if chip == 0 else sums[0]
                    finish(s, level, chip, acc, jnp.zeros((1, HALF), F32))

            in_stages(steps, score, weigh, gather)
            return carry

        lax.fori_loop(0, RATE, segment, 0, unroll=2)

    def run():
        def segment(s, carry):
            for level, chip in tasks:
                scores = [
                    dot(keys[0][level, b], held[chip][2][level, s]) for keys, b in blocks(s, chip)
                ]
                best = column_max(scores)
                acc = jnp.zeros((DX, HALF), F32)
                if chip == 0:
                    old_max = max_in[level, s, 0:1, :]
                    best = jnp.maximum(best, old_max)
                    acc = acc_in[level, s] * jnp.exp2(old_max - best)
                for block, (keys, b) in zip(scores, blocks(s, chip)):
                    acc += dot(keys[1][level, b], jnp.exp2(block * SCALE - best).astype(BF16))
                finish(s, level, chip, acc, best)
            return carry

        lax.fori_loop(0, RATE, segment, 0)

    query_length, key_length = far_lengths(sources)
    plain = is_small(
        jnp.maximum(query_length, length_in[0]), jnp.maximum(key_length, length_in[1])
    )
    pl.when(plain)(run_plain)
    pl.when(jnp.logical_not(plain))(run)
    for s in range(RATE):
        outs[s][:, : GROUP * HALF] = result_s[s]
        outs[s][:, GROUP * HALF :] = tail_s[s].astype(BF16)


def join(acc, best, far, j):
    tail = far[:, GROUP * HALF :].astype(F32)
    lse = jnp.concatenate(
        [
            tail[3 * n : 3 * n + 1] + tail[3 * n + 1 : 3 * n + 2] + tail[3 * n + 2 : 3 * n + 3]
            for n in (2 * j, 2 * j + 1)
        ],
        axis=1,
    )
    overall = jnp.maximum(best, lse)
    near_factor, far_factor = jnp.exp2(best - overall), jnp.exp2(lse - overall)
    total = acc[DH : DH + 1] * near_factor + far_factor
    value = far[:, j * HALF : (j + 1) * HALF].astype(F32) * far_factor
    return ((acc[0:DH] * near_factor + value) / total).astype(BF16)


def combine_kernel(chip, acc_ref, max_ref, *refs):
    far, outs = refs[:-2][::-1], refs[-2:]
    for i in range(2):
        for p, results in enumerate(far):
            outs[i][p, :, 0:HALF] = join(
                acc_ref[p, 2 * i], max_ref[p, 2 * i, 0:1, :], results, 2 * chip + i
            )
            acc = acc_ref[p, 2 * i + 1]
            outs[i][p, :, HALF:] = (acc[0:DH] / acc[DH : DH + 1]).astype(BF16)


def last_own_kernel(inputs, units, tasks, index, mid, top, *refs):
    count = len(inputs) + 2
    near_refs, far, outs, scratch = refs[:count], refs[count:-6], refs[-6:-4], refs[-4:]
    acc_s, max_s, k_s, v_s = scratch
    near_kernel(
        inputs, units, tasks, 1, 0, HG, index, mid, top, *near_refs, acc_s, max_s, k_s, v_s
    )
    combine_kernel(0, acc_s, max_s, *far, *outs)


def project_kernel(sources, index, mid, top, *refs):
    place = (index, mid, top)
    parts, (w_ref, out_ref, held) = refs[:-3], refs[-3:]
    for (j, first), part in zip(sources, parts):
        for p in range(part.shape[0]):
            head = head_of(place, j, first + p)
            slots = class_of_slots(*offsets_of(place, head))
            for s in range(RATE):
                held[head_rows(head), lane_block(slots[s])] = part[
                    p, :, s * BLK : (s + 1) * BLK
                ]
    row = lax.broadcasted_iota(jnp.int32, (TOK, TOK), 0)
    col = lax.broadcasted_iota(jnp.int32, (TOK, TOK), 1)
    picker = (row == RATE * (col % BLK) + col // BLK).astype(BF16)
    attention = dot_nt(picker, held[...]).astype(BF16)
    out_ref[...] = dot(attention, w_ref[...]).astype(BF16)


def whole(shape):
    return pl.BlockSpec(shape, lambda *_: (0,) * len(shape))


def per_head(shape, skip=0, last=None):
    def index(h, *_):
        at = h + skip if last is None else jnp.minimum(h, last)
        return (at,) + (0,) * (len(shape) - 1)

    return pl.BlockSpec(shape, index)


def call(
    kernel, scalars, args, grid, in_specs, outs, scratch, scores,
    limit=VMEM_LIMIT, after=(), through=(), busy=0,
):
    known = len(scalars) + len(args)
    extra = (*after, *through)
    count = len(outs)
    anywhere = pl.BlockSpec(memory_space=pl.ANY)

    def body(*refs):
        results = refs[known + len(extra) :]
        kernel(*refs[:known], *results[:count], *results[count + len(through) :])

    return pl.pallas_call(
        body if extra else kernel,
        grid_spec=pltpu.PrefetchScalarGridSpec(
            num_scalar_prefetch=len(scalars),
            grid=grid,
            in_specs=list(in_specs) + [anywhere] * len(extra),
            out_specs=[spec for spec, _ in outs] + [anywhere] * len(through),
            scratch_shapes=scratch,
        ),
        out_shape=[shape for _, shape in outs]
        + [jax.ShapeDtypeStruct(x.shape, x.dtype) for x in through],
        input_output_aliases={known + len(after) + i: count + i for i in range(len(through))},
        compiler_params=pltpu.CompilerParams(vmem_limit_bytes=limit),
        cost_estimate=pl.CostEstimate(flops=busy, bytes_accessed=0, transcendentals=0),
    )(*scalars, *args, *extra)


def handed_on(arrays, **order):
    return call(lambda: None, (), (), (1,), [], [], [], 0, through=tuple(arrays), **order)


def within(array, apart):
    count = lax.axis_size("seq")
    return lax.ppermute(array, "seq", [(i, i ^ apart) for i in range(count)])


def swap_segments(arrays):
    moved = {s: within(arrays[s - 1], GROUP * s) for s in (3, 2, 1)}
    return [moved[s] for s in (1, 2, 3)]


def shards_four(queries, key_states, value_states, offsets_mid, offsets_top, out_weight):
    width = queries.shape[1]
    place = (lax.axis_index("seq").astype(jnp.int32).reshape(1), offsets_mid, offsets_top)
    full = jax.ShapeDtypeStruct((HG, 3 * DH, TOK), BF16)
    piece = jax.ShapeDtypeStruct((HG, 3 * DH, HALF), BF16)
    pair = jax.ShapeDtypeStruct((2, 3 * DH, HALF), BF16)
    anywhere = pl.BlockSpec(memory_space=pl.ANY)
    shapes = [full] * 2 + [piece] * 4
    own0, own1, sel2, sel3, rest2, rest3 = call(
        pack_kernel, place, (key_states, value_states, queries), (1,),
        [anywhere] * 3,
        [(anywhere, shape) for shape in shapes],
        [pltpu.VMEM((TOK, width), BF16)] * 3
        + [pltpu.VMEM((width, TOK), BF16)] * 3
        + [pltpu.VMEM(shape.shape, BF16) for shape in shapes]
        + [pltpu.SemaphoreType.DMA((3, 2)), pltpu.SemaphoreType.DMA((6, 3))],
        1 << 19, VMEM_MOST,
    )
    own1 = within(own1, 1)
    sel2, sel3 = within(sel2, 2), within(sel3, 3)

    def regroup(a, b, **order):
        return call(
            regroup_kernel, (), (a, b), (1,),
            [whole(a.shape), whole(b.shape)], [(whole(pair.shape), pair)] * 3,
            [], 1 << 17, **order,
        )

    def near(held, units, tasks, old, first=0, heads=HG, step=2, **order):
        sizes = [len(members) * BLK for _, members in units]
        scores = sum(sum(sizes[low:]) * HALF for group in tasks for _, low, _ in group)
        arrays = [*held.values(), *[x for one in old for x in one]]
        shapes = [
            jax.ShapeDtypeStruct((heads, len(group), rows, HALF), F32)
            for group in tasks
            for rows in (DX, 8)
        ]
        return call(
            functools.partial(near_kernel, list(held), units, tasks, len(old), first, step),
            place, arrays, (heads // step,),
            [per_head((step,) + x.shape[1:], first // step) for x in arrays],
            [(per_head((step,) + x.shape[1:]), x) for x in shapes],
            [
                pltpu.VMEM((step, sum(sizes), DH), BF16),
                pltpu.VMEM((step, DX, sum(sizes)), BF16),
            ],
            heads * scores, **order,
        )

    def units_of(a, b):
        return [(0, [(a, 0), (b, 0)]), (1, [(a, 1), (b, 1)])], [
            (None, [(a, 2), (a, 3), (b, 2), (b, 3)])
        ]

    own_sel, own_rest = units_of(0, 1)
    other_sel, other_rest = units_of(2, 3)
    own = [(0, 0), (0, 1), (1, 0), (1, 1)]

    ours = regroup(own0, own1)
    ours = swap_segments(ours)
    held = {(0, 0): own0, (1, 0): own1}
    state_own = near(held, own_sel + own_rest, [[(q, 0, None) for q in own]], [])
    *theirs, rest2, rest3 = regroup(sel2, sel3, after=state_own[1:], through=(rest2, rest3))
    theirs = swap_segments(theirs)
    rest2, rest3 = within(rest2, 2), within(rest3, 3)

    held.update({(2, 0): sel2, (3, 0): sel3})
    units = own_sel + own_rest + other_sel
    tasks = [
        [(q, 3, (0, i)) for i, q in enumerate(own)],
        [((2, 0), 0, None), ((3, 0), 0, None)],
    ]
    arrays = [*held.values(), *state_own]
    near_shapes = [
        jax.ShapeDtypeStruct((HG, len(group), rows, HALF), F32)
        for group in tasks
        for rows in (DX, 8)
    ]
    far_shapes = [
        jax.ShapeDtypeStruct((2, RATE, HALF, DH), BF16),
        jax.ShapeDtypeStruct((2, RATE, DX, HALF), BF16),
        jax.ShapeDtypeStruct((2, RATE, DH, HALF), BF16),
        jax.ShapeDtypeStruct((2, RATE, DX, HALF), F32),
        jax.ShapeDtypeStruct((2, RATE, 8, HALF), F32),
    ]
    piece_0 = pl.BlockSpec((1, 3 * DH, HALF), lambda *_: (0, 0, 0))
    in_scalars = pl.BlockSpec(memory_space=pltpu.SMEM)
    step, steps = 2, HG // 2
    keys = sum(len(members) for _, members in units) * BLK
    out = call(
        functools.partial(
            near_and_far_kernel, (list(held), units, tasks, 1, 0, step), steps
        ),
        place, (*arrays, own0, own1, *ours[::-1]), (steps + 1,),
        [per_head((step,) + x.shape[1:], last=steps - 1) for x in arrays]
        + [piece_0] * 2 + [whole(pair.shape)] * 3,
        [(per_head((step,) + x.shape[1:], last=steps - 1), x) for x in near_shapes]
        + [(whole(x.shape), x) for x in far_shapes]
        + [(in_scalars, jax.ShapeDtypeStruct((2,), F32))],
        [pltpu.VMEM((step, keys, DH), BF16), pltpu.VMEM((step, DX, keys), BF16)],
        1 << 18,
    )
    state_own, state_sel, far_own = out[:2], out[2:4], out[4:]

    result = jax.ShapeDtypeStruct((DH, GROUP * HALF + BLK), BF16)
    results = call(
        far_kernel, place, (sel2, sel3, theirs[1], theirs[0], theirs[2], *far_own), (1,),
        [piece_0] * 2 + [whole(pair.shape)] * 3
        + [whole(x.shape) for x in far_own[:-1]] + [in_scalars],
        [(whole(result.shape), result)] * RATE,
        [pltpu.VMEM(x.shape, BF16) for x in far_shapes[:3]]
        + [
            pltpu.VMEM((RATE, DH, GROUP * HALF), BF16),
            pltpu.VMEM((RATE, DH, BLK), F32),
        ],
        RATE * 2 * 3 * 3 * HALF * HALF, busy=BUSY,
    )
    back = [results[0]] + swap_segments(results[1:])

    held.update({(2, 2): rest2, (3, 2): rest3})
    units = own_sel + own_rest + other_sel + other_rest

    def combine(chip, state, far, **order):
        heads = state[0].shape[0]
        attended = jax.ShapeDtypeStruct((heads, DH, TOK), BF16)
        return call(
            functools.partial(combine_kernel, chip), (), (*state, *far[::-1]), (1,),
            [whole(x.shape) for x in state] + [whole(result.shape)] * heads,
            [(whole(attended.shape), attended)] * 2,
            [],
            1 << 18, **order,
        )

    parts, last = {}, results[0]
    for first, heads in CHUNKS:
        state_other = near(
            held, units,
            [
                [
                    ((2, 0), 5, (0, 0)), ((2, 1), 0, None),
                    ((3, 0), 5, (0, 1)), ((3, 1), 0, None),
                ]
            ],
            [state_sel],
            first, heads, 2, after=(last,),
        )
        if first:
            back[1:] = handed_on(back[1:], after=state_other[1:])
        part2, part3 = combine(1, state_other, back[first : first + heads])
        early = tuple(parts.values())
        parts[2, first], parts[3, first] = within(part2, 2), within(part3, 3)
        last = part3
    pieces = {(2, 2): rest2, (3, 2): rest3, **{q: held[q] for q in ((0, 0), (1, 0))}}
    arrays = [*pieces.values(), *state_own, *back[::-1]]
    attended = jax.ShapeDtypeStruct((HG, DH, TOK), BF16)
    part0, part1 = call(
        functools.partial(
            last_own_kernel, list(pieces), other_rest, [[(q, 0, (0, i)) for i, q in enumerate(own)]]
        ),
        place, arrays, (1,),
        [whole(x.shape) for x in arrays],
        [(whole(attended.shape), attended)] * 2,
        [pltpu.VMEM(x.shape, F32) for x in state_own]
        + [pltpu.VMEM((HG, TOK, DH), BF16), pltpu.VMEM((HG, DX, TOK), BF16)],
        HG * TOK * GROUP * HALF, after=(last, *early),
    )
    parts = dict(zip(parts, handed_on(parts.values(), busy=BUSY)))
    parts[0, 0], parts[1, 0] = part0, within(part1, 1)
    return call(
        functools.partial(project_kernel, list(parts)), place, (*parts.values(), out_weight), (1,),
        [whole(x.shape) for x in parts.values()] + [whole((width, width))],
        [(whole((TOK, width)), jax.ShapeDtypeStruct((TOK, width), BF16))],
        [pltpu.VMEM((width, TOK), BF16)],
        1 << 18,
    )[0]


def shards(queries, key_states, value_states, offsets_mid, offsets_top, out_weight):
    tokens, width = queries.shape
    heads = offsets_mid.shape[0]
    fits = (
        lax.axis_size("head") == 1
        and lax.axis_size("seq") == GROUP * RATE
        and tokens == TOK
        and heads == GROUP * HG
        and width == heads * DH
    )
    run = shards_four if fits else shards_general
    return run(queries, key_states, value_states, offsets_mid, offsets_top, out_weight)


def solution(mesh):
    in_specs = (
        P(("slide", "seq"), "head"),
        P(("slide", "seq"), "head"),
        P(("slide", "seq"), "head"),
        P(),
        P(),
        P("head", None),
    )
    out_specs = P(("slide", "seq", "head"), None)
    return jax.shard_map(shards, mesh=mesh, in_specs=in_specs, out_specs=out_specs, check_vma=False)
```

```python
import functools

import jax
import jax.numpy as jnp
from jax import lax
from jax.experimental import pallas as pl
from jax.experimental.pallas import tpu as pltpu
from jax.sharding import PartitionSpec as P

SEG = 2048
LOG2E = 1.4426950408889634
VMEM_LIMIT = 40 * 1024 * 1024
VMEM_MOST = 60 * 1024 * 1024
BF16 = jnp.bfloat16
F32 = jnp.float32


def partner_2(block, axis, apart):
    count = lax.axis_size(axis)
    route = []
    for low in range(count):
        high = low | 1 << apart
        if high != low and high < count:
            route += [(low, high), (high, low)]
    return lax.ppermute(block, axis, route)


def attend_head(triple_in):
    query_rows, key_rows, value_rows = triple_in
    score_scale = query_rows.shape[-1] ** (-0.5)
    scores = jnp.dot(query_rows, key_rows.T, preferred_element_type=jnp.float32) * score_scale
    row_max = jnp.max(scores, axis=1)
    shifted = jnp.exp(scores - row_max[:, None])
    row_total = jnp.sum(shifted, axis=1)
    weights = shifted.astype(jnp.bfloat16)
    numerator = jnp.dot(weights, value_rows, preferred_element_type=jnp.float32)
    return (numerator, row_total, row_max)


def attend_local(query_rows, pair_rows):
    return lax.map(
        attend_head,
        (
            query_rows.transpose(1, 0, 2),
            pair_rows[:, 0].transpose(1, 0, 2),
            pair_rows[:, 1].transpose(1, 0, 2),
        ),
    )


def pick_rows(states, offsets, rate):
    row_count, inner_count, heads_here, head_width = states.shape
    picker = (jnp.arange(rate)[:, None] == offsets[None, :]).astype(jnp.bfloat16)
    folded = states.reshape(row_count // rate, rate, inner_count, heads_here, head_width)
    return jnp.einsum("archd,rh->achd", folded, picker, preferred_element_type=jnp.float32).astype(
        jnp.bfloat16
    )


def spread_back(numerator, row_total, row_max, offsets, rate):
    heads_here, picked_count, head_width = numerator.shape
    chosen = jnp.arange(rate)[:, None] == offsets[None, :]
    full_num = jnp.where(chosen[None, :, :, None], numerator.transpose(1, 0, 2)[:, None], 0.0)
    full_total = jnp.where(chosen[None], row_total.T[:, None], 0.0)
    full_max = jnp.where(chosen[None], row_max.T[:, None], -1e30)
    return (
        full_num.reshape(picked_count * rate, heads_here, head_width),
        full_total.reshape(picked_count * rate, heads_here),
        full_max.reshape(picked_count * rate, heads_here),
    )


def doubling(buffer, steps_count):
    position = lax.axis_index("seq")
    for bit_index in range(steps_count):
        partner = partner_2(buffer, "seq", bit_index)
        is_lower = position >> bit_index & 1 == 0
        buffer = jnp.where(
            is_lower, jnp.concatenate([buffer, partner], 0), jnp.concatenate([partner, buffer], 0)
        )
    return buffer


def shards_general(queries, key_states, value_states, offsets_mid, offsets_top, out_weight):
    tok_rows = queries.shape[0]
    heads_local = offsets_mid.shape[0] // lax.axis_size("head")
    head_size = queries.shape[1] // heads_local
    seq_devices = lax.axis_size("seq")
    seq_total = tok_rows * seq_devices
    width_mid = min(16 * SEG, seq_total)
    rate_mid = width_mid // SEG
    rate_top = seq_total // SEG
    start_head = lax.axis_index("head") * heads_local
    mid_local = lax.dynamic_slice(offsets_mid, (start_head,), (heads_local,))
    top_local = lax.dynamic_slice(offsets_top, (start_head,), (heads_local,))
    query_heads = queries.reshape(tok_rows, 1, heads_local, head_size)
    paired = jnp.stack([key_states, value_states], axis=1).reshape(
        tok_rows, 2, heads_local, head_size
    )
    near_bits = (SEG // tok_rows).bit_length() - 1
    near_rows = doubling(paired.reshape(tok_rows, -1), near_bits).reshape(
        SEG, 2, heads_local, head_size
    )
    near_num, near_total, near_max = attend_local(query_heads[:, 0], near_rows)
    level_near = spread_back(
        near_num, near_total, near_max, jnp.zeros((heads_local,), jnp.int32), 1
    )
    mid_q = pick_rows(query_heads, mid_local, rate_mid)[:, 0]
    mid_kv = pick_rows(paired, mid_local, rate_mid)
    mid_group = width_mid // tok_rows
    mid_bits = mid_group.bit_length() - 1
    mid_rows = doubling(mid_kv.reshape(mid_kv.shape[0], -1), mid_bits).reshape(
        SEG, 2, heads_local, head_size
    )
    mid_num, mid_total, mid_max = attend_local(mid_q, mid_rows)
    level_mid = spread_back(mid_num, mid_total, mid_max, mid_local, rate_mid)
    top_q = pick_rows(query_heads, top_local, rate_top)[:, 0]
    top_kv = pick_rows(paired, top_local, rate_top)
    top_rows = lax.all_gather(
        top_kv.reshape(top_kv.shape[0], -1), "seq", axis=0, tiled=True
    ).reshape(SEG, 2, heads_local, head_size)
    top_num, top_total, top_max = attend_local(top_q, top_rows)
    level_top = spread_back(top_num, top_total, top_max, top_local, rate_top)
    levels = [level_near, level_mid, level_top]
    overall = jnp.maximum(jnp.maximum(level_near[2], level_mid[2]), level_top[2])
    numerator = jnp.zeros((tok_rows, heads_local, head_size), jnp.float32)
    row_total = jnp.zeros((tok_rows, heads_local), jnp.float32)
    for level_num, level_total, level_max in levels:
        factor = jnp.exp(level_max - overall)
        numerator = numerator + factor[..., None] * level_num
        row_total = row_total + factor * level_total
    attention = (
        (numerator / row_total[..., None])
        .astype(jnp.bfloat16)
        .reshape(tok_rows, heads_local * head_size)
    )
    result = lax.psum_scatter(
        jnp.dot(attention, out_weight, preferred_element_type=jnp.float32),
        "head",
        scatter_dimension=0,
        tiled=True,
    )
    return result.astype(jnp.bfloat16)


RATE = 4
GROUP = 4
HG = 4
DH = 48
BLK = 128
HALF = 2 * BLK
TOK = 512
SCALE = DH**-0.5 * LOG2E
BUSY = 1 << 33
AHEAD = 6
SAFE = 96.0
CHUNKS = ((0, 2), (2, 2))
DX = 64


def dot(a, b):
    return jnp.dot(a, b, preferred_element_type=F32)


def dot_nt(a, b):
    return lax.dot_general(a, b, (((1,), (1,)), ((), ())), preferred_element_type=F32)


def class_of_slots(off_mid, off_top):
    first = off_mid
    second = jnp.where(off_top == off_mid, lax.rem(off_mid + 1, RATE), off_top)
    free0 = (first != 0) & (second != 0)
    free1 = (first != 1) & (second != 1)
    third = jnp.where(free0, 0, jnp.where(free1, 1, 2))
    return first, second, third, 6 - first - second - third


def head_of(place, j, p):
    index = place[0][0]
    return ((index & (GROUP - 1)) ^ j) * HG + ((index // GROUP) ^ p)


def offsets_of(place, head):
    return place[1][head], place[2][head]


def token_picker():
    row = lax.broadcasted_iota(jnp.int32, (TOK, TOK), 0)
    col = lax.broadcasted_iota(jnp.int32, (TOK, TOK), 1)
    return (col == RATE * (row % BLK) + row // BLK).astype(BF16)


def fill_class_major(block, picker, scratch):
    scratch[...] = lax.dot_general(
        block, picker, (((0,), (1,)), ((), ())), preferred_element_type=F32
    ).astype(BF16)


def lane_block(index):
    return pl.ds(pl.multiple_of(index * BLK, BLK), BLK)


def head_rows(head):
    return pl.ds(pl.multiple_of(head * DH, 16), DH)


def pack_kernel(index, mid, top, k_hbm, v_hbm, q_hbm, *refs):
    place = (index, mid, top)
    outs, refs = refs[:6], refs[6:]
    blocks, held, packed = refs[:3], refs[3:6], refs[6:12]
    sems_in, sems_out = refs[12:]
    loads = [
        [
            pltpu.make_async_copy(hbm.at[rows], block.at[rows], sems_in.at[i, n])
            for n, rows in enumerate((slice(0, HALF), slice(HALF, TOK)))
        ]
        for i, (hbm, block) in enumerate(zip((k_hbm, v_hbm, q_hbm), blocks))
    ]
    for pair in loads:
        for load in pair:
            load.start()
    picker = token_picker()
    stores = []
    heads = {(j, p): head_of(place, j, p) for j in range(GROUP) for p in range(HG)}
    classes = {at: class_of_slots(*offsets_of(place, head)) for at, head in heads.items()}
    for n, (load, block, scratch) in enumerate(zip(loads, blocks, held)):
        for half in load:
            half.wait()
        fill_class_major(block[...], picker, scratch)
        rows = slice(n * DH, (n + 1) * DH)
        for i, (j, first, count) in enumerate(
            ((0, 0, 4), (1, 0, 4), (2, 0, 2), (3, 0, 2), (2, 2, 2), (3, 2, 2))
        ):
            for p in range(HG):
                for s in range(count):
                    packed[i][p, rows, s * BLK : (s + 1) * BLK] = scratch[
                        head_rows(heads[j, p]), lane_block(classes[j, p][first + s])
                    ]
            store = pltpu.make_async_copy(
                packed[i].at[:, rows], outs[i].at[:, rows], sems_out.at[i, n]
            )
            store.start()
            stores.append(store)
    for store in stores:
        store.wait()


def regroup_kernel(a_ref, b_ref, *refs):
    for s, out in enumerate(refs[-3:]):
        out[0] = a_ref[s + 1, :, 0:HALF]
        out[1] = b_ref[s + 1, :, 0:HALF]


def upright(keys_t):
    return keys_t.T


def largest(blocks):
    best = None
    for block in blocks:
        wide = block.astype(F32)
        length = jnp.sum(wide * wide, axis=0, keepdims=True)
        for low in range(0, block.shape[1], HALF):
            part = length[:, low : low + HALF]
            best = part if best is None else jnp.maximum(best, part)
    return jnp.max(best)


def is_small(query_length, key_length):
    return query_length * key_length * (SCALE * SCALE) < SAFE * SAFE


def column_max(blocks):
    best = jnp.max(blocks[0], axis=0, keepdims=True)
    for block in blocks[1:]:
        best = jnp.maximum(best, jnp.max(block, axis=0, keepdims=True))
    return best * SCALE


def in_stages(items, score, weigh, gather):
    scores = {n: score(item) for n, item in enumerate(items[:AHEAD])}
    weights = weigh(items[0], scores.pop(0))
    for n, item in enumerate(items):
        if n + AHEAD < len(items):
            scores[n + AHEAD] = score(items[n + AHEAD])
        following = weigh(items[n + 1], scores.pop(n + 1)) if n + 1 < len(items) else None
        gather(item, weights)
        weights = following


def near_kernel(inputs, units, tasks, carried, first, step, index, mid, top, *refs):
    place = (index, mid, top)
    pieces = dict(zip(inputs, refs[: len(inputs)]))
    refs = refs[len(inputs) :]
    old = [refs[2 * i : 2 * i + 2] for i in range(carried)]
    outs = refs[2 * carried : 2 * carried + 2 * len(tasks)]
    k_s, v_s = refs[-2:]
    v_s[:, DH:DX, :] = jnp.ones((step, DX - DH, v_s.shape[2]), BF16)
    lane_slot = lax.broadcasted_iota(jnp.int32, (1, HALF), 1) // BLK

    def lookup(j, slot):
        first = 0 if (j, 0) in pieces and pieces[j, 0].shape[2] > HALF else slot // 2 * 2
        return pieces[j, first], (slot - first) * BLK

    chunks = []
    row = 0
    for label, members in units:
        chunks.append((label, slice(row, row + len(members) * BLK)))
        row += len(members) * BLK
    members = [member for _, group in units for member in group]

    def prepare(h):
        for i, (j, slot) in enumerate(members):
            ref, lane = lookup(j, slot)
            rows = slice(i * BLK, (i + 1) * BLK)
            k_s[h, rows, :] = upright(ref[h, 0:DH, lane : lane + BLK])
            v_s[h, 0:DH, rows] = ref[h, DH : 2 * DH, lane : lane + BLK]

    def counted_again(h):
        off_mid, off_top = offsets_of(place, head_of(place, 0, first + pl.program_id(0) * step + h))
        same = off_mid == off_top
        return [
            jnp.where(lane_slot == 0, jnp.where(same, 1.584962500721156, 1.0), 0.0),
            jnp.where(lane_slot == 1, jnp.where(same, 0.0, 1.0), 0.0),
        ]

    def run(heads):
        again = [counted_again(h) for h in heads]
        flat = [
            (h, again_h, query, low, merge, out, i)
            for h, again_h in zip(heads, again)
            for out, group in enumerate(tasks)
            for i, (query, low, merge) in enumerate(group)
        ]

        def score(task):
            h, _, (j, half), low = task[:4]
            ref, lane = lookup(j, 2 * half)
            query = ref[h, 2 * DH :, lane : lane + HALF]
            return [dot(k_s[h, rows, :], query) for _, rows in chunks[low:]]

        scores = score(flat[0])
        for n, (h, again_h, (_, half), low, merge, out, i) in enumerate(flat):
            following = score(flat[n + 1]) if n + 1 < len(flat) else None
            best = column_max(scores)
            if merge is not None:
                acc_in, max_in = old[merge[0]]
                old_max = max_in[h, merge[1], 0:1, :]
                best = jnp.maximum(best, old_max)
            acc = None
            for (label, rows), block in zip(chunks[low:], scores):
                block = block * SCALE
                if half == 0 and label is not None:
                    block = block - (best - again_h[label])
                else:
                    block = block - best
                part = dot(v_s[h, :, rows], jnp.exp2(block).astype(BF16))
                acc = part if acc is None else acc + part
            if merge is not None:
                acc = acc + acc_in[h, merge[1]] * jnp.exp2(old_max - best)
            acc_ref, max_ref = outs[2 * out : 2 * out + 2]
            acc_ref[h, i] = acc
            max_ref[h, i] = jnp.broadcast_to(best, (8, HALF))
            scores = following

    def run_plain():
        again = [counted_again(h) for h in range(step)]
        steps = [
            (h, query, merge, out, i, c, c == low, c == len(chunks) - 1)
            for h in range(step)
            for out, group in enumerate(tasks)
            for i, (query, low, merge) in enumerate(group)
            for c in range(low, len(chunks))
        ]

        def score(item):
            h, (j, half), c = item[0], item[1], item[5]
            ref, lane = lookup(j, 2 * half)
            return dot(k_s[h, chunks[c][1], :], ref[h, 2 * DH :, lane : lane + HALF])

        def weigh(item, block):
            h, (_, half), c = item[0], item[1], item[5]
            label = chunks[c][0]
            block = block * SCALE
            if half == 0 and label is not None:
                block = block + again[h][label]
            return jnp.exp2(block).astype(BF16)

        held = {}

        def gather(item, weights):
            h, _, merge, out, i, c, begins, ends = item
            part = dot(v_s[h, :, chunks[c][1]], weights)
            acc = part if begins else held[0] + part
            if ends:
                if merge is not None:
                    acc = acc + old[merge[0]][0][h, merge[1]]
                acc_ref, max_ref = outs[2 * out : 2 * out + 2]
                acc_ref[h, i] = acc
                max_ref[h, i] = jnp.zeros((8, HALF), F32)
            held[0] = acc

        in_stages(steps, score, weigh, gather)

    for h in range(step):
        prepare(h)
    plain = is_small(
        largest([ref[h, 2 * DH :, :] for ref in pieces.values() for h in range(step)]),
        largest([ref[h, 0:DH, :] for ref in pieces.values() for h in range(step)]),
    )
    for _, max_in in old:
        plain = plain & (jnp.max(jnp.abs(max_in[...])) == 0.0)

    @pl.when(plain)
    def _():
        run_plain()

    @pl.when(jnp.logical_not(plain))
    def _():
        @pl.loop(0, step)
        def _(h):
            run([h])


def far_slots(place):
    off_mid, off_top = offsets_of(place, head_of(place, 0, 0))
    same = off_mid == off_top
    return same, (0, jnp.where(same, 0, 1))


def far_pieces(place, sources, k_s, v_s, q_s):
    _, slots = far_slots(place)
    for s, pair in enumerate(sources):
        for i, ref in enumerate(pair):
            here = slice(i * BLK, (i + 1) * BLK)
            for level, slot in enumerate(slots):
                k_s[level, s, here, :] = upright(ref[0:DH, lane_block(slot)])
                v_s[level, s, 0:DH, here] = ref[DH : 2 * DH, lane_block(slot)]
                q_s[level, s, :, here] = ref[2 * DH : 3 * DH, lane_block(slot)]
    v_s[:, :, DH:DX, :] = jnp.ones((2, RATE, DX - DH, HALF), BF16)


def far_lengths(sources):
    every = [ref for pair in sources for ref in pair]
    return (
        largest([ref[2 * DH : 3 * DH, 0:HALF] for ref in every]),
        largest([ref[0:DH, 0:HALF] for ref in every]),
    )


def far_own_kernel(index, mid, top, own0, own1, beyond3, beyond2, beyond1, *refs):
    k_s, v_s, q_s, acc_ref, max_ref, length_ref = refs
    sources = [(own0.at[0], own1.at[0])] + [
        (ref.at[0], ref.at[1]) for ref in (beyond1, beyond2, beyond3)
    ]
    far_pieces((index, mid, top), sources, k_s, v_s, q_s)

    def run_plain():
        steps = [(level, d) for level in range(2) for d in range(1, RATE)]

        def segment(s, carry):
            def score(item):
                level, d = item
                return dot(k_s[level, s ^ d], q_s[level, s])

            def weigh(item, block):
                return jnp.exp2(block * SCALE).astype(BF16)

            held = {}

            def gather(item, weights):
                level, d = item
                part = dot(v_s[level, s ^ d], weights)
                held[0] = part if d == 1 else held[0] + part
                if d == RATE - 1:
                    acc_ref[level, s] = held[0]
                    max_ref[level, s] = jnp.zeros((8, HALF), F32)

            in_stages(steps, score, weigh, gather)
            return carry

        lax.fori_loop(0, RATE, segment, 0, unroll=RATE)

    def run():
        def segment(s, carry):
            def score(level):
                return [dot(k_s[level, s ^ d], q_s[level, s]) for d in range(1, RATE)]

            scores = score(0)
            for level in range(2):
                following = score(1) if level == 0 else None
                best = column_max(scores)
                acc = None
                for d in range(1, RATE):
                    block = scores[d - 1] * SCALE - best
                    part = dot(v_s[level, s ^ d], jnp.exp2(block).astype(BF16))
                    acc = part if acc is None else acc + part
                acc_ref[level, s] = acc
                max_ref[level, s] = jnp.broadcast_to(best, (8, HALF))
                scores = following
            return carry

        lax.fori_loop(0, RATE, segment, 0)

    query_length, key_length = far_lengths(sources)
    length_ref[0] = query_length
    length_ref[1] = key_length
    plain = is_small(query_length, key_length)
    pl.when(plain)(run_plain)
    pl.when(jnp.logical_not(plain))(run)


def near_and_far_kernel(near_args, steps, index, mid, top, *refs):
    scalars = (index, mid, top)
    inputs, tasks, carried = near_args[0], near_args[2], near_args[3]
    count = len(inputs) + 2 * carried
    near_in, far_in, refs = refs[:count], refs[count : count + 5], refs[count + 5 :]
    near_out, far_out, scratch = refs[: 2 * len(tasks)], refs[2 * len(tasks) : -2], refs[-2:]

    @pl.when(pl.program_id(0) < steps)
    def _():
        near_kernel(*near_args, *scalars, *near_in, *near_out, *scratch)

    @pl.when(pl.program_id(0) == steps)
    def _():
        far_own_kernel(*scalars, *far_in, *far_out)


def far_kernel(index, mid, top, *refs):
    place = (index, mid, top)
    sel2, sel3, beyond2, beyond1, beyond3, k_own, v_own, q_own, acc_in, max_in, length_in = refs[
        :11
    ]
    outs = refs[11 : 11 + RATE]
    k_s, v_s, q_s, result_s, tail_s = refs[11 + RATE :]
    same, _ = far_slots(place)
    sources = [(sel2.at[0], sel3.at[0])] + [
        (ref.at[0], ref.at[1]) for ref in (beyond1, beyond2, beyond3)
    ]
    far_pieces(place, sources, k_s, v_s, q_s)
    tail_s[...] = jnp.zeros(tail_s.shape, F32)

    tasks = [(level, chip) for level in range(2) for chip in range(2)]
    held = ((k_own, v_own, q_own), (k_s, v_s, q_s))

    def blocks(s, chip):
        return [(held[c], s ^ d) for d in range(1, RATE) for c in ((1,), (0, 1))[chip]]

    def finish(s, level, chip, acc, best):
        total = acc[DH : DH + 1, :]
        result = (acc[0:DH, :] / total).astype(BF16)
        lse = best + jnp.log2(total)
        if level == 0:
            lse = jnp.where(same, lse + 1.0, lse)
        else:
            lse = jnp.where(same, -1e30, lse)
        high = lse.astype(BF16).astype(F32)
        middle = (lse - high).astype(BF16).astype(F32)
        low = lse - high - middle
        for i in range(2):
            n = 2 * (2 * chip + i) + level
            mine = slice(i * BLK, (i + 1) * BLK)
            result_s[s, :, n * BLK : (n + 1) * BLK] = result[:, mine]
            for k, part in enumerate((high, middle, low)):
                tail_s[s, 3 * n + k : 3 * n + k + 1, :] = part[:, mine]

    def run_plain():
        def segment(s, carry):
            steps = [
                (level, chip, keys, b, n)
                for level, chip in tasks
                for n, (keys, b) in enumerate(blocks(s, chip))
            ]

            def score(item):
                level, chip, keys, b, _ = item
                return dot(keys[0][level, b], held[chip][2][level, s])

            def weigh(item, block):
                return jnp.exp2(block * SCALE).astype(BF16)

            sums = {}

            def gather(item, weights):
                level, chip, keys, b, n = item
                part = dot(keys[1][level, b], weights)
                sums[0] = sums[0] + part if n else part
                if n + 1 == len(blocks(s, chip)):
                    acc = sums[0] + acc_in[level, s] if chip == 0 else sums[0]
                    finish(s, level, chip, acc, jnp.zeros((1, HALF), F32))

            in_stages(steps, score, weigh, gather)
            return carry

        lax.fori_loop(0, RATE, segment, 0, unroll=RATE)

    def run():
        def segment(s, carry):
            for level, chip in tasks:
                scores = [
                    dot(keys[0][level, b], held[chip][2][level, s]) for keys, b in blocks(s, chip)
                ]
                best = column_max(scores)
                acc = jnp.zeros((DX, HALF), F32)
                if chip == 0:
                    old_max = max_in[level, s, 0:1, :]
                    best = jnp.maximum(best, old_max)
                    acc = acc_in[level, s] * jnp.exp2(old_max - best)
                for block, (keys, b) in zip(scores, blocks(s, chip)):
                    acc += dot(keys[1][level, b], jnp.exp2(block * SCALE - best).astype(BF16))
                finish(s, level, chip, acc, best)
            return carry

        lax.fori_loop(0, RATE, segment, 0)

    query_length, key_length = far_lengths(sources)
    plain = is_small(
        jnp.maximum(query_length, length_in[0]), jnp.maximum(key_length, length_in[1])
    )
    pl.when(plain)(run_plain)
    pl.when(jnp.logical_not(plain))(run)
    for s in range(RATE):
        outs[s][:, : GROUP * HALF] = result_s[s]
        outs[s][:, GROUP * HALF :] = tail_s[s].astype(BF16)


def join(acc, best, far, j):
    tail = far[:, GROUP * HALF :].astype(F32)
    lse = jnp.concatenate(
        [
            tail[3 * n : 3 * n + 1] + tail[3 * n + 1 : 3 * n + 2] + tail[3 * n + 2 : 3 * n + 3]
            for n in (2 * j, 2 * j + 1)
        ],
        axis=1,
    )
    overall = jnp.maximum(best, lse)
    near_factor, far_factor = jnp.exp2(best - overall), jnp.exp2(lse - overall)
    total = acc[DH : DH + 1] * near_factor + far_factor
    value = far[:, j * HALF : (j + 1) * HALF].astype(F32) * far_factor
    return ((acc[0:DH] * near_factor + value) / total).astype(BF16)


def combine_kernel(chip, acc_ref, max_ref, *refs):
    far, outs = refs[:-2][::-1], refs[-2:]
    for i in range(2):
        for p, results in enumerate(far):
            outs[i][p, :, 0:HALF] = join(
                acc_ref[p, 2 * i], max_ref[p, 2 * i, 0:1, :], results, 2 * chip + i
            )
            acc = acc_ref[p, 2 * i + 1]
            outs[i][p, :, HALF:] = (acc[0:DH] / acc[DH : DH + 1]).astype(BF16)


def last_own_kernel(inputs, units, tasks, index, mid, top, *refs):
    count = len(inputs) + 2
    near_refs, far, outs, scratch = refs[:count], refs[count:-6], refs[-6:-4], refs[-4:]
    acc_s, max_s, k_s, v_s = scratch
    near_kernel(
        inputs, units, tasks, 1, 0, HG, index, mid, top, *near_refs, acc_s, max_s, k_s, v_s
    )
    combine_kernel(0, acc_s, max_s, *far, *outs)


def project_kernel(sources, index, mid, top, *refs):
    place = (index, mid, top)
    parts, (w_ref, out_ref, held) = refs[:-3], refs[-3:]
    for (j, first), part in zip(sources, parts):
        for p in range(part.shape[0]):
            head = head_of(place, j, first + p)
            slots = class_of_slots(*offsets_of(place, head))
            for s in range(RATE):
                held[head_rows(head), lane_block(slots[s])] = part[
                    p, :, s * BLK : (s + 1) * BLK
                ]
    row = lax.broadcasted_iota(jnp.int32, (TOK, TOK), 0)
    col = lax.broadcasted_iota(jnp.int32, (TOK, TOK), 1)
    picker = (row == RATE * (col % BLK) + col // BLK).astype(BF16)
    attention = dot_nt(picker, held[...]).astype(BF16)
    out_ref[...] = dot(attention, w_ref[...]).astype(BF16)


def whole(shape):
    return pl.BlockSpec(shape, lambda *_: (0,) * len(shape))


def per_head(shape, skip=0, last=None):
    def index(h, *_):
        at = h + skip if last is None else jnp.minimum(h, last)
        return (at,) + (0,) * (len(shape) - 1)

    return pl.BlockSpec(shape, index)


def call(
    kernel, scalars, args, grid, in_specs, outs, scratch, scores,
    limit=VMEM_LIMIT, after=(), through=(), busy=0,
):
    known = len(scalars) + len(args)
    extra = (*after, *through)
    count = len(outs)
    anywhere = pl.BlockSpec(memory_space=pl.ANY)

    def body(*refs):
        results = refs[known + len(extra) :]
        kernel(*refs[:known], *results[:count], *results[count + len(through) :])

    return pl.pallas_call(
        body if extra else kernel,
        grid_spec=pltpu.PrefetchScalarGridSpec(
            num_scalar_prefetch=len(scalars),
            grid=grid,
            in_specs=list(in_specs) + [anywhere] * len(extra),
            out_specs=[spec for spec, _ in outs] + [anywhere] * len(through),
            scratch_shapes=scratch,
        ),
        out_shape=[shape for _, shape in outs]
        + [jax.ShapeDtypeStruct(x.shape, x.dtype) for x in through],
        input_output_aliases={known + len(after) + i: count + i for i in range(len(through))},
        compiler_params=pltpu.CompilerParams(vmem_limit_bytes=limit),
        cost_estimate=pl.CostEstimate(flops=busy, bytes_accessed=0, transcendentals=0),
    )(*scalars, *args, *extra)


def handed_on(arrays, **order):
    return call(lambda: None, (), (), (1,), [], [], [], 0, through=tuple(arrays), **order)


def within(array, apart):
    count = lax.axis_size("seq")
    return lax.ppermute(array, "seq", [(i, i ^ apart) for i in range(count)])


def swap_segments(arrays):
    moved = {s: within(arrays[s - 1], GROUP * s) for s in (3, 2, 1)}
    return [moved[s] for s in (1, 2, 3)]


def shards_four(queries, key_states, value_states, offsets_mid, offsets_top, out_weight):
    width = queries.shape[1]
    place = (lax.axis_index("seq").astype(jnp.int32).reshape(1), offsets_mid, offsets_top)
    full = jax.ShapeDtypeStruct((HG, 3 * DH, TOK), BF16)
    piece = jax.ShapeDtypeStruct((HG, 3 * DH, HALF), BF16)
    pair = jax.ShapeDtypeStruct((2, 3 * DH, HALF), BF16)
    anywhere = pl.BlockSpec(memory_space=pl.ANY)
    shapes = [full] * 2 + [piece] * 4
    own0, own1, sel2, sel3, rest2, rest3 = call(
        pack_kernel, place, (key_states, value_states, queries), (1,),
        [anywhere] * 3,
        [(anywhere, shape) for shape in shapes],
        [pltpu.VMEM((TOK, width), BF16)] * 3
        + [pltpu.VMEM((width, TOK), BF16)] * 3
        + [pltpu.VMEM(shape.shape, BF16) for shape in shapes]
        + [pltpu.SemaphoreType.DMA((3, 2)), pltpu.SemaphoreType.DMA((6, 3))],
        1 << 19, VMEM_MOST,
    )
    own1 = within(own1, 1)
    sel2, sel3 = within(sel2, 2), within(sel3, 3)

    def regroup(a, b, **order):
        return call(
            regroup_kernel, (), (a, b), (1,),
            [whole(a.shape), whole(b.shape)], [(whole(pair.shape), pair)] * 3,
            [], 1 << 17, **order,
        )

    def near(held, units, tasks, old, first=0, heads=HG, step=2, **order):
        sizes = [len(members) * BLK for _, members in units]
        scores = sum(sum(sizes[low:]) * HALF for group in tasks for _, low, _ in group)
        arrays = [*held.values(), *[x for one in old for x in one]]
        shapes = [
            jax.ShapeDtypeStruct((heads, len(group), rows, HALF), F32)
            for group in tasks
            for rows in (DX, 8)
        ]
        return call(
            functools.partial(near_kernel, list(held), units, tasks, len(old), first, step),
            place, arrays, (heads // step,),
            [per_head((step,) + x.shape[1:], first // step) for x in arrays],
            [(per_head((step,) + x.shape[1:]), x) for x in shapes],
            [
                pltpu.VMEM((step, sum(sizes), DH), BF16),
                pltpu.VMEM((step, DX, sum(sizes)), BF16),
            ],
            heads * scores, **order,
        )

    def units_of(a, b):
        return [(0, [(a, 0), (b, 0)]), (1, [(a, 1), (b, 1)])], [
            (None, [(a, 2), (a, 3), (b, 2), (b, 3)])
        ]

    own_sel, own_rest = units_of(0, 1)
    other_sel, other_rest = units_of(2, 3)
    own = [(0, 0), (0, 1), (1, 0), (1, 1)]

    ours = regroup(own0, own1)
    ours = swap_segments(ours)
    held = {(0, 0): own0, (1, 0): own1}
    state_own = near(held, own_sel + own_rest, [[(q, 0, None) for q in own]], [])
    *theirs, rest2, rest3 = regroup(sel2, sel3, after=state_own[1:], through=(rest2, rest3))
    theirs = swap_segments(theirs)
    rest2, rest3 = within(rest2, 2), within(rest3, 3)

    held.update({(2, 0): sel2, (3, 0): sel3})
    units = own_sel + own_rest + other_sel
    tasks = [
        [(q, 3, (0, i)) for i, q in enumerate(own)],
        [((2, 0), 0, None), ((3, 0), 0, None)],
    ]
    arrays = [*held.values(), *state_own]
    near_shapes = [
        jax.ShapeDtypeStruct((HG, len(group), rows, HALF), F32)
        for group in tasks
        for rows in (DX, 8)
    ]
    far_shapes = [
        jax.ShapeDtypeStruct((2, RATE, HALF, DH), BF16),
        jax.ShapeDtypeStruct((2, RATE, DX, HALF), BF16),
        jax.ShapeDtypeStruct((2, RATE, DH, HALF), BF16),
        jax.ShapeDtypeStruct((2, RATE, DX, HALF), F32),
        jax.ShapeDtypeStruct((2, RATE, 8, HALF), F32),
    ]
    piece_0 = pl.BlockSpec((1, 3 * DH, HALF), lambda *_: (0, 0, 0))
    in_scalars = pl.BlockSpec(memory_space=pltpu.SMEM)
    step, steps = 2, HG // 2
    keys = sum(len(members) for _, members in units) * BLK
    out = call(
        functools.partial(
            near_and_far_kernel, (list(held), units, tasks, 1, 0, step), steps
        ),
        place, (*arrays, own0, own1, *ours[::-1]), (steps + 1,),
        [per_head((step,) + x.shape[1:], last=steps - 1) for x in arrays]
        + [piece_0] * 2 + [whole(pair.shape)] * 3,
        [(per_head((step,) + x.shape[1:], last=steps - 1), x) for x in near_shapes]
        + [(whole(x.shape), x) for x in far_shapes]
        + [(in_scalars, jax.ShapeDtypeStruct((2,), F32))],
        [pltpu.VMEM((step, keys, DH), BF16), pltpu.VMEM((step, DX, keys), BF16)],
        1 << 18,
    )
    state_own, state_sel, far_own = out[:2], out[2:4], out[4:]

    result = jax.ShapeDtypeStruct((DH, GROUP * HALF + BLK), BF16)
    results = call(
        far_kernel, place, (sel2, sel3, theirs[1], theirs[0], theirs[2], *far_own), (1,),
        [piece_0] * 2 + [whole(pair.shape)] * 3
        + [whole(x.shape) for x in far_own[:-1]] + [in_scalars],
        [(whole(result.shape), result)] * RATE,
        [pltpu.VMEM(x.shape, BF16) for x in far_shapes[:3]]
        + [
            pltpu.VMEM((RATE, DH, GROUP * HALF), BF16),
            pltpu.VMEM((RATE, DH, BLK), F32),
        ],
        RATE * 2 * 3 * 3 * HALF * HALF, busy=BUSY,
    )
    back = [results[0]] + swap_segments(results[1:])

    held.update({(2, 2): rest2, (3, 2): rest3})
    units = own_sel + own_rest + other_sel + other_rest

    def combine(chip, state, far, **order):
        heads = state[0].shape[0]
        attended = jax.ShapeDtypeStruct((heads, DH, TOK), BF16)
        return call(
            functools.partial(combine_kernel, chip), (), (*state, *far[::-1]), (1,),
            [whole(x.shape) for x in state] + [whole(result.shape)] * heads,
            [(whole(attended.shape), attended)] * 2,
            [],
            1 << 18, **order,
        )

    parts, last = {}, results[0]
    for first, heads in CHUNKS:
        state_other = near(
            held, units,
            [
                [
                    ((2, 0), 5, (0, 0)), ((2, 1), 0, None),
                    ((3, 0), 5, (0, 1)), ((3, 1), 0, None),
                ]
            ],
            [state_sel],
            first, heads, 2, after=(last,),
        )
        if first:
            back[1:] = handed_on(back[1:], after=state_other[1:])
        part2, part3 = combine(1, state_other, back[first : first + heads])
        early = tuple(parts.values())
        parts[2, first], parts[3, first] = within(part2, 2), within(part3, 3)
        last = part3
    pieces = {(2, 2): rest2, (3, 2): rest3, **{q: held[q] for q in ((0, 0), (1, 0))}}
    arrays = [*pieces.values(), *state_own, *back[::-1]]
    attended = jax.ShapeDtypeStruct((HG, DH, TOK), BF16)
    part0, part1 = call(
        functools.partial(
            last_own_kernel, list(pieces), other_rest, [[(q, 0, (0, i)) for i, q in enumerate(own)]]
        ),
        place, arrays, (1,),
        [whole(x.shape) for x in arrays],
        [(whole(attended.shape), attended)] * 2,
        [pltpu.VMEM(x.shape, F32) for x in state_own]
        + [pltpu.VMEM((HG, TOK, DH), BF16), pltpu.VMEM((HG, DX, TOK), BF16)],
        HG * TOK * GROUP * HALF, after=(last, *early),
    )
    parts = dict(zip(parts, handed_on(parts.values(), busy=BUSY)))
    parts[0, 0], parts[1, 0] = part0, within(part1, 1)
    return call(
        functools.partial(project_kernel, list(parts)), place, (*parts.values(), out_weight), (1,),
        [whole(x.shape) for x in parts.values()] + [whole((width, width))],
        [(whole((TOK, width)), jax.ShapeDtypeStruct((TOK, width), BF16))],
        [pltpu.VMEM((width, TOK), BF16)],
        1 << 18,
    )[0]


def shards(queries, key_states, value_states, offsets_mid, offsets_top, out_weight):
    tokens, width = queries.shape
    heads = offsets_mid.shape[0]
    fits = (
        lax.axis_size("head") == 1
        and lax.axis_size("seq") == GROUP * RATE
        and tokens == TOK
        and heads == GROUP * HG
        and width == heads * DH
    )
    run = shards_four if fits else shards_general
    return run(queries, key_states, value_states, offsets_mid, offsets_top, out_weight)


def solution(mesh):
    in_specs = (
        P(("slide", "seq"), "head"),
        P(("slide", "seq"), "head"),
        P(("slide", "seq"), "head"),
        P(),
        P(),
        P("head", None),
    )
    out_specs = P(("slide", "seq", "head"), None)
    return jax.shard_map(shards, mesh=mesh, in_specs=in_specs, out_specs=out_specs, check_vma=False)
```

```python
import functools

import jax
import jax.numpy as jnp
from jax import lax
from jax.experimental import pallas as pl
from jax.experimental.pallas import tpu as pltpu
from jax.sharding import PartitionSpec as P

SEG = 2048
LOG2E = 1.4426950408889634
VMEM_LIMIT = 40 * 1024 * 1024
VMEM_MOST = 60 * 1024 * 1024
BF16 = jnp.bfloat16
F32 = jnp.float32


def partner_2(block, axis, apart):
    count = lax.axis_size(axis)
    route = []
    for low in range(count):
        high = low | 1 << apart
        if high != low and high < count:
            route += [(low, high), (high, low)]
    return lax.ppermute(block, axis, route)


def attend_head(triple_in):
    query_rows, key_rows, value_rows = triple_in
    score_scale = query_rows.shape[-1] ** (-0.5)
    scores = jnp.dot(query_rows, key_rows.T, preferred_element_type=jnp.float32) * score_scale
    row_max = jnp.max(scores, axis=1)
    shifted = jnp.exp(scores - row_max[:, None])
    row_total = jnp.sum(shifted, axis=1)
    weights = shifted.astype(jnp.bfloat16)
    numerator = jnp.dot(weights, value_rows, preferred_element_type=jnp.float32)
    return (numerator, row_total, row_max)


def attend_local(query_rows, pair_rows):
    return lax.map(
        attend_head,
        (
            query_rows.transpose(1, 0, 2),
            pair_rows[:, 0].transpose(1, 0, 2),
            pair_rows[:, 1].transpose(1, 0, 2),
        ),
    )


def pick_rows(states, offsets, rate):
    row_count, inner_count, heads_here, head_width = states.shape
    picker = (jnp.arange(rate)[:, None] == offsets[None, :]).astype(jnp.bfloat16)
    folded = states.reshape(row_count // rate, rate, inner_count, heads_here, head_width)
    return jnp.einsum("archd,rh->achd", folded, picker, preferred_element_type=jnp.float32).astype(
        jnp.bfloat16
    )


def spread_back(numerator, row_total, row_max, offsets, rate):
    heads_here, picked_count, head_width = numerator.shape
    chosen = jnp.arange(rate)[:, None] == offsets[None, :]
    full_num = jnp.where(chosen[None, :, :, None], numerator.transpose(1, 0, 2)[:, None], 0.0)
    full_total = jnp.where(chosen[None], row_total.T[:, None], 0.0)
    full_max = jnp.where(chosen[None], row_max.T[:, None], -1e30)
    return (
        full_num.reshape(picked_count * rate, heads_here, head_width),
        full_total.reshape(picked_count * rate, heads_here),
        full_max.reshape(picked_count * rate, heads_here),
    )


def doubling(buffer, steps_count):
    position = lax.axis_index("seq")
    for bit_index in range(steps_count):
        partner = partner_2(buffer, "seq", bit_index)
        is_lower = position >> bit_index & 1 == 0
        buffer = jnp.where(
            is_lower, jnp.concatenate([buffer, partner], 0), jnp.concatenate([partner, buffer], 0)
        )
    return buffer


def shards_general(queries, key_states, value_states, offsets_mid, offsets_top, out_weight):
    tok_rows = queries.shape[0]
    heads_local = offsets_mid.shape[0] // lax.axis_size("head")
    head_size = queries.shape[1] // heads_local
    seq_devices = lax.axis_size("seq")
    seq_total = tok_rows * seq_devices
    width_mid = min(16 * SEG, seq_total)
    rate_mid = width_mid // SEG
    rate_top = seq_total // SEG
    start_head = lax.axis_index("head") * heads_local
    mid_local = lax.dynamic_slice(offsets_mid, (start_head,), (heads_local,))
    top_local = lax.dynamic_slice(offsets_top, (start_head,), (heads_local,))
    query_heads = queries.reshape(tok_rows, 1, heads_local, head_size)
    paired = jnp.stack([key_states, value_states], axis=1).reshape(
        tok_rows, 2, heads_local, head_size
    )
    near_bits = (SEG // tok_rows).bit_length() - 1
    near_rows = doubling(paired.reshape(tok_rows, -1), near_bits).reshape(
        SEG, 2, heads_local, head_size
    )
    near_num, near_total, near_max = attend_local(query_heads[:, 0], near_rows)
    level_near = spread_back(
        near_num, near_total, near_max, jnp.zeros((heads_local,), jnp.int32), 1
    )
    mid_q = pick_rows(query_heads, mid_local, rate_mid)[:, 0]
    mid_kv = pick_rows(paired, mid_local, rate_mid)
    mid_group = width_mid // tok_rows
    mid_bits = mid_group.bit_length() - 1
    mid_rows = doubling(mid_kv.reshape(mid_kv.shape[0], -1), mid_bits).reshape(
        SEG, 2, heads_local, head_size
    )
    mid_num, mid_total, mid_max = attend_local(mid_q, mid_rows)
    level_mid = spread_back(mid_num, mid_total, mid_max, mid_local, rate_mid)
    top_q = pick_rows(query_heads, top_local, rate_top)[:, 0]
    top_kv = pick_rows(paired, top_local, rate_top)
    top_rows = lax.all_gather(
        top_kv.reshape(top_kv.shape[0], -1), "seq", axis=0, tiled=True
    ).reshape(SEG, 2, heads_local, head_size)
    top_num, top_total, top_max = attend_local(top_q, top_rows)
    level_top = spread_back(top_num, top_total, top_max, top_local, rate_top)
    levels = [level_near, level_mid, level_top]
    overall = jnp.maximum(jnp.maximum(level_near[2], level_mid[2]), level_top[2])
    numerator = jnp.zeros((tok_rows, heads_local, head_size), jnp.float32)
    row_total = jnp.zeros((tok_rows, heads_local), jnp.float32)
    for level_num, level_total, level_max in levels:
        factor = jnp.exp(level_max - overall)
        numerator = numerator + factor[..., None] * level_num
        row_total = row_total + factor * level_total
    attention = (
        (numerator / row_total[..., None])
        .astype(jnp.bfloat16)
        .reshape(tok_rows, heads_local * head_size)
    )
    result = lax.psum_scatter(
        jnp.dot(attention, out_weight, preferred_element_type=jnp.float32),
        "head",
        scatter_dimension=0,
        tiled=True,
    )
    return result.astype(jnp.bfloat16)


RATE = 4
GROUP = 4
HG = 4
DH = 48
BLK = 128
HALF = 2 * BLK
TOK = 512
SCALE = DH**-0.5 * LOG2E
BUSY = 1 << 33
AHEAD = 6
SAFE = 96.0
CHUNKS = ((0, 2), (2, 2))
DX = 64


def dot(a, b):
    return jnp.dot(a, b, preferred_element_type=F32)


def dot_nt(a, b):
    return lax.dot_general(a, b, (((1,), (1,)), ((), ())), preferred_element_type=F32)


def class_of_slots(off_mid, off_top):
    first = off_mid
    second = jnp.where(off_top == off_mid, lax.rem(off_mid + 1, RATE), off_top)
    free0 = (first != 0) & (second != 0)
    free1 = (first != 1) & (second != 1)
    third = jnp.where(free0, 0, jnp.where(free1, 1, 2))
    return first, second, third, 6 - first - second - third


def head_of(place, j, p):
    index = place[0][0]
    return ((index & (GROUP - 1)) ^ j) * HG + ((index // GROUP) ^ p)


def offsets_of(place, head):
    return place[1][head], place[2][head]


def token_picker():
    row = lax.broadcasted_iota(jnp.int32, (TOK, TOK), 0)
    col = lax.broadcasted_iota(jnp.int32, (TOK, TOK), 1)
    return (col == RATE * (row % BLK) + row // BLK).astype(BF16)


def fill_class_major(block, picker, scratch):
    scratch[...] = lax.dot_general(
        block, picker, (((0,), (1,)), ((), ())), preferred_element_type=F32
    ).astype(BF16)


def lane_block(index):
    return pl.ds(pl.multiple_of(index * BLK, BLK), BLK)


def head_rows(head):
    return pl.ds(pl.multiple_of(head * DH, 16), DH)


def pack_kernel(index, mid, top, k_hbm, v_hbm, q_hbm, *refs):
    place = (index, mid, top)
    outs, refs = refs[:6], refs[6:]
    blocks, held, packed = refs[:3], refs[3:6], refs[6:12]
    sems_in, sems_out = refs[12:]
    loads = [
        [
            pltpu.make_async_copy(hbm.at[rows], block.at[rows], sems_in.at[i, n])
            for n, rows in enumerate((slice(0, HALF), slice(HALF, TOK)))
        ]
        for i, (hbm, block) in enumerate(zip((k_hbm, v_hbm, q_hbm), blocks))
    ]
    for pair in loads:
        for load in pair:
            load.start()
    picker = token_picker()
    stores = []
    heads = {(j, p): head_of(place, j, p) for j in range(GROUP) for p in range(HG)}
    classes = {at: class_of_slots(*offsets_of(place, head)) for at, head in heads.items()}
    for n, (load, block, scratch) in enumerate(zip(loads, blocks, held)):
        for half in load:
            half.wait()
        fill_class_major(block[...], picker, scratch)
        rows = slice(n * DH, (n + 1) * DH)
        for i, (j, first, count) in enumerate(
            ((0, 0, 4), (1, 0, 4), (2, 0, 2), (3, 0, 2), (2, 2, 2), (3, 2, 2))
        ):
            for p in range(HG):
                for s in range(count):
                    packed[i][p, rows, s * BLK : (s + 1) * BLK] = scratch[
                        head_rows(heads[j, p]), lane_block(classes[j, p][first + s])
                    ]
            store = pltpu.make_async_copy(
                packed[i].at[:, rows], outs[i].at[:, rows], sems_out.at[i, n]
            )
            store.start()
            stores.append(store)
    for store in stores:
        store.wait()


def regroup_kernel(a_ref, b_ref, *refs):
    for s, out in enumerate(refs[-3:]):
        out[0] = a_ref[s + 1, :, 0:HALF]
        out[1] = b_ref[s + 1, :, 0:HALF]


def upright(keys_t):
    return keys_t.T


def largest(blocks):
    best = None
    for block in blocks:
        wide = block.astype(F32)
        length = jnp.sum(wide * wide, axis=0, keepdims=True)
        for low in range(0, block.shape[1], HALF):
            part = length[:, low : low + HALF]
            best = part if best is None else jnp.maximum(best, part)
    return jnp.max(best)


def is_small(query_length, key_length):
    return query_length * key_length * (SCALE * SCALE) < SAFE * SAFE


def column_max(blocks):
    best = jnp.max(blocks[0], axis=0, keepdims=True)
    for block in blocks[1:]:
        best = jnp.maximum(best, jnp.max(block, axis=0, keepdims=True))
    return best * SCALE


def in_stages(items, score, weigh, gather):
    scores = {n: score(item) for n, item in enumerate(items[:AHEAD])}
    weights = weigh(items[0], scores.pop(0))
    for n, item in enumerate(items):
        if n + AHEAD < len(items):
            scores[n + AHEAD] = score(items[n + AHEAD])
        following = weigh(items[n + 1], scores.pop(n + 1)) if n + 1 < len(items) else None
        gather(item, weights)
        weights = following


def near_kernel(inputs, units, tasks, carried, first, step, index, mid, top, *refs):
    place = (index, mid, top)
    pieces = dict(zip(inputs, refs[: len(inputs)]))
    refs = refs[len(inputs) :]
    old = [refs[2 * i : 2 * i + 2] for i in range(carried)]
    outs = refs[2 * carried : 2 * carried + 2 * len(tasks)]
    k_s, v_s = refs[-2:]
    v_s[:, DH:DX, :] = jnp.ones((step, DX - DH, v_s.shape[2]), BF16)
    lane_slot = lax.broadcasted_iota(jnp.int32, (1, HALF), 1) // BLK

    def lookup(j, slot):
        first = 0 if (j, 0) in pieces and pieces[j, 0].shape[2] > HALF else slot // 2 * 2
        return pieces[j, first], (slot - first) * BLK

    chunks = []
    row = 0
    for label, members in units:
        chunks.append((label, slice(row, row + len(members) * BLK)))
        row += len(members) * BLK
    members = [member for _, group in units for member in group]

    def prepare(h):
        for i, (j, slot) in enumerate(members):
            ref, lane = lookup(j, slot)
            rows = slice(i * BLK, (i + 1) * BLK)
            k_s[h, rows, :] = upright(ref[h, 0:DH, lane : lane + BLK])
            v_s[h, 0:DH, rows] = ref[h, DH : 2 * DH, lane : lane + BLK]

    def counted_again(h):
        off_mid, off_top = offsets_of(place, head_of(place, 0, first + pl.program_id(0) * step + h))
        same = off_mid == off_top
        return [
            jnp.where(lane_slot == 0, jnp.where(same, 1.584962500721156, 1.0), 0.0),
            jnp.where(lane_slot == 1, jnp.where(same, 0.0, 1.0), 0.0),
        ]

    def run(heads):
        again = [counted_again(h) for h in heads]
        flat = [
            (h, again_h, query, low, merge, out, i)
            for h, again_h in zip(heads, again)
            for out, group in enumerate(tasks)
            for i, (query, low, merge) in enumerate(group)
        ]

        def score(task):
            h, _, (j, half), low = task[:4]
            ref, lane = lookup(j, 2 * half)
            query = ref[h, 2 * DH :, lane : lane + HALF]
            return [dot(k_s[h, rows, :], query) for _, rows in chunks[low:]]

        scores = score(flat[0])
        for n, (h, again_h, (_, half), low, merge, out, i) in enumerate(flat):
            following = score(flat[n + 1]) if n + 1 < len(flat) else None
            best = column_max(scores)
            if merge is not None:
                acc_in, max_in = old[merge[0]]
                old_max = max_in[h, merge[1], 0:1, :]
                best = jnp.maximum(best, old_max)
            acc = None
            for (label, rows), block in zip(chunks[low:], scores):
                block = block * SCALE
                if half == 0 and label is not None:
                    block = block - (best - again_h[label])
                else:
                    block = block - best
                part = dot(v_s[h, :, rows], jnp.exp2(block).astype(BF16))
                acc = part if acc is None else acc + part
            if merge is not None:
                acc = acc + acc_in[h, merge[1]] * jnp.exp2(old_max - best)
            acc_ref, max_ref = outs[2 * out : 2 * out + 2]
            acc_ref[h, i] = acc
            max_ref[h, i] = jnp.broadcast_to(best, (8, HALF))
            scores = following

    def run_plain():
        again = [counted_again(h) for h in range(step)]
        steps = [
            (h, query, merge, out, i, c, c == low, c == len(chunks) - 1)
            for h in range(step)
            for out, group in enumerate(tasks)
            for i, (query, low, merge) in enumerate(group)
            for c in range(low, len(chunks))
        ]

        def score(item):
            h, (j, half), c = item[0], item[1], item[5]
            ref, lane = lookup(j, 2 * half)
            return dot(k_s[h, chunks[c][1], :], ref[h, 2 * DH :, lane : lane + HALF])

        def weigh(item, block):
            h, (_, half), c = item[0], item[1], item[5]
            label = chunks[c][0]
            block = block * SCALE
            if half == 0 and label is not None:
                block = block + again[h][label]
            return jnp.exp2(block).astype(BF16)

        held = {}

        def gather(item, weights):
            h, _, merge, out, i, c, begins, ends = item
            part = dot(v_s[h, :, chunks[c][1]], weights)
            acc = part if begins else held[0] + part
            if ends:
                if merge is not None:
                    acc = acc + old[merge[0]][0][h, merge[1]]
                acc_ref, max_ref = outs[2 * out : 2 * out + 2]
                acc_ref[h, i] = acc
                max_ref[h, i] = jnp.zeros((8, HALF), F32)
            held[0] = acc

        in_stages(steps, score, weigh, gather)

    for h in range(step):
        prepare(h)
    plain = is_small(
        largest([ref[h, 2 * DH :, :] for ref in pieces.values() for h in range(step)]),
        largest([ref[h, 0:DH, :] for ref in pieces.values() for h in range(step)]),
    )
    for _, max_in in old:
        plain = plain & (jnp.max(jnp.abs(max_in[...])) == 0.0)

    @pl.when(plain)
    def _():
        run_plain()

    @pl.when(jnp.logical_not(plain))
    def _():
        @pl.loop(0, step)
        def _(h):
            run([h])


def far_slots(place):
    off_mid, off_top = offsets_of(place, head_of(place, 0, 0))
    same = off_mid == off_top
    return same, (0, jnp.where(same, 0, 1))


def far_pieces(place, sources, k_s, v_s, q_s):
    _, slots = far_slots(place)
    for s, pair in enumerate(sources):
        for i, ref in enumerate(pair):
            here = slice(i * BLK, (i + 1) * BLK)
            for level, slot in enumerate(slots):
                k_s[level, s, here, :] = upright(ref[0:DH, lane_block(slot)])
                v_s[level, s, 0:DH, here] = ref[DH : 2 * DH, lane_block(slot)]
                q_s[level, s, :, here] = ref[2 * DH : 3 * DH, lane_block(slot)]
    v_s[:, :, DH:DX, :] = jnp.ones((2, RATE, DX - DH, HALF), BF16)


def far_lengths(sources):
    every = [ref for pair in sources for ref in pair]
    return (
        largest([ref[2 * DH : 3 * DH, 0:HALF] for ref in every]),
        largest([ref[0:DH, 0:HALF] for ref in every]),
    )


def far_own_kernel(index, mid, top, own0, own1, beyond3, beyond2, beyond1, *refs):
    k_s, v_s, q_s, acc_ref, max_ref, length_ref = refs
    sources = [(own0.at[0], own1.at[0])] + [
        (ref.at[0], ref.at[1]) for ref in (beyond1, beyond2, beyond3)
    ]
    far_pieces((index, mid, top), sources, k_s, v_s, q_s)

    def run_plain():
        steps = [(level, d) for level in range(2) for d in range(1, RATE)]

        def segment(s, carry):
            def score(item):
                level, d = item
                return dot(k_s[level, s ^ d], q_s[level, s])

            def weigh(item, block):
                return jnp.exp2(block * SCALE).astype(BF16)

            held = {}

            def gather(item, weights):
                level, d = item
                part = dot(v_s[level, s ^ d], weights)
                held[0] = part if d == 1 else held[0] + part
                if d == RATE - 1:
                    acc_ref[level, s] = held[0]
                    max_ref[level, s] = jnp.zeros((8, HALF), F32)

            in_stages(steps, score, weigh, gather)
            return carry

        lax.fori_loop(0, RATE, segment, 0, unroll=RATE)

    def run():
        def segment(s, carry):
            def score(level):
                return [dot(k_s[level, s ^ d], q_s[level, s]) for d in range(1, RATE)]

            scores = score(0)
            for level in range(2):
                following = score(1) if level == 0 else None
                best = column_max(scores)
                acc = None
                for d in range(1, RATE):
                    block = scores[d - 1] * SCALE - best
                    part = dot(v_s[level, s ^ d], jnp.exp2(block).astype(BF16))
                    acc = part if acc is None else acc + part
                acc_ref[level, s] = acc
                max_ref[level, s] = jnp.broadcast_to(best, (8, HALF))
                scores = following
            return carry

        lax.fori_loop(0, RATE, segment, 0)

    query_length, key_length = far_lengths(sources)
    length_ref[0] = query_length
    length_ref[1] = key_length
    plain = is_small(query_length, key_length)
    pl.when(plain)(run_plain)
    pl.when(jnp.logical_not(plain))(run)


def near_and_far_kernel(near_args, steps, index, mid, top, *refs):
    scalars = (index, mid, top)
    inputs, tasks, carried = near_args[0], near_args[2], near_args[3]
    count = len(inputs) + 2 * carried
    near_in, far_in, refs = refs[:count], refs[count : count + 5], refs[count + 5 :]
    near_out, far_out, scratch = refs[: 2 * len(tasks)], refs[2 * len(tasks) : -2], refs[-2:]

    @pl.when(pl.program_id(0) < steps)
    def _():
        near_kernel(*near_args, *scalars, *near_in, *near_out, *scratch)

    @pl.when(pl.program_id(0) == steps)
    def _():
        far_own_kernel(*scalars, *far_in, *far_out)


def far_kernel(index, mid, top, *refs):
    place = (index, mid, top)
    sel2, sel3, beyond2, beyond1, beyond3, k_own, v_own, q_own, acc_in, max_in, length_in = refs[
        :11
    ]
    outs = refs[11 : 11 + RATE]
    k_s, v_s, q_s, result_s, tail_s = refs[11 + RATE :]
    same, _ = far_slots(place)
    sources = [(sel2.at[0], sel3.at[0])] + [
        (ref.at[0], ref.at[1]) for ref in (beyond1, beyond2, beyond3)
    ]
    far_pieces(place, sources, k_s, v_s, q_s)
    tail_s[...] = jnp.zeros(tail_s.shape, F32)

    tasks = [(level, chip) for level in range(2) for chip in range(2)]
    held = ((k_own, v_own, q_own), (k_s, v_s, q_s))

    def blocks(s, chip):
        return [(held[c], s ^ d) for d in range(1, RATE) for c in ((1,), (0, 1))[chip]]

    def finish(s, level, chip, acc, best):
        total = acc[DH : DH + 1, :]
        result = (acc[0:DH, :] / total).astype(BF16)
        lse = best + jnp.log2(total)
        if level == 0:
            lse = jnp.where(same, lse + 1.0, lse)
        else:
            lse = jnp.where(same, -1e30, lse)
        high = lse.astype(BF16).astype(F32)
        middle = (lse - high).astype(BF16).astype(F32)
        low = lse - high - middle
        for i in range(2):
            n = 2 * (2 * chip + i) + level
            mine = slice(i * BLK, (i + 1) * BLK)
            result_s[s, :, n * BLK : (n + 1) * BLK] = result[:, mine]
            for k, part in enumerate((high, middle, low)):
                tail_s[s, 3 * n + k : 3 * n + k + 1, :] = part[:, mine]

    def run_plain():
        def segment(s, carry):
            steps = [
                (level, chip, keys, b, n)
                for level, chip in tasks
                for n, (keys, b) in enumerate(blocks(s, chip))
            ]

            def score(item):
                level, chip, keys, b, _ = item
                return dot(keys[0][level, b], held[chip][2][level, s])

            def weigh(item, block):
                return jnp.exp2(block * SCALE).astype(BF16)

            sums = {}

            def gather(item, weights):
                level, chip, keys, b, n = item
                part = dot(keys[1][level, b], weights)
                sums[0] = sums[0] + part if n else part
                if n + 1 == len(blocks(s, chip)):
                    acc = sums[0] + acc_in[level, s] if chip == 0 else sums[0]
                    finish(s, level, chip, acc, jnp.zeros((1, HALF), F32))

            in_stages(steps, score, weigh, gather)
            return carry

        lax.fori_loop(0, RATE, segment, 0, unroll=RATE)

    def run():
        def segment(s, carry):
            for level, chip in tasks:
                scores = [
                    dot(keys[0][level, b], held[chip][2][level, s]) for keys, b in blocks(s, chip)
                ]
                best = column_max(scores)
                acc = jnp.zeros((DX, HALF), F32)
                if chip == 0:
                    old_max = max_in[level, s, 0:1, :]
                    best = jnp.maximum(best, old_max)
                    acc = acc_in[level, s] * jnp.exp2(old_max - best)
                for block, (keys, b) in zip(scores, blocks(s, chip)):
                    acc += dot(keys[1][level, b], jnp.exp2(block * SCALE - best).astype(BF16))
                finish(s, level, chip, acc, best)
            return carry

        lax.fori_loop(0, RATE, segment, 0)

    query_length, key_length = far_lengths(sources)
    plain = is_small(
        jnp.maximum(query_length, length_in[0]), jnp.maximum(key_length, length_in[1])
    )
    pl.when(plain)(run_plain)
    pl.when(jnp.logical_not(plain))(run)
    for s in range(RATE):
        outs[s][:, : GROUP * HALF] = result_s[s]
        outs[s][:, GROUP * HALF :] = tail_s[s].astype(BF16)


def join(acc, best, far, j):
    tail = far[:, GROUP * HALF :].astype(F32)
    lse = jnp.concatenate(
        [
            tail[3 * n : 3 * n + 1] + tail[3 * n + 1 : 3 * n + 2] + tail[3 * n + 2 : 3 * n + 3]
            for n in (2 * j, 2 * j + 1)
        ],
        axis=1,
    )
    overall = jnp.maximum(best, lse)
    near_factor, far_factor = jnp.exp2(best - overall), jnp.exp2(lse - overall)
    total = acc[DH : DH + 1] * near_factor + far_factor
    value = far[:, j * HALF : (j + 1) * HALF].astype(F32) * far_factor
    return ((acc[0:DH] * near_factor + value) / total).astype(BF16)


def combine_kernel(chip, acc_ref, max_ref, *refs):
    far, outs = refs[:-2][::-1], refs[-2:]
    for i in range(2):
        for p, results in enumerate(far):
            outs[i][p, :, 0:HALF] = join(
                acc_ref[p, 2 * i], max_ref[p, 2 * i, 0:1, :], results, 2 * chip + i
            )
            acc = acc_ref[p, 2 * i + 1]
            outs[i][p, :, HALF:] = (acc[0:DH] / acc[DH : DH + 1]).astype(BF16)


def last_own_kernel(inputs, units, tasks, index, mid, top, *refs):
    count = len(inputs) + 2
    near_refs, far, outs, scratch = refs[:count], refs[count:-6], refs[-6:-4], refs[-4:]
    acc_s, max_s, k_s, v_s = scratch
    near_kernel(
        inputs, units, tasks, 1, 0, HG, index, mid, top, *near_refs, acc_s, max_s, k_s, v_s
    )
    combine_kernel(0, acc_s, max_s, *far, *outs)


def project_kernel(sources, index, mid, top, *refs):
    place = (index, mid, top)
    parts, (w_ref, out_hbm, held, out_ref, sems) = refs[:-5], refs[-5:]
    for (j, first), part in zip(sources, parts):
        for p in range(part.shape[0]):
            head = head_of(place, j, first + p)
            slots = class_of_slots(*offsets_of(place, head))
            for s in range(RATE):
                held[head_rows(head), lane_block(slots[s])] = part[
                    p, :, s * BLK : (s + 1) * BLK
                ]
    row = lax.broadcasted_iota(jnp.int32, (TOK, TOK), 0)
    col = lax.broadcasted_iota(jnp.int32, (TOK, TOK), 1)
    picker = (row == RATE * (col % BLK) + col // BLK).astype(BF16)
    attention = dot_nt(picker, held[...]).astype(BF16)
    stores = []
    for n, rows in enumerate((slice(0, HALF), slice(HALF, TOK))):
        out_ref[rows, :] = dot(attention[rows, :], w_ref[...]).astype(BF16)
        stores.append(pltpu.make_async_copy(out_ref.at[rows], out_hbm.at[rows], sems.at[n]))
        stores[n].start()
    for store in stores:
        store.wait()


def whole(shape):
    return pl.BlockSpec(shape, lambda *_: (0,) * len(shape))


def per_head(shape, skip=0, last=None):
    def index(h, *_):
        at = h + skip if last is None else jnp.minimum(h, last)
        return (at,) + (0,) * (len(shape) - 1)

    return pl.BlockSpec(shape, index)


def call(
    kernel, scalars, args, grid, in_specs, outs, scratch, scores,
    limit=VMEM_LIMIT, after=(), through=(), busy=0,
):
    known = len(scalars) + len(args)
    extra = (*after, *through)
    count = len(outs)
    anywhere = pl.BlockSpec(memory_space=pl.ANY)

    def body(*refs):
        results = refs[known + len(extra) :]
        kernel(*refs[:known], *results[:count], *results[count + len(through) :])

    return pl.pallas_call(
        body if extra else kernel,
        grid_spec=pltpu.PrefetchScalarGridSpec(
            num_scalar_prefetch=len(scalars),
            grid=grid,
            in_specs=list(in_specs) + [anywhere] * len(extra),
            out_specs=[spec for spec, _ in outs] + [anywhere] * len(through),
            scratch_shapes=scratch,
        ),
        out_shape=[shape for _, shape in outs]
        + [jax.ShapeDtypeStruct(x.shape, x.dtype) for x in through],
        input_output_aliases={known + len(after) + i: count + i for i in range(len(through))},
        compiler_params=pltpu.CompilerParams(vmem_limit_bytes=limit),
        cost_estimate=pl.CostEstimate(flops=busy, bytes_accessed=0, transcendentals=0),
    )(*scalars, *args, *extra)


def handed_on(arrays, **order):
    return call(lambda: None, (), (), (1,), [], [], [], 0, through=tuple(arrays), **order)


def within(array, apart):
    count = lax.axis_size("seq")
    return lax.ppermute(array, "seq", [(i, i ^ apart) for i in range(count)])


def swap_segments(arrays):
    moved = {s: within(arrays[s - 1], GROUP * s) for s in (3, 2, 1)}
    return [moved[s] for s in (1, 2, 3)]


def shards_four(queries, key_states, value_states, offsets_mid, offsets_top, out_weight):
    width = queries.shape[1]
    place = (lax.axis_index("seq").astype(jnp.int32).reshape(1), offsets_mid, offsets_top)
    full = jax.ShapeDtypeStruct((HG, 3 * DH, TOK), BF16)
    piece = jax.ShapeDtypeStruct((HG, 3 * DH, HALF), BF16)
    pair = jax.ShapeDtypeStruct((2, 3 * DH, HALF), BF16)
    anywhere = pl.BlockSpec(memory_space=pl.ANY)
    shapes = [full] * 2 + [piece] * 4
    own0, own1, sel2, sel3, rest2, rest3 = call(
        pack_kernel, place, (key_states, value_states, queries), (1,),
        [anywhere] * 3,
        [(anywhere, shape) for shape in shapes],
        [pltpu.VMEM((TOK, width), BF16)] * 3
        + [pltpu.VMEM((width, TOK), BF16)] * 3
        + [pltpu.VMEM(shape.shape, BF16) for shape in shapes]
        + [pltpu.SemaphoreType.DMA((3, 2)), pltpu.SemaphoreType.DMA((6, 3))],
        1 << 19, VMEM_MOST,
    )
    own1 = within(own1, 1)
    sel2, sel3 = within(sel2, 2), within(sel3, 3)

    def regroup(a, b, **order):
        return call(
            regroup_kernel, (), (a, b), (1,),
            [whole(a.shape), whole(b.shape)], [(whole(pair.shape), pair)] * 3,
            [], 1 << 17, **order,
        )

    def near(held, units, tasks, old, first=0, heads=HG, step=2, **order):
        sizes = [len(members) * BLK for _, members in units]
        scores = sum(sum(sizes[low:]) * HALF for group in tasks for _, low, _ in group)
        arrays = [*held.values(), *[x for one in old for x in one]]
        shapes = [
            jax.ShapeDtypeStruct((heads, len(group), rows, HALF), F32)
            for group in tasks
            for rows in (DX, 8)
        ]
        return call(
            functools.partial(near_kernel, list(held), units, tasks, len(old), first, step),
            place, arrays, (heads // step,),
            [per_head((step,) + x.shape[1:], first // step) for x in arrays],
            [(per_head((step,) + x.shape[1:]), x) for x in shapes],
            [
                pltpu.VMEM((step, sum(sizes), DH), BF16),
                pltpu.VMEM((step, DX, sum(sizes)), BF16),
            ],
            heads * scores, **order,
        )

    def units_of(a, b):
        return [(0, [(a, 0), (b, 0)]), (1, [(a, 1), (b, 1)])], [
            (None, [(a, 2), (a, 3), (b, 2), (b, 3)])
        ]

    own_sel, own_rest = units_of(0, 1)
    other_sel, other_rest = units_of(2, 3)
    own = [(0, 0), (0, 1), (1, 0), (1, 1)]

    ours = regroup(own0, own1)
    ours = swap_segments(ours)
    held = {(0, 0): own0, (1, 0): own1}
    state_own = near(held, own_sel + own_rest, [[(q, 0, None) for q in own]], [])
    *theirs, rest2, rest3 = regroup(sel2, sel3, after=state_own[1:], through=(rest2, rest3))
    theirs = swap_segments(theirs)
    rest2, rest3 = within(rest2, 2), within(rest3, 3)

    held.update({(2, 0): sel2, (3, 0): sel3})
    units = own_sel + own_rest + other_sel
    tasks = [
        [(q, 3, (0, i)) for i, q in enumerate(own)],
        [((2, 0), 0, None), ((3, 0), 0, None)],
    ]
    arrays = [*held.values(), *state_own]
    near_shapes = [
        jax.ShapeDtypeStruct((HG, len(group), rows, HALF), F32)
        for group in tasks
        for rows in (DX, 8)
    ]
    far_shapes = [
        jax.ShapeDtypeStruct((2, RATE, HALF, DH), BF16),
        jax.ShapeDtypeStruct((2, RATE, DX, HALF), BF16),
        jax.ShapeDtypeStruct((2, RATE, DH, HALF), BF16),
        jax.ShapeDtypeStruct((2, RATE, DX, HALF), F32),
        jax.ShapeDtypeStruct((2, RATE, 8, HALF), F32),
    ]
    piece_0 = pl.BlockSpec((1, 3 * DH, HALF), lambda *_: (0, 0, 0))
    in_scalars = pl.BlockSpec(memory_space=pltpu.SMEM)
    step, steps = 2, HG // 2
    keys = sum(len(members) for _, members in units) * BLK
    out = call(
        functools.partial(
            near_and_far_kernel, (list(held), units, tasks, 1, 0, step), steps
        ),
        place, (*arrays, own0, own1, *ours[::-1]), (steps + 1,),
        [per_head((step,) + x.shape[1:], last=steps - 1) for x in arrays]
        + [piece_0] * 2 + [whole(pair.shape)] * 3,
        [(per_head((step,) + x.shape[1:], last=steps - 1), x) for x in near_shapes]
        + [(whole(x.shape), x) for x in far_shapes]
        + [(in_scalars, jax.ShapeDtypeStruct((2,), F32))],
        [pltpu.VMEM((step, keys, DH), BF16), pltpu.VMEM((step, DX, keys), BF16)],
        1 << 18,
    )
    state_own, state_sel, far_own = out[:2], out[2:4], out[4:]

    result = jax.ShapeDtypeStruct((DH, GROUP * HALF + BLK), BF16)
    results = call(
        far_kernel, place, (sel2, sel3, theirs[1], theirs[0], theirs[2], *far_own), (1,),
        [piece_0] * 2 + [whole(pair.shape)] * 3
        + [whole(x.shape) for x in far_own[:-1]] + [in_scalars],
        [(whole(result.shape), result)] * RATE,
        [pltpu.VMEM(x.shape, BF16) for x in far_shapes[:3]]
        + [
            pltpu.VMEM((RATE, DH, GROUP * HALF), BF16),
            pltpu.VMEM((RATE, DH, BLK), F32),
        ],
        RATE * 2 * 3 * 3 * HALF * HALF, busy=BUSY,
    )
    back = [results[0]] + swap_segments(results[1:])

    held.update({(2, 2): rest2, (3, 2): rest3})
    units = own_sel + own_rest + other_sel + other_rest

    def combine(chip, state, far, **order):
        heads = state[0].shape[0]
        attended = jax.ShapeDtypeStruct((heads, DH, TOK), BF16)
        return call(
            functools.partial(combine_kernel, chip), (), (*state, *far[::-1]), (1,),
            [whole(x.shape) for x in state] + [whole(result.shape)] * heads,
            [(whole(attended.shape), attended)] * 2,
            [],
            1 << 18, **order,
        )

    parts, last = {}, results[0]
    for first, heads in CHUNKS:
        state_other = near(
            held, units,
            [
                [
                    ((2, 0), 5, (0, 0)), ((2, 1), 0, None),
                    ((3, 0), 5, (0, 1)), ((3, 1), 0, None),
                ]
            ],
            [state_sel],
            first, heads, 2, after=(last,),
        )
        if first:
            back[1:] = handed_on(back[1:], after=state_other[1:])
        part2, part3 = combine(1, state_other, back[first : first + heads])
        early = tuple(parts.values())
        parts[2, first], parts[3, first] = within(part2, 2), within(part3, 3)
        last = part3
    pieces = {(2, 2): rest2, (3, 2): rest3, **{q: held[q] for q in ((0, 0), (1, 0))}}
    arrays = [*pieces.values(), *state_own, *back[::-1]]
    attended = jax.ShapeDtypeStruct((HG, DH, TOK), BF16)
    part0, part1 = call(
        functools.partial(
            last_own_kernel, list(pieces), other_rest, [[(q, 0, (0, i)) for i, q in enumerate(own)]]
        ),
        place, arrays, (1,),
        [whole(x.shape) for x in arrays],
        [(whole(attended.shape), attended)] * 2,
        [pltpu.VMEM(x.shape, F32) for x in state_own]
        + [pltpu.VMEM((HG, TOK, DH), BF16), pltpu.VMEM((HG, DX, TOK), BF16)],
        HG * TOK * GROUP * HALF, after=(last, *early),
    )
    parts = dict(zip(parts, handed_on(parts.values(), busy=BUSY)))
    parts[0, 0], parts[1, 0] = part0, within(part1, 1)
    return call(
        functools.partial(project_kernel, list(parts)), place, (*parts.values(), out_weight), (1,),
        [whole(x.shape) for x in parts.values()] + [whole((width, width))],
        [(anywhere, jax.ShapeDtypeStruct((TOK, width), BF16))],
        [
            pltpu.VMEM((width, TOK), BF16),
            pltpu.VMEM((TOK, width), BF16),
            pltpu.SemaphoreType.DMA((2,)),
        ],
        1 << 18,
    )[0]


def shards(queries, key_states, value_states, offsets_mid, offsets_top, out_weight):
    tokens, width = queries.shape
    heads = offsets_mid.shape[0]
    fits = (
        lax.axis_size("head") == 1
        and lax.axis_size("seq") == GROUP * RATE
        and tokens == TOK
        and heads == GROUP * HG
        and width == heads * DH
    )
    run = shards_four if fits else shards_general
    return run(queries, key_states, value_states, offsets_mid, offsets_top, out_weight)


def solution(mesh):
    in_specs = (
        P(("slide", "seq"), "head"),
        P(("slide", "seq"), "head"),
        P(("slide", "seq"), "head"),
        P(),
        P(),
        P("head", None),
    )
    out_specs = P(("slide", "seq", "head"), None)
    return jax.shard_map(shards, mesh=mesh, in_specs=in_specs, out_specs=out_specs, check_vma=False)
```

```python
import functools

import jax
import jax.numpy as jnp
from jax import lax
from jax.experimental import pallas as pl
from jax.experimental.pallas import tpu as pltpu
from jax.sharding import PartitionSpec as P

SEG = 2048
LOG2E = 1.4426950408889634
VMEM_LIMIT = 40 * 1024 * 1024
VMEM_MOST = 60 * 1024 * 1024
BF16 = jnp.bfloat16
F32 = jnp.float32


def partner_2(block, axis, apart):
    count = lax.axis_size(axis)
    route = []
    for low in range(count):
        high = low | 1 << apart
        if high != low and high < count:
            route += [(low, high), (high, low)]
    return lax.ppermute(block, axis, route)


def attend_head(triple_in):
    query_rows, key_rows, value_rows = triple_in
    score_scale = query_rows.shape[-1] ** (-0.5)
    scores = jnp.dot(query_rows, key_rows.T, preferred_element_type=jnp.float32) * score_scale
    row_max = jnp.max(scores, axis=1)
    shifted = jnp.exp(scores - row_max[:, None])
    row_total = jnp.sum(shifted, axis=1)
    weights = shifted.astype(jnp.bfloat16)
    numerator = jnp.dot(weights, value_rows, preferred_element_type=jnp.float32)
    return (numerator, row_total, row_max)


def attend_local(query_rows, pair_rows):
    return lax.map(
        attend_head,
        (
            query_rows.transpose(1, 0, 2),
            pair_rows[:, 0].transpose(1, 0, 2),
            pair_rows[:, 1].transpose(1, 0, 2),
        ),
    )


def pick_rows(states, offsets, rate):
    row_count, inner_count, heads_here, head_width = states.shape
    picker = (jnp.arange(rate)[:, None] == offsets[None, :]).astype(jnp.bfloat16)
    folded = states.reshape(row_count // rate, rate, inner_count, heads_here, head_width)
    return jnp.einsum("archd,rh->achd", folded, picker, preferred_element_type=jnp.float32).astype(
        jnp.bfloat16
    )


def spread_back(numerator, row_total, row_max, offsets, rate):
    heads_here, picked_count, head_width = numerator.shape
    chosen = jnp.arange(rate)[:, None] == offsets[None, :]
    full_num = jnp.where(chosen[None, :, :, None], numerator.transpose(1, 0, 2)[:, None], 0.0)
    full_total = jnp.where(chosen[None], row_total.T[:, None], 0.0)
    full_max = jnp.where(chosen[None], row_max.T[:, None], -1e30)
    return (
        full_num.reshape(picked_count * rate, heads_here, head_width),
        full_total.reshape(picked_count * rate, heads_here),
        full_max.reshape(picked_count * rate, heads_here),
    )


def doubling(buffer, steps_count):
    position = lax.axis_index("seq")
    for bit_index in range(steps_count):
        partner = partner_2(buffer, "seq", bit_index)
        is_lower = position >> bit_index & 1 == 0
        buffer = jnp.where(
            is_lower, jnp.concatenate([buffer, partner], 0), jnp.concatenate([partner, buffer], 0)
        )
    return buffer


def shards_general(queries, key_states, value_states, offsets_mid, offsets_top, out_weight):
    tok_rows = queries.shape[0]
    heads_local = offsets_mid.shape[0] // lax.axis_size("head")
    head_size = queries.shape[1] // heads_local
    seq_devices = lax.axis_size("seq")
    seq_total = tok_rows * seq_devices
    width_mid = min(16 * SEG, seq_total)
    rate_mid = width_mid // SEG
    rate_top = seq_total // SEG
    start_head = lax.axis_index("head") * heads_local
    mid_local = lax.dynamic_slice(offsets_mid, (start_head,), (heads_local,))
    top_local = lax.dynamic_slice(offsets_top, (start_head,), (heads_local,))
    query_heads = queries.reshape(tok_rows, 1, heads_local, head_size)
    paired = jnp.stack([key_states, value_states], axis=1).reshape(
        tok_rows, 2, heads_local, head_size
    )
    near_bits = (SEG // tok_rows).bit_length() - 1
    near_rows = doubling(paired.reshape(tok_rows, -1), near_bits).reshape(
        SEG, 2, heads_local, head_size
    )
    near_num, near_total, near_max = attend_local(query_heads[:, 0], near_rows)
    level_near = spread_back(
        near_num, near_total, near_max, jnp.zeros((heads_local,), jnp.int32), 1
    )
    mid_q = pick_rows(query_heads, mid_local, rate_mid)[:, 0]
    mid_kv = pick_rows(paired, mid_local, rate_mid)
    mid_group = width_mid // tok_rows
    mid_bits = mid_group.bit_length() - 1
    mid_rows = doubling(mid_kv.reshape(mid_kv.shape[0], -1), mid_bits).reshape(
        SEG, 2, heads_local, head_size
    )
    mid_num, mid_total, mid_max = attend_local(mid_q, mid_rows)
    level_mid = spread_back(mid_num, mid_total, mid_max, mid_local, rate_mid)
    top_q = pick_rows(query_heads, top_local, rate_top)[:, 0]
    top_kv = pick_rows(paired, top_local, rate_top)
    top_rows = lax.all_gather(
        top_kv.reshape(top_kv.shape[0], -1), "seq", axis=0, tiled=True
    ).reshape(SEG, 2, heads_local, head_size)
    top_num, top_total, top_max = attend_local(top_q, top_rows)
    level_top = spread_back(top_num, top_total, top_max, top_local, rate_top)
    levels = [level_near, level_mid, level_top]
    overall = jnp.maximum(jnp.maximum(level_near[2], level_mid[2]), level_top[2])
    numerator = jnp.zeros((tok_rows, heads_local, head_size), jnp.float32)
    row_total = jnp.zeros((tok_rows, heads_local), jnp.float32)
    for level_num, level_total, level_max in levels:
        factor = jnp.exp(level_max - overall)
        numerator = numerator + factor[..., None] * level_num
        row_total = row_total + factor * level_total
    attention = (
        (numerator / row_total[..., None])
        .astype(jnp.bfloat16)
        .reshape(tok_rows, heads_local * head_size)
    )
    result = lax.psum_scatter(
        jnp.dot(attention, out_weight, preferred_element_type=jnp.float32),
        "head",
        scatter_dimension=0,
        tiled=True,
    )
    return result.astype(jnp.bfloat16)


RATE = 4
GROUP = 4
HG = 4
DH = 48
BLK = 128
HALF = 2 * BLK
TOK = 512
SCALE = DH**-0.5 * LOG2E
BUSY = 1 << 33
AHEAD = 6
SAFE = 96.0
CHUNKS = ((0, 2), (2, 2))
DX = 64


def dot(a, b):
    return jnp.dot(a, b, preferred_element_type=F32)


def dot_nt(a, b):
    return lax.dot_general(a, b, (((1,), (1,)), ((), ())), preferred_element_type=F32)


def class_of_slots(off_mid, off_top):
    first = off_mid
    second = jnp.where(off_top == off_mid, lax.rem(off_mid + 1, RATE), off_top)
    free0 = (first != 0) & (second != 0)
    free1 = (first != 1) & (second != 1)
    third = jnp.where(free0, 0, jnp.where(free1, 1, 2))
    return first, second, third, 6 - first - second - third


def head_of(place, j, p):
    index = place[0][0]
    return ((index & (GROUP - 1)) ^ j) * HG + ((index // GROUP) ^ p)


def offsets_of(place, head):
    return place[1][head], place[2][head]


def token_picker():
    row = lax.broadcasted_iota(jnp.int32, (TOK, TOK), 0)
    col = lax.broadcasted_iota(jnp.int32, (TOK, TOK), 1)
    return (col == RATE * (row % BLK) + row // BLK).astype(BF16)


def fill_class_major(block, picker, scratch):
    scratch[...] = lax.dot_general(
        block, picker, (((0,), (1,)), ((), ())), preferred_element_type=F32
    ).astype(BF16)


def lane_block(index):
    return pl.ds(pl.multiple_of(index * BLK, BLK), BLK)


def head_rows(head):
    return pl.ds(pl.multiple_of(head * DH, 16), DH)


def pack_kernel(index, mid, top, k_hbm, v_hbm, q_hbm, *refs):
    place = (index, mid, top)
    outs, refs = refs[:6], refs[6:]
    blocks, held, packed = refs[:3], refs[3:6], refs[6:12]
    sems_in, sems_out = refs[12:]
    loads = [
        [
            pltpu.make_async_copy(hbm.at[rows], block.at[rows], sems_in.at[i, n])
            for n, rows in enumerate((slice(0, HALF), slice(HALF, TOK)))
        ]
        for i, (hbm, block) in enumerate(zip((k_hbm, v_hbm, q_hbm), blocks))
    ]
    for pair in loads:
        for load in pair:
            load.start()
    picker = token_picker()
    stores = []
    heads = {(j, p): head_of(place, j, p) for j in range(GROUP) for p in range(HG)}
    classes = {at: class_of_slots(*offsets_of(place, head)) for at, head in heads.items()}
    for n, (load, block, scratch) in enumerate(zip(loads, blocks, held)):
        for half in load:
            half.wait()
        fill_class_major(block[...], picker, scratch)
        rows = slice(n * DH, (n + 1) * DH)
        for i, (j, first, count) in enumerate(
            ((0, 0, 4), (1, 0, 4), (2, 0, 2), (3, 0, 2), (2, 2, 2), (3, 2, 2))
        ):
            for p in range(HG):
                for s in range(count):
                    packed[i][p, rows, s * BLK : (s + 1) * BLK] = scratch[
                        head_rows(heads[j, p]), lane_block(classes[j, p][first + s])
                    ]
            store = pltpu.make_async_copy(
                packed[i].at[:, rows], outs[i].at[:, rows], sems_out.at[i, n]
            )
            store.start()
            stores.append(store)
    for store in stores:
        store.wait()


def regroup_kernel(a_ref, b_ref, *refs):
    for s, out in enumerate(refs[-3:]):
        out[0] = a_ref[s + 1, :, 0:HALF]
        out[1] = b_ref[s + 1, :, 0:HALF]


def upright(keys_t):
    return keys_t.T


def largest(blocks):
    best = None
    for block in blocks:
        wide = block.astype(F32)
        length = jnp.sum(wide * wide, axis=0, keepdims=True)
        for low in range(0, block.shape[1], HALF):
            part = length[:, low : low + HALF]
            best = part if best is None else jnp.maximum(best, part)
    return jnp.max(best)


def is_small(query_length, key_length):
    return query_length * key_length * (SCALE * SCALE) < SAFE * SAFE


def column_max(blocks):
    best = jnp.max(blocks[0], axis=0, keepdims=True)
    for block in blocks[1:]:
        best = jnp.maximum(best, jnp.max(block, axis=0, keepdims=True))
    return best * SCALE


def in_stages(items, score, weigh, gather):
    scores = {n: score(item) for n, item in enumerate(items[:AHEAD])}
    weights = weigh(items[0], scores.pop(0))
    for n, item in enumerate(items):
        if n + AHEAD < len(items):
            scores[n + AHEAD] = score(items[n + AHEAD])
        following = weigh(items[n + 1], scores.pop(n + 1)) if n + 1 < len(items) else None
        gather(item, weights)
        weights = following


def near_kernel(inputs, units, tasks, carried, first, step, index, mid, top, *refs):
    place = (index, mid, top)
    pieces = dict(zip(inputs, refs[: len(inputs)]))
    refs = refs[len(inputs) :]
    old = [refs[2 * i : 2 * i + 2] for i in range(carried)]
    outs = refs[2 * carried : 2 * carried + 2 * len(tasks)]
    k_s, v_s = refs[-2:]
    v_s[:, DH:DX, :] = jnp.ones((step, DX - DH, v_s.shape[2]), BF16)
    lane_slot = lax.broadcasted_iota(jnp.int32, (1, HALF), 1) // BLK

    def lookup(j, slot):
        first = 0 if (j, 0) in pieces and pieces[j, 0].shape[2] > HALF else slot // 2 * 2
        return pieces[j, first], (slot - first) * BLK

    chunks = []
    row = 0
    for label, members in units:
        chunks.append((label, slice(row, row + len(members) * BLK)))
        row += len(members) * BLK
    members = [member for _, group in units for member in group]

    def prepare(h):
        for i, (j, slot) in enumerate(members):
            ref, lane = lookup(j, slot)
            rows = slice(i * BLK, (i + 1) * BLK)
            k_s[h, rows, :] = upright(ref[h, 0:DH, lane : lane + BLK])
            v_s[h, 0:DH, rows] = ref[h, DH : 2 * DH, lane : lane + BLK]

    def counted_again(h):
        off_mid, off_top = offsets_of(place, head_of(place, 0, first + pl.program_id(0) * step + h))
        same = off_mid == off_top
        return [
            jnp.where(lane_slot == 0, jnp.where(same, 1.584962500721156, 1.0), 0.0),
            jnp.where(lane_slot == 1, jnp.where(same, 0.0, 1.0), 0.0),
        ]

    def run(heads):
        again = [counted_again(h) for h in heads]
        flat = [
            (h, again_h, query, low, merge, out, i)
            for h, again_h in zip(heads, again)
            for out, group in enumerate(tasks)
            for i, (query, low, merge) in enumerate(group)
        ]

        def score(task):
            h, _, (j, half), low = task[:4]
            ref, lane = lookup(j, 2 * half)
            query = ref[h, 2 * DH :, lane : lane + HALF]
            return [dot(k_s[h, rows, :], query) for _, rows in chunks[low:]]

        scores = score(flat[0])
        for n, (h, again_h, (_, half), low, merge, out, i) in enumerate(flat):
            following = score(flat[n + 1]) if n + 1 < len(flat) else None
            best = column_max(scores)
            if merge is not None:
                acc_in, max_in = old[merge[0]]
                old_max = max_in[h, merge[1], 0:1, :]
                best = jnp.maximum(best, old_max)
            acc = None
            for (label, rows), block in zip(chunks[low:], scores):
                block = block * SCALE
                if half == 0 and label is not None:
                    block = block - (best - again_h[label])
                else:
                    block = block - best
                part = dot(v_s[h, :, rows], jnp.exp2(block).astype(BF16))
                acc = part if acc is None else acc + part
            if merge is not None:
                acc = acc + acc_in[h, merge[1]] * jnp.exp2(old_max - best)
            acc_ref, max_ref = outs[2 * out : 2 * out + 2]
            acc_ref[h, i] = acc
            max_ref[h, i] = jnp.broadcast_to(best, (8, HALF))
            scores = following

    def run_plain():
        again = [counted_again(h) for h in range(step)]
        steps = [
            (h, query, merge, out, i, c, c == low, c == len(chunks) - 1)
            for h in range(step)
            for out, group in enumerate(tasks)
            for i, (query, low, merge) in enumerate(group)
            for c in range(low, len(chunks))
        ]

        def score(item):
            h, (j, half), c = item[0], item[1], item[5]
            ref, lane = lookup(j, 2 * half)
            return dot(k_s[h, chunks[c][1], :], ref[h, 2 * DH :, lane : lane + HALF])

        def weigh(item, block):
            h, (_, half), c = item[0], item[1], item[5]
            label = chunks[c][0]
            block = block * SCALE
            if half == 0 and label is not None:
                block = block + again[h][label]
            return jnp.exp2(block).astype(BF16)

        held = {}

        def gather(item, weights):
            h, _, merge, out, i, c, begins, ends = item
            part = dot(v_s[h, :, chunks[c][1]], weights)
            acc = part if begins else held[0] + part
            if ends:
                if merge is not None:
                    acc = acc + old[merge[0]][0][h, merge[1]]
                acc_ref, max_ref = outs[2 * out : 2 * out + 2]
                acc_ref[h, i] = acc
                max_ref[h, i] = jnp.zeros((8, HALF), F32)
            held[0] = acc

        in_stages(steps, score, weigh, gather)

    for h in range(step):
        prepare(h)
    plain = is_small(
        largest([ref[h, 2 * DH :, :] for ref in pieces.values() for h in range(step)]),
        largest([ref[h, 0:DH, :] for ref in pieces.values() for h in range(step)]),
    )
    for _, max_in in old:
        plain = plain & (jnp.max(jnp.abs(max_in[...])) == 0.0)

    @pl.when(plain)
    def _():
        run_plain()

    @pl.when(jnp.logical_not(plain))
    def _():
        @pl.loop(0, step)
        def _(h):
            run([h])


def far_slots(place):
    off_mid, off_top = offsets_of(place, head_of(place, 0, 0))
    same = off_mid == off_top
    return same, (0, jnp.where(same, 0, 1))


def far_pieces(place, sources, k_s, v_s, q_s):
    _, slots = far_slots(place)
    for s, pair in enumerate(sources):
        for i, ref in enumerate(pair):
            here = slice(i * BLK, (i + 1) * BLK)
            for level, slot in enumerate(slots):
                k_s[level, s, here, :] = upright(ref[0:DH, lane_block(slot)])
                v_s[level, s, 0:DH, here] = ref[DH : 2 * DH, lane_block(slot)]
                q_s[level, s, :, here] = ref[2 * DH : 3 * DH, lane_block(slot)]
    v_s[:, :, DH:DX, :] = jnp.ones((2, RATE, DX - DH, HALF), BF16)


def far_lengths(sources):
    every = [ref for pair in sources for ref in pair]
    return (
        largest([ref[2 * DH : 3 * DH, 0:HALF] for ref in every]),
        largest([ref[0:DH, 0:HALF] for ref in every]),
    )


def far_own_kernel(index, mid, top, own0, own1, beyond3, beyond2, beyond1, *refs):
    k_s, v_s, q_s, acc_ref, max_ref, length_ref = refs
    sources = [(own0.at[0], own1.at[0])] + [
        (ref.at[0], ref.at[1]) for ref in (beyond1, beyond2, beyond3)
    ]
    far_pieces((index, mid, top), sources, k_s, v_s, q_s)

    def run_plain():
        steps = [(level, d) for level in range(2) for d in range(1, RATE)]

        def segment(s, carry):
            def score(item):
                level, d = item
                return dot(k_s[level, s ^ d], q_s[level, s])

            def weigh(item, block):
                return jnp.exp2(block * SCALE).astype(BF16)

            held = {}

            def gather(item, weights):
                level, d = item
                part = dot(v_s[level, s ^ d], weights)
                held[0] = part if d == 1 else held[0] + part
                if d == RATE - 1:
                    acc_ref[level, s] = held[0]
                    max_ref[level, s] = jnp.zeros((8, HALF), F32)

            in_stages(steps, score, weigh, gather)
            return carry

        lax.fori_loop(0, RATE, segment, 0, unroll=RATE)

    def run():
        def segment(s, carry):
            def score(level):
                return [dot(k_s[level, s ^ d], q_s[level, s]) for d in range(1, RATE)]

            scores = score(0)
            for level in range(2):
                following = score(1) if level == 0 else None
                best = column_max(scores)
                acc = None
                for d in range(1, RATE):
                    block = scores[d - 1] * SCALE - best
                    part = dot(v_s[level, s ^ d], jnp.exp2(block).astype(BF16))
                    acc = part if acc is None else acc + part
                acc_ref[level, s] = acc
                max_ref[level, s] = jnp.broadcast_to(best, (8, HALF))
                scores = following
            return carry

        lax.fori_loop(0, RATE, segment, 0)

    query_length, key_length = far_lengths(sources)
    length_ref[0] = query_length
    length_ref[1] = key_length
    plain = is_small(query_length, key_length)
    pl.when(plain)(run_plain)
    pl.when(jnp.logical_not(plain))(run)


def near_and_far_kernel(near_args, steps, index, mid, top, *refs):
    scalars = (index, mid, top)
    inputs, tasks, carried = near_args[0], near_args[2], near_args[3]
    count = len(inputs) + 2 * carried
    near_in, far_in, refs = refs[:count], refs[count : count + 5], refs[count + 5 :]
    near_out, far_out, scratch = refs[: 2 * len(tasks)], refs[2 * len(tasks) : -2], refs[-2:]

    @pl.when(pl.program_id(0) < steps)
    def _():
        near_kernel(*near_args, *scalars, *near_in, *near_out, *scratch)

    @pl.when(pl.program_id(0) == steps)
    def _():
        far_own_kernel(*scalars, *far_in, *far_out)


def far_kernel(index, mid, top, *refs):
    place = (index, mid, top)
    sel2, sel3, beyond2, beyond1, beyond3, k_own, v_own, q_own, acc_in, max_in, length_in = refs[
        :11
    ]
    outs = refs[11 : 11 + RATE]
    k_s, v_s, q_s, result_s, tail_s = refs[11 + RATE :]
    same, _ = far_slots(place)
    sources = [(sel2.at[0], sel3.at[0])] + [
        (ref.at[0], ref.at[1]) for ref in (beyond1, beyond2, beyond3)
    ]
    far_pieces(place, sources, k_s, v_s, q_s)
    tail_s[...] = jnp.zeros(tail_s.shape, F32)

    tasks = [(level, chip) for level in range(2) for chip in range(2)]
    held = ((k_own, v_own, q_own), (k_s, v_s, q_s))

    def blocks(s, chip):
        return [(held[c], s ^ d) for d in range(1, RATE) for c in ((1,), (0, 1))[chip]]

    def finish(s, level, chip, acc, best):
        total = acc[DH : DH + 1, :]
        result = (acc[0:DH, :] / total).astype(BF16)
        lse = best + jnp.log2(total)
        if level == 0:
            lse = jnp.where(same, lse + 1.0, lse)
        else:
            lse = jnp.where(same, -1e30, lse)
        high = lse.astype(BF16).astype(F32)
        middle = (lse - high).astype(BF16).astype(F32)
        low = lse - high - middle
        for i in range(2):
            n = 2 * (2 * chip + i) + level
            mine = slice(i * BLK, (i + 1) * BLK)
            result_s[s, :, n * BLK : (n + 1) * BLK] = result[:, mine]
            for k, part in enumerate((high, middle, low)):
                tail_s[s, 3 * n + k : 3 * n + k + 1, :] = part[:, mine]

    def run_plain():
        def segment(s, carry):
            steps = [
                (level, chip, keys, b, n)
                for level, chip in tasks
                for n, (keys, b) in enumerate(blocks(s, chip))
            ]

            def score(item):
                level, chip, keys, b, _ = item
                return dot(keys[0][level, b], held[chip][2][level, s])

            def weigh(item, block):
                return jnp.exp2(block * SCALE).astype(BF16)

            sums = {}

            def gather(item, weights):
                level, chip, keys, b, n = item
                part = dot(keys[1][level, b], weights)
                sums[0] = sums[0] + part if n else part
                if n + 1 == len(blocks(s, chip)):
                    acc = sums[0] + acc_in[level, s] if chip == 0 else sums[0]
                    finish(s, level, chip, acc, jnp.zeros((1, HALF), F32))

            in_stages(steps, score, weigh, gather)
            return carry

        lax.fori_loop(0, RATE, segment, 0, unroll=RATE)

    def run():
        def segment(s, carry):
            for level, chip in tasks:
                scores = [
                    dot(keys[0][level, b], held[chip][2][level, s]) for keys, b in blocks(s, chip)
                ]
                best = column_max(scores)
                acc = jnp.zeros((DX, HALF), F32)
                if chip == 0:
                    old_max = max_in[level, s, 0:1, :]
                    best = jnp.maximum(best, old_max)
                    acc = acc_in[level, s] * jnp.exp2(old_max - best)
                for block, (keys, b) in zip(scores, blocks(s, chip)):
                    acc += dot(keys[1][level, b], jnp.exp2(block * SCALE - best).astype(BF16))
                finish(s, level, chip, acc, best)
            return carry

        lax.fori_loop(0, RATE, segment, 0)

    query_length, key_length = far_lengths(sources)
    plain = is_small(
        jnp.maximum(query_length, length_in[0]), jnp.maximum(key_length, length_in[1])
    )
    pl.when(plain)(run_plain)
    pl.when(jnp.logical_not(plain))(run)
    for s in range(RATE):
        outs[s][:, : GROUP * HALF] = result_s[s]
        outs[s][:, GROUP * HALF :] = tail_s[s].astype(BF16)


def join(acc, best, far, j):
    tail = far[:, GROUP * HALF :].astype(F32)
    lse = jnp.concatenate(
        [
            tail[3 * n : 3 * n + 1] + tail[3 * n + 1 : 3 * n + 2] + tail[3 * n + 2 : 3 * n + 3]
            for n in (2 * j, 2 * j + 1)
        ],
        axis=1,
    )
    overall = jnp.maximum(best, lse)
    near_factor, far_factor = jnp.exp2(best - overall), jnp.exp2(lse - overall)
    total = acc[DH : DH + 1] * near_factor + far_factor
    value = far[:, j * HALF : (j + 1) * HALF].astype(F32) * far_factor
    return ((acc[0:DH] * near_factor + value) / total).astype(BF16)


def combine_kernel(chip, acc_ref, max_ref, *refs):
    far, outs = refs[:-2][::-1], refs[-2:]
    for i in range(2):
        for p, results in enumerate(far):
            outs[i][p, :, 0:HALF] = join(
                acc_ref[p, 2 * i], max_ref[p, 2 * i, 0:1, :], results, 2 * chip + i
            )
            acc = acc_ref[p, 2 * i + 1]
            outs[i][p, :, HALF:] = (acc[0:DH] / acc[DH : DH + 1]).astype(BF16)


def last_own_kernel(inputs, units, tasks, index, mid, top, *refs):
    count = len(inputs) + 2
    near_refs, far, outs, scratch = refs[:count], refs[count:-6], refs[-6:-4], refs[-4:]
    acc_s, max_s, k_s, v_s = scratch
    near_kernel(
        inputs, units, tasks, 1, 0, HG, index, mid, top, *near_refs, acc_s, max_s, k_s, v_s
    )
    combine_kernel(0, acc_s, max_s, *far, *outs)


def project_kernel(sources, index, mid, top, *refs):
    place = (index, mid, top)
    parts, (w_ref, out_ref, held) = refs[:-3], refs[-3:]
    for (j, first), part in zip(sources, parts):
        for p in range(part.shape[0]):
            head = head_of(place, j, first + p)
            slots = class_of_slots(*offsets_of(place, head))
            for s in range(RATE):
                held[head_rows(head), lane_block(slots[s])] = part[
                    p, :, s * BLK : (s + 1) * BLK
                ]
    row = lax.broadcasted_iota(jnp.int32, (TOK, TOK), 0)
    col = lax.broadcasted_iota(jnp.int32, (TOK, TOK), 1)
    picker = (row == RATE * (col % BLK) + col // BLK).astype(BF16)
    attention = dot_nt(picker, held[...]).astype(BF16)
    out_ref[...] = dot(attention, w_ref[...]).astype(BF16)


def whole(shape):
    return pl.BlockSpec(shape, lambda *_: (0,) * len(shape))


def per_head(shape, skip=0, last=None):
    def index(h, *_):
        at = h + skip if last is None else jnp.minimum(h, last)
        return (at,) + (0,) * (len(shape) - 1)

    return pl.BlockSpec(shape, index)


def call(
    kernel, scalars, args, grid, in_specs, outs, scratch, scores,
    limit=VMEM_LIMIT, after=(), through=(), busy=0,
):
    known = len(scalars) + len(args)
    extra = (*after, *through)
    count = len(outs)
    anywhere = pl.BlockSpec(memory_space=pl.ANY)

    def body(*refs):
        results = refs[known + len(extra) :]
        kernel(*refs[:known], *results[:count], *results[count + len(through) :])

    return pl.pallas_call(
        body if extra else kernel,
        grid_spec=pltpu.PrefetchScalarGridSpec(
            num_scalar_prefetch=len(scalars),
            grid=grid,
            in_specs=list(in_specs) + [anywhere] * len(extra),
            out_specs=[spec for spec, _ in outs] + [anywhere] * len(through),
            scratch_shapes=scratch,
        ),
        out_shape=[shape for _, shape in outs]
        + [jax.ShapeDtypeStruct(x.shape, x.dtype) for x in through],
        input_output_aliases={known + len(after) + i: count + i for i in range(len(through))},
        compiler_params=pltpu.CompilerParams(vmem_limit_bytes=limit),
        cost_estimate=pl.CostEstimate(flops=busy, bytes_accessed=0, transcendentals=0),
    )(*scalars, *args, *extra)


def handed_on(arrays, **order):
    return call(lambda: None, (), (), (1,), [], [], [], 0, through=tuple(arrays), **order)


def within(array, apart):
    count = lax.axis_size("seq")
    return lax.ppermute(array, "seq", [(i, i ^ apart) for i in range(count)])


def swap_segments(arrays):
    moved = {s: within(arrays[s - 1], GROUP * s) for s in (3, 2, 1)}
    return [moved[s] for s in (1, 2, 3)]


def shards_four(queries, key_states, value_states, offsets_mid, offsets_top, out_weight):
    width = queries.shape[1]
    place = (lax.axis_index("seq").astype(jnp.int32).reshape(1), offsets_mid, offsets_top)
    full = jax.ShapeDtypeStruct((HG, 3 * DH, TOK), BF16)
    piece = jax.ShapeDtypeStruct((HG, 3 * DH, HALF), BF16)
    pair = jax.ShapeDtypeStruct((2, 3 * DH, HALF), BF16)
    anywhere = pl.BlockSpec(memory_space=pl.ANY)
    shapes = [full] * 2 + [piece] * 4
    own0, own1, sel2, sel3, rest2, rest3 = call(
        pack_kernel, place, (key_states, value_states, queries), (1,),
        [anywhere] * 3,
        [(anywhere, shape) for shape in shapes],
        [pltpu.VMEM((TOK, width), BF16)] * 3
        + [pltpu.VMEM((width, TOK), BF16)] * 3
        + [pltpu.VMEM(shape.shape, BF16) for shape in shapes]
        + [pltpu.SemaphoreType.DMA((3, 2)), pltpu.SemaphoreType.DMA((6, 3))],
        1 << 19, VMEM_MOST,
    )
    own1 = within(own1, 1)
    sel2, sel3 = within(sel2, 2), within(sel3, 3)

    def regroup(a, b, **order):
        return call(
            regroup_kernel, (), (a, b), (1,),
            [whole(a.shape), whole(b.shape)], [(whole(pair.shape), pair)] * 3,
            [], 1 << 17, **order,
        )

    def near(held, units, tasks, old, first=0, heads=HG, step=2, **order):
        sizes = [len(members) * BLK for _, members in units]
        scores = sum(sum(sizes[low:]) * HALF for group in tasks for _, low, _ in group)
        arrays = [*held.values(), *[x for one in old for x in one]]
        shapes = [
            jax.ShapeDtypeStruct((heads, len(group), rows, HALF), F32)
            for group in tasks
            for rows in (DX, 8)
        ]
        return call(
            functools.partial(near_kernel, list(held), units, tasks, len(old), first, step),
            place, arrays, (heads // step,),
            [per_head((step,) + x.shape[1:], first // step) for x in arrays],
            [(per_head((step,) + x.shape[1:]), x) for x in shapes],
            [
                pltpu.VMEM((step, sum(sizes), DH), BF16),
                pltpu.VMEM((step, DX, sum(sizes)), BF16),
            ],
            heads * scores, **order,
        )

    def units_of(a, b):
        return [(0, [(a, 0), (b, 0)]), (1, [(a, 1), (b, 1)])], [
            (None, [(a, 2), (a, 3), (b, 2), (b, 3)])
        ]

    own_sel, own_rest = units_of(0, 1)
    other_sel, other_rest = units_of(2, 3)
    own = [(0, 0), (0, 1), (1, 0), (1, 1)]

    ours = regroup(own0, own1)
    ours = swap_segments(ours)
    held = {(0, 0): own0, (1, 0): own1}
    state_own = near(held, own_sel + own_rest, [[(q, 0, None) for q in own]], [], step=HG)
    *theirs, rest2, rest3 = regroup(sel2, sel3, after=state_own[1:], through=(rest2, rest3))
    theirs = swap_segments(theirs)
    rest2, rest3 = within(rest2, 2), within(rest3, 3)

    held.update({(2, 0): sel2, (3, 0): sel3})
    units = own_sel + own_rest + other_sel
    tasks = [
        [(q, 3, (0, i)) for i, q in enumerate(own)],
        [((2, 0), 0, None), ((3, 0), 0, None)],
    ]
    arrays = [*held.values(), *state_own]
    near_shapes = [
        jax.ShapeDtypeStruct((HG, len(group), rows, HALF), F32)
        for group in tasks
        for rows in (DX, 8)
    ]
    far_shapes = [
        jax.ShapeDtypeStruct((2, RATE, HALF, DH), BF16),
        jax.ShapeDtypeStruct((2, RATE, DX, HALF), BF16),
        jax.ShapeDtypeStruct((2, RATE, DH, HALF), BF16),
        jax.ShapeDtypeStruct((2, RATE, DX, HALF), F32),
        jax.ShapeDtypeStruct((2, RATE, 8, HALF), F32),
    ]
    piece_0 = pl.BlockSpec((1, 3 * DH, HALF), lambda *_: (0, 0, 0))
    in_scalars = pl.BlockSpec(memory_space=pltpu.SMEM)
    step, steps = 2, HG // 2
    keys = sum(len(members) for _, members in units) * BLK
    out = call(
        functools.partial(
            near_and_far_kernel, (list(held), units, tasks, 1, 0, step), steps
        ),
        place, (*arrays, own0, own1, *ours[::-1]), (steps + 1,),
        [per_head((step,) + x.shape[1:], last=steps - 1) for x in arrays]
        + [piece_0] * 2 + [whole(pair.shape)] * 3,
        [(per_head((step,) + x.shape[1:], last=steps - 1), x) for x in near_shapes]
        + [(whole(x.shape), x) for x in far_shapes]
        + [(in_scalars, jax.ShapeDtypeStruct((2,), F32))],
        [pltpu.VMEM((step, keys, DH), BF16), pltpu.VMEM((step, DX, keys), BF16)],
        1 << 18,
    )
    state_own, state_sel, far_own = out[:2], out[2:4], out[4:]

    result = jax.ShapeDtypeStruct((DH, GROUP * HALF + BLK), BF16)
    results = call(
        far_kernel, place, (sel2, sel3, theirs[1], theirs[0], theirs[2], *far_own), (1,),
        [piece_0] * 2 + [whole(pair.shape)] * 3
        + [whole(x.shape) for x in far_own[:-1]] + [in_scalars],
        [(whole(result.shape), result)] * RATE,
        [pltpu.VMEM(x.shape, BF16) for x in far_shapes[:3]]
        + [
            pltpu.VMEM((RATE, DH, GROUP * HALF), BF16),
            pltpu.VMEM((RATE, DH, BLK), F32),
        ],
        RATE * 2 * 3 * 3 * HALF * HALF, busy=BUSY,
    )
    back = [results[0]] + swap_segments(results[1:])

    held.update({(2, 2): rest2, (3, 2): rest3})
    units = own_sel + own_rest + other_sel + other_rest

    def combine(chip, state, far, **order):
        heads = state[0].shape[0]
        attended = jax.ShapeDtypeStruct((heads, DH, TOK), BF16)
        return call(
            functools.partial(combine_kernel, chip), (), (*state, *far[::-1]), (1,),
            [whole(x.shape) for x in state] + [whole(result.shape)] * heads,
            [(whole(attended.shape), attended)] * 2,
            [],
            1 << 18, **order,
        )

    parts, last = {}, results[0]
    for first, heads in CHUNKS:
        state_other = near(
            held, units,
            [
                [
                    ((2, 0), 5, (0, 0)), ((2, 1), 0, None),
                    ((3, 0), 5, (0, 1)), ((3, 1), 0, None),
                ]
            ],
            [state_sel],
            first, heads, 2, after=(last,),
        )
        if first:
            back[1:] = handed_on(back[1:], after=state_other[1:])
        part2, part3 = combine(1, state_other, back[first : first + heads])
        early = tuple(parts.values())
        parts[2, first], parts[3, first] = within(part2, 2), within(part3, 3)
        last = part3
    pieces = {(2, 2): rest2, (3, 2): rest3, **{q: held[q] for q in ((0, 0), (1, 0))}}
    arrays = [*pieces.values(), *state_own, *back[::-1]]
    attended = jax.ShapeDtypeStruct((HG, DH, TOK), BF16)
    part0, part1 = call(
        functools.partial(
            last_own_kernel, list(pieces), other_rest, [[(q, 0, (0, i)) for i, q in enumerate(own)]]
        ),
        place, arrays, (1,),
        [whole(x.shape) for x in arrays],
        [(whole(attended.shape), attended)] * 2,
        [pltpu.VMEM(x.shape, F32) for x in state_own]
        + [pltpu.VMEM((HG, TOK, DH), BF16), pltpu.VMEM((HG, DX, TOK), BF16)],
        HG * TOK * GROUP * HALF, after=(last, *early),
    )
    parts = dict(zip(parts, handed_on(parts.values(), busy=BUSY)))
    parts[0, 0], parts[1, 0] = part0, within(part1, 1)
    return call(
        functools.partial(project_kernel, list(parts)), place, (*parts.values(), out_weight), (1,),
        [whole(x.shape) for x in parts.values()] + [whole((width, width))],
        [(whole((TOK, width)), jax.ShapeDtypeStruct((TOK, width), BF16))],
        [pltpu.VMEM((width, TOK), BF16)],
        1 << 18,
    )[0]


def shards(queries, key_states, value_states, offsets_mid, offsets_top, out_weight):
    tokens, width = queries.shape
    heads = offsets_mid.shape[0]
    fits = (
        lax.axis_size("head") == 1
        and lax.axis_size("seq") == GROUP * RATE
        and tokens == TOK
        and heads == GROUP * HG
        and width == heads * DH
    )
    run = shards_four if fits else shards_general
    return run(queries, key_states, value_states, offsets_mid, offsets_top, out_weight)


def solution(mesh):
    in_specs = (
        P(("slide", "seq"), "head"),
        P(("slide", "seq"), "head"),
        P(("slide", "seq"), "head"),
        P(),
        P(),
        P("head", None),
    )
    out_specs = P(("slide", "seq", "head"), None)
    return jax.shard_map(shards, mesh=mesh, in_specs=in_specs, out_specs=out_specs, check_vma=False)
```

```python
import functools

import jax
import jax.numpy as jnp
from jax import lax
from jax.experimental import pallas as pl
from jax.experimental.pallas import tpu as pltpu
from jax.sharding import PartitionSpec as P

SEG = 2048
LOG2E = 1.4426950408889634
VMEM_LIMIT = 40 * 1024 * 1024
VMEM_MOST = 60 * 1024 * 1024
BF16 = jnp.bfloat16
F32 = jnp.float32


def partner_2(block, axis, apart):
    count = lax.axis_size(axis)
    route = []
    for low in range(count):
        high = low | 1 << apart
        if high != low and high < count:
            route += [(low, high), (high, low)]
    return lax.ppermute(block, axis, route)


def attend_head(triple_in):
    query_rows, key_rows, value_rows = triple_in
    score_scale = query_rows.shape[-1] ** (-0.5)
    scores = jnp.dot(query_rows, key_rows.T, preferred_element_type=jnp.float32) * score_scale
    row_max = jnp.max(scores, axis=1)
    shifted = jnp.exp(scores - row_max[:, None])
    row_total = jnp.sum(shifted, axis=1)
    weights = shifted.astype(jnp.bfloat16)
    numerator = jnp.dot(weights, value_rows, preferred_element_type=jnp.float32)
    return (numerator, row_total, row_max)


def attend_local(query_rows, pair_rows):
    return lax.map(
        attend_head,
        (
            query_rows.transpose(1, 0, 2),
            pair_rows[:, 0].transpose(1, 0, 2),
            pair_rows[:, 1].transpose(1, 0, 2),
        ),
    )


def pick_rows(states, offsets, rate):
    row_count, inner_count, heads_here, head_width = states.shape
    picker = (jnp.arange(rate)[:, None] == offsets[None, :]).astype(jnp.bfloat16)
    folded = states.reshape(row_count // rate, rate, inner_count, heads_here, head_width)
    return jnp.einsum("archd,rh->achd", folded, picker, preferred_element_type=jnp.float32).astype(
        jnp.bfloat16
    )


def spread_back(numerator, row_total, row_max, offsets, rate):
    heads_here, picked_count, head_width = numerator.shape
    chosen = jnp.arange(rate)[:, None] == offsets[None, :]
    full_num = jnp.where(chosen[None, :, :, None], numerator.transpose(1, 0, 2)[:, None], 0.0)
    full_total = jnp.where(chosen[None], row_total.T[:, None], 0.0)
    full_max = jnp.where(chosen[None], row_max.T[:, None], -1e30)
    return (
        full_num.reshape(picked_count * rate, heads_here, head_width),
        full_total.reshape(picked_count * rate, heads_here),
        full_max.reshape(picked_count * rate, heads_here),
    )


def doubling(buffer, steps_count):
    position = lax.axis_index("seq")
    for bit_index in range(steps_count):
        partner = partner_2(buffer, "seq", bit_index)
        is_lower = position >> bit_index & 1 == 0
        buffer = jnp.where(
            is_lower, jnp.concatenate([buffer, partner], 0), jnp.concatenate([partner, buffer], 0)
        )
    return buffer


def shards_general(queries, key_states, value_states, offsets_mid, offsets_top, out_weight):
    tok_rows = queries.shape[0]
    heads_local = offsets_mid.shape[0] // lax.axis_size("head")
    head_size = queries.shape[1] // heads_local
    seq_devices = lax.axis_size("seq")
    seq_total = tok_rows * seq_devices
    width_mid = min(16 * SEG, seq_total)
    rate_mid = width_mid // SEG
    rate_top = seq_total // SEG
    start_head = lax.axis_index("head") * heads_local
    mid_local = lax.dynamic_slice(offsets_mid, (start_head,), (heads_local,))
    top_local = lax.dynamic_slice(offsets_top, (start_head,), (heads_local,))
    query_heads = queries.reshape(tok_rows, 1, heads_local, head_size)
    paired = jnp.stack([key_states, value_states], axis=1).reshape(
        tok_rows, 2, heads_local, head_size
    )
    near_bits = (SEG // tok_rows).bit_length() - 1
    near_rows = doubling(paired.reshape(tok_rows, -1), near_bits).reshape(
        SEG, 2, heads_local, head_size
    )
    near_num, near_total, near_max = attend_local(query_heads[:, 0], near_rows)
    level_near = spread_back(
        near_num, near_total, near_max, jnp.zeros((heads_local,), jnp.int32), 1
    )
    mid_q = pick_rows(query_heads, mid_local, rate_mid)[:, 0]
    mid_kv = pick_rows(paired, mid_local, rate_mid)
    mid_group = width_mid // tok_rows
    mid_bits = mid_group.bit_length() - 1
    mid_rows = doubling(mid_kv.reshape(mid_kv.shape[0], -1), mid_bits).reshape(
        SEG, 2, heads_local, head_size
    )
    mid_num, mid_total, mid_max = attend_local(mid_q, mid_rows)
    level_mid = spread_back(mid_num, mid_total, mid_max, mid_local, rate_mid)
    top_q = pick_rows(query_heads, top_local, rate_top)[:, 0]
    top_kv = pick_rows(paired, top_local, rate_top)
    top_rows = lax.all_gather(
        top_kv.reshape(top_kv.shape[0], -1), "seq", axis=0, tiled=True
    ).reshape(SEG, 2, heads_local, head_size)
    top_num, top_total, top_max = attend_local(top_q, top_rows)
    level_top = spread_back(top_num, top_total, top_max, top_local, rate_top)
    levels = [level_near, level_mid, level_top]
    overall = jnp.maximum(jnp.maximum(level_near[2], level_mid[2]), level_top[2])
    numerator = jnp.zeros((tok_rows, heads_local, head_size), jnp.float32)
    row_total = jnp.zeros((tok_rows, heads_local), jnp.float32)
    for level_num, level_total, level_max in levels:
        factor = jnp.exp(level_max - overall)
        numerator = numerator + factor[..., None] * level_num
        row_total = row_total + factor * level_total
    attention = (
        (numerator / row_total[..., None])
        .astype(jnp.bfloat16)
        .reshape(tok_rows, heads_local * head_size)
    )
    result = lax.psum_scatter(
        jnp.dot(attention, out_weight, preferred_element_type=jnp.float32),
        "head",
        scatter_dimension=0,
        tiled=True,
    )
    return result.astype(jnp.bfloat16)


RATE = 4
GROUP = 4
HG = 4
DH = 48
BLK = 128
HALF = 2 * BLK
TOK = 512
SCALE = DH**-0.5 * LOG2E
BUSY = 1 << 33
AHEAD = 8
SAFE = 96.0
CHUNKS = ((0, 2), (2, 2))
DX = 64


def dot(a, b):
    return jnp.dot(a, b, preferred_element_type=F32)


def dot_nt(a, b):
    return lax.dot_general(a, b, (((1,), (1,)), ((), ())), preferred_element_type=F32)


def class_of_slots(off_mid, off_top):
    first = off_mid
    second = jnp.where(off_top == off_mid, lax.rem(off_mid + 1, RATE), off_top)
    free0 = (first != 0) & (second != 0)
    free1 = (first != 1) & (second != 1)
    third = jnp.where(free0, 0, jnp.where(free1, 1, 2))
    return first, second, third, 6 - first - second - third


def head_of(place, j, p):
    index = place[0][0]
    return ((index & (GROUP - 1)) ^ j) * HG + ((index // GROUP) ^ p)


def offsets_of(place, head):
    return place[1][head], place[2][head]


def token_picker():
    row = lax.broadcasted_iota(jnp.int32, (TOK, TOK), 0)
    col = lax.broadcasted_iota(jnp.int32, (TOK, TOK), 1)
    return (col == RATE * (row % BLK) + row // BLK).astype(BF16)


def fill_class_major(block, picker, scratch):
    scratch[...] = lax.dot_general(
        block, picker, (((0,), (1,)), ((), ())), preferred_element_type=F32
    ).astype(BF16)


def lane_block(index):
    return pl.ds(pl.multiple_of(index * BLK, BLK), BLK)


def head_rows(head):
    return pl.ds(pl.multiple_of(head * DH, 16), DH)


def pack_kernel(index, mid, top, k_hbm, v_hbm, q_hbm, *refs):
    place = (index, mid, top)
    outs, refs = refs[:6], refs[6:]
    blocks, held, packed = refs[:3], refs[3:6], refs[6:12]
    sems_in, sems_out = refs[12:]
    loads = [
        [
            pltpu.make_async_copy(hbm.at[rows], block.at[rows], sems_in.at[i, n])
            for n, rows in enumerate((slice(0, HALF), slice(HALF, TOK)))
        ]
        for i, (hbm, block) in enumerate(zip((k_hbm, v_hbm, q_hbm), blocks))
    ]
    for pair in loads:
        for load in pair:
            load.start()
    picker = token_picker()
    stores = []
    heads = {(j, p): head_of(place, j, p) for j in range(GROUP) for p in range(HG)}
    classes = {at: class_of_slots(*offsets_of(place, head)) for at, head in heads.items()}
    for n, (load, block, scratch) in enumerate(zip(loads, blocks, held)):
        for half in load:
            half.wait()
        fill_class_major(block[...], picker, scratch)
        rows = slice(n * DH, (n + 1) * DH)
        for i, (j, first, count) in enumerate(
            ((0, 0, 4), (1, 0, 4), (2, 0, 2), (3, 0, 2), (2, 2, 2), (3, 2, 2))
        ):
            for p in range(HG):
                for s in range(count):
                    packed[i][p, rows, s * BLK : (s + 1) * BLK] = scratch[
                        head_rows(heads[j, p]), lane_block(classes[j, p][first + s])
                    ]
            store = pltpu.make_async_copy(
                packed[i].at[:, rows], outs[i].at[:, rows], sems_out.at[i, n]
            )
            store.start()
            stores.append(store)
    for store in stores:
        store.wait()


def regroup_kernel(a_ref, b_ref, *refs):
    for s, out in enumerate(refs[-3:]):
        out[0] = a_ref[s + 1, :, 0:HALF]
        out[1] = b_ref[s + 1, :, 0:HALF]


def upright(keys_t):
    return keys_t.T


def largest(blocks):
    best = None
    for block in blocks:
        wide = block.astype(F32)
        length = jnp.sum(wide * wide, axis=0, keepdims=True)
        for low in range(0, block.shape[1], HALF):
            part = length[:, low : low + HALF]
            best = part if best is None else jnp.maximum(best, part)
    return jnp.max(best)


def is_small(query_length, key_length):
    return query_length * key_length * (SCALE * SCALE) < SAFE * SAFE


def column_max(blocks):
    best = jnp.max(blocks[0], axis=0, keepdims=True)
    for block in blocks[1:]:
        best = jnp.maximum(best, jnp.max(block, axis=0, keepdims=True))
    return best * SCALE


def in_stages(items, score, weigh, gather):
    scores = {n: score(item) for n, item in enumerate(items[:AHEAD])}
    weights = weigh(items[0], scores.pop(0))
    for n, item in enumerate(items):
        if n + AHEAD < len(items):
            scores[n + AHEAD] = score(items[n + AHEAD])
        following = weigh(items[n + 1], scores.pop(n + 1)) if n + 1 < len(items) else None
        gather(item, weights)
        weights = following


def near_kernel(inputs, units, tasks, carried, first, step, index, mid, top, *refs):
    place = (index, mid, top)
    pieces = dict(zip(inputs, refs[: len(inputs)]))
    refs = refs[len(inputs) :]
    old = [refs[2 * i : 2 * i + 2] for i in range(carried)]
    outs = refs[2 * carried : 2 * carried + 2 * len(tasks)]
    k_s, v_s = refs[-2:]
    v_s[:, DH:DX, :] = jnp.ones((step, DX - DH, v_s.shape[2]), BF16)
    lane_slot = lax.broadcasted_iota(jnp.int32, (1, HALF), 1) // BLK

    def lookup(j, slot):
        first = 0 if (j, 0) in pieces and pieces[j, 0].shape[2] > HALF else slot // 2 * 2
        return pieces[j, first], (slot - first) * BLK

    chunks = []
    row = 0
    for label, members in units:
        chunks.append((label, slice(row, row + len(members) * BLK)))
        row += len(members) * BLK
    members = [member for _, group in units for member in group]

    def prepare(h):
        for i, (j, slot) in enumerate(members):
            ref, lane = lookup(j, slot)
            rows = slice(i * BLK, (i + 1) * BLK)
            k_s[h, rows, :] = upright(ref[h, 0:DH, lane : lane + BLK])
            v_s[h, 0:DH, rows] = ref[h, DH : 2 * DH, lane : lane + BLK]

    def counted_again(h):
        off_mid, off_top = offsets_of(place, head_of(place, 0, first + pl.program_id(0) * step + h))
        same = off_mid == off_top
        return [
            jnp.where(lane_slot == 0, jnp.where(same, 1.584962500721156, 1.0), 0.0),
            jnp.where(lane_slot == 1, jnp.where(same, 0.0, 1.0), 0.0),
        ]

    def run(heads):
        again = [counted_again(h) for h in heads]
        flat = [
            (h, again_h, query, low, merge, out, i)
            for h, again_h in zip(heads, again)
            for out, group in enumerate(tasks)
            for i, (query, low, merge) in enumerate(group)
        ]

        def score(task):
            h, _, (j, half), low = task[:4]
            ref, lane = lookup(j, 2 * half)
            query = ref[h, 2 * DH :, lane : lane + HALF]
            return [dot(k_s[h, rows, :], query) for _, rows in chunks[low:]]

        scores = score(flat[0])
        for n, (h, again_h, (_, half), low, merge, out, i) in enumerate(flat):
            following = score(flat[n + 1]) if n + 1 < len(flat) else None
            best = column_max(scores)
            if merge is not None:
                acc_in, max_in = old[merge[0]]
                old_max = max_in[h, merge[1], 0:1, :]
                best = jnp.maximum(best, old_max)
            acc = None
            for (label, rows), block in zip(chunks[low:], scores):
                block = block * SCALE
                if half == 0 and label is not None:
                    block = block - (best - again_h[label])
                else:
                    block = block - best
                part = dot(v_s[h, :, rows], jnp.exp2(block).astype(BF16))
                acc = part if acc is None else acc + part
            if merge is not None:
                acc = acc + acc_in[h, merge[1]] * jnp.exp2(old_max - best)
            acc_ref, max_ref = outs[2 * out : 2 * out + 2]
            acc_ref[h, i] = acc
            max_ref[h, i] = jnp.broadcast_to(best, (8, HALF))
            scores = following

    def run_plain():
        again = [counted_again(h) for h in range(step)]
        steps = [
            (h, query, merge, out, i, c, c == low, c == len(chunks) - 1)
            for h in range(step)
            for out, group in enumerate(tasks)
            for i, (query, low, merge) in enumerate(group)
            for c in range(low, len(chunks))
        ]

        def score(item):
            h, (j, half), c = item[0], item[1], item[5]
            ref, lane = lookup(j, 2 * half)
            return dot(k_s[h, chunks[c][1], :], ref[h, 2 * DH :, lane : lane + HALF])

        def weigh(item, block):
            h, (_, half), c = item[0], item[1], item[5]
            label = chunks[c][0]
            block = block * SCALE
            if half == 0 and label is not None:
                block = block + again[h][label]
            return jnp.exp2(block).astype(BF16)

        held = {}

        def gather(item, weights):
            h, _, merge, out, i, c, begins, ends = item
            part = dot(v_s[h, :, chunks[c][1]], weights)
            acc = part if begins else held[0] + part
            if ends:
                if merge is not None:
                    acc = acc + old[merge[0]][0][h, merge[1]]
                acc_ref, max_ref = outs[2 * out : 2 * out + 2]
                acc_ref[h, i] = acc
                max_ref[h, i] = jnp.zeros((8, HALF), F32)
            held[0] = acc

        in_stages(steps, score, weigh, gather)

    for h in range(step):
        prepare(h)
    plain = is_small(
        largest([ref[h, 2 * DH :, :] for ref in pieces.values() for h in range(step)]),
        largest([ref[h, 0:DH, :] for ref in pieces.values() for h in range(step)]),
    )
    for _, max_in in old:
        plain = plain & (jnp.max(jnp.abs(max_in[...])) == 0.0)

    @pl.when(plain)
    def _():
        run_plain()

    @pl.when(jnp.logical_not(plain))
    def _():
        @pl.loop(0, step)
        def _(h):
            run([h])


def far_slots(place):
    off_mid, off_top = offsets_of(place, head_of(place, 0, 0))
    same = off_mid == off_top
    return same, (0, jnp.where(same, 0, 1))


def far_pieces(place, sources, k_s, v_s, q_s):
    _, slots = far_slots(place)
    for s, pair in enumerate(sources):
        for i, ref in enumerate(pair):
            here = slice(i * BLK, (i + 1) * BLK)
            for level, slot in enumerate(slots):
                k_s[level, s, here, :] = upright(ref[0:DH, lane_block(slot)])
                v_s[level, s, 0:DH, here] = ref[DH : 2 * DH, lane_block(slot)]
                q_s[level, s, :, here] = ref[2 * DH : 3 * DH, lane_block(slot)]
    v_s[:, :, DH:DX, :] = jnp.ones((2, RATE, DX - DH, HALF), BF16)


def far_lengths(sources):
    every = [ref for pair in sources for ref in pair]
    return (
        largest([ref[2 * DH : 3 * DH, 0:HALF] for ref in every]),
        largest([ref[0:DH, 0:HALF] for ref in every]),
    )


def far_own_kernel(index, mid, top, own0, own1, beyond3, beyond2, beyond1, *refs):
    k_s, v_s, q_s, acc_ref, max_ref, length_ref = refs
    sources = [(own0.at[0], own1.at[0])] + [
        (ref.at[0], ref.at[1]) for ref in (beyond1, beyond2, beyond3)
    ]
    far_pieces((index, mid, top), sources, k_s, v_s, q_s)

    def run_plain():
        steps = [(level, d) for level in range(2) for d in range(1, RATE)]

        def segment(s, carry):
            def score(item):
                level, d = item
                return dot(k_s[level, s ^ d], q_s[level, s])

            def weigh(item, block):
                return jnp.exp2(block * SCALE).astype(BF16)

            held = {}

            def gather(item, weights):
                level, d = item
                part = dot(v_s[level, s ^ d], weights)
                held[0] = part if d == 1 else held[0] + part
                if d == RATE - 1:
                    acc_ref[level, s] = held[0]
                    max_ref[level, s] = jnp.zeros((8, HALF), F32)

            in_stages(steps, score, weigh, gather)
            return carry

        lax.fori_loop(0, RATE, segment, 0, unroll=RATE)

    def run():
        def segment(s, carry):
            def score(level):
                return [dot(k_s[level, s ^ d], q_s[level, s]) for d in range(1, RATE)]

            scores = score(0)
            for level in range(2):
                following = score(1) if level == 0 else None
                best = column_max(scores)
                acc = None
                for d in range(1, RATE):
                    block = scores[d - 1] * SCALE - best
                    part = dot(v_s[level, s ^ d], jnp.exp2(block).astype(BF16))
                    acc = part if acc is None else acc + part
                acc_ref[level, s] = acc
                max_ref[level, s] = jnp.broadcast_to(best, (8, HALF))
                scores = following
            return carry

        lax.fori_loop(0, RATE, segment, 0)

    query_length, key_length = far_lengths(sources)
    length_ref[0] = query_length
    length_ref[1] = key_length
    plain = is_small(query_length, key_length)
    pl.when(plain)(run_plain)
    pl.when(jnp.logical_not(plain))(run)


def near_and_far_kernel(near_args, steps, index, mid, top, *refs):
    scalars = (index, mid, top)
    inputs, tasks, carried = near_args[0], near_args[2], near_args[3]
    count = len(inputs) + 2 * carried
    near_in, far_in, refs = refs[:count], refs[count : count + 5], refs[count + 5 :]
    near_out, far_out, scratch = refs[: 2 * len(tasks)], refs[2 * len(tasks) : -2], refs[-2:]

    @pl.when(pl.program_id(0) < steps)
    def _():
        near_kernel(*near_args, *scalars, *near_in, *near_out, *scratch)

    @pl.when(pl.program_id(0) == steps)
    def _():
        far_own_kernel(*scalars, *far_in, *far_out)


def far_kernel(index, mid, top, *refs):
    place = (index, mid, top)
    sel2, sel3, beyond2, beyond1, beyond3, k_own, v_own, q_own, acc_in, max_in, length_in = refs[
        :11
    ]
    outs = refs[11 : 11 + RATE]
    k_s, v_s, q_s, result_s, tail_s = refs[11 + RATE :]
    same, _ = far_slots(place)
    sources = [(sel2.at[0], sel3.at[0])] + [
        (ref.at[0], ref.at[1]) for ref in (beyond1, beyond2, beyond3)
    ]
    far_pieces(place, sources, k_s, v_s, q_s)
    tail_s[...] = jnp.zeros(tail_s.shape, F32)

    tasks = [(level, chip) for level in range(2) for chip in range(2)]
    held = ((k_own, v_own, q_own), (k_s, v_s, q_s))

    def blocks(s, chip):
        return [(held[c], s ^ d) for d in range(1, RATE) for c in ((1,), (0, 1))[chip]]

    def finish(s, level, chip, acc, best):
        total = acc[DH : DH + 1, :]
        result = (acc[0:DH, :] / total).astype(BF16)
        lse = best + jnp.log2(total)
        if level == 0:
            lse = jnp.where(same, lse + 1.0, lse)
        else:
            lse = jnp.where(same, -1e30, lse)
        high = lse.astype(BF16).astype(F32)
        middle = (lse - high).astype(BF16).astype(F32)
        low = lse - high - middle
        for i in range(2):
            n = 2 * (2 * chip + i) + level
            mine = slice(i * BLK, (i + 1) * BLK)
            result_s[s, :, n * BLK : (n + 1) * BLK] = result[:, mine]
            for k, part in enumerate((high, middle, low)):
                tail_s[s, 3 * n + k : 3 * n + k + 1, :] = part[:, mine]

    def run_plain():
        def segment(s, carry):
            steps = [
                (level, chip, keys, b, n)
                for level, chip in tasks
                for n, (keys, b) in enumerate(blocks(s, chip))
            ]

            def score(item):
                level, chip, keys, b, _ = item
                return dot(keys[0][level, b], held[chip][2][level, s])

            def weigh(item, block):
                return jnp.exp2(block * SCALE).astype(BF16)

            sums = {}

            def gather(item, weights):
                level, chip, keys, b, n = item
                part = dot(keys[1][level, b], weights)
                sums[0] = sums[0] + part if n else part
                if n + 1 == len(blocks(s, chip)):
                    acc = sums[0] + acc_in[level, s] if chip == 0 else sums[0]
                    finish(s, level, chip, acc, jnp.zeros((1, HALF), F32))

            in_stages(steps, score, weigh, gather)
            return carry

        lax.fori_loop(0, RATE, segment, 0, unroll=RATE)

    def run():
        def segment(s, carry):
            for level, chip in tasks:
                scores = [
                    dot(keys[0][level, b], held[chip][2][level, s]) for keys, b in blocks(s, chip)
                ]
                best = column_max(scores)
                acc = jnp.zeros((DX, HALF), F32)
                if chip == 0:
                    old_max = max_in[level, s, 0:1, :]
                    best = jnp.maximum(best, old_max)
                    acc = acc_in[level, s] * jnp.exp2(old_max - best)
                for block, (keys, b) in zip(scores, blocks(s, chip)):
                    acc += dot(keys[1][level, b], jnp.exp2(block * SCALE - best).astype(BF16))
                finish(s, level, chip, acc, best)
            return carry

        lax.fori_loop(0, RATE, segment, 0)

    query_length, key_length = far_lengths(sources)
    plain = is_small(
        jnp.maximum(query_length, length_in[0]), jnp.maximum(key_length, length_in[1])
    )
    pl.when(plain)(run_plain)
    pl.when(jnp.logical_not(plain))(run)
    for s in range(RATE):
        outs[s][:, : GROUP * HALF] = result_s[s]
        outs[s][:, GROUP * HALF :] = tail_s[s].astype(BF16)


def join(acc, best, far, j):
    tail = far[:, GROUP * HALF :].astype(F32)
    lse = jnp.concatenate(
        [
            tail[3 * n : 3 * n + 1] + tail[3 * n + 1 : 3 * n + 2] + tail[3 * n + 2 : 3 * n + 3]
            for n in (2 * j, 2 * j + 1)
        ],
        axis=1,
    )
    overall = jnp.maximum(best, lse)
    near_factor, far_factor = jnp.exp2(best - overall), jnp.exp2(lse - overall)
    total = acc[DH : DH + 1] * near_factor + far_factor
    value = far[:, j * HALF : (j + 1) * HALF].astype(F32) * far_factor
    return ((acc[0:DH] * near_factor + value) / total).astype(BF16)


def combine_kernel(chip, acc_ref, max_ref, *refs):
    far, outs = refs[:-2][::-1], refs[-2:]
    for i in range(2):
        for p, results in enumerate(far):
            outs[i][p, :, 0:HALF] = join(
                acc_ref[p, 2 * i], max_ref[p, 2 * i, 0:1, :], results, 2 * chip + i
            )
            acc = acc_ref[p, 2 * i + 1]
            outs[i][p, :, HALF:] = (acc[0:DH] / acc[DH : DH + 1]).astype(BF16)


def last_own_kernel(inputs, units, tasks, index, mid, top, *refs):
    count = len(inputs) + 2
    near_refs, far, outs, scratch = refs[:count], refs[count:-6], refs[-6:-4], refs[-4:]
    acc_s, max_s, k_s, v_s = scratch
    near_kernel(
        inputs, units, tasks, 1, 0, HG, index, mid, top, *near_refs, acc_s, max_s, k_s, v_s
    )
    combine_kernel(0, acc_s, max_s, *far, *outs)


def project_kernel(sources, index, mid, top, *refs):
    place = (index, mid, top)
    parts, (w_ref, out_ref, held) = refs[:-3], refs[-3:]
    for (j, first), part in zip(sources, parts):
        for p in range(part.shape[0]):
            head = head_of(place, j, first + p)
            slots = class_of_slots(*offsets_of(place, head))
            for s in range(RATE):
                held[head_rows(head), lane_block(slots[s])] = part[
                    p, :, s * BLK : (s + 1) * BLK
                ]
    row = lax.broadcasted_iota(jnp.int32, (TOK, TOK), 0)
    col = lax.broadcasted_iota(jnp.int32, (TOK, TOK), 1)
    picker = (row == RATE * (col % BLK) + col // BLK).astype(BF16)
    attention = dot_nt(picker, held[...]).astype(BF16)
    out_ref[...] = dot(attention, w_ref[...]).astype(BF16)


def whole(shape):
    return pl.BlockSpec(shape, lambda *_: (0,) * len(shape))


def per_head(shape, skip=0, last=None):
    def index(h, *_):
        at = h + skip if last is None else jnp.minimum(h, last)
        return (at,) + (0,) * (len(shape) - 1)

    return pl.BlockSpec(shape, index)


def call(
    kernel, scalars, args, grid, in_specs, outs, scratch, scores,
    limit=VMEM_LIMIT, after=(), through=(), busy=0,
):
    known = len(scalars) + len(args)
    extra = (*after, *through)
    count = len(outs)
    anywhere = pl.BlockSpec(memory_space=pl.ANY)

    def body(*refs):
        results = refs[known + len(extra) :]
        kernel(*refs[:known], *results[:count], *results[count + len(through) :])

    return pl.pallas_call(
        body if extra else kernel,
        grid_spec=pltpu.PrefetchScalarGridSpec(
            num_scalar_prefetch=len(scalars),
            grid=grid,
            in_specs=list(in_specs) + [anywhere] * len(extra),
            out_specs=[spec for spec, _ in outs] + [anywhere] * len(through),
            scratch_shapes=scratch,
        ),
        out_shape=[shape for _, shape in outs]
        + [jax.ShapeDtypeStruct(x.shape, x.dtype) for x in through],
        input_output_aliases={known + len(after) + i: count + i for i in range(len(through))},
        compiler_params=pltpu.CompilerParams(vmem_limit_bytes=limit),
        cost_estimate=pl.CostEstimate(flops=busy, bytes_accessed=0, transcendentals=0),
    )(*scalars, *args, *extra)


def handed_on(arrays, **order):
    return call(lambda: None, (), (), (1,), [], [], [], 0, through=tuple(arrays), **order)


def within(array, apart):
    count = lax.axis_size("seq")
    return lax.ppermute(array, "seq", [(i, i ^ apart) for i in range(count)])


def swap_segments(arrays):
    moved = {s: within(arrays[s - 1], GROUP * s) for s in (3, 2, 1)}
    return [moved[s] for s in (1, 2, 3)]


def shards_four(queries, key_states, value_states, offsets_mid, offsets_top, out_weight):
    width = queries.shape[1]
    place = (lax.axis_index("seq").astype(jnp.int32).reshape(1), offsets_mid, offsets_top)
    full = jax.ShapeDtypeStruct((HG, 3 * DH, TOK), BF16)
    piece = jax.ShapeDtypeStruct((HG, 3 * DH, HALF), BF16)
    pair = jax.ShapeDtypeStruct((2, 3 * DH, HALF), BF16)
    anywhere = pl.BlockSpec(memory_space=pl.ANY)
    shapes = [full] * 2 + [piece] * 4
    own0, own1, sel2, sel3, rest2, rest3 = call(
        pack_kernel, place, (key_states, value_states, queries), (1,),
        [anywhere] * 3,
        [(anywhere, shape) for shape in shapes],
        [pltpu.VMEM((TOK, width), BF16)] * 3
        + [pltpu.VMEM((width, TOK), BF16)] * 3
        + [pltpu.VMEM(shape.shape, BF16) for shape in shapes]
        + [pltpu.SemaphoreType.DMA((3, 2)), pltpu.SemaphoreType.DMA((6, 3))],
        1 << 19, VMEM_MOST,
    )
    own1 = within(own1, 1)
    sel2, sel3 = within(sel2, 2), within(sel3, 3)

    def regroup(a, b, **order):
        return call(
            regroup_kernel, (), (a, b), (1,),
            [whole(a.shape), whole(b.shape)], [(whole(pair.shape), pair)] * 3,
            [], 1 << 17, **order,
        )

    def near(held, units, tasks, old, first=0, heads=HG, step=2, **order):
        sizes = [len(members) * BLK for _, members in units]
        scores = sum(sum(sizes[low:]) * HALF for group in tasks for _, low, _ in group)
        arrays = [*held.values(), *[x for one in old for x in one]]
        shapes = [
            jax.ShapeDtypeStruct((heads, len(group), rows, HALF), F32)
            for group in tasks
            for rows in (DX, 8)
        ]
        return call(
            functools.partial(near_kernel, list(held), units, tasks, len(old), first, step),
            place, arrays, (heads // step,),
            [per_head((step,) + x.shape[1:], first // step) for x in arrays],
            [(per_head((step,) + x.shape[1:]), x) for x in shapes],
            [
                pltpu.VMEM((step, sum(sizes), DH), BF16),
                pltpu.VMEM((step, DX, sum(sizes)), BF16),
            ],
            heads * scores, **order,
        )

    def units_of(a, b):
        return [(0, [(a, 0), (b, 0)]), (1, [(a, 1), (b, 1)])], [
            (None, [(a, 2), (a, 3), (b, 2), (b, 3)])
        ]

    own_sel, own_rest = units_of(0, 1)
    other_sel, other_rest = units_of(2, 3)
    own = [(0, 0), (0, 1), (1, 0), (1, 1)]

    ours = regroup(own0, own1)
    ours = swap_segments(ours)
    held = {(0, 0): own0, (1, 0): own1}
    state_own = near(held, own_sel + own_rest, [[(q, 0, None) for q in own]], [], step=HG)
    *theirs, rest2, rest3 = regroup(sel2, sel3, after=state_own[1:], through=(rest2, rest3))
    theirs = swap_segments(theirs)
    rest2, rest3 = within(rest2, 2), within(rest3, 3)

    held.update({(2, 0): sel2, (3, 0): sel3})
    units = own_sel + own_rest + other_sel
    tasks = [
        [(q, 3, (0, i)) for i, q in enumerate(own)],
        [((2, 0), 0, None), ((3, 0), 0, None)],
    ]
    arrays = [*held.values(), *state_own]
    near_shapes = [
        jax.ShapeDtypeStruct((HG, len(group), rows, HALF), F32)
        for group in tasks
        for rows in (DX, 8)
    ]
    far_shapes = [
        jax.ShapeDtypeStruct((2, RATE, HALF, DH), BF16),
        jax.ShapeDtypeStruct((2, RATE, DX, HALF), BF16),
        jax.ShapeDtypeStruct((2, RATE, DH, HALF), BF16),
        jax.ShapeDtypeStruct((2, RATE, DX, HALF), F32),
        jax.ShapeDtypeStruct((2, RATE, 8, HALF), F32),
    ]
    piece_0 = pl.BlockSpec((1, 3 * DH, HALF), lambda *_: (0, 0, 0))
    in_scalars = pl.BlockSpec(memory_space=pltpu.SMEM)
    step, steps = 2, HG // 2
    keys = sum(len(members) for _, members in units) * BLK
    out = call(
        functools.partial(
            near_and_far_kernel, (list(held), units, tasks, 1, 0, step), steps
        ),
        place, (*arrays, own0, own1, *ours[::-1]), (steps + 1,),
        [per_head((step,) + x.shape[1:], last=steps - 1) for x in arrays]
        + [piece_0] * 2 + [whole(pair.shape)] * 3,
        [(per_head((step,) + x.shape[1:], last=steps - 1), x) for x in near_shapes]
        + [(whole(x.shape), x) for x in far_shapes]
        + [(in_scalars, jax.ShapeDtypeStruct((2,), F32))],
        [pltpu.VMEM((step, keys, DH), BF16), pltpu.VMEM((step, DX, keys), BF16)],
        1 << 18,
    )
    state_own, state_sel, far_own = out[:2], out[2:4], out[4:]

    result = jax.ShapeDtypeStruct((DH, GROUP * HALF + BLK), BF16)
    results = call(
        far_kernel, place, (sel2, sel3, theirs[1], theirs[0], theirs[2], *far_own), (1,),
        [piece_0] * 2 + [whole(pair.shape)] * 3
        + [whole(x.shape) for x in far_own[:-1]] + [in_scalars],
        [(whole(result.shape), result)] * RATE,
        [pltpu.VMEM(x.shape, BF16) for x in far_shapes[:3]]
        + [
            pltpu.VMEM((RATE, DH, GROUP * HALF), BF16),
            pltpu.VMEM((RATE, DH, BLK), F32),
        ],
        RATE * 2 * 3 * 3 * HALF * HALF, busy=BUSY,
    )
    back = [results[0]] + swap_segments(results[1:])

    held.update({(2, 2): rest2, (3, 2): rest3})
    units = own_sel + own_rest + other_sel + other_rest

    def combine(chip, state, far, **order):
        heads = state[0].shape[0]
        attended = jax.ShapeDtypeStruct((heads, DH, TOK), BF16)
        return call(
            functools.partial(combine_kernel, chip), (), (*state, *far[::-1]), (1,),
            [whole(x.shape) for x in state] + [whole(result.shape)] * heads,
            [(whole(attended.shape), attended)] * 2,
            [],
            1 << 18, **order,
        )

    parts, last = {}, results[0]
    for first, heads in CHUNKS:
        state_other = near(
            held, units,
            [
                [
                    ((2, 0), 5, (0, 0)), ((2, 1), 0, None),
                    ((3, 0), 5, (0, 1)), ((3, 1), 0, None),
                ]
            ],
            [state_sel],
            first, heads, 2, after=(last,),
        )
        if first:
            back[1:] = handed_on(back[1:], after=state_other[1:])
        part2, part3 = combine(1, state_other, back[first : first + heads])
        early = tuple(parts.values())
        parts[2, first], parts[3, first] = within(part2, 2), within(part3, 3)
        last = part3
    pieces = {(2, 2): rest2, (3, 2): rest3, **{q: held[q] for q in ((0, 0), (1, 0))}}
    arrays = [*pieces.values(), *state_own, *back[::-1]]
    attended = jax.ShapeDtypeStruct((HG, DH, TOK), BF16)
    part0, part1 = call(
        functools.partial(
            last_own_kernel, list(pieces), other_rest, [[(q, 0, (0, i)) for i, q in enumerate(own)]]
        ),
        place, arrays, (1,),
        [whole(x.shape) for x in arrays],
        [(whole(attended.shape), attended)] * 2,
        [pltpu.VMEM(x.shape, F32) for x in state_own]
        + [pltpu.VMEM((HG, TOK, DH), BF16), pltpu.VMEM((HG, DX, TOK), BF16)],
        HG * TOK * GROUP * HALF, after=(last, *early),
    )
    parts = dict(zip(parts, handed_on(parts.values(), busy=BUSY)))
    parts[0, 0], parts[1, 0] = part0, within(part1, 1)
    return call(
        functools.partial(project_kernel, list(parts)), place, (*parts.values(), out_weight), (1,),
        [whole(x.shape) for x in parts.values()] + [whole((width, width))],
        [(whole((TOK, width)), jax.ShapeDtypeStruct((TOK, width), BF16))],
        [pltpu.VMEM((width, TOK), BF16)],
        1 << 18,
    )[0]


def shards(queries, key_states, value_states, offsets_mid, offsets_top, out_weight):
    tokens, width = queries.shape
    heads = offsets_mid.shape[0]
    fits = (
        lax.axis_size("head") == 1
        and lax.axis_size("seq") == GROUP * RATE
        and tokens == TOK
        and heads == GROUP * HG
        and width == heads * DH
    )
    run = shards_four if fits else shards_general
    return run(queries, key_states, value_states, offsets_mid, offsets_top, out_weight)


def solution(mesh):
    in_specs = (
        P(("slide", "seq"), "head"),
        P(("slide", "seq"), "head"),
        P(("slide", "seq"), "head"),
        P(),
        P(),
        P("head", None),
    )
    out_specs = P(("slide", "seq", "head"), None)
    return jax.shard_map(shards, mesh=mesh, in_specs=in_specs, out_specs=out_specs, check_vma=False)
```
